32 devices in a mesh: seq: 8 (over z, x), head: 4 (over y, core).
Axes of the slice: x: 2, y: 2, z: 4, core: 2. Of those that a mesh axis runs over, the one named last changes fastest.
Arguments:
- queries: bfloat16 [2048, 512], P('seq', 'head'), may hold values from -16 to 16
- keys: bfloat16 [2048, 512], P('seq', 'head'), may hold values from -16 to 16
- values: bfloat16 [2048, 512], P('seq', 'head'), may hold values from -16 to 16
- out_weight: bfloat16 [512, 512], replicated, may hold values from -0.5 to 0.5
Outputs:
- mixed: bfloat16 [2048, 512], P(('seq', 'head'))
The draws below stay inside these ranges and needn't reach their ends.
All inputs are finite; a program needn't handle non-finite values.
Results may differ from the reference program's by a relative error of at most 0.00185.
The reference program's roundings to bfloat16 on the way count: a program that leaves them out, or rounds other values in their place, can miss the bound.
Values may be sent and summed in bfloat16 or wider, within the bound.
No kernel may reach another device: no remote copies, remote signals or barrier semaphores. Data moves between devices by JAX's collectives and lax.ppermute only.
A program may use at most 128 MiB of HBM per device.

```python
import math
import jax
import jax.numpy as jnp
from jax import lax

D = 512
HEADS = 8
HD = 64
LEAF = 128
TOKENS = 2048


def multiscale(key):
    levels = TOKENS.bit_length() - 1
    coarse_weight = (0.5 / levels) ** 0.5
    summed = jnp.zeros((TOKENS, D), jnp.float32)
    for scale_index in range(levels + 1):
        count_rows = TOKENS >> scale_index
        subkey = jax.random.fold_in(key, scale_index)
        piece = jnp.clip(jax.random.normal(subkey, (count_rows, D), jnp.float32), -3.5, 3.5)
        factor = 0.5 ** 0.5 if scale_index == 0 else coarse_weight
        summed = summed + factor * jnp.repeat(piece, 2 ** scale_index, axis=0)
    return summed


def draw_queries(key, part):
    result = multiscale(jax.random.fold_in(key, 11))
    return result.astype(jnp.bfloat16)


def draw_keys(key, part):
    result = multiscale(jax.random.fold_in(key, 12))
    return result.astype(jnp.bfloat16)


def draw_values(key, part):
    return multiscale(jax.random.fold_in(key, 13)).astype(jnp.bfloat16)


def noise(key, shape, width, reach, kind=jnp.bfloat16):
    entries = jax.random.normal(key, shape, jnp.float32) * width
    return jnp.minimum(jnp.maximum(entries, -reach), reach).astype(kind)


def setup_inputs(seed: int = 0) -> dict:
    key_list = jax.random.split(jax.random.key(seed), 5)
    queries = draw_queries(jax.random.fold_in(key_list[4], 71), 0)
    keys = draw_keys(jax.random.fold_in(key_list[4], 71), 0)
    values = draw_values(jax.random.fold_in(key_list[4], 71), 0)
    out_weight = noise(key_list[3], (D, D), (D // 4) ** -0.5, 0.5)
    return {"queries": queries, "keys": keys, "values": values, "out_weight": out_weight}


def average_pairs(rows_in):
    widened = rows_in.astype(jnp.float32).reshape(rows_in.shape[0] // 2, 2, rows_in.shape[1])
    return (0.5 * (widened[:, 0] + widened[:, 1])).astype(jnp.bfloat16)

def reference(queries, keys, values, out_weight):
    block_count = TOKENS // LEAF
    top_level = block_count.bit_length() - 1
    level_keys = [keys]
    level_values = [values]
    for level in range(1, top_level):
        level_keys.append(average_pairs(level_keys[-1]))
        level_values.append(average_pairs(level_values[-1]))
    padded_keys = [jnp.pad(arr, ((LEAF, LEAF), (0, 0))) for arr in level_keys]
    padded_values = [jnp.pad(arr, ((LEAF, LEAF), (0, 0))) for arr in level_values]
    positions = jnp.arange(LEAF, dtype=jnp.int32)
    upper_half = positions >= LEAF // 2
    scale = 1.0 / math.sqrt(HD)

    def one_block(block):
        start = (block * LEAF).astype(jnp.int32)
        key_parts = [lax.dynamic_slice_in_dim(padded_keys[0], start, 3 * LEAF, 0)]
        value_parts = [lax.dynamic_slice_in_dim(padded_values[0], start, 3 * LEAF, 0)]
        neighbour = block - 1 + jnp.arange(3 * LEAF, dtype=jnp.int32) // LEAF
        valid_parts = [(neighbour >= 0) & (neighbour < block_count)]
        for level in range(1, top_level):
            coarse_block = block >> level
            parity = block >> level - 1 & 1
            level_blocks = block_count >> level
            lower_start = (coarse_block * LEAF).astype(jnp.int32)
            upper_start = ((coarse_block + 2) * LEAF).astype(jnp.int32)
            key_parts.append(lax.dynamic_slice_in_dim(padded_keys[level], lower_start, LEAF, 0))
            key_parts.append(lax.dynamic_slice_in_dim(padded_keys[level], upper_start, LEAF, 0))
            value_parts.append(lax.dynamic_slice_in_dim(padded_values[level], lower_start, LEAF, 0))
            value_parts.append(lax.dynamic_slice_in_dim(padded_values[level], upper_start, LEAF, 0))
            valid_parts.append((coarse_block >= 1) & jnp.logical_not(upper_half & (parity == 0)))
            valid_parts.append((coarse_block + 1 < level_blocks) & jnp.logical_not(jnp.logical_not(upper_half) & (parity == 1)))
        key_set = jnp.concatenate(key_parts, axis=0)
        value_set = jnp.concatenate(value_parts, axis=0)
        valid = jnp.concatenate(valid_parts, axis=0)
        query_rows = lax.dynamic_slice_in_dim(queries, start, LEAF, 0).astype(jnp.float32).reshape(LEAF, HEADS, HD)
        key_heads = key_set.astype(jnp.float32).reshape(-1, HEADS, HD)
        value_heads = value_set.astype(jnp.float32).reshape(-1, HEADS, HD)
        scores = jnp.einsum('qhd,khd->hqk', query_rows, key_heads) * scale
        scores = jnp.where(valid[None, None, :], scores, -jnp.inf)
        peak = lax.optimization_barrier(jnp.max(scores, axis=-1, keepdims=True))
        weights = jnp.exp(scores - peak)
        total = lax.optimization_barrier(jnp.sum(weights, axis=-1))
        rounded = lax.optimization_barrier(weights.astype(jnp.bfloat16)).astype(jnp.float32)
        numer = jnp.einsum('hqk,khd->hqd', rounded, value_heads)
        attended = (numer / total[..., None]).astype(jnp.bfloat16)
        return attended.transpose(1, 0, 2).reshape(LEAF, D)
    blocks = jnp.arange(block_count, dtype=jnp.int32)
    attended = lax.map(one_block, blocks, batch_size=4).reshape(TOKENS, D)
    return jnp.dot(attended, out_weight, preferred_element_type=jnp.float32).astype(jnp.bfloat16)
```

```python
import functools
import math

import jax
import jax.numpy as jnp
from jax import lax
from jax.experimental import pallas as pl
from jax.experimental.pallas import tpu as pltpu
from jax.sharding import PartitionSpec as P

HD = 64
LEAF = 128
HALF = LEAF // 2
NEG = -math.inf


def average_pairs(rows, wide):
    count = rows.shape[0]
    halves = []
    for low in range(0, rows.shape[1], LEAF):
        wide[:count] = rows[:, low : low + LEAF].astype(jnp.float32)
        even = wide[pl.ds(0, count // 2, stride=2), :]
        odd = wide[pl.ds(1, count // 2, stride=2), :]
        halves.append((0.5 * (even + odd)).astype(jnp.bfloat16))
    return jnp.concatenate(halves, axis=1)


def pack_kernel(keys, values, pair, quarter, wide):
    width = keys.shape[1]
    pair[:, :width] = keys[...]
    pair[:, width:] = values[...]
    level_two = average_pairs(average_pairs(pair[...], wide), wide)
    for peer in range(quarter.shape[0]):
        quarter[peer] = level_two


def segments(seq_size):
    far_count = seq_size.bit_length() - 2
    rows = []
    for far in range(1, far_count + 1):
        if seq_size >> far == 2:
            rows.append(LEAF)
        elif far == 1:
            rows.append(3 * HALF)
        else:
            rows.append(2 * LEAF)
    return rows


def attend_kernel(seq_size, queries, own, before, after, far_rows, attended, key_set, wide):
    me = lax.axis_index("seq")
    width = queries.shape[1]
    zero, neg = jnp.float32(0.0), jnp.float32(NEG)

    def bias_of(valid):
        return jnp.where(valid, zero, neg)

    coarse_before = average_pairs(before[...], wide)
    coarse_after = average_pairs(after[...], wide)
    has_before, has_after = bias_of(me >= 1), bias_of(me + 1 < seq_size)

    far_pieces = []
    for far, _ in enumerate(segments(seq_size), 1):
        span = 1 << far
        group = me >> far
        parity = (me >> (far - 1)) & 1
        blocks = seq_size >> far

        def block(number, span=span, far=far):
            found = far_rows[pl.ds(number * span, span)].reshape(span * HALF, 2 * width)
            for _ in range(far - 1):
                found = average_pairs(found, wide)
            return found

        if blocks == 2:
            rows = block(1 - group)
            first = bias_of((group == 1) | (parity == 0))
            second = bias_of((group == 0) | (parity == 1))
            far_pieces += [(rows[:HALF], first), (rows[HALF:], second)]
        elif far == 1:
            third = jnp.where(parity == 0, me + 3, me - 3)
            for peer in (me - 2, me + 2, third):
                ok = (peer >= 0) & (peer < seq_size)
                far_pieces.append((far_rows[jnp.clip(peer, 0, seq_size - 1)], bias_of(ok)))
        else:
            lower = block(jnp.maximum(group - 1, 0))
            upper = block(jnp.minimum(group + 1, blocks - 1))
            has_lower, has_upper = group >= 1, group + 1 < blocks
            far_pieces += [
                (lower[:HALF], bias_of(has_lower)),
                (lower[HALF:], bias_of(has_lower & (parity == 1))),
                (upper[:HALF], bias_of(has_upper & (parity == 0))),
                (upper[HALF:], bias_of(has_upper)),
            ]

    lane = lax.broadcasted_iota(jnp.int32, (1, width), 1)
    first_head = lane < HD
    exponent = math.log2(math.e) / math.sqrt(HD)
    for leaf in range(2):
        if leaf == 0:
            near = [
                (before[LEAF:], has_before),
                (own[...], None),
                (coarse_before[:HALF], has_before),
                (coarse_after, has_after),
            ]
        else:
            near = [
                (own[...], None),
                (after[:LEAF], has_after),
                (coarse_before, has_before),
                (coarse_after[HALF:], has_after),
            ]
        at = 0
        total_rows = key_set.shape[0]
        position = lax.broadcasted_iota(jnp.int32, (1, total_rows), 1)
        bias = jnp.zeros((1, total_rows), jnp.float32)
        for rows, value in near + far_pieces:
            count = rows.shape[0]
            key_set[at : at + count] = rows
            if value is not None:
                bias = jnp.where((position >= at) & (position < at + count), value, bias)
            at += count
        block_queries = queries[leaf * LEAF : (leaf + 1) * LEAF]
        none = jnp.zeros_like(block_queries)
        both = jnp.concatenate(
            [jnp.where(first_head, block_queries, none), jnp.where(first_head, none, block_queries)], axis=0
        )
        scores = lax.dot_general(
            both, key_set[:, :width], (((1,), (1,)), ((), ())), preferred_element_type=jnp.float32
        )
        scores = scores + bias
        peak = jnp.max(scores, axis=1, keepdims=True)
        weights = jnp.exp2((scores - peak) * exponent)
        total = jnp.sum(weights, axis=1, keepdims=True)
        numer = jnp.dot(
            weights.astype(jnp.bfloat16), key_set[:, width:], preferred_element_type=jnp.float32
        )
        shares = numer / total
        attended[leaf * LEAF : (leaf + 1) * LEAF] = jnp.where(
            first_head, shares[:LEAF], shares[LEAF:]
        ).astype(jnp.bfloat16)


def project_kernel(rows, weight, mixed):
    width = rows.shape[2]
    total = jnp.zeros(mixed.shape, jnp.float32)
    for part in range(rows.shape[0]):
        total += jnp.dot(
            rows[part], weight[part * width : (part + 1) * width], preferred_element_type=jnp.float32
        )
    mixed[...] = total.astype(mixed.dtype)


VMEM = pl.BlockSpec(memory_space=pltpu.VMEM)


def shards(queries, keys, values, out_weight):
    tokens, width = queries.shape
    seq_size = lax.axis_size("seq")
    head_size = lax.axis_size("head")
    bf16 = jnp.bfloat16
    wide_rows = max(2 * LEAF, seq_size // 2 * HALF)
    wide = pltpu.VMEM((wide_rows, width), jnp.float32)
    pair, quarter = pl.pallas_call(
        pack_kernel,
        out_shape=(
            jax.ShapeDtypeStruct((tokens, 2 * width), bf16),
            jax.ShapeDtypeStruct((seq_size, HALF, 2 * width), bf16),
        ),
        in_specs=[VMEM] * 2,
        out_specs=(VMEM, VMEM),
        scratch_shapes=[wide],
        name="pack",
    )(keys, values)
    ends = seq_size - 1
    before = lax.ppermute(pair, "seq", [(i, i + 1) for i in range(ends)])
    after = lax.ppermute(pair, "seq", [(i + 1, i) for i in range(ends)])
    far_rows = lax.all_to_all(quarter, "seq", split_axis=0, concat_axis=0)
    set_rows = 3 * LEAF + 3 * HALF + sum(segments(seq_size))
    attended = pl.pallas_call(
        functools.partial(attend_kernel, seq_size),
        out_shape=jax.ShapeDtypeStruct((tokens, width), bf16),
        in_specs=[VMEM] * 5,
        out_specs=VMEM,
        scratch_shapes=[pltpu.VMEM((set_rows, 2 * width), bf16), wide],
        compiler_params=pltpu.CompilerParams(vmem_limit_bytes=40 << 20),
        name="attend",
    )(queries, pair, before, after, far_rows)
    share = tokens // head_size
    gathered = lax.all_to_all(
        attended.reshape(head_size, share, width), "head", split_axis=0, concat_axis=0
    )
    return pl.pallas_call(
        project_kernel,
        out_shape=jax.ShapeDtypeStruct((share, out_weight.shape[1]), bf16),
        in_specs=[VMEM] * 2,
        out_specs=VMEM,
        name="project",
    )(gathered, out_weight)


def solution(mesh):
    in_specs = (P("seq", "head"), P("seq", "head"), P("seq", "head"), P())
    out_specs = P(("seq", "head"), None)
    return jax.shard_map(shards, mesh=mesh, in_specs=in_specs, out_specs=out_specs, check_vma=False)
```

```python
import functools
import math

import jax
import jax.numpy as jnp
from jax import lax
from jax.experimental import pallas as pl
from jax.experimental.pallas import tpu as pltpu
from jax.sharding import PartitionSpec as P

HD = 64
LEAF = 128
HALF = LEAF // 2
NEG = -math.inf


def average_pairs(rows, wide):
    count = rows.shape[0]
    halves = []
    for low in range(0, rows.shape[1], LEAF):
        wide[:count] = rows[:, low : low + LEAF].astype(jnp.float32)
        even = wide[pl.ds(0, count // 2, stride=2), :]
        odd = wide[pl.ds(1, count // 2, stride=2), :]
        halves.append((0.5 * (even + odd)).astype(jnp.bfloat16))
    return jnp.concatenate(halves, axis=1)


def pack_kernel(keys, values, inner, outer, shares, wide):
    me = lax.axis_index("seq")
    odd = me & 1
    rows = jnp.concatenate([keys[...], values[...]], axis=1)
    low, high = rows[:LEAF], rows[LEAF:]
    inner[...] = jnp.where(odd == 1, low, high)
    outer[...] = jnp.where(odd == 1, high, low)
    level_one = average_pairs(rows, wide)
    level_two = average_pairs(level_one, wide)
    for peer in range(shares.shape[0]):
        share = jnp.where(me == peer - 1, level_one[:HALF], level_two)
        shares[peer] = jnp.where(me == peer + 1, level_one[HALF:], share)


def segments(seq_size):
    far_count = seq_size.bit_length() - 2
    rows = []
    for far in range(1, far_count + 1):
        if seq_size >> far == 2:
            rows.append(LEAF)
        elif far == 1:
            rows.append(3 * HALF)
        else:
            rows.append(2 * LEAF)
    return rows


def attend_kernel(seq_size, queries, keys, values, inner, outer, far_rows, attended, key_set, wide):
    me = lax.axis_index("seq")
    width = queries.shape[1]
    zero, neg = jnp.float32(0.0), jnp.float32(NEG)

    def bias_of(valid):
        return jnp.where(valid, zero, neg)

    odd = me & 1
    before = jnp.where(odd == 1, inner[...], outer[...])
    after = jnp.where(odd == 1, outer[...], inner[...])
    far_half_before = far_rows[jnp.maximum(me - 1, 0)]
    far_half_after = far_rows[jnp.minimum(me + 1, seq_size - 1)]
    near_half_before = average_pairs(before, wide)
    near_half_after = average_pairs(after, wide)
    own = jnp.concatenate([keys[...], values[...]], axis=1)
    has_before, has_after = bias_of(me >= 1), bias_of(me + 1 < seq_size)

    far_pieces = []
    for far, _ in enumerate(segments(seq_size), 1):
        span = 1 << far
        group = me >> far
        parity = (me >> (far - 1)) & 1
        blocks = seq_size >> far

        def block(number, span=span, far=far):
            found = far_rows[pl.ds(number * span, span)].reshape(span * HALF, 2 * width)
            for _ in range(far - 1):
                found = average_pairs(found, wide)
            return found

        if blocks == 2:
            rows = block(1 - group)
            first = bias_of((group == 1) | (parity == 0))
            second = bias_of((group == 0) | (parity == 1))
            far_pieces += [(rows[:HALF], first), (rows[HALF:], second)]
        elif far == 1:
            third = jnp.where(parity == 0, me + 3, me - 3)
            for peer in (me - 2, me + 2, third):
                ok = (peer >= 0) & (peer < seq_size)
                far_pieces.append((far_rows[jnp.clip(peer, 0, seq_size - 1)], bias_of(ok)))
        else:
            lower = block(jnp.maximum(group - 1, 0))
            upper = block(jnp.minimum(group + 1, blocks - 1))
            has_lower, has_upper = group >= 1, group + 1 < blocks
            far_pieces += [
                (lower[:HALF], bias_of(has_lower)),
                (lower[HALF:], bias_of(has_lower & (parity == 1))),
                (upper[:HALF], bias_of(has_upper & (parity == 0))),
                (upper[HALF:], bias_of(has_upper)),
            ]

    lane = lax.broadcasted_iota(jnp.int32, (1, width), 1)
    first_head = lane < HD
    exponent = math.log2(math.e) / math.sqrt(HD)
    for leaf in range(2):
        if leaf == 0:
            near = [
                (before, has_before),
                (own, None),
                (far_half_before, has_before),
                (near_half_after, has_after),
                (far_half_after, has_after),
            ]
        else:
            near = [
                (own, None),
                (after, has_after),
                (far_half_before, has_before),
                (near_half_before, has_before),
                (far_half_after, has_after),
            ]
        at = 0
        total_rows = key_set.shape[0]
        position = lax.broadcasted_iota(jnp.int32, (1, total_rows), 1)
        bias = jnp.zeros((1, total_rows), jnp.float32)
        for rows, value in near + far_pieces:
            count = rows.shape[0]
            key_set[at : at + count] = rows
            if value is not None:
                bias = jnp.where((position >= at) & (position < at + count), value, bias)
            at += count
        block_queries = queries[leaf * LEAF : (leaf + 1) * LEAF]
        none = jnp.zeros_like(block_queries)
        both = jnp.concatenate(
            [jnp.where(first_head, block_queries, none), jnp.where(first_head, none, block_queries)], axis=0
        )
        scores = lax.dot_general(
            both, key_set[:, :width], (((1,), (1,)), ((), ())), preferred_element_type=jnp.float32
        )
        scores = scores + bias
        peak = jnp.max(scores, axis=1, keepdims=True)
        weights = jnp.exp2((scores - peak) * exponent)
        total = jnp.sum(weights, axis=1, keepdims=True)
        numer = jnp.dot(
            weights.astype(jnp.bfloat16), key_set[:, width:], preferred_element_type=jnp.float32
        )
        shares = numer / total
        attended[leaf * LEAF : (leaf + 1) * LEAF] = jnp.where(
            first_head, shares[:LEAF], shares[LEAF:]
        ).astype(jnp.bfloat16)


def project_kernel(rows, weight, mixed):
    width = rows.shape[2]
    total = jnp.zeros(mixed.shape, jnp.float32)
    for part in range(rows.shape[0]):
        total += jnp.dot(
            rows[part], weight[part * width : (part + 1) * width], preferred_element_type=jnp.float32
        )
    mixed[...] = total.astype(mixed.dtype)


VMEM = pl.BlockSpec(memory_space=pltpu.VMEM)


def shards(queries, keys, values, out_weight):
    tokens, width = queries.shape
    seq_size = lax.axis_size("seq")
    head_size = lax.axis_size("head")
    bf16 = jnp.bfloat16
    wide_rows = max(2 * LEAF, seq_size // 2 * HALF)
    wide = pltpu.VMEM((wide_rows, width), jnp.float32)
    inner, outer, far_shares = pl.pallas_call(
        pack_kernel,
        out_shape=(
            jax.ShapeDtypeStruct((LEAF, 2 * width), bf16),
            jax.ShapeDtypeStruct((LEAF, 2 * width), bf16),
            jax.ShapeDtypeStruct((seq_size, HALF, 2 * width), bf16),
        ),
        in_specs=[VMEM] * 2,
        out_specs=(VMEM, VMEM, VMEM),
        scratch_shapes=[wide],
        compiler_params=pltpu.CompilerParams(vmem_limit_bytes=16 << 20),
        name="pack",
    )(keys, values)
    pairs = [(i, i ^ 1) for i in range(seq_size)]
    others = [(i, i + 1 if i & 1 else i - 1) for i in range(1, seq_size - 1)]
    far_rows = lax.all_to_all(far_shares, "seq", split_axis=0, concat_axis=0)
    inner = lax.ppermute(inner, "seq", pairs)
    outer = lax.ppermute(outer, "seq", others)
    set_rows = 3 * LEAF + 3 * HALF + sum(segments(seq_size))
    attended = pl.pallas_call(
        functools.partial(attend_kernel, seq_size),
        out_shape=jax.ShapeDtypeStruct((tokens, width), bf16),
        in_specs=[VMEM] * 6,
        out_specs=VMEM,
        scratch_shapes=[pltpu.VMEM((set_rows, 2 * width), bf16), wide],
        compiler_params=pltpu.CompilerParams(vmem_limit_bytes=24 << 20),
        name="attend",
    )(queries, keys, values, inner, outer, far_rows)
    share = tokens // head_size
    gathered = lax.all_to_all(
        attended.reshape(head_size, share, width), "head", split_axis=0, concat_axis=0
    )
    return pl.pallas_call(
        project_kernel,
        out_shape=jax.ShapeDtypeStruct((share, out_weight.shape[1]), bf16),
        in_specs=[VMEM] * 2,
        out_specs=VMEM,
        compiler_params=pltpu.CompilerParams(vmem_limit_bytes=8 << 20),
        name="project",
    )(gathered, out_weight)


def solution(mesh):
    in_specs = (P("seq", "head"), P("seq", "head"), P("seq", "head"), P())
    out_specs = P(("seq", "head"), None)
    return jax.shard_map(shards, mesh=mesh, in_specs=in_specs, out_specs=out_specs, check_vma=False)
```

```python
import functools
import math

import jax
import jax.numpy as jnp
from jax import lax
from jax.experimental import pallas as pl
from jax.experimental.pallas import tpu as pltpu
from jax.sharding import PartitionSpec as P

HD = 64
LEAF = 128
HALF = LEAF // 2
NEG = -math.inf


def average_pairs(rows, wide):
    count = rows.shape[0]
    halves = []
    for low in range(0, rows.shape[1], LEAF):
        wide[:count] = rows[:, low : low + LEAF].astype(jnp.float32)
        even = wide[pl.ds(0, count // 2, stride=2), :]
        odd = wide[pl.ds(1, count // 2, stride=2), :]
        halves.append((0.5 * (even + odd)).astype(jnp.bfloat16))
    return jnp.concatenate(halves, axis=1)


def pack_kernel(far_shares, keys, values, own, inner, outer, quarter, wide, arrived):
    width = keys.shape[1]
    copies = [
        pltpu.make_async_copy(keys, own.at[:, :width], arrived.at[0]),
        pltpu.make_async_copy(values, own.at[:, width:], arrived.at[1]),
    ]
    for copy in copies:
        copy.start()
    me = lax.axis_index("seq")
    odd = me & 1
    for copy in copies:
        copy.wait()
    rows = own[...]
    low, high = rows[:LEAF], rows[LEAF:]
    level_one = average_pairs(rows, wide)
    level_two = average_pairs(level_one, wide)
    first, second = level_one[:HALF], level_one[HALF:]
    inner[:LEAF] = jnp.where(odd == 1, low, high)
    inner[LEAF : LEAF + HALF] = jnp.where(odd == 1, second, first)
    outer[:LEAF] = jnp.where(odd == 1, high, low)
    outer[LEAF:] = jnp.where(odd == 1, first, second)
    if far_shares:
        for peer in range(quarter.shape[0]):
            quarter[peer] = level_two
    else:
        inner[LEAF + HALF :] = level_two
        quarter[...] = level_two


def join_kernel(inner, quarter, block, eighth, wide):
    odd = lax.axis_index("seq") & 1
    theirs = inner[LEAF + HALF :]
    block[:HALF] = jnp.where(odd == 1, theirs, quarter[...])
    block[HALF:] = jnp.where(odd == 1, quarter[...], theirs)
    eighth[...] = average_pairs(block[...], wide)


def set_rows(seq_size):
    rows = 3 * LEAF + 3 * HALF
    for far in range(1, seq_size.bit_length() - 1):
        if seq_size >> far == 2:
            rows += LEAF
        elif far == 1:
            rows += 3 * HALF
        else:
            rows += 2 * LEAF
    return rows


def bias_of(valid):
    return jnp.where(valid, jnp.float32(0.0), jnp.float32(NEG))


def gathered_pieces(seq_size, far_rows, wide):
    me = lax.axis_index("seq")
    pieces = []
    for far in range(1, seq_size.bit_length() - 1):
        span = 1 << far
        group = me >> far
        parity = (me >> (far - 1)) & 1
        blocks = seq_size >> far

        def block(number, span=span, far=far):
            found = far_rows[pl.ds(number * span, span)].reshape(span * HALF, far_rows.shape[2])
            for _ in range(far - 1):
                found = average_pairs(found, wide)
            return found

        if blocks == 2:
            rows = block(1 - group)
            first = bias_of((group == 1) | (parity == 0))
            second = bias_of((group == 0) | (parity == 1))
            pieces += [(rows[:HALF], first), (rows[HALF:], second)]
        elif far == 1:
            third = jnp.where(parity == 0, me + 3, me - 3)
            for peer in (me - 2, me + 2, third):
                ok = (peer >= 0) & (peer < seq_size)
                pieces.append((far_rows[jnp.clip(peer, 0, seq_size - 1)], bias_of(ok)))
        else:
            lower = block(jnp.maximum(group - 1, 0))
            upper = block(jnp.minimum(group + 1, blocks - 1))
            has_lower, has_upper = group >= 1, group + 1 < blocks
            pieces += [
                (lower[:HALF], bias_of(has_lower)),
                (lower[HALF:], bias_of(has_lower & (parity == 1))),
                (upper[:HALF], bias_of(has_upper & (parity == 0))),
                (upper[HALF:], bias_of(has_upper)),
            ]
    return pieces


def paired_pieces(block_2, block_6, eighth_4, wide):
    me = lax.axis_index("seq")
    odd = me & 1
    pair = me >> 1
    middle = (pair == 1) | (pair == 2)
    upper_near = (pair & 1) == 0
    lower = jnp.where(upper_near, block_6[...], block_2[...])
    upper = jnp.where(upper_near, block_2[...], block_6[...])
    has_lower, has_upper = pair >= 1, pair <= 2
    third = jnp.where(odd == 1, lower[HALF:], upper[:HALF])
    has_third = ((odd == 1) & has_lower) | ((odd == 0) & has_upper)
    ends = average_pairs(block_6[...], wide)
    return [
        (lower[:HALF], bias_of(has_lower)),
        (upper[HALF:], bias_of(has_upper)),
        (third, bias_of(has_third)),
        (eighth_4[...], bias_of(pair >= 0)),
        (ends, bias_of(jnp.logical_not(middle))),
    ]


def attend_kernel(seq_size, queries, own, inner, outer, *rest):
    *far, attended, key_set, wide = rest
    me = lax.axis_index("seq")
    width = queries.shape[1]
    odd = me & 1
    from_inner, from_outer = inner[: LEAF + HALF], outer[...]
    before = jnp.where(odd == 1, from_inner, from_outer)
    after = jnp.where(odd == 1, from_outer, from_inner)
    edge_before, edge_after = before[:LEAF], after[:LEAF]
    far_half_before, far_half_after = before[LEAF:], after[LEAF:]
    near_half_before = average_pairs(edge_before, wide)
    near_half_after = average_pairs(edge_after, wide)
    has_before, has_after = bias_of(me >= 1), bias_of(me + 1 < seq_size)
    if len(far) == 1:
        far_pieces = gathered_pieces(seq_size, far[0], wide)
    else:
        far_pieces = paired_pieces(*far, wide)

    lane = lax.broadcasted_iota(jnp.int32, (1, width), 1)
    first_head = lane < HD
    exponent = math.log2(math.e) / math.sqrt(HD)
    for leaf in range(2):
        if leaf == 0:
            near = [
                (edge_before, has_before),
                (own[...], None),
                (far_half_before, has_before),
                (near_half_after, has_after),
                (far_half_after, has_after),
            ]
        else:
            near = [
                (own[...], None),
                (edge_after, has_after),
                (far_half_before, has_before),
                (near_half_before, has_before),
                (far_half_after, has_after),
            ]
        at = 0
        total_rows = key_set.shape[0]
        position = lax.broadcasted_iota(jnp.int32, (1, total_rows), 1)
        bias = jnp.zeros((1, total_rows), jnp.float32)
        for rows, value in near + far_pieces:
            count = rows.shape[0]
            key_set[at : at + count] = rows
            if value is not None:
                bias = jnp.where((position >= at) & (position < at + count), value, bias)
            at += count
        block_queries = queries[leaf * LEAF : (leaf + 1) * LEAF]
        none = jnp.zeros_like(block_queries)
        both = jnp.concatenate(
            [jnp.where(first_head, block_queries, none), jnp.where(first_head, none, block_queries)], axis=0
        )
        scores = lax.dot_general(
            both, key_set[:, :width], (((1,), (1,)), ((), ())), preferred_element_type=jnp.float32
        )
        scores = scores + bias
        peak = jnp.max(scores, axis=1, keepdims=True)
        weights = jnp.exp2((scores - peak) * exponent)
        total = jnp.sum(weights, axis=1, keepdims=True)
        numer = jnp.dot(
            weights.astype(jnp.bfloat16), key_set[:, width:], preferred_element_type=jnp.float32
        )
        shares = numer / total
        attended[leaf * LEAF : (leaf + 1) * LEAF] = jnp.where(
            first_head, shares[:LEAF], shares[LEAF:]
        ).astype(jnp.bfloat16)


def project_kernel(rows, weight, mixed):
    width = rows.shape[2]
    total = jnp.zeros(mixed.shape, jnp.float32)
    for part in range(rows.shape[0]):
        total += jnp.dot(
            rows[part], weight[part * width : (part + 1) * width], preferred_element_type=jnp.float32
        )
    mixed[...] = total.astype(mixed.dtype)


VMEM = pl.BlockSpec(memory_space=pltpu.VMEM)
HBM = pl.BlockSpec(memory_space=pltpu.HBM)


def kernel_call(body, name, megabytes, ins, outs, scratch):
    shapes = tuple(jax.ShapeDtypeStruct(shape, jnp.bfloat16) for shape in outs)
    return pl.pallas_call(
        body,
        out_shape=shapes,
        in_specs=ins,
        out_specs=(VMEM,) * len(outs),
        scratch_shapes=scratch,
        compiler_params=pltpu.CompilerParams(vmem_limit_bytes=megabytes << 20),
        name=name,
    )


def shards(queries, keys, values, out_weight):
    tokens, width = queries.shape
    seq_size = lax.axis_size("seq")
    head_size = lax.axis_size("head")
    pair_width = 2 * width
    paired = seq_size == 8
    wide_rows = 2 * LEAF if paired else max(2 * LEAF, seq_size // 2 * HALF)
    wide = pltpu.VMEM((wide_rows, width), jnp.float32)

    def swap(array, bit):
        return lax.ppermute(array, "seq", [(i, i ^ bit) for i in range(seq_size)])

    own, inner, outer, quarter = kernel_call(
        functools.partial(pack_kernel, not paired),
        "pack",
        16,
        [HBM] * 2,
        [
            (tokens, pair_width),
            (LEAF + HALF + (HALF if paired else 0), pair_width),
            (LEAF + HALF, pair_width),
            (HALF, pair_width) if paired else (seq_size, HALF, pair_width),
        ],
        [wide, pltpu.SemaphoreType.DMA((2,))],
    )(keys, values)
    inner = swap(inner, 1)
    others = [(i, i + 1 if i & 1 else i - 1) for i in range(1, seq_size - 1)]
    outer = lax.ppermute(outer, "seq", others)
    if paired:
        block, eighth = kernel_call(
            join_kernel,
            "join",
            8,
            [VMEM] * 2,
            [(LEAF, pair_width), (HALF, pair_width)],
            [wide],
        )(inner, quarter)
        far = (swap(block, 2), swap(block, 6), swap(eighth, 4))
    else:
        far = (lax.all_to_all(quarter, "seq", split_axis=0, concat_axis=0),)
    (attended,) = kernel_call(
        functools.partial(attend_kernel, seq_size),
        "attend",
        24,
        [VMEM] * (4 + len(far)),
        [(tokens, width)],
        [pltpu.VMEM((set_rows(seq_size), pair_width), jnp.bfloat16), wide],
    )(queries, own, inner, outer, *far)
    share = tokens // head_size
    gathered = lax.all_to_all(
        attended.reshape(head_size, share, width), "head", split_axis=0, concat_axis=0
    )
    (mixed,) = kernel_call(
        project_kernel, "project", 8, [VMEM] * 2, [(share, out_weight.shape[1])], []
    )(gathered, out_weight)
    return mixed


def solution(mesh):
    in_specs = (P("seq", "head"), P("seq", "head"), P("seq", "head"), P())
    out_specs = P(("seq", "head"), None)
    return jax.shard_map(shards, mesh=mesh, in_specs=in_specs, out_specs=out_specs, check_vma=False)
```

```python
import functools
import math

import jax
import jax.numpy as jnp
from jax import lax
from jax.experimental import pallas as pl
from jax.experimental.pallas import tpu as pltpu
from jax.sharding import PartitionSpec as P

HD = 64
LEAF = 128
HALF = LEAF // 2
NEG = -math.inf


def average_pairs(rows, wide):
    count = rows.shape[0]
    halves = []
    for low in range(0, rows.shape[1], LEAF):
        wide[:count] = rows[:, low : low + LEAF].astype(jnp.float32)
        even = wide[pl.ds(0, count // 2, stride=2), :]
        odd = wide[pl.ds(1, count // 2, stride=2), :]
        halves.append((0.5 * (even + odd)).astype(jnp.bfloat16))
    return jnp.concatenate(halves, axis=1)


def pack_kernel(far_shares, queries, keys, values, own_queries, own, inner, outer, quarter, wide, arrived):
    width = keys.shape[1]
    copies = [
        pltpu.make_async_copy(keys, own.at[:, :width], arrived.at[0]),
        pltpu.make_async_copy(values, own.at[:, width:], arrived.at[1]),
        pltpu.make_async_copy(queries, own_queries, arrived.at[2]),
    ]
    for copy in copies:
        copy.start()
    me = lax.axis_index("seq")
    odd = me & 1
    for copy in copies:
        copy.wait()
    rows = own[...]
    low, high = rows[:LEAF], rows[LEAF:]
    level_one = average_pairs(rows, wide)
    level_two = average_pairs(level_one, wide)
    first, second = level_one[:HALF], level_one[HALF:]
    inner[:LEAF] = jnp.where(odd == 1, low, high)
    inner[LEAF : LEAF + HALF] = jnp.where(odd == 1, second, first)
    outer[:LEAF] = jnp.where(odd == 1, high, low)
    outer[LEAF:] = jnp.where(odd == 1, first, second)
    if far_shares:
        for peer in range(quarter.shape[0]):
            quarter[peer] = level_two
    else:
        inner[LEAF + HALF :] = level_two
        quarter[...] = level_two


def join_kernel(inner, quarter, block, eighth, wide):
    odd = lax.axis_index("seq") & 1
    theirs = inner[LEAF + HALF :]
    block[:HALF] = jnp.where(odd == 1, theirs, quarter[...])
    block[HALF:] = jnp.where(odd == 1, quarter[...], theirs)
    eighth[...] = average_pairs(block[...], wide)


def set_rows(seq_size):
    rows = 3 * LEAF + 3 * HALF
    for far in range(1, seq_size.bit_length() - 1):
        if seq_size >> far == 2:
            rows += LEAF
        elif far == 1:
            rows += 3 * HALF
        else:
            rows += 2 * LEAF
    return rows


def bias_of(valid):
    return jnp.where(valid, jnp.float32(0.0), jnp.float32(NEG))


def gathered_pieces(seq_size, far_rows, wide):
    me = lax.axis_index("seq")
    pieces = []
    for far in range(1, seq_size.bit_length() - 1):
        span = 1 << far
        group = me >> far
        parity = (me >> (far - 1)) & 1
        blocks = seq_size >> far

        def block(number, span=span, far=far):
            found = far_rows[pl.ds(number * span, span)].reshape(span * HALF, far_rows.shape[2])
            for _ in range(far - 1):
                found = average_pairs(found, wide)
            return found

        if blocks == 2:
            rows = block(1 - group)
            first = bias_of((group == 1) | (parity == 0))
            second = bias_of((group == 0) | (parity == 1))
            pieces += [(rows[:HALF], first), (rows[HALF:], second)]
        elif far == 1:
            third = jnp.where(parity == 0, me + 3, me - 3)
            for peer in (me - 2, me + 2, third):
                ok = (peer >= 0) & (peer < seq_size)
                pieces.append((far_rows[jnp.clip(peer, 0, seq_size - 1)], bias_of(ok)))
        else:
            lower = block(jnp.maximum(group - 1, 0))
            upper = block(jnp.minimum(group + 1, blocks - 1))
            has_lower, has_upper = group >= 1, group + 1 < blocks
            pieces += [
                (lower[:HALF], bias_of(has_lower)),
                (lower[HALF:], bias_of(has_lower & (parity == 1))),
                (upper[:HALF], bias_of(has_upper & (parity == 0))),
                (upper[HALF:], bias_of(has_upper)),
            ]
    return pieces


def paired_pieces(block_2, block_6, eighth_4, wide):
    me = lax.axis_index("seq")
    odd = me & 1
    pair = me >> 1
    middle = (pair == 1) | (pair == 2)
    upper_near = (pair & 1) == 0
    lower = jnp.where(upper_near, block_6[...], block_2[...])
    upper = jnp.where(upper_near, block_2[...], block_6[...])
    has_lower, has_upper = pair >= 1, pair <= 2
    third = jnp.where(odd == 1, lower[HALF:], upper[:HALF])
    has_third = ((odd == 1) & has_lower) | ((odd == 0) & has_upper)
    ends = average_pairs(block_6[...], wide)
    return [
        (lower[:HALF], bias_of(has_lower)),
        (upper[HALF:], bias_of(has_upper)),
        (third, bias_of(has_third)),
        (eighth_4[...], bias_of(pair >= 0)),
        (ends, bias_of(jnp.logical_not(middle))),
    ]


def attend_kernel(seq_size, far_count, queries, own, inner, outer, *rest):
    far, shares, scratch = rest[:far_count], rest[far_count:-3], rest[-3:]
    attended, key_set, wide = scratch
    me = lax.axis_index("seq")
    width = queries.shape[1]
    odd = me & 1
    from_inner, from_outer = inner[: LEAF + HALF], outer[...]
    before = jnp.where(odd == 1, from_inner, from_outer)
    after = jnp.where(odd == 1, from_outer, from_inner)
    edge_before, edge_after = before[:LEAF], after[:LEAF]
    far_half_before, far_half_after = before[LEAF:], after[LEAF:]
    near_half_before = average_pairs(edge_before, wide)
    near_half_after = average_pairs(edge_after, wide)
    has_before, has_after = bias_of(me >= 1), bias_of(me + 1 < seq_size)
    if len(far) == 1:
        far_pieces = gathered_pieces(seq_size, far[0], wide)
    else:
        far_pieces = paired_pieces(*far, wide)

    lane = lax.broadcasted_iota(jnp.int32, (1, width), 1)
    first_head = lane < HD
    exponent = math.log2(math.e) / math.sqrt(HD)
    for leaf in range(2):
        if leaf == 0:
            near = [
                (edge_before, has_before),
                (own[...], None),
                (far_half_before, has_before),
                (near_half_after, has_after),
                (far_half_after, has_after),
            ]
        else:
            near = [
                (own[...], None),
                (edge_after, has_after),
                (far_half_before, has_before),
                (near_half_before, has_before),
                (far_half_after, has_after),
            ]
        at = 0
        total_rows = key_set.shape[0]
        position = lax.broadcasted_iota(jnp.int32, (1, total_rows), 1)
        bias = jnp.zeros((1, total_rows), jnp.float32)
        for rows, value in near + far_pieces:
            count = rows.shape[0]
            key_set[at : at + count] = rows
            if value is not None:
                bias = jnp.where((position >= at) & (position < at + count), value, bias)
            at += count
        block_queries = queries[leaf * LEAF : (leaf + 1) * LEAF]
        none = jnp.zeros_like(block_queries)
        both = jnp.concatenate(
            [jnp.where(first_head, block_queries, none), jnp.where(first_head, none, block_queries)], axis=0
        )
        scores = lax.dot_general(
            both, key_set[:, :width], (((1,), (1,)), ((), ())), preferred_element_type=jnp.float32
        )
        scores = scores + bias
        peak = jnp.max(scores, axis=1, keepdims=True)
        weights = jnp.exp2((scores - peak) * exponent)
        total = jnp.sum(weights, axis=1, keepdims=True)
        numer = jnp.dot(
            weights.astype(jnp.bfloat16), key_set[:, width:], preferred_element_type=jnp.float32
        )
        mean = numer / total
        attended[leaf * LEAF : (leaf + 1) * LEAF] = jnp.where(
            first_head, mean[:LEAF], mean[LEAF:]
        ).astype(jnp.bfloat16)
    mine = lax.axis_index("head")
    for step, share in enumerate(shares):
        count = share.shape[0]
        share[...] = attended[pl.ds(pl.multiple_of((mine ^ step) * count, count), count)]


def project_kernel(*refs):
    *parts, weight, mixed = refs
    mine = lax.axis_index("head")
    total = jnp.zeros(mixed.shape, jnp.float32)
    for step, part in enumerate(parts):
        width = part.shape[1]
        columns = pl.ds(pl.multiple_of((mine ^ step) * width, width), width)
        total += jnp.dot(part[...], weight[columns], preferred_element_type=jnp.float32)
    mixed[...] = total.astype(mixed.dtype)


VMEM = pl.BlockSpec(memory_space=pltpu.VMEM)
HBM = pl.BlockSpec(memory_space=pltpu.HBM)


def kernel_call(body, name, megabytes, ins, outs, scratch):
    shapes = tuple(jax.ShapeDtypeStruct(shape, jnp.bfloat16) for shape in outs)
    return pl.pallas_call(
        body,
        out_shape=shapes,
        in_specs=ins,
        out_specs=(VMEM,) * len(outs),
        scratch_shapes=scratch,
        compiler_params=pltpu.CompilerParams(vmem_limit_bytes=megabytes << 20),
        name=name,
    )


def shards(queries, keys, values, out_weight):
    tokens, width = queries.shape
    seq_size = lax.axis_size("seq")
    head_size = lax.axis_size("head")
    pair_width = 2 * width
    paired = seq_size == 8
    wide_rows = 2 * LEAF if paired else max(2 * LEAF, seq_size // 2 * HALF)
    wide = pltpu.VMEM((wide_rows, width), jnp.float32)

    def swap(array, bit, axis="seq"):
        return lax.ppermute(array, axis, [(i, i ^ bit) for i in range(lax.axis_size(axis))])

    own_queries, own, inner, outer, quarter = kernel_call(
        functools.partial(pack_kernel, not paired),
        "pack",
        16,
        [HBM] * 3,
        [
            (tokens, width),
            (tokens, pair_width),
            (LEAF + HALF + (HALF if paired else 0), pair_width),
            (LEAF + HALF, pair_width),
            (HALF, pair_width) if paired else (seq_size, HALF, pair_width),
        ],
        [wide, pltpu.SemaphoreType.DMA((3,))],
    )(*(pltpu.with_memory_space_constraint(array, pltpu.HBM) for array in (queries, keys, values)))
    inner = swap(inner, 1)
    others = [(i, i + 1 if i & 1 else i - 1) for i in range(1, seq_size - 1)]
    outer = lax.ppermute(outer, "seq", others)
    if paired:
        block, eighth = kernel_call(
            join_kernel,
            "join",
            8,
            [VMEM] * 2,
            [(LEAF, pair_width), (HALF, pair_width)],
            [wide],
        )(inner, quarter)
        far = (swap(block, 2), swap(block, 6), swap(eighth, 4))
    else:
        far = (lax.all_to_all(quarter, "seq", split_axis=0, concat_axis=0),)
    share = tokens // head_size
    shares = kernel_call(
        functools.partial(attend_kernel, seq_size, len(far)),
        "attend",
        24,
        [VMEM] * (4 + len(far)),
        [(share, width)] * head_size,
        [
            pltpu.VMEM((tokens, width), jnp.bfloat16),
            pltpu.VMEM((set_rows(seq_size), pair_width), jnp.bfloat16),
            wide,
        ],
    )(own_queries, own, inner, outer, *far)
    parts = [swap(part, step, "head") if step else part for step, part in enumerate(shares)]
    (mixed,) = kernel_call(
        project_kernel, "project", 8, [VMEM] * (head_size + 1), [(share, out_weight.shape[1])], []
    )(*parts, out_weight)
    return mixed


def solution(mesh):
    in_specs = (P("seq", "head"), P("seq", "head"), P("seq", "head"), P())
    out_specs = P(("seq", "head"), None)
    return jax.shard_map(shards, mesh=mesh, in_specs=in_specs, out_specs=out_specs, check_vma=False)
```

```python
import functools
import math

import jax
import jax.numpy as jnp
from jax import lax
from jax.experimental import pallas as pl
from jax.experimental.pallas import tpu as pltpu
from jax.sharding import PartitionSpec as P

HD = 64
LEAF = 128
HALF = LEAF // 2
NEG = -math.inf


def average_pairs(rows, wide):
    count = rows.shape[0]
    halves = []
    for low in range(0, rows.shape[1], LEAF):
        wide[:count] = rows[:, low : low + LEAF].astype(jnp.float32)
        even = wide[pl.ds(0, count // 2, stride=2), :]
        odd = wide[pl.ds(1, count // 2, stride=2), :]
        halves.append((0.5 * (even + odd)).astype(jnp.bfloat16))
    return jnp.concatenate(halves, axis=1)


def pack_kernel(far_shares, queries, keys, values, own_queries, own, inner, outer, quarter, wide, arrived):
    width = keys.shape[1]
    copies = [
        pltpu.make_async_copy(keys, own.at[:, :width], arrived.at[0]),
        pltpu.make_async_copy(values, own.at[:, width:], arrived.at[1]),
        pltpu.make_async_copy(queries, own_queries, arrived.at[2]),
    ]
    for copy in copies:
        copy.start()
    me = lax.axis_index("seq")
    odd = me & 1
    for copy in copies:
        copy.wait()
    rows = own[...]
    low, high = rows[:LEAF], rows[LEAF:]
    level_one = average_pairs(rows, wide)
    level_two = average_pairs(level_one, wide)
    first, second = level_one[:HALF], level_one[HALF:]
    inner[:LEAF] = jnp.where(odd == 1, low, high)
    inner[LEAF:] = jnp.where(odd == 1, second, first)
    outer[:LEAF] = jnp.where(odd == 1, high, low)
    outer[LEAF:] = jnp.where(odd == 1, first, second)
    if far_shares:
        for peer in range(quarter.shape[0]):
            quarter[peer] = level_two
    else:
        quarter[...] = level_two


def join_kernel(inner, quarter, block, eighth, wide):
    odd = lax.axis_index("seq") & 1
    edge_half = average_pairs(inner[:LEAF], wide)
    other_half = inner[LEAF:]
    theirs = jnp.concatenate(
        [jnp.where(odd == 1, other_half, edge_half), jnp.where(odd == 1, edge_half, other_half)], axis=0
    )
    theirs = average_pairs(theirs, wide)
    block[:HALF] = jnp.where(odd == 1, theirs, quarter[...])
    block[HALF:] = jnp.where(odd == 1, quarter[...], theirs)
    eighth[...] = average_pairs(block[...], wide)


def set_rows(seq_size):
    rows = 3 * LEAF + 3 * HALF
    for far in range(1, seq_size.bit_length() - 1):
        if seq_size >> far == 2:
            rows += LEAF
        elif far == 1:
            rows += 3 * HALF
        else:
            rows += 2 * LEAF
    return rows


def bias_of(valid):
    return jnp.where(valid, jnp.float32(0.0), jnp.float32(NEG))


def gathered_pieces(seq_size, far_rows, wide):
    me = lax.axis_index("seq")
    pieces = []
    for far in range(1, seq_size.bit_length() - 1):
        span = 1 << far
        group = me >> far
        parity = (me >> (far - 1)) & 1
        blocks = seq_size >> far

        def block(number, span=span, far=far):
            found = far_rows[pl.ds(number * span, span)].reshape(span * HALF, far_rows.shape[2])
            for _ in range(far - 1):
                found = average_pairs(found, wide)
            return found

        if blocks == 2:
            rows = block(1 - group)
            first = bias_of((group == 1) | (parity == 0))
            second = bias_of((group == 0) | (parity == 1))
            pieces += [(rows[:HALF], first), (rows[HALF:], second)]
        elif far == 1:
            third = jnp.where(parity == 0, me + 3, me - 3)
            for peer in (me - 2, me + 2, third):
                ok = (peer >= 0) & (peer < seq_size)
                pieces.append((far_rows[jnp.clip(peer, 0, seq_size - 1)], bias_of(ok)))
        else:
            lower = block(jnp.maximum(group - 1, 0))
            upper = block(jnp.minimum(group + 1, blocks - 1))
            has_lower, has_upper = group >= 1, group + 1 < blocks
            pieces += [
                (lower[:HALF], bias_of(has_lower)),
                (lower[HALF:], bias_of(has_lower & (parity == 1))),
                (upper[:HALF], bias_of(has_upper & (parity == 0))),
                (upper[HALF:], bias_of(has_upper)),
            ]
    return pieces


def paired_pieces(block_2, block_6, eighth_4, wide):
    me = lax.axis_index("seq")
    odd = me & 1
    pair = me >> 1
    middle = (pair == 1) | (pair == 2)
    upper_near = (pair & 1) == 0
    lower = jnp.where(upper_near, block_6[...], block_2[...])
    upper = jnp.where(upper_near, block_2[...], block_6[...])
    has_lower, has_upper = pair >= 1, pair <= 2
    third = jnp.where(odd == 1, lower[HALF:], upper[:HALF])
    has_third = ((odd == 1) & has_lower) | ((odd == 0) & has_upper)
    ends = average_pairs(block_6[...], wide)
    return [
        (lower[:HALF], bias_of(has_lower)),
        (upper[HALF:], bias_of(has_upper)),
        (third, bias_of(has_third)),
        (eighth_4[...], bias_of(pair >= 0)),
        (ends, bias_of(jnp.logical_not(middle))),
    ]


def attend_kernel(seq_size, far_count, queries, own, inner, outer, *rest):
    far, shares, scratch = rest[:far_count], rest[far_count:-3], rest[-3:]
    attended, key_set, wide = scratch
    me = lax.axis_index("seq")
    width = queries.shape[1]
    odd = me & 1
    from_inner, from_outer = inner[...], outer[...]
    before = jnp.where(odd == 1, from_inner, from_outer)
    after = jnp.where(odd == 1, from_outer, from_inner)
    edge_before, edge_after = before[:LEAF], after[:LEAF]
    far_half_before, far_half_after = before[LEAF:], after[LEAF:]
    near_half_before = average_pairs(edge_before, wide)
    near_half_after = average_pairs(edge_after, wide)
    has_before, has_after = bias_of(me >= 1), bias_of(me + 1 < seq_size)
    if len(far) == 1:
        far_pieces = gathered_pieces(seq_size, far[0], wide)
    else:
        far_pieces = paired_pieces(*far, wide)

    lane = lax.broadcasted_iota(jnp.int32, (1, width), 1)
    first_head = lane < HD
    exponent = math.log2(math.e) / math.sqrt(HD)
    for leaf in range(2):
        if leaf == 0:
            near = [
                (edge_before, has_before),
                (own[...], None),
                (far_half_before, has_before),
                (near_half_after, has_after),
                (far_half_after, has_after),
            ]
        else:
            near = [
                (own[...], None),
                (edge_after, has_after),
                (far_half_before, has_before),
                (near_half_before, has_before),
                (far_half_after, has_after),
            ]
        at = 0
        total_rows = key_set.shape[0]
        position = lax.broadcasted_iota(jnp.int32, (1, total_rows), 1)
        bias = jnp.zeros((1, total_rows), jnp.float32)
        for rows, value in near + far_pieces:
            count = rows.shape[0]
            key_set[at : at + count] = rows
            if value is not None:
                bias = jnp.where((position >= at) & (position < at + count), value, bias)
            at += count
        block_queries = queries[leaf * LEAF : (leaf + 1) * LEAF]
        none = jnp.zeros_like(block_queries)
        both = jnp.concatenate(
            [jnp.where(first_head, block_queries, none), jnp.where(first_head, none, block_queries)], axis=0
        )
        scores = lax.dot_general(
            both, key_set[:, :width], (((1,), (1,)), ((), ())), preferred_element_type=jnp.float32
        )
        scores = scores + bias
        peak = jnp.max(scores, axis=1, keepdims=True)
        weights = jnp.exp2((scores - peak) * exponent)
        total = jnp.sum(weights, axis=1, keepdims=True)
        numer = jnp.dot(
            weights.astype(jnp.bfloat16), key_set[:, width:], preferred_element_type=jnp.float32
        )
        mean = numer / total
        attended[leaf * LEAF : (leaf + 1) * LEAF] = jnp.where(
            first_head, mean[:LEAF], mean[LEAF:]
        ).astype(jnp.bfloat16)
    mine = lax.axis_index("head")
    for step, share in enumerate(shares):
        count = share.shape[0]
        share[...] = attended[pl.ds(pl.multiple_of((mine ^ step) * count, count), count)]


def project_kernel(*refs):
    *parts, weight, mixed = refs
    mine = lax.axis_index("head")
    total = jnp.zeros(mixed.shape, jnp.float32)
    for step, part in enumerate(parts):
        width = part.shape[1]
        columns = pl.ds(pl.multiple_of((mine ^ step) * width, width), width)
        total += jnp.dot(part[...], weight[columns], preferred_element_type=jnp.float32)
    mixed[...] = total.astype(mixed.dtype)


VMEM = pl.BlockSpec(memory_space=pltpu.VMEM)
HBM = pl.BlockSpec(memory_space=pltpu.HBM)


def kernel_call(body, name, megabytes, ins, outs, scratch):
    shapes = tuple(jax.ShapeDtypeStruct(shape, jnp.bfloat16) for shape in outs)
    return pl.pallas_call(
        body,
        out_shape=shapes,
        in_specs=ins,
        out_specs=(VMEM,) * len(outs),
        scratch_shapes=scratch,
        compiler_params=pltpu.CompilerParams(vmem_limit_bytes=megabytes << 20),
        name=name,
    )


def shards(queries, keys, values, out_weight):
    tokens, width = queries.shape
    seq_size = lax.axis_size("seq")
    head_size = lax.axis_size("head")
    pair_width = 2 * width
    paired = seq_size == 8
    wide_rows = 2 * LEAF if paired else max(2 * LEAF, seq_size // 2 * HALF)
    wide = pltpu.VMEM((wide_rows, width), jnp.float32)

    def swap(array, bit, axis="seq"):
        return lax.ppermute(array, axis, [(i, i ^ bit) for i in range(lax.axis_size(axis))])

    own_queries, own, inner, outer, quarter = kernel_call(
        functools.partial(pack_kernel, not paired),
        "pack",
        16,
        [HBM] * 3,
        [
            (tokens, width),
            (tokens, pair_width),
            (LEAF + HALF, pair_width),
            (LEAF + HALF, pair_width),
            (HALF, pair_width) if paired else (seq_size, HALF, pair_width),
        ],
        [wide, pltpu.SemaphoreType.DMA((3,))],
    )(*(pltpu.with_memory_space_constraint(array, pltpu.HBM) for array in (queries, keys, values)))
    inner = swap(inner, 1)
    others = [(i, i + 1 if i & 1 else i - 1) for i in range(1, seq_size - 1)]
    outer = lax.ppermute(outer, "seq", others)
    if paired:
        block, eighth = kernel_call(
            join_kernel,
            "join",
            8,
            [VMEM] * 2,
            [(LEAF, pair_width), (HALF, pair_width)],
            [wide],
        )(inner, quarter)
        block_6 = swap(block, 6)
        far = (swap(block, 2), block_6, swap(eighth, 4))
    else:
        far = (lax.all_to_all(quarter, "seq", split_axis=0, concat_axis=0),)
    share = tokens // head_size
    shares = kernel_call(
        functools.partial(attend_kernel, seq_size, len(far)),
        "attend",
        24,
        [VMEM] * (4 + len(far)),
        [(share, width)] * head_size,
        [
            pltpu.VMEM((tokens, width), jnp.bfloat16),
            pltpu.VMEM((set_rows(seq_size), pair_width), jnp.bfloat16),
            wide,
        ],
    )(own_queries, own, inner, outer, *far)
    parts = [swap(part, step, "head") if step else part for step, part in enumerate(shares)]
    (mixed,) = kernel_call(
        project_kernel, "project", 8, [VMEM] * (head_size + 1), [(share, out_weight.shape[1])], []
    )(*parts, out_weight)
    return mixed


def solution(mesh):
    in_specs = (P("seq", "head"), P("seq", "head"), P("seq", "head"), P())
    out_specs = P(("seq", "head"), None)
    return jax.shard_map(shards, mesh=mesh, in_specs=in_specs, out_specs=out_specs, check_vma=False)
```

```python
import functools
import math

import jax
import jax.numpy as jnp
from jax import lax
from jax.experimental import pallas as pl
from jax.experimental.pallas import tpu as pltpu
from jax.sharding import PartitionSpec as P

HD = 64
LEAF = 128
HALF = LEAF // 2
NEG = -math.inf


def average_pairs(rows, wide):
    count = rows.shape[0]
    halves = []
    for low in range(0, rows.shape[1], LEAF):
        wide[:count] = rows[:, low : low + LEAF].astype(jnp.float32)
        even = wide[pl.ds(0, count // 2, stride=2), :]
        odd = wide[pl.ds(1, count // 2, stride=2), :]
        halves.append((0.5 * (even + odd)).astype(jnp.bfloat16))
    return jnp.concatenate(halves, axis=1)


def pack_kernel(far_shares, queries, keys, values, own_queries, own, inner, outer, quarter, wide, arrived):
    width = keys.shape[1]
    copies = [
        pltpu.make_async_copy(keys, own.at[:, :width], arrived.at[0]),
        pltpu.make_async_copy(values, own.at[:, width:], arrived.at[1]),
        pltpu.make_async_copy(queries, own_queries, arrived.at[2]),
    ]
    for copy in copies:
        copy.start()
    me = lax.axis_index("seq")
    odd = me & 1
    for copy in copies:
        copy.wait()
    rows = own[...]
    low, high = rows[:LEAF], rows[LEAF:]
    level_one = average_pairs(rows, wide)
    level_two = average_pairs(level_one, wide)
    first, second = level_one[:HALF], level_one[HALF:]
    inner[:LEAF] = jnp.where(odd == 1, low, high)
    inner[LEAF:] = jnp.where(odd == 1, second, first)
    outer[:LEAF] = jnp.where(odd == 1, high, low)
    outer[LEAF:] = jnp.where(odd == 1, first, second)
    if far_shares:
        for peer in range(quarter.shape[0]):
            quarter[peer] = level_two
    else:
        quarter[...] = level_two


def join_kernel(inner, quarter, block, eighth, wide):
    odd = lax.axis_index("seq") & 1
    edge_half = average_pairs(inner[:LEAF], wide)
    other_half = inner[LEAF:]
    theirs = jnp.concatenate(
        [jnp.where(odd == 1, other_half, edge_half), jnp.where(odd == 1, edge_half, other_half)], axis=0
    )
    theirs = average_pairs(theirs, wide)
    block[:HALF] = jnp.where(odd == 1, theirs, quarter[...])
    block[HALF:] = jnp.where(odd == 1, quarter[...], theirs)
    eighth[...] = average_pairs(block[...], wide)


def set_rows(seq_size):
    rows = 3 * LEAF + 3 * HALF
    for far in range(1, seq_size.bit_length() - 1):
        if seq_size >> far == 2:
            rows += LEAF
        elif far == 1:
            rows += 3 * HALF
        else:
            rows += 2 * LEAF
    return rows


def bias_of(valid):
    return jnp.where(valid, jnp.float32(0.0), jnp.float32(NEG))


def gathered_pieces(seq_size, far_rows, wide):
    me = lax.axis_index("seq")
    pieces = []
    for far in range(1, seq_size.bit_length() - 1):
        span = 1 << far
        group = me >> far
        parity = (me >> (far - 1)) & 1
        blocks = seq_size >> far

        def block(number, span=span, far=far):
            found = far_rows[pl.ds(number * span, span)].reshape(span * HALF, far_rows.shape[2])
            for _ in range(far - 1):
                found = average_pairs(found, wide)
            return found

        if blocks == 2:
            rows = block(1 - group)
            first = bias_of((group == 1) | (parity == 0))
            second = bias_of((group == 0) | (parity == 1))
            pieces += [(rows[:HALF], first), (rows[HALF:], second)]
        elif far == 1:
            third = jnp.where(parity == 0, me + 3, me - 3)
            for peer in (me - 2, me + 2, third):
                ok = (peer >= 0) & (peer < seq_size)
                pieces.append((far_rows[jnp.clip(peer, 0, seq_size - 1)], bias_of(ok)))
        else:
            lower = block(jnp.maximum(group - 1, 0))
            upper = block(jnp.minimum(group + 1, blocks - 1))
            has_lower, has_upper = group >= 1, group + 1 < blocks
            pieces += [
                (lower[:HALF], bias_of(has_lower)),
                (lower[HALF:], bias_of(has_lower & (parity == 1))),
                (upper[:HALF], bias_of(has_upper & (parity == 0))),
                (upper[HALF:], bias_of(has_upper)),
            ]
    return pieces


def paired_pieces(block_6, block_2, eighth_4, wide):
    me = lax.axis_index("seq")
    odd = me & 1
    pair = me >> 1
    middle = (pair == 1) | (pair == 2)
    upper_near = (pair & 1) == 0
    lower = jnp.where(upper_near, block_6[...], block_2[...])
    upper = jnp.where(upper_near, block_2[...], block_6[...])
    has_lower, has_upper = pair >= 1, pair <= 2
    third = jnp.where(odd == 1, lower[HALF:], upper[:HALF])
    has_third = ((odd == 1) & has_lower) | ((odd == 0) & has_upper)
    ends = average_pairs(block_6[...], wide)
    return [
        (lower[:HALF], bias_of(has_lower)),
        (upper[HALF:], bias_of(has_upper)),
        (third, bias_of(has_third)),
        (eighth_4[...], bias_of(pair >= 0)),
        (ends, bias_of(jnp.logical_not(middle))),
    ]


def attend_kernel(seq_size, far_count, queries, own, inner, outer, *rest):
    far, shares, scratch = rest[:far_count], rest[far_count:-3], rest[-3:]
    attended, key_set, wide = scratch
    me = lax.axis_index("seq")
    width = queries.shape[1]
    odd = me & 1
    from_inner, from_outer = inner[...], outer[...]
    before = jnp.where(odd == 1, from_inner, from_outer)
    after = jnp.where(odd == 1, from_outer, from_inner)
    edge_before, edge_after = before[:LEAF], after[:LEAF]
    far_half_before, far_half_after = before[LEAF:], after[LEAF:]
    near_half_before = average_pairs(edge_before, wide)
    near_half_after = average_pairs(edge_after, wide)
    has_before, has_after = bias_of(me >= 1), bias_of(me + 1 < seq_size)
    if len(far) == 1:
        far_pieces = gathered_pieces(seq_size, far[0], wide)
    else:
        far_pieces = paired_pieces(*far, wide)

    lane = lax.broadcasted_iota(jnp.int32, (1, width), 1)
    first_head = lane < HD
    exponent = math.log2(math.e) / math.sqrt(HD)
    for leaf in range(2):
        if leaf == 0:
            near = [
                (edge_before, has_before),
                (own[...], None),
                (far_half_before, has_before),
                (near_half_after, has_after),
                (far_half_after, has_after),
            ]
        else:
            near = [
                (own[...], None),
                (edge_after, has_after),
                (far_half_before, has_before),
                (near_half_before, has_before),
                (far_half_after, has_after),
            ]
        at = 0
        total_rows = key_set.shape[0]
        position = lax.broadcasted_iota(jnp.int32, (1, total_rows), 1)
        bias = jnp.zeros((1, total_rows), jnp.float32)
        for rows, value in near + far_pieces:
            count = rows.shape[0]
            key_set[at : at + count] = rows
            if value is not None:
                bias = jnp.where((position >= at) & (position < at + count), value, bias)
            at += count
        block_queries = queries[leaf * LEAF : (leaf + 1) * LEAF]
        none = jnp.zeros_like(block_queries)
        both = jnp.concatenate(
            [jnp.where(first_head, block_queries, none), jnp.where(first_head, none, block_queries)], axis=0
        )
        scores = lax.dot_general(
            both, key_set[:, :width], (((1,), (1,)), ((), ())), preferred_element_type=jnp.float32
        )
        scores = scores + bias
        peak = jnp.max(scores, axis=1, keepdims=True)
        weights = jnp.exp2((scores - peak) * exponent)
        total = jnp.sum(weights, axis=1, keepdims=True)
        numer = jnp.dot(
            weights.astype(jnp.bfloat16), key_set[:, width:], preferred_element_type=jnp.float32
        )
        mean = numer / total
        attended[leaf * LEAF : (leaf + 1) * LEAF] = jnp.where(
            first_head, mean[:LEAF], mean[LEAF:]
        ).astype(jnp.bfloat16)
    mine = lax.axis_index("head")
    for step, share in enumerate(shares):
        count = share.shape[0]
        share[...] = attended[pl.ds(pl.multiple_of((mine ^ step) * count, count), count)]


def project_kernel(*refs):
    *parts, weight, mixed = refs
    mine = lax.axis_index("head")
    total = jnp.zeros(mixed.shape, jnp.float32)
    for step, part in enumerate(reversed(parts)):
        width = part.shape[1]
        columns = pl.ds(pl.multiple_of((mine ^ step) * width, width), width)
        total += jnp.dot(part[...], weight[columns], preferred_element_type=jnp.float32)
    mixed[...] = total.astype(mixed.dtype)


VMEM = pl.BlockSpec(memory_space=pltpu.VMEM)
HBM = pl.BlockSpec(memory_space=pltpu.HBM)


def kernel_call(body, name, megabytes, ins, outs, scratch):
    shapes = tuple(jax.ShapeDtypeStruct(shape, jnp.bfloat16) for shape in outs)
    return pl.pallas_call(
        body,
        out_shape=shapes,
        in_specs=ins,
        out_specs=(VMEM,) * len(outs),
        scratch_shapes=scratch,
        compiler_params=pltpu.CompilerParams(vmem_limit_bytes=megabytes << 20),
        name=name,
    )


def shards(queries, keys, values, out_weight):
    tokens, width = queries.shape
    seq_size = lax.axis_size("seq")
    head_size = lax.axis_size("head")
    pair_width = 2 * width
    paired = seq_size == 8
    wide_rows = 2 * LEAF if paired else max(2 * LEAF, seq_size // 2 * HALF)
    wide = pltpu.VMEM((wide_rows, width), jnp.float32)

    def swap(array, bit, axis="seq"):
        return lax.ppermute(array, axis, [(i, i ^ bit) for i in range(lax.axis_size(axis))])

    own_queries, own, inner, outer, quarter = kernel_call(
        functools.partial(pack_kernel, not paired),
        "pack",
        16,
        [HBM] * 3,
        [
            (tokens, width),
            (tokens, pair_width),
            (LEAF + HALF, pair_width),
            (LEAF + HALF, pair_width),
            (HALF, pair_width) if paired else (seq_size, HALF, pair_width),
        ],
        [wide, pltpu.SemaphoreType.DMA((3,))],
    )(*(pltpu.with_memory_space_constraint(array, pltpu.HBM) for array in (queries, keys, values)))
    inner = swap(inner, 1)
    others = [(i, i + 1 if i & 1 else i - 1) for i in range(1, seq_size - 1)]
    outer = lax.ppermute(outer, "seq", others)
    if paired:
        block, eighth = kernel_call(
            join_kernel,
            "join",
            8,
            [VMEM] * 2,
            [(LEAF, pair_width), (HALF, pair_width)],
            [wide],
        )(inner, quarter)
        far = (swap(block, 6), swap(block, 2), swap(eighth, 4))
    else:
        far = (lax.all_to_all(quarter, "seq", split_axis=0, concat_axis=0),)
    share = tokens // head_size
    shares = kernel_call(
        functools.partial(attend_kernel, seq_size, len(far)),
        "attend",
        24,
        [VMEM] * (4 + len(far)),
        [(share, width)] * head_size,
        [
            pltpu.VMEM((tokens, width), jnp.bfloat16),
            pltpu.VMEM((set_rows(seq_size), pair_width), jnp.bfloat16),
            wide,
        ],
    )(own_queries, own, inner, outer, *far)
    parts = [swap(shares[step], step, "head") for step in range(head_size - 1, 0, -1)]
    (mixed,) = kernel_call(
        project_kernel, "project", 8, [VMEM] * (head_size + 1), [(share, out_weight.shape[1])], []
    )(*parts, shares[0], out_weight)
    return mixed


def solution(mesh):
    in_specs = (P("seq", "head"), P("seq", "head"), P("seq", "head"), P())
    out_specs = P(("seq", "head"), None)
    return jax.shard_map(shards, mesh=mesh, in_specs=in_specs, out_specs=out_specs, check_vma=False)
```

```python
import functools
import math

import jax
import jax.numpy as jnp
from jax import lax
from jax.experimental import pallas as pl
from jax.experimental.pallas import tpu as pltpu
from jax.sharding import PartitionSpec as P

HD = 64
LEAF = 128
HALF = LEAF // 2
NEG = -math.inf


def average_pairs(rows, wide):
    count = rows.shape[0]
    halves = []
    for low in range(0, rows.shape[1], LEAF):
        wide[:count] = rows[:, low : low + LEAF].astype(jnp.float32)
        even = wide[pl.ds(0, count // 2, stride=2), :]
        odd = wide[pl.ds(1, count // 2, stride=2), :]
        halves.append((0.5 * (even + odd)).astype(jnp.bfloat16))
    return jnp.concatenate(halves, axis=1)


def pack_kernel(far_shares, queries, keys, values, own_queries, own, inner, outer, quarter, wide, arrived):
    width = keys.shape[1]
    copies = [
        pltpu.make_async_copy(keys, own.at[:, :width], arrived.at[0]),
        pltpu.make_async_copy(values, own.at[:, width:], arrived.at[1]),
        pltpu.make_async_copy(queries, own_queries, arrived.at[2]),
    ]
    for copy in copies:
        copy.start()
    me = lax.axis_index("seq")
    odd = me & 1
    for copy in copies:
        copy.wait()
    rows = own[...]
    low, high = rows[:LEAF], rows[LEAF:]
    level_one = average_pairs(rows, wide)
    level_two = average_pairs(level_one, wide)
    first, second = level_one[:HALF], level_one[HALF:]
    inner[:LEAF] = jnp.where(odd == 1, low, high)
    inner[LEAF:] = jnp.where(odd == 1, second, first)
    outer[:LEAF] = jnp.where(odd == 1, high, low)
    outer[LEAF:] = jnp.where(odd == 1, first, second)
    if far_shares:
        for peer in range(quarter.shape[0]):
            quarter[peer] = level_two
    else:
        quarter[...] = level_two


def join_kernel(inner, quarter, block, short, eighth, wide):
    me = lax.axis_index("seq")
    odd = me & 1
    edge_half = average_pairs(inner[:LEAF], wide)
    other_half = inner[LEAF:]
    theirs = jnp.concatenate(
        [jnp.where(odd == 1, other_half, edge_half), jnp.where(odd == 1, edge_half, other_half)], axis=0
    )
    theirs = average_pairs(theirs, wide)
    block[:HALF] = jnp.where(odd == 1, theirs, quarter[...])
    block[HALF:] = jnp.where(odd == 1, quarter[...], theirs)
    level_three = average_pairs(block[...], wide)
    eighth[...] = level_three
    round_the_end = (me == 6) | (me == 1)
    short[...] = jnp.where(round_the_end, level_three, quarter[...])


def set_rows(seq_size):
    rows = 3 * LEAF + 3 * HALF
    for far in range(1, seq_size.bit_length() - 1):
        if seq_size >> far == 2:
            rows += LEAF
        elif far == 1:
            rows += 3 * HALF
        else:
            rows += 2 * LEAF
    return rows


def bias_of(valid):
    return jnp.where(valid, jnp.float32(0.0), jnp.float32(NEG))


def gathered_pieces(seq_size, far_rows, wide):
    me = lax.axis_index("seq")
    pieces = []
    for far in range(1, seq_size.bit_length() - 1):
        span = 1 << far
        group = me >> far
        parity = (me >> (far - 1)) & 1
        blocks = seq_size >> far

        def block(number, span=span, far=far):
            found = far_rows[pl.ds(number * span, span)].reshape(span * HALF, far_rows.shape[2])
            for _ in range(far - 1):
                found = average_pairs(found, wide)
            return found

        if blocks == 2:
            rows = block(1 - group)
            first = bias_of((group == 1) | (parity == 0))
            second = bias_of((group == 0) | (parity == 1))
            pieces += [(rows[:HALF], first), (rows[HALF:], second)]
        elif far == 1:
            third = jnp.where(parity == 0, me + 3, me - 3)
            for peer in (me - 2, me + 2, third):
                ok = (peer >= 0) & (peer < seq_size)
                pieces.append((far_rows[jnp.clip(peer, 0, seq_size - 1)], bias_of(ok)))
        else:
            lower = block(jnp.maximum(group - 1, 0))
            upper = block(jnp.minimum(group + 1, blocks - 1))
            has_lower, has_upper = group >= 1, group + 1 < blocks
            pieces += [
                (lower[:HALF], bias_of(has_lower)),
                (lower[HALF:], bias_of(has_lower & (parity == 1))),
                (upper[:HALF], bias_of(has_upper & (parity == 0))),
                (upper[HALF:], bias_of(has_upper)),
            ]
    return pieces


def paired_pieces(long, short, eighth, wide):
    me = lax.axis_index("seq")
    at_end = (me == 6) | (me == 1)
    return [
        (long[:HALF], bias_of(jnp.logical_not(at_end))),
        (long[HALF:], bias_of(jnp.logical_not(at_end))),
        (average_pairs(long[...], wide), bias_of(at_end)),
        (short[...], None),
        (eighth[...], None),
    ]


def attend_kernel(seq_size, far_count, queries, own, inner, outer, *rest):
    far, shares, scratch = rest[:far_count], rest[far_count:-3], rest[-3:]
    attended, key_set, wide = scratch
    me = lax.axis_index("seq")
    width = queries.shape[1]
    odd = me & 1
    from_inner, from_outer = inner[...], outer[...]
    before = jnp.where(odd == 1, from_inner, from_outer)
    after = jnp.where(odd == 1, from_outer, from_inner)
    edge_before, edge_after = before[:LEAF], after[:LEAF]
    far_half_before, far_half_after = before[LEAF:], after[LEAF:]
    near_half_before = average_pairs(edge_before, wide)
    near_half_after = average_pairs(edge_after, wide)
    has_before, has_after = bias_of(me >= 1), bias_of(me + 1 < seq_size)
    if len(far) == 1:
        far_pieces = gathered_pieces(seq_size, far[0], wide)
    else:
        far_pieces = paired_pieces(*far, wide)

    lane = lax.broadcasted_iota(jnp.int32, (1, width), 1)
    first_head = lane < HD
    exponent = math.log2(math.e) / math.sqrt(HD)
    for leaf in range(2):
        if leaf == 0:
            near = [
                (edge_before, has_before),
                (own[...], None),
                (far_half_before, has_before),
                (near_half_after, has_after),
                (far_half_after, has_after),
            ]
        else:
            near = [
                (own[...], None),
                (edge_after, has_after),
                (far_half_before, has_before),
                (near_half_before, has_before),
                (far_half_after, has_after),
            ]
        at = 0
        total_rows = key_set.shape[0]
        position = lax.broadcasted_iota(jnp.int32, (1, total_rows), 1)
        bias = jnp.zeros((1, total_rows), jnp.float32)
        for rows, value in near + far_pieces:
            count = rows.shape[0]
            key_set[at : at + count] = rows
            if value is not None:
                bias = jnp.where((position >= at) & (position < at + count), value, bias)
            at += count
        block_queries = queries[leaf * LEAF : (leaf + 1) * LEAF]
        none = jnp.zeros_like(block_queries)
        both = jnp.concatenate(
            [jnp.where(first_head, block_queries, none), jnp.where(first_head, none, block_queries)], axis=0
        )
        scores = lax.dot_general(
            both, key_set[:, :width], (((1,), (1,)), ((), ())), preferred_element_type=jnp.float32
        )
        scores = scores + bias
        peak = jnp.max(scores, axis=1, keepdims=True)
        weights = jnp.exp2((scores - peak) * exponent)
        total = jnp.sum(weights, axis=1, keepdims=True)
        numer = jnp.dot(
            weights.astype(jnp.bfloat16), key_set[:, width:], preferred_element_type=jnp.float32
        )
        mean = numer / total
        attended[leaf * LEAF : (leaf + 1) * LEAF] = jnp.where(
            first_head, mean[:LEAF], mean[LEAF:]
        ).astype(jnp.bfloat16)
    mine = lax.axis_index("head")
    for step, share in enumerate(shares):
        count = share.shape[0]
        share[...] = attended[pl.ds(pl.multiple_of((mine ^ step) * count, count), count)]


def project_kernel(*refs):
    *parts, weight, mixed = refs
    mine = lax.axis_index("head")
    total = jnp.zeros(mixed.shape, jnp.float32)
    for step, part in enumerate(reversed(parts)):
        width = part.shape[1]
        columns = pl.ds(pl.multiple_of((mine ^ step) * width, width), width)
        total += jnp.dot(part[...], weight[columns], preferred_element_type=jnp.float32)
    mixed[...] = total.astype(mixed.dtype)


VMEM = pl.BlockSpec(memory_space=pltpu.VMEM)
HBM = pl.BlockSpec(memory_space=pltpu.HBM)


def kernel_call(body, name, megabytes, ins, outs, scratch):
    shapes = tuple(jax.ShapeDtypeStruct(shape, jnp.bfloat16) for shape in outs)
    return pl.pallas_call(
        body,
        out_shape=shapes,
        in_specs=ins,
        out_specs=(VMEM,) * len(outs),
        scratch_shapes=scratch,
        compiler_params=pltpu.CompilerParams(vmem_limit_bytes=megabytes << 20),
        name=name,
    )


def shards(queries, keys, values, out_weight):
    tokens, width = queries.shape
    seq_size = lax.axis_size("seq")
    head_size = lax.axis_size("head")
    pair_width = 2 * width
    paired = seq_size == 8
    wide_rows = 2 * LEAF if paired else max(2 * LEAF, seq_size // 2 * HALF)
    wide = pltpu.VMEM((wide_rows, width), jnp.float32)

    def swap(array, bit, axis="seq"):
        return lax.ppermute(array, axis, [(i, i ^ bit) for i in range(lax.axis_size(axis))])

    own_queries, own, inner, outer, quarter = kernel_call(
        functools.partial(pack_kernel, not paired),
        "pack",
        16,
        [HBM] * 3,
        [
            (tokens, width),
            (tokens, pair_width),
            (LEAF + HALF, pair_width),
            (LEAF + HALF, pair_width),
            (HALF, pair_width) if paired else (seq_size, HALF, pair_width),
        ],
        [wide, pltpu.SemaphoreType.DMA((3,))],
    )(*(pltpu.with_memory_space_constraint(array, pltpu.HBM) for array in (queries, keys, values)))
    inner = swap(inner, 1)
    others = [(i, i + 1 if i & 1 else i - 1) for i in range(1, seq_size - 1)]
    outer = lax.ppermute(outer, "seq", others)
    if paired:
        block, short, eighth = kernel_call(
            join_kernel,
            "join",
            8,
            [VMEM] * 2,
            [(LEAF, pair_width), (HALF, pair_width), (HALF, pair_width)],
            [wide],
        )(inner, quarter)
        down_up = [(i, (i + 2 if i & 1 else i - 2) % seq_size) for i in range(seq_size)]
        up_down = [(target, source) for source, target in down_up]
        far = (
            lax.ppermute(block, "seq", down_up),
            lax.ppermute(short, "seq", up_down),
            swap(eighth, 4),
        )
    else:
        far = (lax.all_to_all(quarter, "seq", split_axis=0, concat_axis=0),)
    share = tokens // head_size
    shares = kernel_call(
        functools.partial(attend_kernel, seq_size, len(far)),
        "attend",
        24,
        [VMEM] * (4 + len(far)),
        [(share, width)] * head_size,
        [
            pltpu.VMEM((tokens, width), jnp.bfloat16),
            pltpu.VMEM((set_rows(seq_size), pair_width), jnp.bfloat16),
            wide,
        ],
    )(own_queries, own, inner, outer, *far)
    parts = [swap(shares[step], step, "head") for step in range(head_size - 1, 0, -1)]
    (mixed,) = kernel_call(
        project_kernel, "project", 8, [VMEM] * (head_size + 1), [(share, out_weight.shape[1])], []
    )(*parts, shares[0], out_weight)
    return mixed


def solution(mesh):
    in_specs = (P("seq", "head"), P("seq", "head"), P("seq", "head"), P())
    out_specs = P(("seq", "head"), None)
    return jax.shard_map(shards, mesh=mesh, in_specs=in_specs, out_specs=out_specs, check_vma=False)
```

```python
import functools
import math

import jax
import jax.numpy as jnp
from jax import lax
from jax.experimental import pallas as pl
from jax.experimental.pallas import tpu as pltpu
from jax.sharding import PartitionSpec as P

HD = 64
LEAF = 128
HALF = LEAF // 2
NEG = -math.inf


def average_pairs(rows, wide):
    count = rows.shape[0]
    halves = []
    for low in range(0, rows.shape[1], LEAF):
        wide[:count] = rows[:, low : low + LEAF].astype(jnp.float32)
        even = wide[pl.ds(0, count // 2, stride=2), :]
        odd = wide[pl.ds(1, count // 2, stride=2), :]
        halves.append((0.5 * (even + odd)).astype(jnp.bfloat16))
    return jnp.concatenate(halves, axis=1)


def pack_kernel(far_shares, queries, keys, values, own_queries, own, inner, outer, quarter, wide, arrived):
    width = keys.shape[1]
    copies = [
        pltpu.make_async_copy(keys, own.at[:, :width], arrived.at[0]),
        pltpu.make_async_copy(values, own.at[:, width:], arrived.at[1]),
        pltpu.make_async_copy(queries, own_queries, arrived.at[2]),
    ]
    for copy in copies:
        copy.start()
    me = lax.axis_index("seq")
    odd = me & 1
    for copy in copies:
        copy.wait()
    rows = own[...]
    low, high = rows[:LEAF], rows[LEAF:]
    level_one = average_pairs(rows, wide)
    level_two = average_pairs(level_one, wide)
    first, second = level_one[:HALF], level_one[HALF:]
    inner[:LEAF] = jnp.where(odd == 1, low, high)
    inner[LEAF:] = jnp.where(odd == 1, second, first)
    outer[:LEAF] = jnp.where(odd == 1, high, low)
    outer[LEAF:] = jnp.where(odd == 1, first, second)
    if far_shares:
        for peer in range(quarter.shape[0]):
            quarter[peer] = level_two
    else:
        quarter[...] = level_two


def join_kernel(inner, quarter, block, eighth, wide):
    odd = lax.axis_index("seq") & 1
    edge_half = average_pairs(inner[:LEAF], wide)
    other_half = inner[LEAF:]
    theirs = jnp.concatenate(
        [jnp.where(odd == 1, other_half, edge_half), jnp.where(odd == 1, edge_half, other_half)], axis=0
    )
    theirs = average_pairs(theirs, wide)
    block[:HALF] = jnp.where(odd == 1, theirs, quarter[...])
    block[HALF:] = jnp.where(odd == 1, quarter[...], theirs)
    eighth[...] = average_pairs(block[...], wide)


NEAR_ROWS = 3 * LEAF + 3 * HALF


def far_row_count(seq_size):
    rows = 0
    for far in range(1, seq_size.bit_length() - 1):
        if seq_size >> far == 2:
            rows += LEAF
        elif far == 1:
            rows += 3 * HALF
        else:
            rows += 2 * LEAF
    return rows


def bias_of(valid):
    return jnp.where(valid, jnp.float32(0.0), jnp.float32(NEG))


def gathered_pieces(seq_size, far_rows, wide):
    me = lax.axis_index("seq")
    pieces = []
    for far in range(1, seq_size.bit_length() - 1):
        span = 1 << far
        group = me >> far
        parity = (me >> (far - 1)) & 1
        blocks = seq_size >> far

        def block(number, span=span, far=far):
            found = far_rows[pl.ds(number * span, span)].reshape(span * HALF, far_rows.shape[2])
            for _ in range(far - 1):
                found = average_pairs(found, wide)
            return found

        if blocks == 2:
            rows = block(1 - group)
            first = bias_of((group == 1) | (parity == 0))
            second = bias_of((group == 0) | (parity == 1))
            pieces += [(rows[:HALF], first), (rows[HALF:], second)]
        elif far == 1:
            third = jnp.where(parity == 0, me + 3, me - 3)
            for peer in (me - 2, me + 2, third):
                ok = (peer >= 0) & (peer < seq_size)
                pieces.append((far_rows[jnp.clip(peer, 0, seq_size - 1)], bias_of(ok)))
        else:
            lower = block(jnp.maximum(group - 1, 0))
            upper = block(jnp.minimum(group + 1, blocks - 1))
            has_lower, has_upper = group >= 1, group + 1 < blocks
            pieces += [
                (lower[:HALF], bias_of(has_lower)),
                (lower[HALF:], bias_of(has_lower & (parity == 1))),
                (upper[:HALF], bias_of(has_upper & (parity == 0))),
                (upper[HALF:], bias_of(has_upper)),
            ]
    return pieces


def paired_pieces(block_6, block_2, eighth_4, wide):
    me = lax.axis_index("seq")
    odd = me & 1
    pair = me >> 1
    middle = (pair == 1) | (pair == 2)
    upper_near = (pair & 1) == 0
    lower = jnp.where(upper_near, block_6[...], block_2[...])
    upper = jnp.where(upper_near, block_2[...], block_6[...])
    has_lower, has_upper = pair >= 1, pair <= 2
    third = jnp.where(odd == 1, lower[HALF:], upper[:HALF])
    has_third = ((odd == 1) & has_lower) | ((odd == 0) & has_upper)
    ends = average_pairs(block_6[...], wide)
    return [
        (lower[:HALF], bias_of(has_lower)),
        (upper[HALF:], bias_of(has_upper)),
        (third, bias_of(has_third)),
        (eighth_4[...], bias_of(pair >= 0)),
        (ends, bias_of(jnp.logical_not(middle))),
    ]


def place(pieces, values, keys):
    at = 0
    width = values.shape[1]
    total_rows = values.shape[0]
    position = lax.broadcasted_iota(jnp.int32, (1, total_rows), 1)
    bias = jnp.zeros((1, total_rows), jnp.float32)
    for rows, value in pieces:
        count = rows.shape[0]
        keys[at : at + count] = rows[:, :width]
        values[at : at + count] = rows[:, width:]
        if value is not None:
            bias = jnp.where((position >= at) & (position < at + count), value, bias)
        at += count
    return bias


def split_heads(rows):
    first_head = lax.broadcasted_iota(jnp.int32, (1, rows.shape[1]), 1) < HD
    none = jnp.zeros_like(rows)
    return jnp.concatenate(
        [jnp.where(first_head, rows, none), jnp.where(first_head, none, rows)], axis=0
    )


def scores_of(queries, keys):
    return lax.dot_general(
        queries, keys[...], (((1,), (1,)), ((), ())), preferred_element_type=jnp.float32
    )


def near_kernel(seq_size, queries, own, inner, outer, scores, values, keys, wide):
    me = lax.axis_index("seq")
    odd = me & 1
    from_inner, from_outer = inner[...], outer[...]
    before = jnp.where(odd == 1, from_inner, from_outer)
    after = jnp.where(odd == 1, from_outer, from_inner)
    edge_before, edge_after = before[:LEAF], after[:LEAF]
    far_half_before, far_half_after = before[LEAF:], after[LEAF:]
    near_half_before = average_pairs(edge_before, wide)
    near_half_after = average_pairs(edge_after, wide)
    has_before, has_after = bias_of(me >= 1), bias_of(me + 1 < seq_size)
    for leaf in range(2):
        if leaf == 0:
            near = [
                (edge_before, has_before),
                (own[...], None),
                (far_half_before, has_before),
                (near_half_after, has_after),
                (far_half_after, has_after),
            ]
        else:
            near = [
                (own[...], None),
                (edge_after, has_after),
                (far_half_before, has_before),
                (near_half_before, has_before),
                (far_half_after, has_after),
            ]
        bias = place(near, values.at[leaf], keys)
        rows = split_heads(queries[leaf * LEAF : (leaf + 1) * LEAF])
        scores[leaf] = scores_of(rows, keys) + bias


def attend_kernel(seq_size, far_count, queries, near_scores, near_values, *rest):
    far, shares, scratch = rest[:far_count], rest[far_count:-4], rest[-4:]
    attended, keys, values, wide = scratch
    if far_count == 1:
        pieces = gathered_pieces(seq_size, far[0], wide)
    else:
        pieces = paired_pieces(*far, wide)
    bias = place(pieces, values, keys)
    first_head = lax.broadcasted_iota(jnp.int32, (1, values.shape[1]), 1) < HD
    exponent = math.log2(math.e) / math.sqrt(HD)
    for leaf in range(2):
        rows = split_heads(queries[leaf * LEAF : (leaf + 1) * LEAF])
        near = near_scores[leaf]
        far_scores = scores_of(rows, keys) + bias
        peak = jnp.maximum(
            jnp.max(near, axis=1, keepdims=True), jnp.max(far_scores, axis=1, keepdims=True)
        )
        near = jnp.exp2((near - peak) * exponent)
        far_weights = jnp.exp2((far_scores - peak) * exponent)
        total = jnp.sum(near, axis=1, keepdims=True) + jnp.sum(far_weights, axis=1, keepdims=True)
        numer = jnp.dot(
            near.astype(jnp.bfloat16), near_values[leaf], preferred_element_type=jnp.float32
        ) + jnp.dot(
            far_weights.astype(jnp.bfloat16), values[...], preferred_element_type=jnp.float32
        )
        mean = numer / total
        attended[leaf * LEAF : (leaf + 1) * LEAF] = jnp.where(
            first_head, mean[:LEAF], mean[LEAF:]
        ).astype(jnp.bfloat16)
    mine = lax.axis_index("head")
    for step, share in enumerate(shares):
        count = share.shape[0]
        share[...] = attended[pl.ds(pl.multiple_of((mine ^ step) * count, count), count)]


def project_kernel(*refs):
    *parts, weight, mixed = refs
    mine = lax.axis_index("head")
    total = jnp.zeros(mixed.shape, jnp.float32)
    for step, part in enumerate(reversed(parts)):
        width = part.shape[1]
        columns = pl.ds(pl.multiple_of((mine ^ step) * width, width), width)
        total += jnp.dot(part[...], weight[columns], preferred_element_type=jnp.float32)
    mixed[...] = total.astype(mixed.dtype)


VMEM = pl.BlockSpec(memory_space=pltpu.VMEM)
HBM = pl.BlockSpec(memory_space=pltpu.HBM)


def kernel_call(body, name, megabytes, ins, outs, scratch, flops=0):
    shapes = tuple(
        out if isinstance(out, jax.ShapeDtypeStruct) else jax.ShapeDtypeStruct(out, jnp.bfloat16)
        for out in outs
    )
    return pl.pallas_call(
        body,
        out_shape=shapes,
        in_specs=ins,
        out_specs=(VMEM,) * len(outs),
        scratch_shapes=scratch,
        compiler_params=pltpu.CompilerParams(vmem_limit_bytes=megabytes << 20),
        cost_estimate=pl.CostEstimate(flops=flops, bytes_accessed=1 << 20, transcendentals=0),
        name=name,
    )


def shards(queries, keys, values, out_weight):
    tokens, width = queries.shape
    seq_size = lax.axis_size("seq")
    head_size = lax.axis_size("head")
    pair_width = 2 * width
    paired = seq_size == 8
    wide_rows = 2 * LEAF if paired else max(2 * LEAF, seq_size // 2 * HALF)
    wide = pltpu.VMEM((wide_rows, width), jnp.float32)

    def swap(array, bit, axis="seq"):
        return lax.ppermute(array, axis, [(i, i ^ bit) for i in range(lax.axis_size(axis))])

    own_queries, own, inner, outer, quarter = kernel_call(
        functools.partial(pack_kernel, not paired),
        "pack",
        16,
        [HBM] * 3,
        [
            (tokens, width),
            (tokens, pair_width),
            (LEAF + HALF, pair_width),
            (LEAF + HALF, pair_width),
            (HALF, pair_width) if paired else (seq_size, HALF, pair_width),
        ],
        [wide, pltpu.SemaphoreType.DMA((3,))],
    )(*(pltpu.with_memory_space_constraint(array, pltpu.HBM) for array in (queries, keys, values)))
    inner = swap(inner, 1)
    others = [(i, i + 1 if i & 1 else i - 1) for i in range(1, seq_size - 1)]
    outer = lax.ppermute(outer, "seq", others)
    if paired:
        block, eighth = kernel_call(
            join_kernel,
            "join",
            8,
            [VMEM] * 2,
            [(LEAF, pair_width), (HALF, pair_width)],
            [wide],
        )(inner, quarter)
        far = (swap(block, 6), swap(block, 2), swap(eighth, 4))
    else:
        far = (lax.all_to_all(quarter, "seq", split_axis=0, concat_axis=0),)
    share = tokens // head_size
    near_scores, near_values = kernel_call(
        functools.partial(near_kernel, seq_size),
        "near",
        16,
        [VMEM] * 4,
        [
            jax.ShapeDtypeStruct((2, 2 * LEAF, NEAR_ROWS), jnp.float32),
            (2, NEAR_ROWS, width),
        ],
        [pltpu.VMEM((NEAR_ROWS, width), jnp.bfloat16), wide],
        flops=8 * LEAF * NEAR_ROWS * width,
    )(own_queries, own, inner, outer)
    far_rows = far_row_count(seq_size)
    shares = kernel_call(
        functools.partial(attend_kernel, seq_size, len(far)),
        "attend",
        24,
        [VMEM] * (3 + len(far)),
        [(share, width)] * head_size,
        [
            pltpu.VMEM((tokens, width), jnp.bfloat16),
            pltpu.VMEM((far_rows, width), jnp.bfloat16),
            pltpu.VMEM((far_rows, width), jnp.bfloat16),
            wide,
        ],
        flops=16 * LEAF * (NEAR_ROWS + far_rows) * width,
    )(own_queries, near_scores, near_values, *far)
    parts = [swap(shares[step], step, "head") for step in range(head_size - 1, 0, -1)]
    (mixed,) = kernel_call(
        project_kernel, "project", 8, [VMEM] * (head_size + 1), [(share, out_weight.shape[1])], []
    )(*parts, shares[0], out_weight)
    return mixed


def solution(mesh):
    in_specs = (P("seq", "head"), P("seq", "head"), P("seq", "head"), P())
    out_specs = P(("seq", "head"), None)
    return jax.shard_map(shards, mesh=mesh, in_specs=in_specs, out_specs=out_specs, check_vma=False)
```

```python
import functools
import math

import jax
import jax.numpy as jnp
from jax import lax
from jax.experimental import pallas as pl
from jax.experimental.pallas import tpu as pltpu
from jax.sharding import PartitionSpec as P

HD = 64
LEAF = 128
HALF = LEAF // 2
NEG = -math.inf


def average_pairs(rows, wide):
    count = rows.shape[0]
    halves = []
    for low in range(0, rows.shape[1], LEAF):
        wide[:count] = rows[:, low : low + LEAF].astype(jnp.float32)
        even = wide[pl.ds(0, count // 2, stride=2), :]
        odd = wide[pl.ds(1, count // 2, stride=2), :]
        halves.append((0.5 * (even + odd)).astype(jnp.bfloat16))
    return jnp.concatenate(halves, axis=1)


def pack_kernel(far_shares, queries, keys, values, own_queries, own, inner, outer, quarter, wide, arrived):
    width = keys.shape[1]
    copies = [
        pltpu.make_async_copy(keys, own.at[:, :width], arrived.at[0]),
        pltpu.make_async_copy(values, own.at[:, width:], arrived.at[1]),
        pltpu.make_async_copy(queries, own_queries, arrived.at[2]),
    ]
    for copy in copies:
        copy.start()
    me = lax.axis_index("seq")
    odd = me & 1
    for copy in copies:
        copy.wait()
    rows = own[...]
    low, high = rows[:LEAF], rows[LEAF:]
    level_one = average_pairs(rows, wide)
    level_two = average_pairs(level_one, wide)
    first, second = level_one[:HALF], level_one[HALF:]
    inner[:LEAF] = jnp.where(odd == 1, low, high)
    inner[LEAF:] = jnp.where(odd == 1, second, first)
    outer[:LEAF] = jnp.where(odd == 1, high, low)
    outer[LEAF:] = jnp.where(odd == 1, first, second)
    if far_shares:
        for peer in range(quarter.shape[0]):
            quarter[peer] = level_two
    else:
        quarter[...] = level_two


def join_kernel(inner, quarter, block, eighth, wide):
    odd = lax.axis_index("seq") & 1
    edge_half = average_pairs(inner[:LEAF], wide)
    other_half = inner[LEAF:]
    theirs = jnp.concatenate(
        [jnp.where(odd == 1, other_half, edge_half), jnp.where(odd == 1, edge_half, other_half)], axis=0
    )
    theirs = average_pairs(theirs, wide)
    block[:HALF] = jnp.where(odd == 1, theirs, quarter[...])
    block[HALF:] = jnp.where(odd == 1, quarter[...], theirs)
    eighth[...] = average_pairs(block[...], wide)


NEAR_ROWS = 4 * LEAF
PAD = 16


def far_row_count(seq_size):
    rows = HALF
    for far in range(1, seq_size.bit_length() - 1):
        if seq_size >> far == 2:
            rows += LEAF
        elif far == 1:
            rows += 3 * HALF
        else:
            rows += 2 * LEAF
    return rows


def bias_of(valid):
    return jnp.where(valid, jnp.float32(0.0), jnp.float32(NEG))


def gathered_pieces(seq_size, far_rows, wide):
    me = lax.axis_index("seq")
    pieces = []
    for far in range(1, seq_size.bit_length() - 1):
        span = 1 << far
        group = me >> far
        parity = (me >> (far - 1)) & 1
        blocks = seq_size >> far

        def block(number, span=span, far=far):
            found = far_rows[pl.ds(number * span, span)].reshape(span * HALF, far_rows.shape[2])
            for _ in range(far - 1):
                found = average_pairs(found, wide)
            return found

        if blocks == 2:
            rows = block(1 - group)
            first = bias_of((group == 1) | (parity == 0))
            second = bias_of((group == 0) | (parity == 1))
            pieces += [(rows[:HALF], first), (rows[HALF:], second)]
        elif far == 1:
            third = jnp.where(parity == 0, me + 3, me - 3)
            for peer in (me - 2, me + 2, third):
                ok = (peer >= 0) & (peer < seq_size)
                pieces.append((far_rows[jnp.clip(peer, 0, seq_size - 1)], bias_of(ok)))
        else:
            lower = block(jnp.maximum(group - 1, 0))
            upper = block(jnp.minimum(group + 1, blocks - 1))
            has_lower, has_upper = group >= 1, group + 1 < blocks
            pieces += [
                (lower[:HALF], bias_of(has_lower)),
                (lower[HALF:], bias_of(has_lower & (parity == 1))),
                (upper[:HALF], bias_of(has_upper & (parity == 0))),
                (upper[HALF:], bias_of(has_upper)),
            ]
    return pieces


def paired_pieces(block_6, block_2, eighth_4, wide):
    me = lax.axis_index("seq")
    odd = me & 1
    pair = me >> 1
    middle = (pair == 1) | (pair == 2)
    upper_near = (pair & 1) == 0
    lower = jnp.where(upper_near, block_6[...], block_2[...])
    upper = jnp.where(upper_near, block_2[...], block_6[...])
    has_lower, has_upper = pair >= 1, pair <= 2
    third = jnp.where(odd == 1, lower[HALF:], upper[:HALF])
    has_third = ((odd == 1) & has_lower) | ((odd == 0) & has_upper)
    ends = average_pairs(block_6[...], wide)
    return [
        (lower[:HALF], bias_of(has_lower)),
        (upper[HALF:], bias_of(has_upper)),
        (third, bias_of(has_third)),
        (eighth_4[...], bias_of(pair >= 0)),
        (ends, bias_of(jnp.logical_not(middle))),
    ]


def place(pieces, values, keys):
    at = 0
    width = values.shape[1]
    total_rows = values.shape[0]
    position = lax.broadcasted_iota(jnp.int32, (1, total_rows), 1)
    bias = jnp.zeros((1, total_rows), jnp.float32)
    for rows, value in pieces:
        count = rows.shape[0]
        keys[at : at + count] = rows[:, :width]
        values[at : at + count] = rows[:, width:]
        if value is not None:
            bias = jnp.where((position >= at) & (position < at + count), value, bias)
        at += count
    return bias


def split_heads(rows):
    first_head = lax.broadcasted_iota(jnp.int32, (1, rows.shape[1]), 1) < HD
    none = jnp.zeros_like(rows)
    return jnp.concatenate(
        [jnp.where(first_head, rows, none), jnp.where(first_head, none, rows)], axis=0
    )


def scores_of(queries, keys):
    return lax.dot_general(
        queries, keys[...], (((1,), (1,)), ((), ())), preferred_element_type=jnp.float32
    )


def near_kernel(seq_size, queries, own, inner, outer, scores, values, shared, keys, wide):
    me = lax.axis_index("seq")
    odd = me & 1
    from_inner, from_outer = inner[...], outer[...]
    before = jnp.where(odd == 1, from_inner, from_outer)
    after = jnp.where(odd == 1, from_outer, from_inner)
    edge_before, edge_after = before[:LEAF], after[:LEAF]
    far_half_after = after[LEAF:]
    shared[...] = before[LEAF:]
    near_half_before = average_pairs(edge_before, wide)
    near_half_after = average_pairs(edge_after, wide)
    has_before, has_after = bias_of(me >= 1), bias_of(me + 1 < seq_size)
    for leaf in range(2):
        if leaf == 0:
            near = [
                (edge_before, has_before),
                (own[...], None),
                (near_half_after, has_after),
                (far_half_after, has_after),
            ]
        else:
            near = [
                (own[...], None),
                (edge_after, has_after),
                (near_half_before, has_before),
                (far_half_after, has_after),
            ]
        bias = place(near, values.at[leaf], keys)
        rows = split_heads(queries[leaf * LEAF : (leaf + 1) * LEAF])
        scores[leaf] = scores_of(rows, keys) + bias


def attend_leaf(leaf, queries, near_scores, near_values, keys, values, bias, same, other):
    first_head = lax.broadcasted_iota(jnp.int32, (1, values.shape[1]), 1) < HD
    exponent = math.log2(math.e) / math.sqrt(HD)
    rows = split_heads(queries[pl.ds(pl.multiple_of(leaf * LEAF, LEAF), LEAF)])
    near = near_scores[leaf]
    far_scores = scores_of(rows, keys) + bias
    peak = jnp.maximum(
        jnp.max(near, axis=1, keepdims=True), jnp.max(far_scores, axis=1, keepdims=True)
    )
    near = jnp.exp2((near - peak) * exponent)
    far_weights = jnp.exp2((far_scores - peak) * exponent)
    total = jnp.sum(near, axis=1, keepdims=True) + jnp.sum(far_weights, axis=1, keepdims=True)
    numer = jnp.dot(
        near.astype(jnp.bfloat16), near_values[leaf], preferred_element_type=jnp.float32
    ) + jnp.dot(far_weights.astype(jnp.bfloat16), values[...], preferred_element_type=jnp.float32)
    mean = numer / total
    attended = jnp.where(first_head, mean[:LEAF], mean[LEAF:]).astype(jnp.bfloat16)
    second = (lax.axis_index("head") & 1) == 1
    same[:HALF] = jnp.where(second, attended[HALF:], attended[:HALF])
    other[:HALF] = jnp.where(second, attended[:HALF], attended[HALF:])


def leaves_kernel(seq_size, queries, near_scores, near_values, shared, *rest):
    *far, same, other, keys, values, bias, wide = rest
    if len(far) == 1:
        pieces = gathered_pieces(seq_size, far[0], wide)
    else:
        pieces = paired_pieces(*far, wide)
    shared_bias = bias_of(lax.axis_index("seq") >= 1)
    bias[...] = jnp.broadcast_to(place([(shared, shared_bias)] + pieces, values, keys), bias.shape)
    leaf = (lax.axis_index("head") >> 1) ^ 1
    attend_leaf(leaf, queries, near_scores, near_values, keys, values, bias[:1], same, other)
    for share in (same, other):
        share[HALF:] = jnp.zeros((PAD, share.shape[1]), share.dtype)


def stays_kernel(queries, near_scores, near_values, keys, values, bias, same, other):
    leaf = lax.axis_index("head") >> 1
    attend_leaf(leaf, queries, near_scores, near_values, keys, values, bias[:1], same, other)


def project_kernel(*refs):
    *parts, weight, mixed = refs
    mine = lax.axis_index("head")
    total = jnp.zeros(mixed.shape, jnp.float32)
    for step, part in enumerate(reversed(parts)):
        width = part.shape[1]
        columns = pl.ds(pl.multiple_of((mine ^ step) * width, width), width)
        total += jnp.dot(part[: mixed.shape[0]], weight[columns], preferred_element_type=jnp.float32)
    mixed[...] = total.astype(mixed.dtype)


VMEM = pl.BlockSpec(memory_space=pltpu.VMEM)
HBM = pl.BlockSpec(memory_space=pltpu.HBM)


def kernel_call(body, name, megabytes, ins, outs, scratch, flops=0):
    shapes = tuple(
        out if isinstance(out, jax.ShapeDtypeStruct) else jax.ShapeDtypeStruct(out, jnp.bfloat16)
        for out in outs
    )
    return pl.pallas_call(
        body,
        out_shape=shapes,
        in_specs=ins,
        out_specs=(VMEM,) * len(outs),
        scratch_shapes=scratch,
        compiler_params=pltpu.CompilerParams(vmem_limit_bytes=megabytes << 20),
        cost_estimate=pl.CostEstimate(flops=flops, bytes_accessed=1 << 20, transcendentals=0),
        name=name,
    )


def shards(queries, keys, values, out_weight):
    tokens, width = queries.shape
    seq_size = lax.axis_size("seq")
    head_size = lax.axis_size("head")
    pair_width = 2 * width
    paired = seq_size == 8
    wide_rows = 2 * LEAF if paired else max(2 * LEAF, seq_size // 2 * HALF)
    wide = pltpu.VMEM((wide_rows, width), jnp.float32)

    def swap(array, bit, axis="seq"):
        return lax.ppermute(array, axis, [(i, i ^ bit) for i in range(lax.axis_size(axis))])

    own_queries, own, inner, outer, quarter = kernel_call(
        functools.partial(pack_kernel, not paired),
        "pack",
        16,
        [HBM] * 3,
        [
            (tokens, width),
            (tokens, pair_width),
            (LEAF + HALF, pair_width),
            (LEAF + HALF, pair_width),
            (HALF, pair_width) if paired else (seq_size, HALF, pair_width),
        ],
        [wide, pltpu.SemaphoreType.DMA((3,))],
    )(*(pltpu.with_memory_space_constraint(array, pltpu.HBM) for array in (queries, keys, values)))
    inner = swap(inner, 1)
    others = [(i, i + 1 if i & 1 else i - 1) for i in range(1, seq_size - 1)]
    outer = lax.ppermute(outer, "seq", others)
    if paired:
        block, eighth = kernel_call(
            join_kernel,
            "join",
            8,
            [VMEM] * 2,
            [(LEAF, pair_width), (HALF, pair_width)],
            [wide],
        )(inner, quarter)
        far = (swap(block, 6), swap(block, 2), swap(eighth, 4))
    else:
        far = (lax.all_to_all(quarter, "seq", split_axis=0, concat_axis=0),)
    share = tokens // head_size
    near_scores, near_values, shared = kernel_call(
        functools.partial(near_kernel, seq_size),
        "near",
        16,
        [VMEM] * 4,
        [
            jax.ShapeDtypeStruct((2, 2 * LEAF, NEAR_ROWS), jnp.float32),
            (2, NEAR_ROWS, width),
            (HALF, pair_width),
        ],
        [pltpu.VMEM((NEAR_ROWS, width), jnp.bfloat16), wide],
        flops=8 * LEAF * NEAR_ROWS * width,
    )(own_queries, own, inner, outer)
    far_rows = far_row_count(seq_size)

    leaf_flops = 8 * LEAF * (NEAR_ROWS + far_rows) * width
    share_2, share_3, far_keys, far_values, far_bias = kernel_call(
        functools.partial(leaves_kernel, seq_size),
        "leaves",
        24,
        [VMEM] * (4 + len(far)),
        [
            (share + PAD, width),
            (share + PAD, width),
            (far_rows, width),
            (far_rows, width),
            jax.ShapeDtypeStruct((8, far_rows), jnp.float32),
        ],
        [wide],
        flops=leaf_flops,
    )(own_queries, near_scores, near_values, shared, *far)
    share_0, share_1 = kernel_call(
        stays_kernel, "stays", 16, [VMEM] * 6, [(share, width)] * 2, [], flops=leaf_flops
    )(own_queries, near_scores, near_values, far_keys, far_values, far_bias)
    parts = [swap(share_3, 3, "head"), swap(share_2, 2, "head"), swap(share_1, 1, "head"), share_0]
    (mixed,) = kernel_call(
        project_kernel, "project", 8, [VMEM] * (head_size + 1), [(share, out_weight.shape[1])], []
    )(*parts, out_weight)
    return mixed


def solution(mesh):
    in_specs = (P("seq", "head"), P("seq", "head"), P("seq", "head"), P())
    out_specs = P(("seq", "head"), None)
    return jax.shard_map(shards, mesh=mesh, in_specs=in_specs, out_specs=out_specs, check_vma=False)
```

```python
import functools
import math

import jax
import jax.numpy as jnp
from jax import lax
from jax.experimental import pallas as pl
from jax.experimental.pallas import tpu as pltpu
from jax.sharding import PartitionSpec as P

HD = 64
LEAF = 128
HALF = LEAF // 2
NEG = -math.inf


def average_pairs(rows, wide):
    count = rows.shape[0]
    halves = []
    for low in range(0, rows.shape[1], LEAF):
        wide[:count] = rows[:, low : low + LEAF].astype(jnp.float32)
        even = wide[pl.ds(0, count // 2, stride=2), :]
        odd = wide[pl.ds(1, count // 2, stride=2), :]
        halves.append((0.5 * (even + odd)).astype(jnp.bfloat16))
    return jnp.concatenate(halves, axis=1)


def pack_kernel(far_shares, queries, keys, values, own_queries, own, inner, outer, quarter, wide, arrived):
    width = keys.shape[1]
    copies = [
        pltpu.make_async_copy(keys, own.at[:, :width], arrived.at[0]),
        pltpu.make_async_copy(values, own.at[:, width:], arrived.at[1]),
        pltpu.make_async_copy(queries, own_queries, arrived.at[2]),
    ]
    for copy in copies:
        copy.start()
    me = lax.axis_index("seq")
    odd = me & 1
    for copy in copies:
        copy.wait()
    rows = own[...]
    low, high = rows[:LEAF], rows[LEAF:]
    level_one = average_pairs(rows, wide)
    level_two = average_pairs(level_one, wide)
    first, second = level_one[:HALF], level_one[HALF:]
    inner[:LEAF] = jnp.where(odd == 1, low, high)
    inner[LEAF:] = jnp.where(odd == 1, second, first)
    outer[:LEAF] = jnp.where(odd == 1, high, low)
    outer[LEAF:] = jnp.where(odd == 1, first, second)
    if far_shares:
        for peer in range(quarter.shape[0]):
            quarter[peer] = level_two
    else:
        quarter[...] = level_two


def join_kernel(inner, quarter, block, eighth, wide):
    odd = lax.axis_index("seq") & 1
    edge_half = average_pairs(inner[:LEAF], wide)
    other_half = inner[LEAF:]
    theirs = jnp.concatenate(
        [jnp.where(odd == 1, other_half, edge_half), jnp.where(odd == 1, edge_half, other_half)], axis=0
    )
    theirs = average_pairs(theirs, wide)
    block[:HALF] = jnp.where(odd == 1, theirs, quarter[...])
    block[HALF:] = jnp.where(odd == 1, quarter[...], theirs)
    eighth[...] = average_pairs(block[...], wide)


NEAR_ROWS = 4 * LEAF
PAD = 16


def far_row_count(seq_size):
    rows = HALF
    for far in range(1, seq_size.bit_length() - 1):
        if seq_size >> far == 2:
            rows += LEAF
        elif far == 1:
            rows += 3 * HALF
        else:
            rows += 2 * LEAF
    return rows


def bias_of(valid):
    return jnp.where(valid, jnp.float32(0.0), jnp.float32(NEG))


def gathered_pieces(seq_size, far_rows, wide):
    me = lax.axis_index("seq")
    pieces = []
    for far in range(1, seq_size.bit_length() - 1):
        span = 1 << far
        group = me >> far
        parity = (me >> (far - 1)) & 1
        blocks = seq_size >> far

        def block(number, span=span, far=far):
            found = far_rows[pl.ds(number * span, span)].reshape(span * HALF, far_rows.shape[2])
            for _ in range(far - 1):
                found = average_pairs(found, wide)
            return found

        if blocks == 2:
            rows = block(1 - group)
            first = bias_of((group == 1) | (parity == 0))
            second = bias_of((group == 0) | (parity == 1))
            pieces += [(rows[:HALF], first), (rows[HALF:], second)]
        elif far == 1:
            third = jnp.where(parity == 0, me + 3, me - 3)
            for peer in (me - 2, me + 2, third):
                ok = (peer >= 0) & (peer < seq_size)
                pieces.append((far_rows[jnp.clip(peer, 0, seq_size - 1)], bias_of(ok)))
        else:
            lower = block(jnp.maximum(group - 1, 0))
            upper = block(jnp.minimum(group + 1, blocks - 1))
            has_lower, has_upper = group >= 1, group + 1 < blocks
            pieces += [
                (lower[:HALF], bias_of(has_lower)),
                (lower[HALF:], bias_of(has_lower & (parity == 1))),
                (upper[:HALF], bias_of(has_upper & (parity == 0))),
                (upper[HALF:], bias_of(has_upper)),
            ]
    return pieces


def paired_pieces(block_6, block_2, eighth_4, wide):
    me = lax.axis_index("seq")
    odd = me & 1
    pair = me >> 1
    middle = (pair == 1) | (pair == 2)
    upper_near = (pair & 1) == 0
    lower = jnp.where(upper_near, block_6[...], block_2[...])
    upper = jnp.where(upper_near, block_2[...], block_6[...])
    has_lower, has_upper = pair >= 1, pair <= 2
    third = jnp.where(odd == 1, lower[HALF:], upper[:HALF])
    has_third = ((odd == 1) & has_lower) | ((odd == 0) & has_upper)
    ends = average_pairs(block_6[...], wide)
    return [
        (lower[:HALF], bias_of(has_lower)),
        (upper[HALF:], bias_of(has_upper)),
        (third, bias_of(has_third)),
        (eighth_4[...], bias_of(pair >= 0)),
        (ends, bias_of(jnp.logical_not(middle))),
    ]


def place(pieces, values, keys):
    at = 0
    width = values.shape[1]
    total_rows = values.shape[0]
    position = lax.broadcasted_iota(jnp.int32, (1, total_rows), 1)
    bias = jnp.zeros((1, total_rows), jnp.float32)
    for rows, value in pieces:
        count = rows.shape[0]
        keys[at : at + count] = rows[:, :width]
        values[at : at + count] = rows[:, width:]
        if value is not None:
            bias = jnp.where((position >= at) & (position < at + count), value, bias)
        at += count
    return bias


def split_heads(rows):
    first_head = lax.broadcasted_iota(jnp.int32, (1, rows.shape[1]), 1) < HD
    none = jnp.zeros_like(rows)
    return jnp.concatenate(
        [jnp.where(first_head, rows, none), jnp.where(first_head, none, rows)], axis=0
    )


def scores_of(queries, keys):
    return lax.dot_general(
        queries, keys[...], (((1,), (1,)), ((), ())), preferred_element_type=jnp.float32
    )


def near_kernel(seq_size, queries, own, inner, outer, scores, values, shared, keys, wide):
    me = lax.axis_index("seq")
    odd = me & 1
    from_inner, from_outer = inner[...], outer[...]
    before = jnp.where(odd == 1, from_inner, from_outer)
    after = jnp.where(odd == 1, from_outer, from_inner)
    edge_before, edge_after = before[:LEAF], after[:LEAF]
    far_half_after = after[LEAF:]
    shared[...] = before[LEAF:]
    near_half_before = average_pairs(edge_before, wide)
    near_half_after = average_pairs(edge_after, wide)
    has_before, has_after = bias_of(me >= 1), bias_of(me + 1 < seq_size)
    for leaf in range(2):
        if leaf == 0:
            near = [
                (edge_before, has_before),
                (own[...], None),
                (near_half_after, has_after),
                (far_half_after, has_after),
            ]
        else:
            near = [
                (own[...], None),
                (edge_after, has_after),
                (near_half_before, has_before),
                (far_half_after, has_after),
            ]
        bias = place(near, values.at[leaf], keys)
        rows = split_heads(queries[leaf * LEAF : (leaf + 1) * LEAF])
        scores[leaf] = scores_of(rows, keys) + bias


def attend_leaf(leaf, queries, near_scores, near_values, keys, values, bias, same, other):
    first_head = lax.broadcasted_iota(jnp.int32, (1, values.shape[1]), 1) < HD
    exponent = math.log2(math.e) / math.sqrt(HD)
    rows = split_heads(queries[pl.ds(pl.multiple_of(leaf * LEAF, LEAF), LEAF)])
    means = []
    for head in range(2):
        span = slice(head * LEAF, (head + 1) * LEAF)
        near = near_scores[leaf, span]
        far_scores = scores_of(rows[span], keys) + bias
        peak = jnp.maximum(
            jnp.max(near, axis=1, keepdims=True), jnp.max(far_scores, axis=1, keepdims=True)
        )
        near = jnp.exp2((near - peak) * exponent)
        far_weights = jnp.exp2((far_scores - peak) * exponent)
        total = jnp.sum(near, axis=1, keepdims=True) + jnp.sum(far_weights, axis=1, keepdims=True)
        numer = jnp.dot(
            near.astype(jnp.bfloat16), near_values[leaf], preferred_element_type=jnp.float32
        ) + jnp.dot(
            far_weights.astype(jnp.bfloat16), values[...], preferred_element_type=jnp.float32
        )
        means.append(numer / total)
    attended = jnp.where(first_head, means[0], means[1]).astype(jnp.bfloat16)
    second = (lax.axis_index("head") & 1) == 1
    same[:HALF] = jnp.where(second, attended[HALF:], attended[:HALF])
    other[:HALF] = jnp.where(second, attended[:HALF], attended[HALF:])


def leaves_kernel(seq_size, queries, near_scores, near_values, shared, *rest):
    *far, same, other, keys, values, bias, wide = rest
    if len(far) == 1:
        pieces = gathered_pieces(seq_size, far[0], wide)
    else:
        pieces = paired_pieces(*far, wide)
    shared_bias = bias_of(lax.axis_index("seq") >= 1)
    bias[...] = jnp.broadcast_to(place([(shared, shared_bias)] + pieces, values, keys), bias.shape)
    leaf = (lax.axis_index("head") >> 1) ^ 1
    attend_leaf(leaf, queries, near_scores, near_values, keys, values, bias[:1], same, other)
    for share in (same, other):
        share[HALF:] = jnp.zeros((PAD, share.shape[1]), share.dtype)


def stays_kernel(queries, near_scores, near_values, keys, values, bias, same, other):
    leaf = lax.axis_index("head") >> 1
    attend_leaf(leaf, queries, near_scores, near_values, keys, values, bias[:1], same, other)


def project_kernel(*refs):
    *parts, weight, mixed = refs
    mine = lax.axis_index("head")
    total = jnp.zeros(mixed.shape, jnp.float32)
    for step, part in enumerate(reversed(parts)):
        width = part.shape[1]
        columns = pl.ds(pl.multiple_of((mine ^ step) * width, width), width)
        total += jnp.dot(part[: mixed.shape[0]], weight[columns], preferred_element_type=jnp.float32)
    mixed[...] = total.astype(mixed.dtype)


VMEM = pl.BlockSpec(memory_space=pltpu.VMEM)
HBM = pl.BlockSpec(memory_space=pltpu.HBM)


def kernel_call(body, name, megabytes, ins, outs, scratch, flops=0):
    shapes = tuple(
        out if isinstance(out, jax.ShapeDtypeStruct) else jax.ShapeDtypeStruct(out, jnp.bfloat16)
        for out in outs
    )
    return pl.pallas_call(
        body,
        out_shape=shapes,
        in_specs=ins,
        out_specs=(VMEM,) * len(outs),
        scratch_shapes=scratch,
        compiler_params=pltpu.CompilerParams(vmem_limit_bytes=megabytes << 20),
        cost_estimate=pl.CostEstimate(flops=flops, bytes_accessed=1 << 20, transcendentals=0),
        name=name,
    )


def shards(queries, keys, values, out_weight):
    tokens, width = queries.shape
    seq_size = lax.axis_size("seq")
    head_size = lax.axis_size("head")
    pair_width = 2 * width
    paired = seq_size == 8
    wide_rows = 2 * LEAF if paired else max(2 * LEAF, seq_size // 2 * HALF)
    wide = pltpu.VMEM((wide_rows, width), jnp.float32)

    def swap(array, bit, axis="seq"):
        return lax.ppermute(array, axis, [(i, i ^ bit) for i in range(lax.axis_size(axis))])

    own_queries, own, inner, outer, quarter = kernel_call(
        functools.partial(pack_kernel, not paired),
        "pack",
        16,
        [HBM] * 3,
        [
            (tokens, width),
            (tokens, pair_width),
            (LEAF + HALF, pair_width),
            (LEAF + HALF, pair_width),
            (HALF, pair_width) if paired else (seq_size, HALF, pair_width),
        ],
        [wide, pltpu.SemaphoreType.DMA((3,))],
    )(*(pltpu.with_memory_space_constraint(array, pltpu.HBM) for array in (queries, keys, values)))
    inner = swap(inner, 1)
    others = [(i, i + 1 if i & 1 else i - 1) for i in range(1, seq_size - 1)]
    outer = lax.ppermute(outer, "seq", others)
    if paired:
        block, eighth = kernel_call(
            join_kernel,
            "join",
            8,
            [VMEM] * 2,
            [(LEAF, pair_width), (HALF, pair_width)],
            [wide],
        )(inner, quarter)
        far = (swap(block, 6), swap(block, 2), swap(eighth, 4))
    else:
        far = (lax.all_to_all(quarter, "seq", split_axis=0, concat_axis=0),)
    share = tokens // head_size
    near_scores, near_values, shared = kernel_call(
        functools.partial(near_kernel, seq_size),
        "near",
        16,
        [VMEM] * 4,
        [
            jax.ShapeDtypeStruct((2, 2 * LEAF, NEAR_ROWS), jnp.float32),
            (2, NEAR_ROWS, width),
            (HALF, pair_width),
        ],
        [pltpu.VMEM((NEAR_ROWS, width), jnp.bfloat16), wide],
        flops=8 * LEAF * NEAR_ROWS * width,
    )(own_queries, own, inner, outer)
    far_rows = far_row_count(seq_size)

    leaf_flops = 8 * LEAF * (NEAR_ROWS + far_rows) * width
    share_2, share_3, far_keys, far_values, far_bias = kernel_call(
        functools.partial(leaves_kernel, seq_size),
        "leaves",
        24,
        [VMEM] * (4 + len(far)),
        [
            (share + PAD, width),
            (share + PAD, width),
            (far_rows, width),
            (far_rows, width),
            jax.ShapeDtypeStruct((8, far_rows), jnp.float32),
        ],
        [wide],
        flops=leaf_flops,
    )(own_queries, near_scores, near_values, shared, *far)
    share_0, share_1 = kernel_call(
        stays_kernel, "stays", 16, [VMEM] * 6, [(share, width)] * 2, [], flops=leaf_flops
    )(own_queries, near_scores, near_values, far_keys, far_values, far_bias)
    parts = [swap(share_3, 3, "head"), swap(share_2, 2, "head"), swap(share_1, 1, "head"), share_0]
    (mixed,) = kernel_call(
        project_kernel, "project", 8, [VMEM] * (head_size + 1), [(share, out_weight.shape[1])], []
    )(*parts, out_weight)
    return mixed


def solution(mesh):
    in_specs = (P("seq", "head"), P("seq", "head"), P("seq", "head"), P())
    out_specs = P(("seq", "head"), None)
    return jax.shard_map(shards, mesh=mesh, in_specs=in_specs, out_specs=out_specs, check_vma=False)
```

```python
import functools
import math

import jax
import jax.numpy as jnp
from jax import lax
from jax.experimental import pallas as pl
from jax.experimental.pallas import tpu as pltpu
from jax.sharding import PartitionSpec as P

HD = 64
LEAF = 128
HALF = LEAF // 2
NEG = -math.inf


def average_pairs(rows, wide):
    count = rows.shape[0]
    halves = []
    for low in range(0, rows.shape[1], LEAF):
        wide[:count] = rows[:, low : low + LEAF].astype(jnp.float32)
        even = wide[pl.ds(0, count // 2, stride=2), :]
        odd = wide[pl.ds(1, count // 2, stride=2), :]
        halves.append((0.5 * (even + odd)).astype(jnp.bfloat16))
    return jnp.concatenate(halves, axis=1)


def pack_kernel(far_shares, queries, keys, values, own_queries, own, inner, outer, quarter, wide, arrived):
    width = keys.shape[1]
    copies = [
        pltpu.make_async_copy(keys, own.at[:, :width], arrived.at[0]),
        pltpu.make_async_copy(values, own.at[:, width:], arrived.at[1]),
        pltpu.make_async_copy(queries, own_queries, arrived.at[2]),
    ]
    for copy in copies:
        copy.start()
    me = lax.axis_index("seq")
    odd = me & 1
    for copy in copies:
        copy.wait()
    rows = own[...]
    low, high = rows[:LEAF], rows[LEAF:]
    level_one = average_pairs(rows, wide)
    level_two = average_pairs(level_one, wide)
    first, second = level_one[:HALF], level_one[HALF:]
    inner[:LEAF] = jnp.where(odd == 1, low, high)
    inner[LEAF:] = jnp.where(odd == 1, second, first)
    outer[:LEAF] = jnp.where(odd == 1, high, low)
    outer[LEAF:] = jnp.where(odd == 1, first, second)
    if far_shares:
        for peer in range(quarter.shape[0]):
            quarter[peer] = level_two
    else:
        quarter[...] = level_two


def join_kernel(inner, quarter, block, across, eighth, wide):
    me = lax.axis_index("seq")
    odd = me & 1
    edge_half = average_pairs(inner[:LEAF], wide)
    other_half = inner[LEAF:]
    theirs = jnp.concatenate(
        [jnp.where(odd == 1, other_half, edge_half), jnp.where(odd == 1, edge_half, other_half)], axis=0
    )
    theirs = average_pairs(theirs, wide)
    block[:HALF] = jnp.where(odd == 1, theirs, quarter[...])
    block[HALF:] = jnp.where(odd == 1, quarter[...], theirs)
    level_three = average_pairs(block[...], wide)
    eighth[...] = level_three
    middle = (me >= 2) & (me < 6)
    across[:HALF] = jnp.where(middle, block[:HALF], level_three)
    across[HALF:] = block[HALF:]


NEAR_ROWS = 4 * LEAF
PAD = 16


def far_row_count(seq_size):
    rows = HALF
    for far in range(1, seq_size.bit_length() - 1):
        if seq_size >> far == 2:
            rows += LEAF
        elif far == 1:
            rows += 3 * HALF
        else:
            rows += 2 * LEAF
    return rows


def bias_of(valid):
    return jnp.where(valid, jnp.float32(0.0), jnp.float32(NEG))


def gathered_pieces(seq_size, far_rows, wide):
    me = lax.axis_index("seq")
    pieces = []
    for far in range(1, seq_size.bit_length() - 1):
        span = 1 << far
        group = me >> far
        parity = (me >> (far - 1)) & 1
        blocks = seq_size >> far

        def block(number, span=span, far=far):
            found = far_rows[pl.ds(number * span, span)].reshape(span * HALF, far_rows.shape[2])
            for _ in range(far - 1):
                found = average_pairs(found, wide)
            return found

        if blocks == 2:
            rows = block(1 - group)
            first = bias_of((group == 1) | (parity == 0))
            second = bias_of((group == 0) | (parity == 1))
            pieces += [(rows[:HALF], first), (rows[HALF:], second)]
        elif far == 1:
            third = jnp.where(parity == 0, me + 3, me - 3)
            for peer in (me - 2, me + 2, third):
                ok = (peer >= 0) & (peer < seq_size)
                pieces.append((far_rows[jnp.clip(peer, 0, seq_size - 1)], bias_of(ok)))
        else:
            lower = block(jnp.maximum(group - 1, 0))
            upper = block(jnp.minimum(group + 1, blocks - 1))
            has_lower, has_upper = group >= 1, group + 1 < blocks
            pieces += [
                (lower[:HALF], bias_of(has_lower)),
                (lower[HALF:], bias_of(has_lower & (parity == 1))),
                (upper[:HALF], bias_of(has_upper & (parity == 0))),
                (upper[HALF:], bias_of(has_upper)),
            ]
    return pieces


def paired_pieces(block_6, block_2, eighth_4):
    me = lax.axis_index("seq")
    odd = me & 1
    pair = me >> 1
    middle = (pair == 1) | (pair == 2)
    upper_near = (pair & 1) == 0
    lower = jnp.where(upper_near, block_6[...], block_2[...])
    upper = jnp.where(upper_near, block_2[...], block_6[...])
    has_lower, has_upper = pair >= 1, pair <= 2
    third = jnp.where(odd == 1, lower[HALF:], upper[:HALF])
    has_third = ((odd == 1) & has_lower) | ((odd == 0) & has_upper)
    return [
        (lower[:HALF], bias_of(has_lower)),
        (upper[HALF:], bias_of(has_upper)),
        (third, bias_of(has_third)),
        (eighth_4[...], bias_of(pair >= 0)),
        (block_6[:HALF], bias_of(jnp.logical_not(middle))),
    ]


def place(pieces, values, keys):
    at = 0
    width = values.shape[1]
    total_rows = values.shape[0]
    position = lax.broadcasted_iota(jnp.int32, (1, total_rows), 1)
    bias = jnp.zeros((1, total_rows), jnp.float32)
    for rows, value in pieces:
        count = rows.shape[0]
        keys[at : at + count] = rows[:, :width]
        values[at : at + count] = rows[:, width:]
        if value is not None:
            bias = jnp.where((position >= at) & (position < at + count), value, bias)
        at += count
    return bias


def split_heads(rows):
    first_head = lax.broadcasted_iota(jnp.int32, (1, rows.shape[1]), 1) < HD
    none = jnp.zeros_like(rows)
    return jnp.concatenate(
        [jnp.where(first_head, rows, none), jnp.where(first_head, none, rows)], axis=0
    )


def scores_of(queries, keys):
    return lax.dot_general(
        queries, keys[...], (((1,), (1,)), ((), ())), preferred_element_type=jnp.float32
    )


def near_kernel(seq_size, queries, own, inner, outer, scores, values, shared, keys, wide):
    me = lax.axis_index("seq")
    odd = me & 1
    from_inner, from_outer = inner[...], outer[...]
    before = jnp.where(odd == 1, from_inner, from_outer)
    after = jnp.where(odd == 1, from_outer, from_inner)
    edge_before, edge_after = before[:LEAF], after[:LEAF]
    far_half_after = after[LEAF:]
    shared[...] = before[LEAF:]
    near_half_before = average_pairs(edge_before, wide)
    near_half_after = average_pairs(edge_after, wide)
    has_before, has_after = bias_of(me >= 1), bias_of(me + 1 < seq_size)
    for leaf in range(2):
        if leaf == 0:
            near = [
                (edge_before, has_before),
                (own[...], None),
                (near_half_after, has_after),
                (far_half_after, has_after),
            ]
        else:
            near = [
                (own[...], None),
                (edge_after, has_after),
                (near_half_before, has_before),
                (far_half_after, has_after),
            ]
        bias = place(near, values.at[leaf], keys)
        rows = split_heads(queries[leaf * LEAF : (leaf + 1) * LEAF])
        scores[leaf] = scores_of(rows, keys) + bias


def attend_leaf(leaf, queries, near_scores, near_values, keys, values, bias, same, other):
    first_head = lax.broadcasted_iota(jnp.int32, (1, values.shape[1]), 1) < HD
    exponent = math.log2(math.e) / math.sqrt(HD)
    rows = split_heads(queries[pl.ds(pl.multiple_of(leaf * LEAF, LEAF), LEAF)])
    near = near_scores[leaf]
    far_scores = scores_of(rows, keys) + bias
    peak = jnp.maximum(
        jnp.max(near, axis=1, keepdims=True), jnp.max(far_scores, axis=1, keepdims=True)
    )
    near = jnp.exp2((near - peak) * exponent)
    far_weights = jnp.exp2((far_scores - peak) * exponent)
    total = jnp.sum(near, axis=1, keepdims=True) + jnp.sum(far_weights, axis=1, keepdims=True)
    numer = jnp.dot(
        near.astype(jnp.bfloat16), near_values[leaf], preferred_element_type=jnp.float32
    ) + jnp.dot(far_weights.astype(jnp.bfloat16), values[...], preferred_element_type=jnp.float32)
    mean = numer / total
    attended = jnp.where(first_head, mean[:LEAF], mean[LEAF:]).astype(jnp.bfloat16)
    second = (lax.axis_index("head") & 1) == 1
    same[:HALF] = jnp.where(second, attended[HALF:], attended[:HALF])
    other[:HALF] = jnp.where(second, attended[:HALF], attended[HALF:])


def leaves_kernel(seq_size, queries, near_scores, near_values, shared, *rest):
    *far, same, other, keys, values, bias, wide = rest
    if len(far) == 1:
        pieces = gathered_pieces(seq_size, far[0], wide)
    else:
        pieces = paired_pieces(*far)
    shared_bias = bias_of(lax.axis_index("seq") >= 1)
    bias[...] = jnp.broadcast_to(place([(shared, shared_bias)] + pieces, values, keys), bias.shape)
    leaf = (lax.axis_index("head") >> 1) ^ 1
    attend_leaf(leaf, queries, near_scores, near_values, keys, values, bias[:1], same, other)
    for share in (same, other):
        share[HALF:] = jnp.zeros((PAD, share.shape[1]), share.dtype)


def stays_kernel(queries, near_scores, near_values, keys, values, bias, same, other):
    leaf = lax.axis_index("head") >> 1
    attend_leaf(leaf, queries, near_scores, near_values, keys, values, bias[:1], same, other)


def side_by_side(same, other, rows, columns):
    second = (lax.axis_index("head") & 1) == 1
    width = same.shape[1]
    columns[:, :width] = jnp.where(second, other[:rows], same[:rows])
    columns[:, width:] = jnp.where(second, same[:rows], other[:rows])
    return columns[...]


def chip_rows(weight, chip, count):
    return weight[pl.ds(pl.multiple_of(chip * count, count), count)]


def begin_kernel(same, other, weight, partial, columns):
    chip = lax.axis_index("head") >> 1
    shares = side_by_side(same, other, partial.shape[0], columns)
    partial[...] = jnp.dot(
        shares, chip_rows(weight, chip, columns.shape[1]), preferred_element_type=jnp.float32
    )


def project_kernel(partial, other, same, weight, mixed, columns):
    chip = (lax.axis_index("head") >> 1) ^ 1
    shares = side_by_side(same, other, partial.shape[0], columns)
    total = partial[...] + jnp.dot(
        shares, chip_rows(weight, chip, columns.shape[1]), preferred_element_type=jnp.float32
    )
    mixed[...] = total.astype(mixed.dtype)


VMEM = pl.BlockSpec(memory_space=pltpu.VMEM)
HBM = pl.BlockSpec(memory_space=pltpu.HBM)


def kernel_call(body, name, megabytes, ins, outs, scratch, flops=0):
    shapes = tuple(
        out if isinstance(out, jax.ShapeDtypeStruct) else jax.ShapeDtypeStruct(out, jnp.bfloat16)
        for out in outs
    )
    return pl.pallas_call(
        body,
        out_shape=shapes,
        in_specs=ins,
        out_specs=(VMEM,) * len(outs),
        scratch_shapes=scratch,
        compiler_params=pltpu.CompilerParams(vmem_limit_bytes=megabytes << 20),
        cost_estimate=pl.CostEstimate(flops=flops, bytes_accessed=1 << 20, transcendentals=0),
        name=name,
    )


def shards(queries, keys, values, out_weight):
    tokens, width = queries.shape
    seq_size = lax.axis_size("seq")
    head_size = lax.axis_size("head")
    pair_width = 2 * width
    paired = seq_size == 8
    wide_rows = 2 * LEAF if paired else max(2 * LEAF, seq_size // 2 * HALF)
    wide = pltpu.VMEM((wide_rows, width), jnp.float32)

    def swap(array, bit, axis="seq"):
        return lax.ppermute(array, axis, [(i, i ^ bit) for i in range(lax.axis_size(axis))])

    own_queries, own, inner, outer, quarter = kernel_call(
        functools.partial(pack_kernel, not paired),
        "pack",
        16,
        [HBM] * 3,
        [
            (tokens, width),
            (tokens, pair_width),
            (LEAF + HALF, pair_width),
            (LEAF + HALF, pair_width),
            (HALF, pair_width) if paired else (seq_size, HALF, pair_width),
        ],
        [wide, pltpu.SemaphoreType.DMA((3,))],
    )(*(pltpu.with_memory_space_constraint(array, pltpu.HBM) for array in (queries, keys, values)))
    inner = swap(inner, 1)
    others = [(i, i + 1 if i & 1 else i - 1) for i in range(1, seq_size - 1)]
    outer = lax.ppermute(outer, "seq", others)
    if paired:
        block, across, eighth = kernel_call(
            join_kernel,
            "join",
            8,
            [VMEM] * 2,
            [(LEAF, pair_width), (LEAF, pair_width), (HALF, pair_width)],
            [wide],
        )(inner, quarter)
        far = (swap(across, 6), swap(block, 2), swap(eighth, 4))
    else:
        far = (lax.all_to_all(quarter, "seq", split_axis=0, concat_axis=0),)
    share = tokens // head_size
    near_scores, near_values, shared = kernel_call(
        functools.partial(near_kernel, seq_size),
        "near",
        16,
        [VMEM] * 4,
        [
            jax.ShapeDtypeStruct((2, 2 * LEAF, NEAR_ROWS), jnp.float32),
            (2, NEAR_ROWS, width),
            (HALF, pair_width),
        ],
        [pltpu.VMEM((NEAR_ROWS, width), jnp.bfloat16), wide],
        flops=8 * LEAF * NEAR_ROWS * width,
    )(own_queries, own, inner, outer)
    far_rows = far_row_count(seq_size)

    leaf_flops = 8 * LEAF * (NEAR_ROWS + far_rows) * width
    share_2, share_3, far_keys, far_values, far_bias = kernel_call(
        functools.partial(leaves_kernel, seq_size),
        "leaves",
        24,
        [VMEM] * (4 + len(far)),
        [
            (share + PAD, width),
            (share + PAD, width),
            (far_rows, width),
            (far_rows, width),
            jax.ShapeDtypeStruct((8, far_rows), jnp.float32),
        ],
        [wide],
        flops=leaf_flops,
    )(own_queries, near_scores, near_values, shared, *far)
    share_0, share_1 = kernel_call(
        stays_kernel, "stays", 16, [VMEM] * 6, [(share, width)] * 2, [], flops=leaf_flops
    )(own_queries, near_scores, near_values, far_keys, far_values, far_bias)
    columns = pltpu.VMEM((share, pair_width), jnp.bfloat16)
    part_3, part_2 = swap(share_3, 3, "head"), swap(share_2, 2, "head")
    (partial,) = kernel_call(
        begin_kernel,
        "begin",
        8,
        [VMEM] * 3,
        [jax.ShapeDtypeStruct((share, out_weight.shape[1]), jnp.float32)],
        [columns],
    )(share_0, swap(share_1, 1, "head"), out_weight)
    (mixed,) = kernel_call(
        project_kernel, "project", 8, [VMEM] * 4, [(share, out_weight.shape[1])], [columns]
    )(partial, part_3, part_2, out_weight)
    return mixed


def solution(mesh):
    in_specs = (P("seq", "head"), P("seq", "head"), P("seq", "head"), P())
    out_specs = P(("seq", "head"), None)
    return jax.shard_map(shards, mesh=mesh, in_specs=in_specs, out_specs=out_specs, check_vma=False)
```

```python
import functools
import math

import jax
import jax.numpy as jnp
from jax import lax
from jax.experimental import pallas as pl
from jax.experimental.pallas import tpu as pltpu
from jax.sharding import PartitionSpec as P

HD = 64
LEAF = 128
HALF = LEAF // 2
NEG = -math.inf


def average_pairs(rows, wide):
    count = rows.shape[0]
    halves = []
    for low in range(0, rows.shape[1], LEAF):
        wide[:count] = rows[:, low : low + LEAF].astype(jnp.float32)
        even = wide[pl.ds(0, count // 2, stride=2), :]
        odd = wide[pl.ds(1, count // 2, stride=2), :]
        halves.append((0.5 * (even + odd)).astype(jnp.bfloat16))
    return jnp.concatenate(halves, axis=1)


def pack_kernel(far_shares, queries, keys, values, own_queries, own, inner, outer, quarter, wide, arrived):
    width = keys.shape[1]
    copies = [
        pltpu.make_async_copy(keys, own.at[:, :width], arrived.at[0]),
        pltpu.make_async_copy(values, own.at[:, width:], arrived.at[1]),
        pltpu.make_async_copy(queries, own_queries, arrived.at[2]),
    ]
    for copy in copies:
        copy.start()
    me = lax.axis_index("seq")
    odd = me & 1
    for copy in copies:
        copy.wait()
    rows = own[...]
    low, high = rows[:LEAF], rows[LEAF:]
    level_one = average_pairs(rows, wide)
    level_two = average_pairs(level_one, wide)
    first, second = level_one[:HALF], level_one[HALF:]
    inner[:LEAF] = jnp.where(odd == 1, low, high)
    inner[LEAF:] = jnp.where(odd == 1, second, first)
    outer[:LEAF] = jnp.where(odd == 1, high, low)
    outer[LEAF:] = jnp.where(odd == 1, first, second)
    if far_shares:
        for peer in range(quarter.shape[0]):
            quarter[peer] = level_two
    else:
        quarter[...] = level_two


def join_kernel(inner, quarter, upward, downward, eighth, wide):
    me = lax.axis_index("seq")
    odd = me & 1
    edge_half = average_pairs(inner[:LEAF], wide)
    other_half = inner[LEAF:]
    theirs = jnp.concatenate(
        [jnp.where(odd == 1, other_half, edge_half), jnp.where(odd == 1, edge_half, other_half)], axis=0
    )
    theirs = average_pairs(theirs, wide)
    first = jnp.where(odd == 1, theirs, quarter[...])
    second = jnp.where(odd == 1, quarter[...], theirs)
    level_three = average_pairs(jnp.concatenate([first, second], axis=0), wide)
    upward[:HALF] = jnp.where(me >= 6, level_three, first)
    upward[HALF:] = second
    downward[:HALF] = jnp.where(me < 2, level_three, first)
    downward[HALF:] = second
    eighth[...] = level_three


NEAR_ROWS = 4 * LEAF
PAD = 16


def far_row_count(seq_size):
    rows = HALF
    for far in range(1, seq_size.bit_length() - 1):
        if seq_size >> far == 2:
            rows += LEAF
        elif far == 1:
            rows += 3 * HALF
        else:
            rows += 2 * LEAF
    return rows


def bias_of(valid):
    return jnp.where(valid, jnp.float32(0.0), jnp.float32(NEG))


def gathered_pieces(seq_size, far_rows, wide):
    me = lax.axis_index("seq")
    pieces = []
    for far in range(1, seq_size.bit_length() - 1):
        span = 1 << far
        group = me >> far
        parity = (me >> (far - 1)) & 1
        blocks = seq_size >> far

        def block(number, span=span, far=far):
            found = far_rows[pl.ds(number * span, span)].reshape(span * HALF, far_rows.shape[2])
            for _ in range(far - 1):
                found = average_pairs(found, wide)
            return found

        if blocks == 2:
            rows = block(1 - group)
            first = bias_of((group == 1) | (parity == 0))
            second = bias_of((group == 0) | (parity == 1))
            pieces += [(rows[:HALF], first), (rows[HALF:], second)]
        elif far == 1:
            third = jnp.where(parity == 0, me + 3, me - 3)
            for peer in (me - 2, me + 2, third):
                ok = (peer >= 0) & (peer < seq_size)
                pieces.append((far_rows[jnp.clip(peer, 0, seq_size - 1)], bias_of(ok)))
        else:
            lower = block(jnp.maximum(group - 1, 0))
            upper = block(jnp.minimum(group + 1, blocks - 1))
            has_lower, has_upper = group >= 1, group + 1 < blocks
            pieces += [
                (lower[:HALF], bias_of(has_lower)),
                (lower[HALF:], bias_of(has_lower & (parity == 1))),
                (upper[:HALF], bias_of(has_upper & (parity == 0))),
                (upper[HALF:], bias_of(has_upper)),
            ]
    return pieces


def paired_pieces(lower, upper, eighth):
    me = lax.axis_index("seq")
    odd = me & 1
    has_lower, has_upper = me >= 2, me < 6
    has_third = ((odd == 1) & has_lower) | ((odd == 0) & has_upper)
    return [
        (lower[:HALF], None),
        (upper[HALF:], bias_of(has_upper)),
        (jnp.where(odd == 1, lower[HALF:], upper[:HALF]), bias_of(has_third)),
        (eighth[...], None),
        (upper[:HALF], bias_of(jnp.logical_not(has_upper))),
    ]


def place(pieces, values, keys):
    at = 0
    width = values.shape[1]
    total_rows = values.shape[0]
    position = lax.broadcasted_iota(jnp.int32, (1, total_rows), 1)
    bias = jnp.zeros((1, total_rows), jnp.float32)
    for rows, value in pieces:
        count = rows.shape[0]
        keys[at : at + count] = rows[:, :width]
        values[at : at + count] = rows[:, width:]
        if value is not None:
            bias = jnp.where((position >= at) & (position < at + count), value, bias)
        at += count
    return bias


def split_heads(rows):
    first_head = lax.broadcasted_iota(jnp.int32, (1, rows.shape[1]), 1) < HD
    none = jnp.zeros_like(rows)
    return jnp.concatenate(
        [jnp.where(first_head, rows, none), jnp.where(first_head, none, rows)], axis=0
    )


def scores_of(queries, keys):
    return lax.dot_general(
        queries, keys[...], (((1,), (1,)), ((), ())), preferred_element_type=jnp.float32
    )


def near_kernel(seq_size, queries, own, inner, outer, scores, values, shared, keys, wide):
    me = lax.axis_index("seq")
    odd = me & 1
    from_inner, from_outer = inner[...], outer[...]
    before = jnp.where(odd == 1, from_inner, from_outer)
    after = jnp.where(odd == 1, from_outer, from_inner)
    edge_before, edge_after = before[:LEAF], after[:LEAF]
    far_half_after = after[LEAF:]
    shared[...] = before[LEAF:]
    near_half_before = average_pairs(edge_before, wide)
    near_half_after = average_pairs(edge_after, wide)
    has_before, has_after = bias_of(me >= 1), bias_of(me + 1 < seq_size)
    for leaf in range(2):
        if leaf == 0:
            near = [
                (edge_before, has_before),
                (own[...], None),
                (near_half_after, has_after),
                (far_half_after, has_after),
            ]
        else:
            near = [
                (own[...], None),
                (edge_after, has_after),
                (near_half_before, has_before),
                (far_half_after, has_after),
            ]
        bias = place(near, values.at[leaf], keys)
        rows = split_heads(queries[leaf * LEAF : (leaf + 1) * LEAF])
        scores[leaf] = scores_of(rows, keys) + bias


def attend_leaf(leaf, queries, near_scores, near_values, keys, values, bias, same, other):
    first_head = lax.broadcasted_iota(jnp.int32, (1, values.shape[1]), 1) < HD
    exponent = math.log2(math.e) / math.sqrt(HD)
    rows = split_heads(queries[pl.ds(pl.multiple_of(leaf * LEAF, LEAF), LEAF)])
    near = near_scores[leaf]
    far_scores = scores_of(rows, keys) + bias
    peak = jnp.maximum(
        jnp.max(near, axis=1, keepdims=True), jnp.max(far_scores, axis=1, keepdims=True)
    )
    near = jnp.exp2((near - peak) * exponent)
    far_weights = jnp.exp2((far_scores - peak) * exponent)
    total = jnp.sum(near, axis=1, keepdims=True) + jnp.sum(far_weights, axis=1, keepdims=True)
    numer = jnp.dot(
        near.astype(jnp.bfloat16), near_values[leaf], preferred_element_type=jnp.float32
    ) + jnp.dot(far_weights.astype(jnp.bfloat16), values[...], preferred_element_type=jnp.float32)
    mean = numer / total
    attended = jnp.where(first_head, mean[:LEAF], mean[LEAF:]).astype(jnp.bfloat16)
    second = (lax.axis_index("head") & 1) == 1
    same[:HALF] = jnp.where(second, attended[HALF:], attended[:HALF])
    other[:HALF] = jnp.where(second, attended[:HALF], attended[HALF:])


def leaves_kernel(seq_size, queries, near_scores, near_values, shared, *rest):
    *far, same, other, keys, values, bias, wide = rest
    if len(far) == 1:
        pieces = gathered_pieces(seq_size, far[0], wide)
    else:
        pieces = paired_pieces(*far)
    shared_bias = bias_of(lax.axis_index("seq") >= 1)
    bias[...] = jnp.broadcast_to(place([(shared, shared_bias)] + pieces, values, keys), bias.shape)
    leaf = (lax.axis_index("head") >> 1) ^ 1
    attend_leaf(leaf, queries, near_scores, near_values, keys, values, bias[:1], same, other)
    for share in (same, other):
        share[HALF:] = jnp.zeros((PAD, share.shape[1]), share.dtype)


def stays_kernel(queries, near_scores, near_values, keys, values, bias, same, other):
    leaf = lax.axis_index("head") >> 1
    attend_leaf(leaf, queries, near_scores, near_values, keys, values, bias[:1], same, other)


def side_by_side(same, other, rows, columns):
    second = (lax.axis_index("head") & 1) == 1
    width = same.shape[1]
    columns[:, :width] = jnp.where(second, other[:rows], same[:rows])
    columns[:, width:] = jnp.where(second, same[:rows], other[:rows])
    return columns[...]


def chip_rows(weight, chip, count):
    return weight[pl.ds(pl.multiple_of(chip * count, count), count)]


def begin_kernel(same, other, weight, partial, columns):
    chip = lax.axis_index("head") >> 1
    shares = side_by_side(same, other, partial.shape[0], columns)
    partial[...] = jnp.dot(
        shares, chip_rows(weight, chip, columns.shape[1]), preferred_element_type=jnp.float32
    )


def project_kernel(partial, other, same, weight, mixed, columns):
    chip = (lax.axis_index("head") >> 1) ^ 1
    shares = side_by_side(same, other, partial.shape[0], columns)
    total = partial[...] + jnp.dot(
        shares, chip_rows(weight, chip, columns.shape[1]), preferred_element_type=jnp.float32
    )
    mixed[...] = total.astype(mixed.dtype)


VMEM = pl.BlockSpec(memory_space=pltpu.VMEM)
HBM = pl.BlockSpec(memory_space=pltpu.HBM)


def kernel_call(body, name, megabytes, ins, outs, scratch, flops=0):
    shapes = tuple(
        out if isinstance(out, jax.ShapeDtypeStruct) else jax.ShapeDtypeStruct(out, jnp.bfloat16)
        for out in outs
    )
    return pl.pallas_call(
        body,
        out_shape=shapes,
        in_specs=ins,
        out_specs=(VMEM,) * len(outs),
        scratch_shapes=scratch,
        compiler_params=pltpu.CompilerParams(vmem_limit_bytes=megabytes << 20),
        cost_estimate=pl.CostEstimate(flops=flops, bytes_accessed=1 << 20, transcendentals=0),
        name=name,
    )


def shards(queries, keys, values, out_weight):
    tokens, width = queries.shape
    seq_size = lax.axis_size("seq")
    head_size = lax.axis_size("head")
    pair_width = 2 * width
    paired = seq_size == 8
    wide_rows = 2 * LEAF if paired else max(2 * LEAF, seq_size // 2 * HALF)
    wide = pltpu.VMEM((wide_rows, width), jnp.float32)

    def swap(array, bit, axis="seq"):
        return lax.ppermute(array, axis, [(i, i ^ bit) for i in range(lax.axis_size(axis))])

    own_queries, own, inner, outer, quarter = kernel_call(
        functools.partial(pack_kernel, not paired),
        "pack",
        16,
        [HBM] * 3,
        [
            (tokens, width),
            (tokens, pair_width),
            (LEAF + HALF, pair_width),
            (LEAF + HALF, pair_width),
            (HALF, pair_width) if paired else (seq_size, HALF, pair_width),
        ],
        [wide, pltpu.SemaphoreType.DMA((3,))],
    )(*(pltpu.with_memory_space_constraint(array, pltpu.HBM) for array in (queries, keys, values)))
    inner = swap(inner, 1)
    others = [(i, i + 1 if i & 1 else i - 1) for i in range(1, seq_size - 1)]
    outer = lax.ppermute(outer, "seq", others)
    if paired:
        upward, downward, eighth = kernel_call(
            join_kernel,
            "join",
            8,
            [VMEM] * 2,
            [(LEAF, pair_width), (LEAF, pair_width), (HALF, pair_width)],
            [wide],
        )(inner, quarter)
        shift = [(i, (i + 2) % seq_size) for i in range(seq_size)]
        far = (
            lax.ppermute(upward, "seq", shift),
            lax.ppermute(downward, "seq", [(target, source) for source, target in shift]),
            swap(eighth, 4),
        )
    else:
        far = (lax.all_to_all(quarter, "seq", split_axis=0, concat_axis=0),)
    share = tokens // head_size
    near_scores, near_values, shared = kernel_call(
        functools.partial(near_kernel, seq_size),
        "near",
        16,
        [VMEM] * 4,
        [
            jax.ShapeDtypeStruct((2, 2 * LEAF, NEAR_ROWS), jnp.float32),
            (2, NEAR_ROWS, width),
            (HALF, pair_width),
        ],
        [pltpu.VMEM((NEAR_ROWS, width), jnp.bfloat16), wide],
        flops=8 * LEAF * NEAR_ROWS * width,
    )(own_queries, own, inner, outer)
    far_rows = far_row_count(seq_size)

    leaf_flops = 8 * LEAF * (NEAR_ROWS + far_rows) * width
    share_2, share_3, far_keys, far_values, far_bias = kernel_call(
        functools.partial(leaves_kernel, seq_size),
        "leaves",
        24,
        [VMEM] * (4 + len(far)),
        [
            (share + PAD, width),
            (share + PAD, width),
            (far_rows, width),
            (far_rows, width),
            jax.ShapeDtypeStruct((8, far_rows), jnp.float32),
        ],
        [wide],
        flops=leaf_flops,
    )(own_queries, near_scores, near_values, shared, *far)
    share_0, share_1 = kernel_call(
        stays_kernel, "stays", 16, [VMEM] * 6, [(share, width)] * 2, [], flops=leaf_flops
    )(own_queries, near_scores, near_values, far_keys, far_values, far_bias)
    columns = pltpu.VMEM((share, pair_width), jnp.bfloat16)
    part_3, part_2 = swap(share_3, 3, "head"), swap(share_2, 2, "head")
    (partial,) = kernel_call(
        begin_kernel,
        "begin",
        8,
        [VMEM] * 3,
        [jax.ShapeDtypeStruct((share, out_weight.shape[1]), jnp.float32)],
        [columns],
    )(share_0, swap(share_1, 1, "head"), out_weight)
    (mixed,) = kernel_call(
        project_kernel, "project", 8, [VMEM] * 4, [(share, out_weight.shape[1])], [columns]
    )(partial, part_3, part_2, out_weight)
    return mixed


def solution(mesh):
    in_specs = (P("seq", "head"), P("seq", "head"), P("seq", "head"), P())
    out_specs = P(("seq", "head"), None)
    return jax.shard_map(shards, mesh=mesh, in_specs=in_specs, out_specs=out_specs, check_vma=False)
```

```python
import functools
import math

import jax
import jax.numpy as jnp
from jax import lax
from jax.experimental import pallas as pl
from jax.experimental.pallas import tpu as pltpu
from jax.sharding import PartitionSpec as P

HD = 64
LEAF = 128
HALF = LEAF // 2
NEG = -math.inf


def average_pairs(rows, wide):
    count = rows.shape[0]
    halves = []
    for low in range(0, rows.shape[1], LEAF):
        wide[:count] = rows[:, low : low + LEAF].astype(jnp.float32)
        even = wide[pl.ds(0, count // 2, stride=2), :]
        odd = wide[pl.ds(1, count // 2, stride=2), :]
        halves.append((0.5 * (even + odd)).astype(jnp.bfloat16))
    return jnp.concatenate(halves, axis=1)


def pack_kernel(far_shares, queries, keys, values, own_queries, own, inner, outer, quarter, wide, arrived):
    width = keys.shape[1]
    copies = [
        pltpu.make_async_copy(keys, own.at[:, :width], arrived.at[0]),
        pltpu.make_async_copy(values, own.at[:, width:], arrived.at[1]),
        pltpu.make_async_copy(queries, own_queries, arrived.at[2]),
    ]
    for copy in copies:
        copy.start()
    me = lax.axis_index("seq")
    odd = me & 1
    for copy in copies:
        copy.wait()
    rows = own[...]
    low, high = rows[:LEAF], rows[LEAF:]
    level_one = average_pairs(rows, wide)
    level_two = average_pairs(level_one, wide)
    first, second = level_one[:HALF], level_one[HALF:]
    inner[:LEAF] = jnp.where(odd == 1, low, high)
    inner[LEAF:] = jnp.where(odd == 1, second, first)
    outer[:LEAF] = jnp.where(odd == 1, high, low)
    outer[LEAF:] = jnp.where(odd == 1, first, second)
    if far_shares:
        for peer in range(quarter.shape[0]):
            quarter[peer] = level_two
    else:
        quarter[...] = level_two


def join_kernel(inner, quarter, upward, block, eighth, wide):
    me = lax.axis_index("seq")
    odd = me & 1
    edge_half = average_pairs(inner[:LEAF], wide)
    other_half = inner[LEAF:]
    theirs = jnp.concatenate(
        [jnp.where(odd == 1, other_half, edge_half), jnp.where(odd == 1, edge_half, other_half)], axis=0
    )
    theirs = average_pairs(theirs, wide)
    first = jnp.where(odd == 1, theirs, quarter[...])
    second = jnp.where(odd == 1, quarter[...], theirs)
    level_three = average_pairs(jnp.concatenate([first, second], axis=0), wide)
    upward[:HALF] = jnp.where(me >= 6, level_three, first)
    upward[HALF:] = second
    block[:HALF] = first
    block[HALF:] = second
    eighth[...] = level_three


NEAR_ROWS = 4 * LEAF
PAD = 16


def far_row_count(seq_size):
    rows = HALF
    for far in range(1, seq_size.bit_length() - 1):
        if seq_size >> far == 2:
            rows += LEAF
        elif far == 1:
            rows += 3 * HALF
        else:
            rows += 2 * LEAF
    return rows


def bias_of(valid):
    return jnp.where(valid, jnp.float32(0.0), jnp.float32(NEG))


def gathered_pieces(seq_size, far_rows, wide):
    me = lax.axis_index("seq")
    pieces = []
    for far in range(1, seq_size.bit_length() - 1):
        span = 1 << far
        group = me >> far
        parity = (me >> (far - 1)) & 1
        blocks = seq_size >> far

        def block(number, span=span, far=far):
            found = far_rows[pl.ds(number * span, span)].reshape(span * HALF, far_rows.shape[2])
            for _ in range(far - 1):
                found = average_pairs(found, wide)
            return found

        if blocks == 2:
            rows = block(1 - group)
            first = bias_of((group == 1) | (parity == 0))
            second = bias_of((group == 0) | (parity == 1))
            pieces += [(rows[:HALF], first), (rows[HALF:], second)]
        elif far == 1:
            third = jnp.where(parity == 0, me + 3, me - 3)
            for peer in (me - 2, me + 2, third):
                ok = (peer >= 0) & (peer < seq_size)
                pieces.append((far_rows[jnp.clip(peer, 0, seq_size - 1)], bias_of(ok)))
        else:
            lower = block(jnp.maximum(group - 1, 0))
            upper = block(jnp.minimum(group + 1, blocks - 1))
            has_lower, has_upper = group >= 1, group + 1 < blocks
            pieces += [
                (lower[:HALF], bias_of(has_lower)),
                (lower[HALF:], bias_of(has_lower & (parity == 1))),
                (upper[:HALF], bias_of(has_upper & (parity == 0))),
                (upper[HALF:], bias_of(has_upper)),
            ]
    return pieces


def paired_pieces(lower, upper, eighth, first_eighth):
    me = lax.axis_index("seq")
    odd = me & 1
    has_lower, has_upper = me >= 2, me < 6
    has_third = ((odd == 1) & has_lower) | ((odd == 0) & has_upper)
    return [
        (lower[:HALF], None),
        (upper[HALF:], bias_of(has_upper)),
        (jnp.where(odd == 1, lower[HALF:], upper[:HALF]), bias_of(has_third)),
        (eighth[...], None),
        (first_eighth[...], bias_of(jnp.logical_not(has_upper))),
    ]


def place(pieces, values, keys):
    at = 0
    width = values.shape[1]
    total_rows = values.shape[0]
    position = lax.broadcasted_iota(jnp.int32, (1, total_rows), 1)
    bias = jnp.zeros((1, total_rows), jnp.float32)
    for rows, value in pieces:
        count = rows.shape[0]
        keys[at : at + count] = rows[:, :width]
        values[at : at + count] = rows[:, width:]
        if value is not None:
            bias = jnp.where((position >= at) & (position < at + count), value, bias)
        at += count
    return bias


def split_heads(rows):
    first_head = lax.broadcasted_iota(jnp.int32, (1, rows.shape[1]), 1) < HD
    none = jnp.zeros_like(rows)
    return jnp.concatenate(
        [jnp.where(first_head, rows, none), jnp.where(first_head, none, rows)], axis=0
    )


def scores_of(queries, keys):
    return lax.dot_general(
        queries, keys[...], (((1,), (1,)), ((), ())), preferred_element_type=jnp.float32
    )


def near_kernel(seq_size, queries, own, inner, outer, scores, values, shared, keys, wide):
    me = lax.axis_index("seq")
    odd = me & 1
    from_inner, from_outer = inner[...], outer[...]
    before = jnp.where(odd == 1, from_inner, from_outer)
    after = jnp.where(odd == 1, from_outer, from_inner)
    edge_before, edge_after = before[:LEAF], after[:LEAF]
    far_half_after = after[LEAF:]
    shared[...] = before[LEAF:]
    near_half_before = average_pairs(edge_before, wide)
    near_half_after = average_pairs(edge_after, wide)
    has_before, has_after = bias_of(me >= 1), bias_of(me + 1 < seq_size)
    for leaf in range(2):
        if leaf == 0:
            near = [
                (edge_before, has_before),
                (own[...], None),
                (near_half_after, has_after),
                (far_half_after, has_after),
            ]
        else:
            near = [
                (own[...], None),
                (edge_after, has_after),
                (near_half_before, has_before),
                (far_half_after, has_after),
            ]
        bias = place(near, values.at[leaf], keys)
        rows = split_heads(queries[leaf * LEAF : (leaf + 1) * LEAF])
        scores[leaf] = scores_of(rows, keys) + bias


def attend_leaf(leaf, queries, near_scores, near_values, keys, values, bias, same, other):
    first_head = lax.broadcasted_iota(jnp.int32, (1, values.shape[1]), 1) < HD
    exponent = math.log2(math.e) / math.sqrt(HD)
    rows = split_heads(queries[pl.ds(pl.multiple_of(leaf * LEAF, LEAF), LEAF)])
    near = near_scores[leaf]
    far_scores = scores_of(rows, keys) + bias
    peak = jnp.maximum(
        jnp.max(near, axis=1, keepdims=True), jnp.max(far_scores, axis=1, keepdims=True)
    )
    near = jnp.exp2((near - peak) * exponent)
    far_weights = jnp.exp2((far_scores - peak) * exponent)
    total = jnp.sum(near, axis=1, keepdims=True) + jnp.sum(far_weights, axis=1, keepdims=True)
    numer = jnp.dot(
        near.astype(jnp.bfloat16), near_values[leaf], preferred_element_type=jnp.float32
    ) + jnp.dot(far_weights.astype(jnp.bfloat16), values[...], preferred_element_type=jnp.float32)
    mean = numer / total
    attended = jnp.where(first_head, mean[:LEAF], mean[LEAF:]).astype(jnp.bfloat16)
    second = (lax.axis_index("head") & 1) == 1
    same[:HALF] = jnp.where(second, attended[HALF:], attended[:HALF])
    other[:HALF] = jnp.where(second, attended[:HALF], attended[HALF:])


def leaves_kernel(seq_size, queries, near_scores, near_values, shared, *rest):
    *far, same, other, keys, values, bias, wide = rest
    if len(far) == 1:
        pieces = gathered_pieces(seq_size, far[0], wide)
    else:
        pieces = paired_pieces(*far)
    shared_bias = bias_of(lax.axis_index("seq") >= 1)
    bias[...] = jnp.broadcast_to(place([(shared, shared_bias)] + pieces, values, keys), bias.shape)
    leaf = (lax.axis_index("head") >> 1) ^ 1
    attend_leaf(leaf, queries, near_scores, near_values, keys, values, bias[:1], same, other)
    for share in (same, other):
        share[HALF:] = jnp.zeros((PAD, share.shape[1]), share.dtype)


def stays_kernel(queries, near_scores, near_values, keys, values, bias, same, other):
    leaf = lax.axis_index("head") >> 1
    attend_leaf(leaf, queries, near_scores, near_values, keys, values, bias[:1], same, other)


def side_by_side(same, other, rows, columns):
    second = (lax.axis_index("head") & 1) == 1
    width = same.shape[1]
    columns[:, :width] = jnp.where(second, other[:rows], same[:rows])
    columns[:, width:] = jnp.where(second, same[:rows], other[:rows])
    return columns[...]


def chip_rows(weight, chip, count):
    return weight[pl.ds(pl.multiple_of(chip * count, count), count)]


def begin_kernel(same, other, weight, partial, columns):
    chip = lax.axis_index("head") >> 1
    shares = side_by_side(same, other, partial.shape[0], columns)
    partial[...] = jnp.dot(
        shares, chip_rows(weight, chip, columns.shape[1]), preferred_element_type=jnp.float32
    )


def project_kernel(partial, other, same, weight, mixed, columns):
    chip = (lax.axis_index("head") >> 1) ^ 1
    shares = side_by_side(same, other, partial.shape[0], columns)
    total = partial[...] + jnp.dot(
        shares, chip_rows(weight, chip, columns.shape[1]), preferred_element_type=jnp.float32
    )
    mixed[...] = total.astype(mixed.dtype)


VMEM = pl.BlockSpec(memory_space=pltpu.VMEM)
HBM = pl.BlockSpec(memory_space=pltpu.HBM)


def kernel_call(body, name, megabytes, ins, outs, scratch, flops=0):
    shapes = tuple(
        out if isinstance(out, jax.ShapeDtypeStruct) else jax.ShapeDtypeStruct(out, jnp.bfloat16)
        for out in outs
    )
    return pl.pallas_call(
        body,
        out_shape=shapes,
        in_specs=ins,
        out_specs=(VMEM,) * len(outs),
        scratch_shapes=scratch,
        compiler_params=pltpu.CompilerParams(vmem_limit_bytes=megabytes << 20),
        cost_estimate=pl.CostEstimate(flops=flops, bytes_accessed=1 << 20, transcendentals=0),
        name=name,
    )


def shards(queries, keys, values, out_weight):
    tokens, width = queries.shape
    seq_size = lax.axis_size("seq")
    head_size = lax.axis_size("head")
    pair_width = 2 * width
    paired = seq_size == 8
    wide_rows = 2 * LEAF if paired else max(2 * LEAF, seq_size // 2 * HALF)
    wide = pltpu.VMEM((wide_rows, width), jnp.float32)

    def swap(array, bit, axis="seq"):
        return lax.ppermute(array, axis, [(i, i ^ bit) for i in range(lax.axis_size(axis))])

    own_queries, own, inner, outer, quarter = kernel_call(
        functools.partial(pack_kernel, not paired),
        "pack",
        16,
        [HBM] * 3,
        [
            (tokens, width),
            (tokens, pair_width),
            (LEAF + HALF, pair_width),
            (LEAF + HALF, pair_width),
            (HALF, pair_width) if paired else (seq_size, HALF, pair_width),
        ],
        [wide, pltpu.SemaphoreType.DMA((3,))],
    )(*(pltpu.with_memory_space_constraint(array, pltpu.HBM) for array in (queries, keys, values)))
    inner = swap(inner, 1)
    others = [(i, i + 1 if i & 1 else i - 1) for i in range(1, seq_size - 1)]
    outer = lax.ppermute(outer, "seq", others)
    if paired:
        upward, block, eighth = kernel_call(
            join_kernel,
            "join",
            8,
            [VMEM] * 2,
            [(LEAF, pair_width), (LEAF, pair_width), (HALF, pair_width)],
            [wide],
        )(inner, quarter)
        far = (
            lax.ppermute(upward, "seq", [(i, (i + 2) % seq_size) for i in range(seq_size)]),
            lax.ppermute(block, "seq", [(i + 2, i) for i in range(seq_size - 2)]),
            swap(eighth, 4),
            lax.ppermute(eighth, "seq", [(i, i + 6) for i in range(2)]),
        )
    else:
        far = (lax.all_to_all(quarter, "seq", split_axis=0, concat_axis=0),)
    share = tokens // head_size
    near_scores, near_values, shared = kernel_call(
        functools.partial(near_kernel, seq_size),
        "near",
        16,
        [VMEM] * 4,
        [
            jax.ShapeDtypeStruct((2, 2 * LEAF, NEAR_ROWS), jnp.float32),
            (2, NEAR_ROWS, width),
            (HALF, pair_width),
        ],
        [pltpu.VMEM((NEAR_ROWS, width), jnp.bfloat16), wide],
        flops=8 * LEAF * NEAR_ROWS * width,
    )(own_queries, own, inner, outer)
    far_rows = far_row_count(seq_size)

    leaf_flops = 8 * LEAF * (NEAR_ROWS + far_rows) * width
    share_2, share_3, far_keys, far_values, far_bias = kernel_call(
        functools.partial(leaves_kernel, seq_size),
        "leaves",
        24,
        [VMEM] * (4 + len(far)),
        [
            (share + PAD, width),
            (share + PAD, width),
            (far_rows, width),
            (far_rows, width),
            jax.ShapeDtypeStruct((8, far_rows), jnp.float32),
        ],
        [wide],
        flops=leaf_flops,
    )(own_queries, near_scores, near_values, shared, *far)
    share_0, share_1 = kernel_call(
        stays_kernel, "stays", 16, [VMEM] * 6, [(share, width)] * 2, [], flops=leaf_flops
    )(own_queries, near_scores, near_values, far_keys, far_values, far_bias)
    columns = pltpu.VMEM((share, pair_width), jnp.bfloat16)
    part_3, part_2 = swap(share_3, 3, "head"), swap(share_2, 2, "head")
    (partial,) = kernel_call(
        begin_kernel,
        "begin",
        8,
        [VMEM] * 3,
        [jax.ShapeDtypeStruct((share, out_weight.shape[1]), jnp.float32)],
        [columns],
    )(share_0, swap(share_1, 1, "head"), out_weight)
    (mixed,) = kernel_call(
        project_kernel, "project", 8, [VMEM] * 4, [(share, out_weight.shape[1])], [columns]
    )(partial, part_3, part_2, out_weight)
    return mixed


def solution(mesh):
    in_specs = (P("seq", "head"), P("seq", "head"), P("seq", "head"), P())
    out_specs = P(("seq", "head"), None)
    return jax.shard_map(shards, mesh=mesh, in_specs=in_specs, out_specs=out_specs, check_vma=False)
```

```python
import functools
import math

import jax
import jax.numpy as jnp
from jax import lax
from jax.experimental import pallas as pl
from jax.experimental.pallas import tpu as pltpu
from jax.sharding import PartitionSpec as P

HD = 64
LEAF = 128
HALF = LEAF // 2
NEG = -math.inf


def average_pairs(rows, wide):
    count = rows.shape[0]
    halves = []
    for low in range(0, rows.shape[1], LEAF):
        wide[:count] = rows[:, low : low + LEAF].astype(jnp.float32)
        even = wide[pl.ds(0, count // 2, stride=2), :]
        odd = wide[pl.ds(1, count // 2, stride=2), :]
        halves.append((0.5 * (even + odd)).astype(jnp.bfloat16))
    return jnp.concatenate(halves, axis=1)


def pack_kernel(far_shares, queries, keys, values, own_queries, own, inner, outer, quarter, wide, arrived):
    width = keys.shape[1]
    copies = [
        pltpu.make_async_copy(keys, own.at[:, :width], arrived.at[0]),
        pltpu.make_async_copy(values, own.at[:, width:], arrived.at[1]),
        pltpu.make_async_copy(queries, own_queries, arrived.at[2]),
    ]
    for copy in copies:
        copy.start()
    me = lax.axis_index("seq")
    odd = me & 1
    for copy in copies:
        copy.wait()
    rows = own[...]
    low, high = rows[:LEAF], rows[LEAF:]
    level_one = average_pairs(rows, wide)
    level_two = average_pairs(level_one, wide)
    first, second = level_one[:HALF], level_one[HALF:]
    inner[:LEAF] = jnp.where(odd == 1, low, high)
    inner[LEAF:] = jnp.where(odd == 1, second, first)
    outer[:LEAF] = jnp.where(odd == 1, high, low)
    outer[LEAF:] = jnp.where(odd == 1, first, second)
    if far_shares:
        for peer in range(quarter.shape[0]):
            quarter[peer] = level_two
    else:
        quarter[...] = level_two


def join_kernel(inner, quarter, block, across, eighth, wide):
    me = lax.axis_index("seq")
    odd = me & 1
    edge_half = average_pairs(inner[:LEAF], wide)
    other_half = inner[LEAF:]
    theirs = jnp.concatenate(
        [jnp.where(odd == 1, other_half, edge_half), jnp.where(odd == 1, edge_half, other_half)], axis=0
    )
    theirs = average_pairs(theirs, wide)
    block[:HALF] = jnp.where(odd == 1, theirs, quarter[...])
    block[HALF:] = jnp.where(odd == 1, quarter[...], theirs)
    level_three = average_pairs(block[...], wide)
    eighth[...] = level_three
    middle = (me >= 2) & (me < 6)
    across[:HALF] = jnp.where(middle, block[:HALF], level_three)
    across[HALF:] = block[HALF:]


NEAR_ROWS = 4 * LEAF
PAD = 16


def far_row_count(seq_size):
    rows = HALF
    for far in range(1, seq_size.bit_length() - 1):
        if seq_size >> far == 2:
            rows += LEAF
        elif far == 1:
            rows += 3 * HALF
        else:
            rows += 2 * LEAF
    return rows


def bias_of(valid):
    return jnp.where(valid, jnp.float32(0.0), jnp.float32(NEG))


def gathered_pieces(seq_size, far_rows, wide):
    me = lax.axis_index("seq")
    pieces = []
    for far in range(1, seq_size.bit_length() - 1):
        span = 1 << far
        group = me >> far
        parity = (me >> (far - 1)) & 1
        blocks = seq_size >> far

        def block(number, span=span, far=far):
            found = far_rows[pl.ds(number * span, span)].reshape(span * HALF, far_rows.shape[2])
            for _ in range(far - 1):
                found = average_pairs(found, wide)
            return found

        if blocks == 2:
            rows = block(1 - group)
            first = bias_of((group == 1) | (parity == 0))
            second = bias_of((group == 0) | (parity == 1))
            pieces += [(rows[:HALF], first), (rows[HALF:], second)]
        elif far == 1:
            third = jnp.where(parity == 0, me + 3, me - 3)
            for peer in (me - 2, me + 2, third):
                ok = (peer >= 0) & (peer < seq_size)
                pieces.append((far_rows[jnp.clip(peer, 0, seq_size - 1)], bias_of(ok)))
        else:
            lower = block(jnp.maximum(group - 1, 0))
            upper = block(jnp.minimum(group + 1, blocks - 1))
            has_lower, has_upper = group >= 1, group + 1 < blocks
            pieces += [
                (lower[:HALF], bias_of(has_lower)),
                (lower[HALF:], bias_of(has_lower & (parity == 1))),
                (upper[:HALF], bias_of(has_upper & (parity == 0))),
                (upper[HALF:], bias_of(has_upper)),
            ]
    return pieces


def paired_pieces(block_6, block_2, eighth_4):
    me = lax.axis_index("seq")
    odd = me & 1
    pair = me >> 1
    middle = (pair == 1) | (pair == 2)
    upper_near = (pair & 1) == 0
    lower = jnp.where(upper_near, block_6[...], block_2[...])
    upper = jnp.where(upper_near, block_2[...], block_6[...])
    has_lower, has_upper = pair >= 1, pair <= 2
    third = jnp.where(odd == 1, lower[HALF:], upper[:HALF])
    has_third = ((odd == 1) & has_lower) | ((odd == 0) & has_upper)
    return [
        (lower[:HALF], bias_of(has_lower)),
        (upper[HALF:], bias_of(has_upper)),
        (third, bias_of(has_third)),
        (eighth_4[...], bias_of(pair >= 0)),
        (block_6[:HALF], bias_of(jnp.logical_not(middle))),
    ]


def place(pieces, values, keys):
    at = 0
    width = values.shape[1]
    total_rows = values.shape[0]
    position = lax.broadcasted_iota(jnp.int32, (1, total_rows), 1)
    bias = jnp.zeros((1, total_rows), jnp.float32)
    for rows, value in pieces:
        count = rows.shape[0]
        keys[at : at + count] = rows[:, :width]
        values[at : at + count] = rows[:, width:]
        if value is not None:
            bias = jnp.where((position >= at) & (position < at + count), value, bias)
        at += count
    return bias


def split_heads(rows):
    first_head = lax.broadcasted_iota(jnp.int32, (1, rows.shape[1]), 1) < HD
    none = jnp.zeros_like(rows)
    return jnp.concatenate(
        [jnp.where(first_head, rows, none), jnp.where(first_head, none, rows)], axis=0
    )


def scores_of(queries, keys):
    return lax.dot_general(
        queries, keys[...], (((1,), (1,)), ((), ())), preferred_element_type=jnp.float32
    )


def near_kernel(seq_size, queries, own, inner, outer, scores, values, shared, keys, wide):
    me = lax.axis_index("seq")
    odd = me & 1
    from_inner, from_outer = inner[...], outer[...]
    before = jnp.where(odd == 1, from_inner, from_outer)
    after = jnp.where(odd == 1, from_outer, from_inner)
    edge_before, edge_after = before[:LEAF], after[:LEAF]
    far_half_after = after[LEAF:]
    shared[...] = before[LEAF:]
    near_half_before = average_pairs(edge_before, wide)
    near_half_after = average_pairs(edge_after, wide)
    has_before, has_after = bias_of(me >= 1), bias_of(me + 1 < seq_size)
    for leaf in range(2):
        if leaf == 0:
            near = [
                (edge_before, has_before),
                (own[...], None),
                (near_half_after, has_after),
                (far_half_after, has_after),
            ]
        else:
            near = [
                (own[...], None),
                (edge_after, has_after),
                (near_half_before, has_before),
                (far_half_after, has_after),
            ]
        bias = place(near, values.at[leaf], keys)
        rows = split_heads(queries[leaf * LEAF : (leaf + 1) * LEAF])
        scores[leaf] = scores_of(rows, keys) + bias


def attend_leaf(leaf, queries, near_scores, near_values, keys, values, bias, same, other):
    first_head = lax.broadcasted_iota(jnp.int32, (1, values.shape[1]), 1) < HD
    exponent = math.log2(math.e) / math.sqrt(HD)
    rows = split_heads(queries[pl.ds(pl.multiple_of(leaf * LEAF, LEAF), LEAF)])
    near = near_scores[leaf]
    far_scores = scores_of(rows, keys) + bias
    peak = jnp.maximum(
        jnp.max(near, axis=1, keepdims=True), jnp.max(far_scores, axis=1, keepdims=True)
    )
    near = jnp.exp2((near - peak) * exponent)
    far_weights = jnp.exp2((far_scores - peak) * exponent)
    total = jnp.sum(near, axis=1, keepdims=True) + jnp.sum(far_weights, axis=1, keepdims=True)
    numer = jnp.dot(
        near.astype(jnp.bfloat16), near_values[leaf], preferred_element_type=jnp.float32
    ) + jnp.dot(far_weights.astype(jnp.bfloat16), values[...], preferred_element_type=jnp.float32)
    mean = numer / total
    attended = jnp.where(first_head, mean[:LEAF], mean[LEAF:]).astype(jnp.bfloat16)
    second = (lax.axis_index("head") & 1) == 1
    same[:HALF] = jnp.where(second, attended[HALF:], attended[:HALF])
    other[:HALF] = jnp.where(second, attended[:HALF], attended[HALF:])


def leaves_kernel(seq_size, queries, near_scores, near_values, shared, *rest):
    *far, same, other, keys, values, bias, wide = rest
    if len(far) == 1:
        pieces = gathered_pieces(seq_size, far[0], wide)
    else:
        pieces = paired_pieces(*far)
    shared_bias = bias_of(lax.axis_index("seq") >= 1)
    bias[...] = jnp.broadcast_to(place([(shared, shared_bias)] + pieces, values, keys), bias.shape)
    leaf = (lax.axis_index("head") >> 1) ^ 1
    attend_leaf(leaf, queries, near_scores, near_values, keys, values, bias[:1], same, other)
    for share in (same, other):
        share[HALF:] = jnp.zeros((PAD, share.shape[1]), share.dtype)


def stays_kernel(queries, near_scores, near_values, keys, values, bias, same, other):
    leaf = lax.axis_index("head") >> 1
    attend_leaf(leaf, queries, near_scores, near_values, keys, values, bias[:1], same, other)


def side_by_side(same, other, rows, columns):
    second = (lax.axis_index("head") & 1) == 1
    width = same.shape[1]
    columns[:, :width] = jnp.where(second, other[:rows], same[:rows])
    columns[:, width:] = jnp.where(second, same[:rows], other[:rows])
    return columns[...]


def chip_rows(weight, chip, count):
    return weight[pl.ds(pl.multiple_of(chip * count, count), count)]


def begin_kernel(same, other, weight, partial, columns):
    chip = lax.axis_index("head") >> 1
    shares = side_by_side(same, other, partial.shape[0], columns)
    partial[...] = jnp.dot(
        shares, chip_rows(weight, chip, columns.shape[1]), preferred_element_type=jnp.float32
    )


def project_kernel(partial, other, same, weight, mixed, columns):
    chip = (lax.axis_index("head") >> 1) ^ 1
    shares = side_by_side(same, other, partial.shape[0], columns)
    total = partial[...] + jnp.dot(
        shares, chip_rows(weight, chip, columns.shape[1]), preferred_element_type=jnp.float32
    )
    mixed[...] = total.astype(mixed.dtype)


VMEM = pl.BlockSpec(memory_space=pltpu.VMEM)
HBM = pl.BlockSpec(memory_space=pltpu.HBM)


def kernel_call(body, name, megabytes, ins, outs, scratch, flops=0):
    shapes = tuple(
        out if isinstance(out, jax.ShapeDtypeStruct) else jax.ShapeDtypeStruct(out, jnp.bfloat16)
        for out in outs
    )
    return pl.pallas_call(
        body,
        out_shape=shapes,
        in_specs=ins,
        out_specs=(VMEM,) * len(outs),
        scratch_shapes=scratch,
        compiler_params=pltpu.CompilerParams(vmem_limit_bytes=megabytes << 20),
        cost_estimate=pl.CostEstimate(flops=flops, bytes_accessed=1 << 20, transcendentals=0),
        name=name,
    )


def shards(queries, keys, values, out_weight):
    tokens, width = queries.shape
    seq_size = lax.axis_size("seq")
    head_size = lax.axis_size("head")
    pair_width = 2 * width
    paired = seq_size == 8
    wide_rows = 2 * LEAF if paired else max(2 * LEAF, seq_size // 2 * HALF)
    wide = pltpu.VMEM((wide_rows, width), jnp.float32)

    def swap(array, bit, axis="seq"):
        return lax.ppermute(array, axis, [(i, i ^ bit) for i in range(lax.axis_size(axis))])

    own_queries, own, inner, outer, quarter = kernel_call(
        functools.partial(pack_kernel, not paired),
        "pack",
        16,
        [HBM] * 3,
        [
            (tokens, width),
            (tokens, pair_width),
            (LEAF + HALF, pair_width),
            (LEAF + HALF, pair_width),
            (HALF, pair_width) if paired else (seq_size, HALF, pair_width),
        ],
        [wide, pltpu.SemaphoreType.DMA((3,))],
    )(*(pltpu.with_memory_space_constraint(array, pltpu.HBM) for array in (queries, keys, values)))
    inner = swap(inner, 1)
    ends = [(i, i) for i in (0, seq_size - 1)]
    others = ends + [(i, i + 1 if i & 1 else i - 1) for i in range(1, seq_size - 1)]
    outer = lax.ppermute(outer, "seq", others)
    if paired:
        block, across, eighth = kernel_call(
            join_kernel,
            "join",
            8,
            [VMEM] * 2,
            [(LEAF, pair_width), (LEAF, pair_width), (HALF, pair_width)],
            [wide],
        )(inner, quarter)
        far = (swap(across, 6), swap(block, 2), swap(eighth, 4))
    else:
        far = (lax.all_to_all(quarter, "seq", split_axis=0, concat_axis=0),)
    share = tokens // head_size
    near_scores, near_values, shared = kernel_call(
        functools.partial(near_kernel, seq_size),
        "near",
        16,
        [VMEM] * 4,
        [
            jax.ShapeDtypeStruct((2, 2 * LEAF, NEAR_ROWS), jnp.float32),
            (2, NEAR_ROWS, width),
            (HALF, pair_width),
        ],
        [pltpu.VMEM((NEAR_ROWS, width), jnp.bfloat16), wide],
        flops=8 * LEAF * NEAR_ROWS * width,
    )(own_queries, own, inner, outer)
    far_rows = far_row_count(seq_size)

    leaf_flops = 8 * LEAF * (NEAR_ROWS + far_rows) * width
    share_2, share_3, far_keys, far_values, far_bias = kernel_call(
        functools.partial(leaves_kernel, seq_size),
        "leaves",
        24,
        [VMEM] * (4 + len(far)),
        [
            (share + PAD, width),
            (share + PAD, width),
            (far_rows, width),
            (far_rows, width),
            jax.ShapeDtypeStruct((8, far_rows), jnp.float32),
        ],
        [wide],
        flops=leaf_flops,
    )(own_queries, near_scores, near_values, shared, *far)
    share_0, share_1 = kernel_call(
        stays_kernel, "stays", 16, [VMEM] * 6, [(share, width)] * 2, [], flops=leaf_flops
    )(own_queries, near_scores, near_values, far_keys, far_values, far_bias)
    columns = pltpu.VMEM((share, pair_width), jnp.bfloat16)
    part_3, part_2 = swap(share_3, 3, "head"), swap(share_2, 2, "head")
    (partial,) = kernel_call(
        begin_kernel,
        "begin",
        8,
        [VMEM] * 3,
        [jax.ShapeDtypeStruct((share, out_weight.shape[1]), jnp.float32)],
        [columns],
    )(share_0, swap(share_1, 1, "head"), out_weight)
    (mixed,) = kernel_call(
        project_kernel, "project", 8, [VMEM] * 4, [(share, out_weight.shape[1])], [columns]
    )(partial, part_3, part_2, out_weight)
    return mixed


def solution(mesh):
    in_specs = (P("seq", "head"), P("seq", "head"), P("seq", "head"), P())
    out_specs = P(("seq", "head"), None)
    return jax.shard_map(shards, mesh=mesh, in_specs=in_specs, out_specs=out_specs, check_vma=False)
```

```python
import functools
import math

import jax
import jax.numpy as jnp
from jax import lax
from jax.experimental import pallas as pl
from jax.experimental.pallas import tpu as pltpu
from jax.sharding import PartitionSpec as P

HD = 64
LEAF = 128
HALF = LEAF // 2
NEG = -math.inf


def average_pairs(rows, wide):
    count = rows.shape[0]
    halves = []
    for low in range(0, rows.shape[1], LEAF):
        wide[:count] = rows[:, low : low + LEAF].astype(jnp.float32)
        even = wide[pl.ds(0, count // 2, stride=2), :]
        odd = wide[pl.ds(1, count // 2, stride=2), :]
        halves.append((0.5 * (even + odd)).astype(jnp.bfloat16))
    return jnp.concatenate(halves, axis=1)


def pack_kernel(far_shares, queries, keys, values, own_queries, own, inner, outer, quarter, wide, arrived):
    width = keys.shape[1]
    copies = [
        pltpu.make_async_copy(keys, own.at[:, :width], arrived.at[0]),
        pltpu.make_async_copy(values, own.at[:, width:], arrived.at[1]),
        pltpu.make_async_copy(queries, own_queries, arrived.at[2]),
    ]
    for copy in copies:
        copy.start()
    me = lax.axis_index("seq")
    odd = me & 1
    for copy in copies:
        copy.wait()
    rows = own[...]
    low, high = rows[:LEAF], rows[LEAF:]
    level_one = average_pairs(rows, wide)
    level_two = average_pairs(level_one, wide)
    first, second = level_one[:HALF], level_one[HALF:]
    inner[:LEAF] = jnp.where(odd == 1, low, high)
    inner[LEAF:] = jnp.where(odd == 1, second, first)
    outer[:LEAF] = jnp.where(odd == 1, high, low)
    outer[LEAF:] = jnp.where(odd == 1, first, second)
    if far_shares:
        for peer in range(quarter.shape[0]):
            quarter[peer] = level_two
    else:
        quarter[...] = level_two


def join_kernel(inner, quarter, short, block, eighth, wide):
    me = lax.axis_index("seq")
    odd = me & 1
    edge_half = average_pairs(inner[:LEAF], wide)
    other_half = inner[LEAF:]
    theirs = jnp.concatenate(
        [jnp.where(odd == 1, other_half, edge_half), jnp.where(odd == 1, edge_half, other_half)], axis=0
    )
    theirs = average_pairs(theirs, wide)
    first = jnp.where(odd == 1, theirs, quarter[...])
    second = jnp.where(odd == 1, quarter[...], theirs)
    level_three = average_pairs(jnp.concatenate([first, second], axis=0), wide)
    short[...] = jnp.where((me == 6) | (me == 1), level_three, quarter[...])
    block[:HALF] = jnp.where((me == 0) | (me == 7), level_three, first)
    block[HALF:] = second
    eighth[...] = level_three


NEAR_ROWS = 4 * LEAF
PAD = 16


def last_row_count(seq_size, paired):
    if paired:
        return 3 * HALF
    rows = 0
    for far in range(1, seq_size.bit_length() - 1):
        if seq_size >> far == 2:
            rows += LEAF
        elif far == 1:
            rows += 3 * HALF
        else:
            rows += 2 * LEAF
    return rows


def bias_of(valid):
    return jnp.where(valid, jnp.float32(0.0), jnp.float32(NEG))


def gathered_pieces(seq_size, far_rows, wide):
    me = lax.axis_index("seq")
    pieces = []
    for far in range(1, seq_size.bit_length() - 1):
        span = 1 << far
        group = me >> far
        parity = (me >> (far - 1)) & 1
        blocks = seq_size >> far

        def block(number, span=span, far=far):
            found = far_rows[pl.ds(number * span, span)].reshape(span * HALF, far_rows.shape[2])
            for _ in range(far - 1):
                found = average_pairs(found, wide)
            return found

        if blocks == 2:
            rows = block(1 - group)
            first = bias_of((group == 1) | (parity == 0))
            second = bias_of((group == 0) | (parity == 1))
            pieces += [(rows[:HALF], first), (rows[HALF:], second)]
        elif far == 1:
            third = jnp.where(parity == 0, me + 3, me - 3)
            for peer in (me - 2, me + 2, third):
                ok = (peer >= 0) & (peer < seq_size)
                pieces.append((far_rows[jnp.clip(peer, 0, seq_size - 1)], bias_of(ok)))
        else:
            lower = block(jnp.maximum(group - 1, 0))
            upper = block(jnp.minimum(group + 1, blocks - 1))
            has_lower, has_upper = group >= 1, group + 1 < blocks
            pieces += [
                (lower[:HALF], bias_of(has_lower)),
                (lower[HALF:], bias_of(has_lower & (parity == 1))),
                (upper[:HALF], bias_of(has_upper & (parity == 0))),
                (upper[HALF:], bias_of(has_upper)),
            ]
    return pieces


def paired_pieces(block, eighth):
    me = lax.axis_index("seq")
    inside = jnp.logical_not((me == 6) | (me == 1))
    return [(block[:HALF], None), (block[HALF:], bias_of(inside)), (eighth[...], None)]


def place(pieces, values, keys):
    at = 0
    width = values.shape[1]
    total_rows = values.shape[0]
    position = lax.broadcasted_iota(jnp.int32, (1, total_rows), 1)
    bias = jnp.zeros((1, total_rows), jnp.float32)
    for rows, value in pieces:
        count = rows.shape[0]
        keys[at : at + count] = rows[:, :width]
        values[at : at + count] = rows[:, width:]
        if value is not None:
            bias = jnp.where((position >= at) & (position < at + count), value, bias)
        at += count
    return bias


def split_heads(rows):
    first_head = lax.broadcasted_iota(jnp.int32, (1, rows.shape[1]), 1) < HD
    none = jnp.zeros_like(rows)
    return jnp.concatenate(
        [jnp.where(first_head, rows, none), jnp.where(first_head, none, rows)], axis=0
    )


def scores_of(queries, keys):
    return lax.dot_general(
        queries, keys[...], (((1,), (1,)), ((), ())), preferred_element_type=jnp.float32
    )


def near_kernel(seq_size, queries, own, inner, outer, scores, values, shared, keys, wide):
    me = lax.axis_index("seq")
    odd = me & 1
    from_inner, from_outer = inner[...], outer[...]
    before = jnp.where(odd == 1, from_inner, from_outer)
    after = jnp.where(odd == 1, from_outer, from_inner)
    edge_before, edge_after = before[:LEAF], after[:LEAF]
    far_half_after = after[LEAF:]
    shared[...] = before[LEAF:]
    near_half_before = average_pairs(edge_before, wide)
    near_half_after = average_pairs(edge_after, wide)
    has_before, has_after = bias_of(me >= 1), bias_of(me + 1 < seq_size)
    for leaf in range(2):
        if leaf == 0:
            near = [
                (edge_before, has_before),
                (own[...], None),
                (near_half_after, has_after),
                (far_half_after, has_after),
            ]
        else:
            near = [
                (own[...], None),
                (edge_after, has_after),
                (near_half_before, has_before),
                (far_half_after, has_after),
            ]
        bias = place(near, values.at[leaf], keys)
        rows = split_heads(queries[leaf * LEAF : (leaf + 1) * LEAF])
        scores[leaf] = scores_of(rows, keys) + bias


def mid_kernel(queries, shared, *rest):
    *short, scores, values, keys = rest
    pieces = [(shared, bias_of(lax.axis_index("seq") >= 1))] + [(rows, None) for rows in short]
    bias = place(pieces, values, keys)
    for leaf in range(2):
        rows = split_heads(queries[leaf * LEAF : (leaf + 1) * LEAF])
        scores[leaf] = scores_of(rows, keys) + bias


def attend_leaf(leaf, queries, scored, keys, values, bias, same, other):
    first_head = lax.broadcasted_iota(jnp.int32, (1, values.shape[1]), 1) < HD
    exponent = math.log2(math.e) / math.sqrt(HD)
    rows = split_heads(queries[pl.ds(pl.multiple_of(leaf * LEAF, LEAF), LEAF)])
    near_scores, near_values, mid_scores, mid_values = scored
    parts = [
        (near_scores[leaf], near_values[leaf]),
        (mid_scores[leaf], mid_values[...]),
        (scores_of(rows, keys) + bias, values[...]),
    ]
    peak = functools.reduce(
        jnp.maximum, [jnp.max(scores, axis=1, keepdims=True) for scores, _ in parts]
    )
    total, numer = 0.0, 0.0
    for scores, part_values in parts:
        weights = jnp.exp2((scores - peak) * exponent)
        total = total + jnp.sum(weights, axis=1, keepdims=True)
        numer = numer + jnp.dot(
            weights.astype(jnp.bfloat16), part_values, preferred_element_type=jnp.float32
        )
    mean = numer / total
    attended = jnp.where(first_head, mean[:LEAF], mean[LEAF:]).astype(jnp.bfloat16)
    second = (lax.axis_index("head") & 1) == 1
    same[:HALF] = jnp.where(second, attended[HALF:], attended[:HALF])
    other[:HALF] = jnp.where(second, attended[:HALF], attended[HALF:])


def leaves_kernel(seq_size, queries, near_scores, near_values, mid_scores, mid_values, *rest):
    *far, same, other, keys, values, bias, wide = rest
    if len(far) == 1:
        pieces = gathered_pieces(seq_size, far[0], wide)
    else:
        pieces = paired_pieces(*far)
    bias[...] = jnp.broadcast_to(place(pieces, values, keys), bias.shape)
    leaf = (lax.axis_index("head") >> 1) ^ 1
    scored = (near_scores, near_values, mid_scores, mid_values)
    attend_leaf(leaf, queries, scored, keys, values, bias[:1], same, other)
    for share in (same, other):
        share[HALF:] = jnp.zeros((PAD, share.shape[1]), share.dtype)


def stays_kernel(
    queries, near_scores, near_values, mid_scores, mid_values, keys, values, bias, same, other
):
    leaf = lax.axis_index("head") >> 1
    scored = (near_scores, near_values, mid_scores, mid_values)
    attend_leaf(leaf, queries, scored, keys, values, bias[:1], same, other)


def side_by_side(same, other, rows, columns):
    second = (lax.axis_index("head") & 1) == 1
    width = same.shape[1]
    columns[:, :width] = jnp.where(second, other[:rows], same[:rows])
    columns[:, width:] = jnp.where(second, same[:rows], other[:rows])
    return columns[...]


def chip_rows(weight, chip, count):
    return weight[pl.ds(pl.multiple_of(chip * count, count), count)]


def begin_kernel(same, other, weight, partial, columns):
    chip = lax.axis_index("head") >> 1
    shares = side_by_side(same, other, partial.shape[0], columns)
    partial[...] = jnp.dot(
        shares, chip_rows(weight, chip, columns.shape[1]), preferred_element_type=jnp.float32
    )


def project_kernel(partial, other, same, weight, mixed, columns):
    chip = (lax.axis_index("head") >> 1) ^ 1
    shares = side_by_side(same, other, partial.shape[0], columns)
    total = partial[...] + jnp.dot(
        shares, chip_rows(weight, chip, columns.shape[1]), preferred_element_type=jnp.float32
    )
    mixed[...] = total.astype(mixed.dtype)


VMEM = pl.BlockSpec(memory_space=pltpu.VMEM)
HBM = pl.BlockSpec(memory_space=pltpu.HBM)


def kernel_call(body, name, megabytes, ins, outs, scratch, flops=0):
    shapes = tuple(
        out if isinstance(out, jax.ShapeDtypeStruct) else jax.ShapeDtypeStruct(out, jnp.bfloat16)
        for out in outs
    )
    return pl.pallas_call(
        body,
        out_shape=shapes,
        in_specs=ins,
        out_specs=(VMEM,) * len(outs),
        scratch_shapes=scratch,
        compiler_params=pltpu.CompilerParams(vmem_limit_bytes=megabytes << 20),
        cost_estimate=pl.CostEstimate(flops=flops, bytes_accessed=1 << 20, transcendentals=0),
        name=name,
    )


def shards(queries, keys, values, out_weight):
    tokens, width = queries.shape
    seq_size = lax.axis_size("seq")
    head_size = lax.axis_size("head")
    pair_width = 2 * width
    paired = seq_size == 8
    wide_rows = 2 * LEAF if paired else max(2 * LEAF, seq_size // 2 * HALF)
    wide = pltpu.VMEM((wide_rows, width), jnp.float32)

    def swap(array, bit, axis="seq"):
        return lax.ppermute(array, axis, [(i, i ^ bit) for i in range(lax.axis_size(axis))])

    own_queries, own, inner, outer, quarter = kernel_call(
        functools.partial(pack_kernel, not paired),
        "pack",
        16,
        [HBM] * 3,
        [
            (tokens, width),
            (tokens, pair_width),
            (LEAF + HALF, pair_width),
            (LEAF + HALF, pair_width),
            (HALF, pair_width) if paired else (seq_size, HALF, pair_width),
        ],
        [wide, pltpu.SemaphoreType.DMA((3,))],
    )(*(pltpu.with_memory_space_constraint(array, pltpu.HBM) for array in (queries, keys, values)))
    inner = swap(inner, 1)
    others = [(i, i + 1 if i & 1 else i - 1) for i in range(1, seq_size - 1)]
    outer = lax.ppermute(outer, "seq", others)
    if paired:
        short, block, eighth = kernel_call(
            join_kernel,
            "join",
            8,
            [VMEM] * 2,
            [(HALF, pair_width), (LEAF, pair_width), (HALF, pair_width)],
            [wide],
        )(inner, quarter)
        shift = [(i, (i - 2 if i & 1 else i + 2) % seq_size) for i in range(seq_size)]
        early = (lax.ppermute(short, "seq", shift),)
        far = (
            lax.ppermute(block, "seq", [(target, source) for source, target in shift]),
            swap(eighth, 4),
        )
    else:
        early = ()
        far = (lax.all_to_all(quarter, "seq", split_axis=0, concat_axis=0),)
    share = tokens // head_size
    near_scores, near_values, shared = kernel_call(
        functools.partial(near_kernel, seq_size),
        "near",
        16,
        [VMEM] * 4,
        [
            jax.ShapeDtypeStruct((2, 2 * LEAF, NEAR_ROWS), jnp.float32),
            (2, NEAR_ROWS, width),
            (HALF, pair_width),
        ],
        [pltpu.VMEM((NEAR_ROWS, width), jnp.bfloat16), wide],
        flops=8 * LEAF * NEAR_ROWS * width,
    )(own_queries, own, inner, outer)
    mid_rows = HALF * (1 + len(early))
    mid_scores, mid_values = kernel_call(
        mid_kernel,
        "mid",
        8,
        [VMEM] * (2 + len(early)),
        [jax.ShapeDtypeStruct((2, 2 * LEAF, mid_rows), jnp.float32), (mid_rows, width)],
        [pltpu.VMEM((mid_rows, width), jnp.bfloat16)],
        flops=520 * 10**6,
    )(own_queries, shared, *early)
    scored = (near_scores, near_values, mid_scores, mid_values)
    last_rows = last_row_count(seq_size, paired)
    leaf_flops = 8 * LEAF * (NEAR_ROWS + mid_rows + last_rows) * width
    share_2, share_3, far_keys, far_values, far_bias = kernel_call(
        functools.partial(leaves_kernel, seq_size),
        "leaves",
        24,
        [VMEM] * (5 + len(far)),
        [
            (share + PAD, width),
            (share + PAD, width),
            (last_rows, width),
            (last_rows, width),
            jax.ShapeDtypeStruct((8, last_rows), jnp.float32),
        ],
        [wide],
        flops=leaf_flops,
    )(own_queries, *scored, *far)
    share_0, share_1 = kernel_call(
        stays_kernel, "stays", 16, [VMEM] * 8, [(share, width)] * 2, [], flops=leaf_flops
    )(own_queries, *scored, far_keys, far_values, far_bias)
    columns = pltpu.VMEM((share, pair_width), jnp.bfloat16)
    part_3, part_2 = swap(share_3, 3, "head"), swap(share_2, 2, "head")
    (partial,) = kernel_call(
        begin_kernel,
        "begin",
        8,
        [VMEM] * 3,
        [jax.ShapeDtypeStruct((share, out_weight.shape[1]), jnp.float32)],
        [columns],
    )(share_0, swap(share_1, 1, "head"), out_weight)
    (mixed,) = kernel_call(
        project_kernel, "project", 8, [VMEM] * 4, [(share, out_weight.shape[1])], [columns]
    )(partial, part_3, part_2, out_weight)
    return mixed


def solution(mesh):
    in_specs = (P("seq", "head"), P("seq", "head"), P("seq", "head"), P())
    out_specs = P(("seq", "head"), None)
    return jax.shard_map(shards, mesh=mesh, in_specs=in_specs, out_specs=out_specs, check_vma=False)
```

```python
import functools
import math

import jax
import jax.numpy as jnp
from jax import lax
from jax.experimental import pallas as pl
from jax.experimental.pallas import tpu as pltpu
from jax.sharding import PartitionSpec as P

HD = 64
LEAF = 128
HALF = LEAF // 2
NEG = -math.inf


def average_pairs(rows, wide):
    count = rows.shape[0]
    halves = []
    for low in range(0, rows.shape[1], LEAF):
        wide[:count] = rows[:, low : low + LEAF].astype(jnp.float32)
        even = wide[pl.ds(0, count // 2, stride=2), :]
        odd = wide[pl.ds(1, count // 2, stride=2), :]
        halves.append((0.5 * (even + odd)).astype(jnp.bfloat16))
    return jnp.concatenate(halves, axis=1)


def pack_kernel(far_shares, queries, keys, values, own_queries, own, inner, outer, quarter, wide, arrived):
    width = keys.shape[1]
    copies = [
        pltpu.make_async_copy(keys, own.at[:, :width], arrived.at[0]),
        pltpu.make_async_copy(values, own.at[:, width:], arrived.at[1]),
        pltpu.make_async_copy(queries, own_queries, arrived.at[2]),
    ]
    for copy in copies:
        copy.start()
    me = lax.axis_index("seq")
    odd = me & 1
    for copy in copies:
        copy.wait()
    rows = own[...]
    low, high = rows[:LEAF], rows[LEAF:]
    level_one = average_pairs(rows, wide)
    level_two = average_pairs(level_one, wide)
    first, second = level_one[:HALF], level_one[HALF:]
    inner[:LEAF] = jnp.where(odd == 1, low, high)
    inner[LEAF:] = jnp.where(odd == 1, second, first)
    outer[:LEAF] = jnp.where(odd == 1, high, low)
    outer[LEAF:] = jnp.where(odd == 1, first, second)
    if far_shares:
        for peer in range(quarter.shape[0]):
            quarter[peer] = level_two
    else:
        quarter[...] = level_two


def join_kernel(inner, quarter, upward, downward, eighth, wide):
    me = lax.axis_index("seq")
    odd = me & 1
    edge_half = average_pairs(inner[:LEAF], wide)
    other_half = inner[LEAF:]
    theirs = jnp.concatenate(
        [jnp.where(odd == 1, other_half, edge_half), jnp.where(odd == 1, edge_half, other_half)], axis=0
    )
    theirs = average_pairs(theirs, wide)
    first = jnp.where(odd == 1, theirs, quarter[...])
    second = jnp.where(odd == 1, quarter[...], theirs)
    level_three = average_pairs(jnp.concatenate([first, second], axis=0), wide)
    upward[:HALF] = jnp.where(me >= 6, level_three, first)
    upward[HALF:] = second
    downward[:HALF] = jnp.where(me < 2, level_three, first)
    downward[HALF:] = second
    eighth[...] = level_three


NEAR_ROWS = 4 * LEAF
PAD = 16


def last_row_count(seq_size, paired):
    if paired:
        return LEAF
    rows = 0
    for far in range(1, seq_size.bit_length() - 1):
        if seq_size >> far == 2:
            rows += LEAF
        elif far == 1:
            rows += 3 * HALF
        else:
            rows += 2 * LEAF
    return rows


def bias_of(valid):
    return jnp.where(valid, jnp.float32(0.0), jnp.float32(NEG))


def gathered_pieces(seq_size, far_rows, wide):
    me = lax.axis_index("seq")
    pieces = []
    for far in range(1, seq_size.bit_length() - 1):
        span = 1 << far
        group = me >> far
        parity = (me >> (far - 1)) & 1
        blocks = seq_size >> far

        def block(number, span=span, far=far):
            found = far_rows[pl.ds(number * span, span)].reshape(span * HALF, far_rows.shape[2])
            for _ in range(far - 1):
                found = average_pairs(found, wide)
            return found

        if blocks == 2:
            rows = block(1 - group)
            first = bias_of((group == 1) | (parity == 0))
            second = bias_of((group == 0) | (parity == 1))
            pieces += [(rows[:HALF], first), (rows[HALF:], second)]
        elif far == 1:
            third = jnp.where(parity == 0, me + 3, me - 3)
            for peer in (me - 2, me + 2, third):
                ok = (peer >= 0) & (peer < seq_size)
                pieces.append((far_rows[jnp.clip(peer, 0, seq_size - 1)], bias_of(ok)))
        else:
            lower = block(jnp.maximum(group - 1, 0))
            upper = block(jnp.minimum(group + 1, blocks - 1))
            has_lower, has_upper = group >= 1, group + 1 < blocks
            pieces += [
                (lower[:HALF], bias_of(has_lower)),
                (lower[HALF:], bias_of(has_lower & (parity == 1))),
                (upper[:HALF], bias_of(has_upper & (parity == 0))),
                (upper[HALF:], bias_of(has_upper)),
            ]
    return pieces


def early_pieces(lower, eighth):
    me = lax.axis_index("seq")
    whole = ((me & 1) == 1) & (me >= 2)
    return [(lower[:HALF], None), (lower[HALF:], bias_of(whole)), (eighth[...], None)]


def late_pieces(upper):
    me = lax.axis_index("seq")
    whole = ((me & 1) == 0) | (me >= 6)
    return [(upper[:HALF], bias_of(whole)), (upper[HALF:], bias_of(me < 6))]


def place(pieces, values, keys):
    at = 0
    width = values.shape[1]
    total_rows = values.shape[0]
    position = lax.broadcasted_iota(jnp.int32, (1, total_rows), 1)
    bias = jnp.zeros((1, total_rows), jnp.float32)
    for rows, value in pieces:
        count = rows.shape[0]
        keys[at : at + count] = rows[:, :width]
        values[at : at + count] = rows[:, width:]
        if value is not None:
            bias = jnp.where((position >= at) & (position < at + count), value, bias)
        at += count
    return bias


def split_heads(rows):
    first_head = lax.broadcasted_iota(jnp.int32, (1, rows.shape[1]), 1) < HD
    none = jnp.zeros_like(rows)
    return jnp.concatenate(
        [jnp.where(first_head, rows, none), jnp.where(first_head, none, rows)], axis=0
    )


def scores_of(queries, keys):
    return lax.dot_general(
        queries, keys[...], (((1,), (1,)), ((), ())), preferred_element_type=jnp.float32
    )


def near_kernel(seq_size, queries, own, inner, outer, scores, values, shared, keys, wide):
    me = lax.axis_index("seq")
    odd = me & 1
    from_inner, from_outer = inner[...], outer[...]
    before = jnp.where(odd == 1, from_inner, from_outer)
    after = jnp.where(odd == 1, from_outer, from_inner)
    edge_before, edge_after = before[:LEAF], after[:LEAF]
    far_half_after = after[LEAF:]
    shared[...] = before[LEAF:]
    near_half_before = average_pairs(edge_before, wide)
    near_half_after = average_pairs(edge_after, wide)
    has_before, has_after = bias_of(me >= 1), bias_of(me + 1 < seq_size)
    for leaf in range(2):
        if leaf == 0:
            near = [
                (edge_before, has_before),
                (own[...], None),
                (near_half_after, has_after),
                (far_half_after, has_after),
            ]
        else:
            near = [
                (own[...], None),
                (edge_after, has_after),
                (near_half_before, has_before),
                (far_half_after, has_after),
            ]
        bias = place(near, values.at[leaf], keys)
        rows = split_heads(queries[leaf * LEAF : (leaf + 1) * LEAF])
        scores[leaf] = scores_of(rows, keys) + bias


def mid_kernel(queries, shared, *rest):
    *early, scores, values, keys = rest
    pieces = [(shared, bias_of(lax.axis_index("seq") >= 1))]
    if early:
        pieces += early_pieces(*early)
    bias = place(pieces, values, keys)
    for leaf in range(2):
        rows = split_heads(queries[leaf * LEAF : (leaf + 1) * LEAF])
        scores[leaf] = scores_of(rows, keys) + bias


def attend_leaf(leaf, queries, scored, keys, values, bias, same, other):
    first_head = lax.broadcasted_iota(jnp.int32, (1, values.shape[1]), 1) < HD
    exponent = math.log2(math.e) / math.sqrt(HD)
    rows = split_heads(queries[pl.ds(pl.multiple_of(leaf * LEAF, LEAF), LEAF)])
    near_scores, near_values, mid_scores, mid_values = scored
    parts = [
        (near_scores[leaf], near_values[leaf]),
        (mid_scores[leaf], mid_values[...]),
        (scores_of(rows, keys) + bias, values[...]),
    ]
    peak = functools.reduce(
        jnp.maximum, [jnp.max(scores, axis=1, keepdims=True) for scores, _ in parts]
    )
    total, numer = 0.0, 0.0
    for scores, part_values in parts:
        weights = jnp.exp2((scores - peak) * exponent)
        total = total + jnp.sum(weights, axis=1, keepdims=True)
        numer = numer + jnp.dot(
            weights.astype(jnp.bfloat16), part_values, preferred_element_type=jnp.float32
        )
    mean = numer / total
    attended = jnp.where(first_head, mean[:LEAF], mean[LEAF:]).astype(jnp.bfloat16)
    second = (lax.axis_index("head") & 1) == 1
    same[:HALF] = jnp.where(second, attended[HALF:], attended[:HALF])
    other[:HALF] = jnp.where(second, attended[:HALF], attended[HALF:])


def leaves_kernel(seq_size, paired, queries, near_scores, near_values, mid_scores, mid_values, *rest):
    late, same, other, keys, values, bias, wide = rest
    pieces = late_pieces(late) if paired else gathered_pieces(seq_size, late, wide)
    bias[...] = jnp.broadcast_to(place(pieces, values, keys), bias.shape)
    leaf = (lax.axis_index("head") >> 1) ^ 1
    scored = (near_scores, near_values, mid_scores, mid_values)
    attend_leaf(leaf, queries, scored, keys, values, bias[:1], same, other)
    for share in (same, other):
        share[HALF:] = jnp.zeros((PAD, share.shape[1]), share.dtype)


def stays_kernel(
    queries, near_scores, near_values, mid_scores, mid_values, keys, values, bias, same, other
):
    leaf = lax.axis_index("head") >> 1
    scored = (near_scores, near_values, mid_scores, mid_values)
    attend_leaf(leaf, queries, scored, keys, values, bias[:1], same, other)


def side_by_side(same, other, rows, columns):
    second = (lax.axis_index("head") & 1) == 1
    width = same.shape[1]
    columns[:, :width] = jnp.where(second, other[:rows], same[:rows])
    columns[:, width:] = jnp.where(second, same[:rows], other[:rows])
    return columns[...]


def chip_rows(weight, chip, count):
    return weight[pl.ds(pl.multiple_of(chip * count, count), count)]


def begin_kernel(same, other, weight, partial, columns):
    chip = lax.axis_index("head") >> 1
    shares = side_by_side(same, other, partial.shape[0], columns)
    partial[...] = jnp.dot(
        shares, chip_rows(weight, chip, columns.shape[1]), preferred_element_type=jnp.float32
    )


def project_kernel(partial, other, same, weight, mixed, columns):
    chip = (lax.axis_index("head") >> 1) ^ 1
    shares = side_by_side(same, other, partial.shape[0], columns)
    total = partial[...] + jnp.dot(
        shares, chip_rows(weight, chip, columns.shape[1]), preferred_element_type=jnp.float32
    )
    mixed[...] = total.astype(mixed.dtype)


VMEM = pl.BlockSpec(memory_space=pltpu.VMEM)
HBM = pl.BlockSpec(memory_space=pltpu.HBM)


def kernel_call(body, name, megabytes, ins, outs, scratch, flops=0):
    shapes = tuple(
        out if isinstance(out, jax.ShapeDtypeStruct) else jax.ShapeDtypeStruct(out, jnp.bfloat16)
        for out in outs
    )
    return pl.pallas_call(
        body,
        out_shape=shapes,
        in_specs=ins,
        out_specs=(VMEM,) * len(outs),
        scratch_shapes=scratch,
        compiler_params=pltpu.CompilerParams(vmem_limit_bytes=megabytes << 20),
        cost_estimate=pl.CostEstimate(flops=flops, bytes_accessed=1 << 20, transcendentals=0),
        name=name,
    )


def shards(queries, keys, values, out_weight):
    tokens, width = queries.shape
    seq_size = lax.axis_size("seq")
    head_size = lax.axis_size("head")
    pair_width = 2 * width
    paired = seq_size == 8
    wide_rows = 2 * LEAF if paired else max(2 * LEAF, seq_size // 2 * HALF)
    wide = pltpu.VMEM((wide_rows, width), jnp.float32)

    def swap(array, bit, axis="seq"):
        return lax.ppermute(array, axis, [(i, i ^ bit) for i in range(lax.axis_size(axis))])

    own_queries, own, inner, outer, quarter = kernel_call(
        functools.partial(pack_kernel, not paired),
        "pack",
        16,
        [HBM] * 3,
        [
            (tokens, width),
            (tokens, pair_width),
            (LEAF + HALF, pair_width),
            (LEAF + HALF, pair_width),
            (HALF, pair_width) if paired else (seq_size, HALF, pair_width),
        ],
        [wide, pltpu.SemaphoreType.DMA((3,))],
    )(*(pltpu.with_memory_space_constraint(array, pltpu.HBM) for array in (queries, keys, values)))
    inner = swap(inner, 1)
    others = [(i, i + 1 if i & 1 else i - 1) for i in range(1, seq_size - 1)]
    outer = lax.ppermute(outer, "seq", others)
    if paired:
        upward, downward, eighth = kernel_call(
            join_kernel,
            "join",
            8,
            [VMEM] * 2,
            [(LEAF, pair_width), (LEAF, pair_width), (HALF, pair_width)],
            [wide],
        )(inner, quarter)
        shift = [(i, (i + 2) % seq_size) for i in range(seq_size)]
        early = (lax.ppermute(upward, "seq", shift), swap(eighth, 4))
        late = lax.ppermute(downward, "seq", [(target, source) for source, target in shift])
    else:
        early = ()
        late = lax.all_to_all(quarter, "seq", split_axis=0, concat_axis=0)
    share = tokens // head_size
    near_scores, near_values, shared = kernel_call(
        functools.partial(near_kernel, seq_size),
        "near",
        16,
        [VMEM] * 4,
        [
            jax.ShapeDtypeStruct((2, 2 * LEAF, NEAR_ROWS), jnp.float32),
            (2, NEAR_ROWS, width),
            (HALF, pair_width),
        ],
        [pltpu.VMEM((NEAR_ROWS, width), jnp.bfloat16), wide],
        flops=8 * LEAF * NEAR_ROWS * width,
    )(own_queries, own, inner, outer)
    mid_rows = 4 * HALF if paired else HALF
    mid_scores, mid_values = kernel_call(
        mid_kernel,
        "mid",
        8,
        [VMEM] * (2 + len(early)),
        [jax.ShapeDtypeStruct((2, 2 * LEAF, mid_rows), jnp.float32), (mid_rows, width)],
        [pltpu.VMEM((mid_rows, width), jnp.bfloat16)],
        flops=10**9,
    )(own_queries, shared, *early)
    scored = (near_scores, near_values, mid_scores, mid_values)
    last_rows = last_row_count(seq_size, paired)
    leaf_flops = 8 * LEAF * (NEAR_ROWS + mid_rows + last_rows) * width
    share_2, share_3, far_keys, far_values, far_bias = kernel_call(
        functools.partial(leaves_kernel, seq_size, paired),
        "leaves",
        24,
        [VMEM] * 6,
        [
            (share + PAD, width),
            (share + PAD, width),
            (last_rows, width),
            (last_rows, width),
            jax.ShapeDtypeStruct((8, last_rows), jnp.float32),
        ],
        [wide],
        flops=leaf_flops,
    )(own_queries, *scored, late)
    share_0, share_1 = kernel_call(
        stays_kernel, "stays", 16, [VMEM] * 8, [(share, width)] * 2, [], flops=leaf_flops
    )(own_queries, *scored, far_keys, far_values, far_bias)
    columns = pltpu.VMEM((share, pair_width), jnp.bfloat16)
    part_3, part_2 = swap(share_3, 3, "head"), swap(share_2, 2, "head")
    (partial,) = kernel_call(
        begin_kernel,
        "begin",
        8,
        [VMEM] * 3,
        [jax.ShapeDtypeStruct((share, out_weight.shape[1]), jnp.float32)],
        [columns],
    )(share_0, swap(share_1, 1, "head"), out_weight)
    (mixed,) = kernel_call(
        project_kernel, "project", 8, [VMEM] * 4, [(share, out_weight.shape[1])], [columns]
    )(partial, part_3, part_2, out_weight)
    return mixed


def solution(mesh):
    in_specs = (P("seq", "head"), P("seq", "head"), P("seq", "head"), P())
    out_specs = P(("seq", "head"), None)
    return jax.shard_map(shards, mesh=mesh, in_specs=in_specs, out_specs=out_specs, check_vma=False)
```

```python
import functools
import math

import jax
import jax.numpy as jnp
from jax import lax
from jax.experimental import pallas as pl
from jax.experimental.pallas import tpu as pltpu
from jax.sharding import PartitionSpec as P

HD = 64
LEAF = 128
HALF = LEAF // 2
NEG = -math.inf


def average_pairs(rows, wide):
    count = rows.shape[0]
    halves = []
    for low in range(0, rows.shape[1], LEAF):
        wide[:count] = rows[:, low : low + LEAF].astype(jnp.float32)
        even = wide[pl.ds(0, count // 2, stride=2), :]
        odd = wide[pl.ds(1, count // 2, stride=2), :]
        halves.append((0.5 * (even + odd)).astype(jnp.bfloat16))
    return jnp.concatenate(halves, axis=1)


def pack_kernel(far_shares, queries, keys, values, own_queries, own, inner, outer, quarter, wide, arrived):
    width = keys.shape[1]
    copies = [
        pltpu.make_async_copy(keys, own.at[:, :width], arrived.at[0]),
        pltpu.make_async_copy(values, own.at[:, width:], arrived.at[1]),
        pltpu.make_async_copy(queries, own_queries, arrived.at[2]),
    ]
    for copy in copies:
        copy.start()
    me = lax.axis_index("seq")
    odd = me & 1
    for copy in copies:
        copy.wait()
    rows = own[...]
    low, high = rows[:LEAF], rows[LEAF:]
    level_one = average_pairs(rows, wide)
    level_two = average_pairs(level_one, wide)
    first, second = level_one[:HALF], level_one[HALF:]
    inner[:LEAF] = jnp.where(odd == 1, low, high)
    inner[LEAF:] = jnp.where(odd == 1, second, first)
    outer[:LEAF] = jnp.where(odd == 1, high, low)
    outer[LEAF:] = jnp.where(odd == 1, first, second)
    if far_shares:
        for peer in range(quarter.shape[0]):
            quarter[peer] = level_two
    else:
        quarter[...] = level_two


def join_kernel(inner, quarter, opening, downward, closing, eighth, wide):
    me = lax.axis_index("seq")
    odd = me & 1
    pair = me >> 1
    edge_half = average_pairs(inner[:LEAF], wide)
    other_half = inner[LEAF:]
    theirs = jnp.concatenate(
        [jnp.where(odd == 1, other_half, edge_half), jnp.where(odd == 1, edge_half, other_half)], axis=0
    )
    theirs = average_pairs(theirs, wide)
    first = jnp.where(odd == 1, theirs, quarter[...])
    second = jnp.where(odd == 1, quarter[...], theirs)
    level_three = average_pairs(jnp.concatenate([first, second], axis=0), wide)
    opening[:HALF] = jnp.where(pair == 0, first, level_three)
    downward[:HALF] = jnp.where(pair == 0, level_three, first)
    closing[:HALF] = jnp.where(pair == 3, level_three, first)
    for sent in (opening, downward, closing):
        sent[HALF:] = second
    eighth[...] = level_three


NEAR_ROWS = 4 * LEAF
PAD = 16


def last_row_count(seq_size, paired):
    if paired:
        return 2 * LEAF
    rows = 0
    for far in range(1, seq_size.bit_length() - 1):
        if seq_size >> far == 2:
            rows += LEAF
        elif far == 1:
            rows += 3 * HALF
        else:
            rows += 2 * LEAF
    return rows


def bias_of(valid):
    return jnp.where(valid, jnp.float32(0.0), jnp.float32(NEG))


def gathered_pieces(seq_size, far_rows, wide):
    me = lax.axis_index("seq")
    pieces = []
    for far in range(1, seq_size.bit_length() - 1):
        span = 1 << far
        group = me >> far
        parity = (me >> (far - 1)) & 1
        blocks = seq_size >> far

        def block(number, span=span, far=far):
            found = far_rows[pl.ds(number * span, span)].reshape(span * HALF, far_rows.shape[2])
            for _ in range(far - 1):
                found = average_pairs(found, wide)
            return found

        if blocks == 2:
            rows = block(1 - group)
            first = bias_of((group == 1) | (parity == 0))
            second = bias_of((group == 0) | (parity == 1))
            pieces += [(rows[:HALF], first), (rows[HALF:], second)]
        elif far == 1:
            third = jnp.where(parity == 0, me + 3, me - 3)
            for peer in (me - 2, me + 2, third):
                ok = (peer >= 0) & (peer < seq_size)
                pieces.append((far_rows[jnp.clip(peer, 0, seq_size - 1)], bias_of(ok)))
        else:
            lower = block(jnp.maximum(group - 1, 0))
            upper = block(jnp.minimum(group + 1, blocks - 1))
            has_lower, has_upper = group >= 1, group + 1 < blocks
            pieces += [
                (lower[:HALF], bias_of(has_lower)),
                (lower[HALF:], bias_of(has_lower & (parity == 1))),
                (upper[:HALF], bias_of(has_upper & (parity == 0))),
                (upper[HALF:], bias_of(has_upper)),
            ]
    return pieces


def early_pieces(opening, eighth):
    pair = lax.axis_index("seq") >> 1
    return [(jnp.where(pair == 2, eighth[...], opening[:HALF]), None)]


def late_pieces(opening, eighth, upper, closing):
    me = lax.axis_index("seq")
    odd = (me & 1) == 1
    pair = me >> 1
    return [
        (jnp.where(pair == 0, eighth[...], closing[:HALF]), None),
        (jnp.where(pair == 1, opening[HALF:], closing[HALF:]), bias_of(odd & (pair >= 1))),
        (upper[:HALF], bias_of(jnp.logical_not(odd) | (pair == 3))),
        (upper[HALF:], bias_of(pair <= 2)),
    ]


def place(pieces, values, keys):
    at = 0
    width = values.shape[1]
    total_rows = values.shape[0]
    position = lax.broadcasted_iota(jnp.int32, (1, total_rows), 1)
    bias = jnp.zeros((1, total_rows), jnp.float32)
    for rows, value in pieces:
        count = rows.shape[0]
        keys[at : at + count] = rows[:, :width]
        values[at : at + count] = rows[:, width:]
        if value is not None:
            bias = jnp.where((position >= at) & (position < at + count), value, bias)
        at += count
    return bias


def split_heads(rows):
    first_head = lax.broadcasted_iota(jnp.int32, (1, rows.shape[1]), 1) < HD
    none = jnp.zeros_like(rows)
    return jnp.concatenate(
        [jnp.where(first_head, rows, none), jnp.where(first_head, none, rows)], axis=0
    )


def scores_of(queries, keys):
    return lax.dot_general(
        queries, keys[...], (((1,), (1,)), ((), ())), preferred_element_type=jnp.float32
    )


def near_kernel(seq_size, queries, own, inner, outer, scores, values, shared, keys, wide):
    me = lax.axis_index("seq")
    odd = me & 1
    from_inner, from_outer = inner[...], outer[...]
    before = jnp.where(odd == 1, from_inner, from_outer)
    after = jnp.where(odd == 1, from_outer, from_inner)
    edge_before, edge_after = before[:LEAF], after[:LEAF]
    far_half_after = after[LEAF:]
    shared[...] = before[LEAF:]
    near_half_before = average_pairs(edge_before, wide)
    near_half_after = average_pairs(edge_after, wide)
    has_before, has_after = bias_of(me >= 1), bias_of(me + 1 < seq_size)
    for leaf in range(2):
        if leaf == 0:
            near = [
                (edge_before, has_before),
                (own[...], None),
                (near_half_after, has_after),
                (far_half_after, has_after),
            ]
        else:
            near = [
                (own[...], None),
                (edge_after, has_after),
                (near_half_before, has_before),
                (far_half_after, has_after),
            ]
        bias = place(near, values.at[leaf], keys)
        rows = split_heads(queries[leaf * LEAF : (leaf + 1) * LEAF])
        scores[leaf] = scores_of(rows, keys) + bias


def mid_kernel(queries, shared, *rest):
    *early, scores, values, keys = rest
    pieces = [(shared, bias_of(lax.axis_index("seq") >= 1))]
    if early:
        pieces += early_pieces(*early)
    bias = place(pieces, values, keys)
    for leaf in range(2):
        rows = split_heads(queries[leaf * LEAF : (leaf + 1) * LEAF])
        scores[leaf] = scores_of(rows, keys) + bias


def attend_leaf(leaf, queries, scored, keys, values, bias, same, other):
    first_head = lax.broadcasted_iota(jnp.int32, (1, values.shape[1]), 1) < HD
    exponent = math.log2(math.e) / math.sqrt(HD)
    rows = split_heads(queries[pl.ds(pl.multiple_of(leaf * LEAF, LEAF), LEAF)])
    near_scores, near_values, mid_scores, mid_values = scored
    parts = [
        (near_scores[leaf], near_values[leaf]),
        (mid_scores[leaf], mid_values[...]),
        (scores_of(rows, keys) + bias, values[...]),
    ]
    peak = functools.reduce(
        jnp.maximum, [jnp.max(scores, axis=1, keepdims=True) for scores, _ in parts]
    )
    total, numer = 0.0, 0.0
    for scores, part_values in parts:
        weights = jnp.exp2((scores - peak) * exponent)
        total = total + jnp.sum(weights, axis=1, keepdims=True)
        numer = numer + jnp.dot(
            weights.astype(jnp.bfloat16), part_values, preferred_element_type=jnp.float32
        )
    mean = numer / total
    attended = jnp.where(first_head, mean[:LEAF], mean[LEAF:]).astype(jnp.bfloat16)
    second = (lax.axis_index("head") & 1) == 1
    same[:HALF] = jnp.where(second, attended[HALF:], attended[:HALF])
    other[:HALF] = jnp.where(second, attended[:HALF], attended[HALF:])


def leaves_kernel(seq_size, paired, queries, near_scores, near_values, mid_scores, mid_values, *rest):
    *late, same, other, keys, values, bias, wide = rest
    pieces = late_pieces(*late) if paired else gathered_pieces(seq_size, late[0], wide)
    bias[...] = jnp.broadcast_to(place(pieces, values, keys), bias.shape)
    leaf = (lax.axis_index("head") >> 1) ^ 1
    scored = (near_scores, near_values, mid_scores, mid_values)
    attend_leaf(leaf, queries, scored, keys, values, bias[:1], same, other)
    for share in (same, other):
        share[HALF:] = jnp.zeros((PAD, share.shape[1]), share.dtype)


def stays_kernel(
    queries, near_scores, near_values, mid_scores, mid_values, keys, values, bias, same, other
):
    leaf = lax.axis_index("head") >> 1
    scored = (near_scores, near_values, mid_scores, mid_values)
    attend_leaf(leaf, queries, scored, keys, values, bias[:1], same, other)


def side_by_side(same, other, rows, columns):
    second = (lax.axis_index("head") & 1) == 1
    width = same.shape[1]
    columns[:, :width] = jnp.where(second, other[:rows], same[:rows])
    columns[:, width:] = jnp.where(second, same[:rows], other[:rows])
    return columns[...]


def chip_rows(weight, chip, count):
    return weight[pl.ds(pl.multiple_of(chip * count, count), count)]


def begin_kernel(same, other, weight, partial, columns):
    chip = lax.axis_index("head") >> 1
    shares = side_by_side(same, other, partial.shape[0], columns)
    partial[...] = jnp.dot(
        shares, chip_rows(weight, chip, columns.shape[1]), preferred_element_type=jnp.float32
    )


def project_kernel(partial, other, same, weight, mixed, columns):
    chip = (lax.axis_index("head") >> 1) ^ 1
    shares = side_by_side(same, other, partial.shape[0], columns)
    total = partial[...] + jnp.dot(
        shares, chip_rows(weight, chip, columns.shape[1]), preferred_element_type=jnp.float32
    )
    mixed[...] = total.astype(mixed.dtype)


VMEM = pl.BlockSpec(memory_space=pltpu.VMEM)
HBM = pl.BlockSpec(memory_space=pltpu.HBM)


def kernel_call(body, name, megabytes, ins, outs, scratch, flops=0):
    shapes = tuple(
        out if isinstance(out, jax.ShapeDtypeStruct) else jax.ShapeDtypeStruct(out, jnp.bfloat16)
        for out in outs
    )
    return pl.pallas_call(
        body,
        out_shape=shapes,
        in_specs=ins,
        out_specs=(VMEM,) * len(outs),
        scratch_shapes=scratch,
        compiler_params=pltpu.CompilerParams(vmem_limit_bytes=megabytes << 20),
        cost_estimate=pl.CostEstimate(flops=flops, bytes_accessed=1 << 20, transcendentals=0),
        name=name,
    )


def shards(queries, keys, values, out_weight):
    tokens, width = queries.shape
    seq_size = lax.axis_size("seq")
    head_size = lax.axis_size("head")
    pair_width = 2 * width
    paired = seq_size == 8
    wide_rows = 2 * LEAF if paired else max(2 * LEAF, seq_size // 2 * HALF)
    wide = pltpu.VMEM((wide_rows, width), jnp.float32)

    def swap(array, bit, axis="seq"):
        return lax.ppermute(array, axis, [(i, i ^ bit) for i in range(lax.axis_size(axis))])

    own_queries, own, inner, outer, quarter = kernel_call(
        functools.partial(pack_kernel, not paired),
        "pack",
        16,
        [HBM] * 3,
        [
            (tokens, width),
            (tokens, pair_width),
            (LEAF + HALF, pair_width),
            (LEAF + HALF, pair_width),
            (HALF, pair_width) if paired else (seq_size, HALF, pair_width),
        ],
        [wide, pltpu.SemaphoreType.DMA((3,))],
    )(*(pltpu.with_memory_space_constraint(array, pltpu.HBM) for array in (queries, keys, values)))
    inner = swap(inner, 1)
    others = [(i, i + 1 if i & 1 else i - 1) for i in range(1, seq_size - 1)]
    outer = lax.ppermute(outer, "seq", others)
    if paired:
        opening, downward, closing, eighth = kernel_call(
            join_kernel,
            "join",
            8,
            [VMEM] * 2,
            [(LEAF, pair_width)] * 3 + [(HALF, pair_width)],
            [wide],
        )(inner, quarter)

        def over_pairs(array, targets):
            spans = [(2 * p + x, 2 * t + x) for p, t in enumerate(targets) for x in range(2)]
            return lax.ppermute(array, "seq", spans)

        early = (over_pairs(opening, (1, 3, 2, 0)), over_pairs(eighth, (2, 1, 0, 3)))
        late = early + (over_pairs(downward, (3, 0, 1, 2)), over_pairs(closing, (0, 2, 3, 1)))
    else:
        early = ()
        late = (lax.all_to_all(quarter, "seq", split_axis=0, concat_axis=0),)
    share = tokens // head_size
    near_scores, near_values, shared = kernel_call(
        functools.partial(near_kernel, seq_size),
        "near",
        16,
        [VMEM] * 4,
        [
            jax.ShapeDtypeStruct((2, 2 * LEAF, NEAR_ROWS), jnp.float32),
            (2, NEAR_ROWS, width),
            (HALF, pair_width),
        ],
        [pltpu.VMEM((NEAR_ROWS, width), jnp.bfloat16), wide],
        flops=8 * LEAF * NEAR_ROWS * width,
    )(own_queries, own, inner, outer)
    mid_rows = LEAF if paired else HALF
    mid_scores, mid_values = kernel_call(
        mid_kernel,
        "mid",
        8,
        [VMEM] * (2 + len(early)),
        [jax.ShapeDtypeStruct((2, 2 * LEAF, mid_rows), jnp.float32), (mid_rows, width)],
        [pltpu.VMEM((mid_rows, width), jnp.bfloat16)],
        flops=10**9,
    )(own_queries, shared, *early)
    scored = (near_scores, near_values, mid_scores, mid_values)
    last_rows = last_row_count(seq_size, paired)
    leaf_flops = 8 * LEAF * (NEAR_ROWS + mid_rows + last_rows) * width
    share_2, share_3, far_keys, far_values, far_bias = kernel_call(
        functools.partial(leaves_kernel, seq_size, paired),
        "leaves",
        24,
        [VMEM] * (5 + len(late)),
        [
            (share + PAD, width),
            (share + PAD, width),
            (last_rows, width),
            (last_rows, width),
            jax.ShapeDtypeStruct((8, last_rows), jnp.float32),
        ],
        [wide],
        flops=leaf_flops,
    )(own_queries, *scored, *late)
    share_0, share_1 = kernel_call(
        stays_kernel, "stays", 16, [VMEM] * 8, [(share, width)] * 2, [], flops=leaf_flops
    )(own_queries, *scored, far_keys, far_values, far_bias)
    columns = pltpu.VMEM((share, pair_width), jnp.bfloat16)
    part_3, part_2 = swap(share_3, 3, "head"), swap(share_2, 2, "head")
    (partial,) = kernel_call(
        begin_kernel,
        "begin",
        8,
        [VMEM] * 3,
        [jax.ShapeDtypeStruct((share, out_weight.shape[1]), jnp.float32)],
        [columns],
    )(share_0, swap(share_1, 1, "head"), out_weight)
    (mixed,) = kernel_call(
        project_kernel, "project", 8, [VMEM] * 4, [(share, out_weight.shape[1])], [columns]
    )(partial, part_3, part_2, out_weight)
    return mixed


def solution(mesh):
    in_specs = (P("seq", "head"), P("seq", "head"), P("seq", "head"), P())
    out_specs = P(("seq", "head"), None)
    return jax.shard_map(shards, mesh=mesh, in_specs=in_specs, out_specs=out_specs, check_vma=False)
```

```python
import functools
import math

import jax
import jax.numpy as jnp
from jax import lax
from jax.experimental import pallas as pl
from jax.experimental.pallas import tpu as pltpu
from jax.sharding import PartitionSpec as P

HD = 64
LEAF = 128
HALF = LEAF // 2
NEG = -math.inf


def average_pairs(rows, wide):
    count = rows.shape[0]
    halves = []
    for low in range(0, rows.shape[1], LEAF):
        wide[:count] = rows[:, low : low + LEAF].astype(jnp.float32)
        even = wide[pl.ds(0, count // 2, stride=2), :]
        odd = wide[pl.ds(1, count // 2, stride=2), :]
        halves.append((0.5 * (even + odd)).astype(jnp.bfloat16))
    return jnp.concatenate(halves, axis=1)


def pack_kernel(far_shares, queries, keys, values, own_queries, own, inner, outer, quarter, wide, arrived):
    width = keys.shape[1]
    copies = [
        pltpu.make_async_copy(keys, own.at[:, :width], arrived.at[0]),
        pltpu.make_async_copy(values, own.at[:, width:], arrived.at[1]),
        pltpu.make_async_copy(queries, own_queries, arrived.at[2]),
    ]
    for copy in copies:
        copy.start()
    me = lax.axis_index("seq")
    odd = me & 1
    for copy in copies:
        copy.wait()
    rows = own[...]
    low, high = rows[:LEAF], rows[LEAF:]
    level_one = average_pairs(rows, wide)
    level_two = average_pairs(level_one, wide)
    first, second = level_one[:HALF], level_one[HALF:]
    inner[:LEAF] = jnp.where(odd == 1, low, high)
    inner[LEAF:] = jnp.where(odd == 1, second, first)
    outer[:LEAF] = jnp.where(odd == 1, high, low)
    outer[LEAF:] = jnp.where(odd == 1, first, second)
    if far_shares:
        for peer in range(quarter.shape[0]):
            quarter[peer] = level_two
    else:
        quarter[...] = level_two


def join_kernel(inner, quarter, opening, downward, closing, eighth, wide):
    me = lax.axis_index("seq")
    odd = me & 1
    pair = me >> 1
    edge_half = average_pairs(inner[:LEAF], wide)
    other_half = inner[LEAF:]
    theirs = jnp.concatenate(
        [jnp.where(odd == 1, other_half, edge_half), jnp.where(odd == 1, edge_half, other_half)], axis=0
    )
    theirs = average_pairs(theirs, wide)
    first = jnp.where(odd == 1, theirs, quarter[...])
    second = jnp.where(odd == 1, quarter[...], theirs)
    level_three = average_pairs(jnp.concatenate([first, second], axis=0), wide)
    opening[:HALF] = jnp.where(pair == 0, first, level_three)
    downward[:HALF] = jnp.where(pair == 0, level_three, first)
    closing[:HALF] = jnp.where(pair == 3, level_three, first)
    for sent in (opening, downward, closing):
        sent[HALF:] = second
    eighth[...] = level_three


NEAR_ROWS = 4 * LEAF
PAD = 16


def last_row_count(seq_size, paired):
    if paired:
        return 2 * LEAF
    rows = 0
    for far in range(1, seq_size.bit_length() - 1):
        if seq_size >> far == 2:
            rows += LEAF
        elif far == 1:
            rows += 3 * HALF
        else:
            rows += 2 * LEAF
    return rows


def bias_of(valid):
    return jnp.where(valid, jnp.float32(0.0), jnp.float32(NEG))


def gathered_pieces(seq_size, far_rows, wide):
    me = lax.axis_index("seq")
    pieces = []
    for far in range(1, seq_size.bit_length() - 1):
        span = 1 << far
        group = me >> far
        parity = (me >> (far - 1)) & 1
        blocks = seq_size >> far

        def block(number, span=span, far=far):
            found = far_rows[pl.ds(number * span, span)].reshape(span * HALF, far_rows.shape[2])
            for _ in range(far - 1):
                found = average_pairs(found, wide)
            return found

        if blocks == 2:
            rows = block(1 - group)
            first = bias_of((group == 1) | (parity == 0))
            second = bias_of((group == 0) | (parity == 1))
            pieces += [(rows[:HALF], first), (rows[HALF:], second)]
        elif far == 1:
            third = jnp.where(parity == 0, me + 3, me - 3)
            for peer in (me - 2, me + 2, third):
                ok = (peer >= 0) & (peer < seq_size)
                pieces.append((far_rows[jnp.clip(peer, 0, seq_size - 1)], bias_of(ok)))
        else:
            lower = block(jnp.maximum(group - 1, 0))
            upper = block(jnp.minimum(group + 1, blocks - 1))
            has_lower, has_upper = group >= 1, group + 1 < blocks
            pieces += [
                (lower[:HALF], bias_of(has_lower)),
                (lower[HALF:], bias_of(has_lower & (parity == 1))),
                (upper[:HALF], bias_of(has_upper & (parity == 0))),
                (upper[HALF:], bias_of(has_upper)),
            ]
    return pieces


def early_pieces(opening, eighth):
    pair = lax.axis_index("seq") >> 1
    return [(jnp.where(pair == 2, eighth[...], opening[:HALF]), None)]


def late_pieces(opening, eighth, upper, closing):
    me = lax.axis_index("seq")
    odd = (me & 1) == 1
    pair = me >> 1
    return [
        (jnp.where(pair == 0, eighth[...], closing[:HALF]), None),
        (jnp.where(pair == 1, opening[HALF:], closing[HALF:]), bias_of(odd & (pair >= 1))),
        (upper[:HALF], bias_of(jnp.logical_not(odd) | (pair == 3))),
        (upper[HALF:], bias_of(pair <= 2)),
    ]


def place(pieces, values, keys):
    at = 0
    width = values.shape[1]
    total_rows = values.shape[0]
    position = lax.broadcasted_iota(jnp.int32, (1, total_rows), 1)
    bias = jnp.zeros((1, total_rows), jnp.float32)
    for rows, value in pieces:
        count = rows.shape[0]
        keys[at : at + count] = rows[:, :width]
        values[at : at + count] = rows[:, width:]
        if value is not None:
            bias = jnp.where((position >= at) & (position < at + count), value, bias)
        at += count
    return bias


def split_heads(rows):
    first_head = lax.broadcasted_iota(jnp.int32, (1, rows.shape[1]), 1) < HD
    none = jnp.zeros_like(rows)
    return jnp.concatenate(
        [jnp.where(first_head, rows, none), jnp.where(first_head, none, rows)], axis=0
    )


def scores_of(queries, keys):
    return lax.dot_general(
        queries, keys[...], (((1,), (1,)), ((), ())), preferred_element_type=jnp.float32
    )


def near_kernel(seq_size, queries, own, inner, outer, scores, values, shared, keys, wide):
    me = lax.axis_index("seq")
    odd = me & 1
    from_inner, from_outer = inner[...], outer[...]
    before = jnp.where(odd == 1, from_inner, from_outer)
    after = jnp.where(odd == 1, from_outer, from_inner)
    edge_before, edge_after = before[:LEAF], after[:LEAF]
    far_half_after = after[LEAF:]
    shared[...] = before[LEAF:]
    near_half_before = average_pairs(edge_before, wide)
    near_half_after = average_pairs(edge_after, wide)
    has_before, has_after = bias_of(me >= 1), bias_of(me + 1 < seq_size)
    for leaf in range(2):
        if leaf == 0:
            near = [
                (edge_before, has_before),
                (own[...], None),
                (near_half_after, has_after),
                (far_half_after, has_after),
            ]
        else:
            near = [
                (own[...], None),
                (edge_after, has_after),
                (near_half_before, has_before),
                (far_half_after, has_after),
            ]
        bias = place(near, values.at[leaf], keys)
        rows = split_heads(queries[leaf * LEAF : (leaf + 1) * LEAF])
        scores[leaf] = scores_of(rows, keys) + bias


def mid_kernel(queries, shared, *rest):
    *early, scores, values, keys = rest
    pieces = [(shared, bias_of(lax.axis_index("seq") >= 1))]
    if early:
        pieces += early_pieces(*early)
    bias = place(pieces, values, keys)
    for leaf in range(2):
        rows = split_heads(queries[leaf * LEAF : (leaf + 1) * LEAF])
        scores[leaf] = scores_of(rows, keys) + bias


def attend_leaf(leaf, queries, scored, keys, values, bias, same, other):
    first_head = lax.broadcasted_iota(jnp.int32, (1, values.shape[1]), 1) < HD
    exponent = math.log2(math.e) / math.sqrt(HD)
    rows = split_heads(queries[pl.ds(pl.multiple_of(leaf * LEAF, LEAF), LEAF)])
    near_scores, near_values, mid_scores, mid_values = scored
    parts = [
        (near_scores[leaf], near_values[leaf]),
        (mid_scores[leaf], mid_values[...]),
        (scores_of(rows, keys) + bias, values[...]),
    ]
    peak = functools.reduce(
        jnp.maximum, [jnp.max(scores, axis=1, keepdims=True) for scores, _ in parts]
    )
    total, numer = 0.0, 0.0
    for scores, part_values in parts:
        weights = jnp.exp2((scores - peak) * exponent)
        total = total + jnp.sum(weights, axis=1, keepdims=True)
        numer = numer + jnp.dot(
            weights.astype(jnp.bfloat16), part_values, preferred_element_type=jnp.float32
        )
    mean = numer / total
    attended = jnp.where(first_head, mean[:LEAF], mean[LEAF:]).astype(jnp.bfloat16)
    second = (lax.axis_index("head") & 1) == 1
    same[:HALF] = jnp.where(second, attended[HALF:], attended[:HALF])
    other[:HALF] = jnp.where(second, attended[:HALF], attended[HALF:])


def leaves_kernel(seq_size, paired, queries, near_scores, near_values, mid_scores, mid_values, *rest):
    *late, same, other, keys, values, bias, wide = rest
    pieces = late_pieces(*late) if paired else gathered_pieces(seq_size, late[0], wide)
    bias[...] = jnp.broadcast_to(place(pieces, values, keys), bias.shape)
    leaf = (lax.axis_index("head") >> 1) ^ 1
    scored = (near_scores, near_values, mid_scores, mid_values)
    attend_leaf(leaf, queries, scored, keys, values, bias[:1], same, other)
    for share in (same, other):
        share[HALF:] = jnp.zeros((PAD, share.shape[1]), share.dtype)


def stays_kernel(
    queries, near_scores, near_values, mid_scores, mid_values, keys, values, bias, same, other
):
    leaf = lax.axis_index("head") >> 1
    scored = (near_scores, near_values, mid_scores, mid_values)
    attend_leaf(leaf, queries, scored, keys, values, bias[:1], same, other)


def side_by_side(same, other, rows, columns):
    second = (lax.axis_index("head") & 1) == 1
    width = same.shape[1]
    columns[:, :width] = jnp.where(second, other[:rows], same[:rows])
    columns[:, width:] = jnp.where(second, same[:rows], other[:rows])
    return columns[...]


def chip_rows(weight, chip, count):
    return weight[pl.ds(pl.multiple_of(chip * count, count), count)]


def begin_kernel(same, other, weight, partial, columns):
    chip = lax.axis_index("head") >> 1
    shares = side_by_side(same, other, partial.shape[0], columns)
    partial[...] = jnp.dot(
        shares, chip_rows(weight, chip, columns.shape[1]), preferred_element_type=jnp.float32
    )


def project_kernel(partial, other, same, weight, mixed, columns):
    chip = (lax.axis_index("head") >> 1) ^ 1
    shares = side_by_side(same, other, partial.shape[0], columns)
    total = partial[...] + jnp.dot(
        shares, chip_rows(weight, chip, columns.shape[1]), preferred_element_type=jnp.float32
    )
    mixed[...] = total.astype(mixed.dtype)


VMEM = pl.BlockSpec(memory_space=pltpu.VMEM)
HBM = pl.BlockSpec(memory_space=pltpu.HBM)


def kernel_call(body, name, megabytes, ins, outs, scratch, flops=0):
    shapes = tuple(
        out if isinstance(out, jax.ShapeDtypeStruct) else jax.ShapeDtypeStruct(out, jnp.bfloat16)
        for out in outs
    )
    return pl.pallas_call(
        body,
        out_shape=shapes,
        in_specs=ins,
        out_specs=(VMEM,) * len(outs),
        scratch_shapes=scratch,
        compiler_params=pltpu.CompilerParams(vmem_limit_bytes=megabytes << 20),
        cost_estimate=pl.CostEstimate(flops=flops, bytes_accessed=1 << 20, transcendentals=0),
        name=name,
    )


def shards(queries, keys, values, out_weight):
    tokens, width = queries.shape
    seq_size = lax.axis_size("seq")
    head_size = lax.axis_size("head")
    pair_width = 2 * width
    paired = seq_size == 8
    wide_rows = 2 * LEAF if paired else max(2 * LEAF, seq_size // 2 * HALF)
    wide = pltpu.VMEM((wide_rows, width), jnp.float32)

    def swap(array, bit, axis="seq"):
        return lax.ppermute(array, axis, [(i, i ^ bit) for i in range(lax.axis_size(axis))])

    own_queries, own, inner, outer, quarter = kernel_call(
        functools.partial(pack_kernel, not paired),
        "pack",
        16,
        [HBM] * 3,
        [
            (tokens, width),
            (tokens, pair_width),
            (LEAF + HALF, pair_width),
            (LEAF + HALF, pair_width),
            (HALF, pair_width) if paired else (seq_size, HALF, pair_width),
        ],
        [wide, pltpu.SemaphoreType.DMA((3,))],
    )(*(pltpu.with_memory_space_constraint(array, pltpu.HBM) for array in (queries, keys, values)))
    inner = swap(inner, 1)

    def to_spans(array, targets):
        return lax.ppermute(
            array,
            ("seq", "head"),
            [
                (s * head_size + h, t * head_size + (h if s != t else h ^ 1))
                for s, t in enumerate(targets)
                for h in range(head_size)
            ],
        )

    last = seq_size - 1
    outer = to_spans(outer, [s if s in (0, last) else s + 1 if s & 1 else s - 1 for s in range(seq_size)])
    if paired:
        opening, downward, closing, eighth = kernel_call(
            join_kernel,
            "join",
            8,
            [VMEM] * 2,
            [(LEAF, pair_width)] * 3 + [(HALF, pair_width)],
            [wide],
        )(inner, quarter)

        def over_pairs(array, targets):
            return to_spans(array, [2 * t + x for t in targets for x in range(2)])

        early = (over_pairs(opening, (1, 3, 2, 0)), over_pairs(eighth, (2, 1, 0, 3)))
        late = early + (over_pairs(downward, (3, 0, 1, 2)), over_pairs(closing, (0, 2, 3, 1)))
    else:
        early = ()
        late = (lax.all_to_all(quarter, "seq", split_axis=0, concat_axis=0),)
    share = tokens // head_size
    near_scores, near_values, shared = kernel_call(
        functools.partial(near_kernel, seq_size),
        "near",
        16,
        [VMEM] * 4,
        [
            jax.ShapeDtypeStruct((2, 2 * LEAF, NEAR_ROWS), jnp.float32),
            (2, NEAR_ROWS, width),
            (HALF, pair_width),
        ],
        [pltpu.VMEM((NEAR_ROWS, width), jnp.bfloat16), wide],
        flops=8 * LEAF * NEAR_ROWS * width,
    )(own_queries, own, inner, outer)
    mid_rows = LEAF if paired else HALF
    mid_scores, mid_values = kernel_call(
        mid_kernel,
        "mid",
        8,
        [VMEM] * (2 + len(early)),
        [jax.ShapeDtypeStruct((2, 2 * LEAF, mid_rows), jnp.float32), (mid_rows, width)],
        [pltpu.VMEM((mid_rows, width), jnp.bfloat16)],
        flops=10**9,
    )(own_queries, shared, *early)
    scored = (near_scores, near_values, mid_scores, mid_values)
    last_rows = last_row_count(seq_size, paired)
    leaf_flops = 8 * LEAF * (NEAR_ROWS + mid_rows + last_rows) * width
    share_2, share_3, far_keys, far_values, far_bias = kernel_call(
        functools.partial(leaves_kernel, seq_size, paired),
        "leaves",
        24,
        [VMEM] * (5 + len(late)),
        [
            (share + PAD, width),
            (share + PAD, width),
            (last_rows, width),
            (last_rows, width),
            jax.ShapeDtypeStruct((8, last_rows), jnp.float32),
        ],
        [wide],
        flops=leaf_flops,
    )(own_queries, *scored, *late)
    share_0, share_1 = kernel_call(
        stays_kernel, "stays", 16, [VMEM] * 8, [(share, width)] * 2, [], flops=leaf_flops
    )(own_queries, *scored, far_keys, far_values, far_bias)
    columns = pltpu.VMEM((share, pair_width), jnp.bfloat16)
    part_3, part_2 = swap(share_3, 3, "head"), swap(share_2, 2, "head")
    (partial,) = kernel_call(
        begin_kernel,
        "begin",
        8,
        [VMEM] * 3,
        [jax.ShapeDtypeStruct((share, out_weight.shape[1]), jnp.float32)],
        [columns],
    )(share_0, swap(share_1, 1, "head"), out_weight)
    (mixed,) = kernel_call(
        project_kernel, "project", 8, [VMEM] * 4, [(share, out_weight.shape[1])], [columns]
    )(partial, part_3, part_2, out_weight)
    return mixed


def solution(mesh):
    in_specs = (P("seq", "head"), P("seq", "head"), P("seq", "head"), P())
    out_specs = P(("seq", "head"), None)
    return jax.shard_map(shards, mesh=mesh, in_specs=in_specs, out_specs=out_specs, check_vma=False)
```

```python
import functools
import math

import jax
import jax.numpy as jnp
from jax import lax
from jax.experimental import pallas as pl
from jax.experimental.pallas import tpu as pltpu
from jax.sharding import PartitionSpec as P

HD = 64
LEAF = 128
HALF = LEAF // 2
NEG = -math.inf


def average_pairs(rows, wide):
    count = rows.shape[0]
    halves = []
    for low in range(0, rows.shape[1], LEAF):
        wide[:count] = rows[:, low : low + LEAF].astype(jnp.float32)
        even = wide[pl.ds(0, count // 2, stride=2), :]
        odd = wide[pl.ds(1, count // 2, stride=2), :]
        halves.append((0.5 * (even + odd)).astype(jnp.bfloat16))
    return jnp.concatenate(halves, axis=1)


def pack_kernel(far_shares, queries, keys, values, own_queries, own, inner, outer, quarter, wide, arrived):
    width = keys.shape[1]
    copies = [
        pltpu.make_async_copy(keys, own.at[:, :width], arrived.at[0]),
        pltpu.make_async_copy(values, own.at[:, width:], arrived.at[1]),
        pltpu.make_async_copy(queries, own_queries, arrived.at[2]),
    ]
    for copy in copies:
        copy.start()
    me = lax.axis_index("seq")
    odd = me & 1
    for copy in copies:
        copy.wait()
    rows = own[...]
    low, high = rows[:LEAF], rows[LEAF:]
    level_one = average_pairs(rows, wide)
    level_two = average_pairs(level_one, wide)
    first, second = level_one[:HALF], level_one[HALF:]
    inner[:LEAF] = jnp.where(odd == 1, low, high)
    inner[LEAF:] = jnp.where(odd == 1, second, first)
    outer[:LEAF] = jnp.where(odd == 1, high, low)
    outer[LEAF:] = jnp.where(odd == 1, first, second)
    if far_shares:
        for peer in range(quarter.shape[0]):
            quarter[peer] = level_two
    else:
        quarter[...] = level_two


def join_kernel(theirs, quarter, opening, downward, closing, eighth, wide):
    me = lax.axis_index("seq")
    odd = me & 1
    pair = me >> 1
    first = jnp.where(odd == 1, theirs[...], quarter[...])
    second = jnp.where(odd == 1, quarter[...], theirs[...])
    level_three = average_pairs(jnp.concatenate([first, second], axis=0), wide)
    opening[:HALF] = jnp.where(pair == 0, first, level_three)
    downward[:HALF] = jnp.where(pair == 0, level_three, first)
    closing[:HALF] = jnp.where(pair == 3, level_three, first)
    for sent in (opening, downward, closing):
        sent[HALF:] = second
    eighth[...] = level_three


NEAR_ROWS = 4 * LEAF
PAD = 16


def last_row_count(seq_size, paired):
    if paired:
        return 2 * LEAF
    rows = 0
    for far in range(1, seq_size.bit_length() - 1):
        if seq_size >> far == 2:
            rows += LEAF
        elif far == 1:
            rows += 3 * HALF
        else:
            rows += 2 * LEAF
    return rows


def bias_of(valid):
    return jnp.where(valid, jnp.float32(0.0), jnp.float32(NEG))


def gathered_pieces(seq_size, far_rows, wide):
    me = lax.axis_index("seq")
    pieces = []
    for far in range(1, seq_size.bit_length() - 1):
        span = 1 << far
        group = me >> far
        parity = (me >> (far - 1)) & 1
        blocks = seq_size >> far

        def block(number, span=span, far=far):
            found = far_rows[pl.ds(number * span, span)].reshape(span * HALF, far_rows.shape[2])
            for _ in range(far - 1):
                found = average_pairs(found, wide)
            return found

        if blocks == 2:
            rows = block(1 - group)
            first = bias_of((group == 1) | (parity == 0))
            second = bias_of((group == 0) | (parity == 1))
            pieces += [(rows[:HALF], first), (rows[HALF:], second)]
        elif far == 1:
            third = jnp.where(parity == 0, me + 3, me - 3)
            for peer in (me - 2, me + 2, third):
                ok = (peer >= 0) & (peer < seq_size)
                pieces.append((far_rows[jnp.clip(peer, 0, seq_size - 1)], bias_of(ok)))
        else:
            lower = block(jnp.maximum(group - 1, 0))
            upper = block(jnp.minimum(group + 1, blocks - 1))
            has_lower, has_upper = group >= 1, group + 1 < blocks
            pieces += [
                (lower[:HALF], bias_of(has_lower)),
                (lower[HALF:], bias_of(has_lower & (parity == 1))),
                (upper[:HALF], bias_of(has_upper & (parity == 0))),
                (upper[HALF:], bias_of(has_upper)),
            ]
    return pieces


def early_pieces(opening, eighth):
    pair = lax.axis_index("seq") >> 1
    return [(jnp.where(pair == 2, eighth[...], opening[:HALF]), None)]


def late_pieces(opening, eighth, upper, closing):
    me = lax.axis_index("seq")
    odd = (me & 1) == 1
    pair = me >> 1
    return [
        (jnp.where(pair == 0, eighth[...], closing[:HALF]), None),
        (jnp.where(pair == 1, opening[HALF:], closing[HALF:]), bias_of(odd & (pair >= 1))),
        (upper[:HALF], bias_of(jnp.logical_not(odd) | (pair == 3))),
        (upper[HALF:], bias_of(pair <= 2)),
    ]


def place(pieces, values, keys):
    at = 0
    width = values.shape[1]
    total_rows = values.shape[0]
    position = lax.broadcasted_iota(jnp.int32, (1, total_rows), 1)
    bias = jnp.zeros((1, total_rows), jnp.float32)
    for rows, value in pieces:
        count = rows.shape[0]
        keys[at : at + count] = rows[:, :width]
        values[at : at + count] = rows[:, width:]
        if value is not None:
            bias = jnp.where((position >= at) & (position < at + count), value, bias)
        at += count
    return bias


def split_heads(rows):
    first_head = lax.broadcasted_iota(jnp.int32, (1, rows.shape[1]), 1) < HD
    none = jnp.zeros_like(rows)
    return jnp.concatenate(
        [jnp.where(first_head, rows, none), jnp.where(first_head, none, rows)], axis=0
    )


def scores_of(queries, keys):
    return lax.dot_general(
        queries, keys[...], (((1,), (1,)), ((), ())), preferred_element_type=jnp.float32
    )


def near_kernel(seq_size, queries, own, inner, outer, scores, values, shared, keys, wide):
    me = lax.axis_index("seq")
    odd = me & 1
    from_inner, from_outer = inner[...], outer[...]
    before = jnp.where(odd == 1, from_inner, from_outer)
    after = jnp.where(odd == 1, from_outer, from_inner)
    edge_before, edge_after = before[:LEAF], after[:LEAF]
    far_half_after = after[LEAF:]
    shared[...] = before[LEAF:]
    near_half_before = average_pairs(edge_before, wide)
    near_half_after = average_pairs(edge_after, wide)
    has_before, has_after = bias_of(me >= 1), bias_of(me + 1 < seq_size)
    for leaf in range(2):
        if leaf == 0:
            near = [
                (edge_before, has_before),
                (own[...], None),
                (near_half_after, has_after),
                (far_half_after, has_after),
            ]
        else:
            near = [
                (own[...], None),
                (edge_after, has_after),
                (near_half_before, has_before),
                (far_half_after, has_after),
            ]
        bias = place(near, values.at[leaf], keys)
        rows = split_heads(queries[leaf * LEAF : (leaf + 1) * LEAF])
        scores[leaf] = scores_of(rows, keys) + bias


def mid_kernel(queries, shared, *rest):
    *early, scores, values, keys = rest
    pieces = [(shared, bias_of(lax.axis_index("seq") >= 1))]
    if early:
        pieces += early_pieces(*early)
    bias = place(pieces, values, keys)
    for leaf in range(2):
        rows = split_heads(queries[leaf * LEAF : (leaf + 1) * LEAF])
        scores[leaf] = scores_of(rows, keys) + bias


def attend_leaf(leaf, queries, scored, keys, values, bias, same, other):
    first_head = lax.broadcasted_iota(jnp.int32, (1, values.shape[1]), 1) < HD
    exponent = math.log2(math.e) / math.sqrt(HD)
    rows = split_heads(queries[pl.ds(pl.multiple_of(leaf * LEAF, LEAF), LEAF)])
    near_scores, near_values, mid_scores, mid_values = scored
    parts = [
        (near_scores[leaf], near_values[leaf]),
        (mid_scores[leaf], mid_values[...]),
        (scores_of(rows, keys) + bias, values[...]),
    ]
    peak = functools.reduce(
        jnp.maximum, [jnp.max(scores, axis=1, keepdims=True) for scores, _ in parts]
    )
    total, numer = 0.0, 0.0
    for scores, part_values in parts:
        weights = jnp.exp2((scores - peak) * exponent)
        total = total + jnp.sum(weights, axis=1, keepdims=True)
        numer = numer + jnp.dot(
            weights.astype(jnp.bfloat16), part_values, preferred_element_type=jnp.float32
        )
    mean = numer / total
    attended = jnp.where(first_head, mean[:LEAF], mean[LEAF:]).astype(jnp.bfloat16)
    second = (lax.axis_index("head") & 1) == 1
    same[:HALF] = jnp.where(second, attended[HALF:], attended[:HALF])
    other[:HALF] = jnp.where(second, attended[:HALF], attended[HALF:])


def leaves_kernel(seq_size, paired, queries, near_scores, near_values, mid_scores, mid_values, *rest):
    *late, same, other, keys, values, bias, wide = rest
    pieces = late_pieces(*late) if paired else gathered_pieces(seq_size, late[0], wide)
    bias[...] = jnp.broadcast_to(place(pieces, values, keys), bias.shape)
    leaf = (lax.axis_index("head") >> 1) ^ 1
    scored = (near_scores, near_values, mid_scores, mid_values)
    attend_leaf(leaf, queries, scored, keys, values, bias[:1], same, other)
    for share in (same, other):
        share[HALF:] = jnp.zeros((PAD, share.shape[1]), share.dtype)


def stays_kernel(
    queries, near_scores, near_values, mid_scores, mid_values, keys, values, bias, same, other
):
    leaf = lax.axis_index("head") >> 1
    scored = (near_scores, near_values, mid_scores, mid_values)
    attend_leaf(leaf, queries, scored, keys, values, bias[:1], same, other)


def side_by_side(same, other, rows, columns):
    second = (lax.axis_index("head") & 1) == 1
    width = same.shape[1]
    columns[:, :width] = jnp.where(second, other[:rows], same[:rows])
    columns[:, width:] = jnp.where(second, same[:rows], other[:rows])
    return columns[...]


def chip_rows(weight, chip, count):
    return weight[pl.ds(pl.multiple_of(chip * count, count), count)]


def begin_kernel(same, other, weight, partial, columns):
    chip = lax.axis_index("head") >> 1
    shares = side_by_side(same, other, partial.shape[0], columns)
    partial[...] = jnp.dot(
        shares, chip_rows(weight, chip, columns.shape[1]), preferred_element_type=jnp.float32
    )


def project_kernel(partial, other, same, weight, mixed, columns):
    chip = (lax.axis_index("head") >> 1) ^ 1
    shares = side_by_side(same, other, partial.shape[0], columns)
    total = partial[...] + jnp.dot(
        shares, chip_rows(weight, chip, columns.shape[1]), preferred_element_type=jnp.float32
    )
    mixed[...] = total.astype(mixed.dtype)


VMEM = pl.BlockSpec(memory_space=pltpu.VMEM)
HBM = pl.BlockSpec(memory_space=pltpu.HBM)


def kernel_call(body, name, megabytes, ins, outs, scratch, flops=0):
    shapes = tuple(
        out if isinstance(out, jax.ShapeDtypeStruct) else jax.ShapeDtypeStruct(out, jnp.bfloat16)
        for out in outs
    )
    return pl.pallas_call(
        body,
        out_shape=shapes,
        in_specs=ins,
        out_specs=(VMEM,) * len(outs),
        scratch_shapes=scratch,
        compiler_params=pltpu.CompilerParams(vmem_limit_bytes=megabytes << 20),
        cost_estimate=pl.CostEstimate(flops=flops, bytes_accessed=1 << 20, transcendentals=0),
        name=name,
    )


def shards(queries, keys, values, out_weight):
    tokens, width = queries.shape
    seq_size = lax.axis_size("seq")
    head_size = lax.axis_size("head")
    pair_width = 2 * width
    paired = seq_size == 8
    wide_rows = 2 * LEAF if paired else max(2 * LEAF, seq_size // 2 * HALF)
    wide = pltpu.VMEM((wide_rows, width), jnp.float32)

    def swap(array, bit, axis="seq"):
        return lax.ppermute(array, axis, [(i, i ^ bit) for i in range(lax.axis_size(axis))])

    own_queries, own, inner, outer, quarter = kernel_call(
        functools.partial(pack_kernel, not paired),
        "pack",
        16,
        [HBM] * 3,
        [
            (tokens, width),
            (tokens, pair_width),
            (LEAF + HALF, pair_width),
            (LEAF + HALF, pair_width),
            (HALF, pair_width) if paired else (seq_size, HALF, pair_width),
        ],
        [wide, pltpu.SemaphoreType.DMA((3,))],
    )(*(pltpu.with_memory_space_constraint(array, pltpu.HBM) for array in (queries, keys, values)))
    inner = swap(inner, 1)

    def to_spans(array, targets):
        return lax.ppermute(
            array,
            ("seq", "head"),
            [
                (s * head_size + h, t * head_size + (h if s != t else h ^ 1))
                for s, t in enumerate(targets)
                for h in range(head_size)
            ],
        )

    last = seq_size - 1
    outer = to_spans(outer, [s if s in (0, last) else s + 1 if s & 1 else s - 1 for s in range(seq_size)])
    if paired:
        opening, downward, closing, eighth = kernel_call(
            join_kernel,
            "join",
            8,
            [VMEM] * 2,
            [(LEAF, pair_width)] * 3 + [(HALF, pair_width)],
            [wide],
            flops=3 * 10**8,
        )(swap(quarter, 1), quarter)

        def over_pairs(array, targets):
            return to_spans(array, [2 * t + x for t in targets for x in range(2)])

        early = (over_pairs(opening, (1, 3, 2, 0)), over_pairs(eighth, (2, 1, 0, 3)))
        late = early + (over_pairs(downward, (3, 0, 1, 2)), over_pairs(closing, (0, 2, 3, 1)))
    else:
        early = ()
        late = (lax.all_to_all(quarter, "seq", split_axis=0, concat_axis=0),)
    share = tokens // head_size
    near_scores, near_values, shared = kernel_call(
        functools.partial(near_kernel, seq_size),
        "near",
        16,
        [VMEM] * 4,
        [
            jax.ShapeDtypeStruct((2, 2 * LEAF, NEAR_ROWS), jnp.float32),
            (2, NEAR_ROWS, width),
            (HALF, pair_width),
        ],
        [pltpu.VMEM((NEAR_ROWS, width), jnp.bfloat16), wide],
        flops=8 * LEAF * NEAR_ROWS * width,
    )(own_queries, own, inner, outer)
    mid_rows = LEAF if paired else HALF
    mid_scores, mid_values = kernel_call(
        mid_kernel,
        "mid",
        8,
        [VMEM] * (2 + len(early)),
        [jax.ShapeDtypeStruct((2, 2 * LEAF, mid_rows), jnp.float32), (mid_rows, width)],
        [pltpu.VMEM((mid_rows, width), jnp.bfloat16)],
        flops=10**9,
    )(own_queries, shared, *early)
    scored = (near_scores, near_values, mid_scores, mid_values)
    last_rows = last_row_count(seq_size, paired)
    leaf_flops = 8 * LEAF * (NEAR_ROWS + mid_rows + last_rows) * width
    share_2, share_3, far_keys, far_values, far_bias = kernel_call(
        functools.partial(leaves_kernel, seq_size, paired),
        "leaves",
        24,
        [VMEM] * (5 + len(late)),
        [
            (share + PAD, width),
            (share + PAD, width),
            (last_rows, width),
            (last_rows, width),
            jax.ShapeDtypeStruct((8, last_rows), jnp.float32),
        ],
        [wide],
        flops=leaf_flops,
    )(own_queries, *scored, *late)
    share_0, share_1 = kernel_call(
        stays_kernel, "stays", 16, [VMEM] * 8, [(share, width)] * 2, [], flops=leaf_flops
    )(own_queries, *scored, far_keys, far_values, far_bias)
    columns = pltpu.VMEM((share, pair_width), jnp.bfloat16)
    part_3, part_2 = swap(share_3, 3, "head"), swap(share_2, 2, "head")
    (partial,) = kernel_call(
        begin_kernel,
        "begin",
        8,
        [VMEM] * 3,
        [jax.ShapeDtypeStruct((share, out_weight.shape[1]), jnp.float32)],
        [columns],
    )(share_0, swap(share_1, 1, "head"), out_weight)
    (mixed,) = kernel_call(
        project_kernel, "project", 8, [VMEM] * 4, [(share, out_weight.shape[1])], [columns]
    )(partial, part_3, part_2, out_weight)
    return mixed


def solution(mesh):
    in_specs = (P("seq", "head"), P("seq", "head"), P("seq", "head"), P())
    out_specs = P(("seq", "head"), None)
    return jax.shard_map(shards, mesh=mesh, in_specs=in_specs, out_specs=out_specs, check_vma=False)
```

```python
import functools
import math

import jax
import jax.numpy as jnp
from jax import lax
from jax.experimental import pallas as pl
from jax.experimental.pallas import tpu as pltpu
from jax.sharding import PartitionSpec as P

HD = 64
LEAF = 128
HALF = LEAF // 2
NEG = -math.inf


def average_pairs(rows, wide):
    count = rows.shape[0]
    halves = []
    for low in range(0, rows.shape[1], LEAF):
        wide[:count] = rows[:, low : low + LEAF].astype(jnp.float32)
        even = wide[pl.ds(0, count // 2, stride=2), :]
        odd = wide[pl.ds(1, count // 2, stride=2), :]
        halves.append((0.5 * (even + odd)).astype(jnp.bfloat16))
    return jnp.concatenate(halves, axis=1)


def pack_kernel(far_shares, queries, keys, values, own_queries, own, inner, outer, quarter, wide, arrived):
    width = keys.shape[1]
    copies = [
        pltpu.make_async_copy(keys, own.at[:, :width], arrived.at[0]),
        pltpu.make_async_copy(values, own.at[:, width:], arrived.at[1]),
        pltpu.make_async_copy(queries, own_queries, arrived.at[2]),
    ]
    for copy in copies:
        copy.start()
    me = lax.axis_index("seq")
    odd = me & 1
    for copy in copies:
        copy.wait()
    rows = own[...]
    low, high = rows[:LEAF], rows[LEAF:]
    level_one = average_pairs(rows, wide)
    level_two = average_pairs(level_one, wide)
    first, second = level_one[:HALF], level_one[HALF:]
    inner[:LEAF] = jnp.where(odd == 1, low, high)
    inner[LEAF:] = jnp.where(odd == 1, second, first)
    outer[:LEAF] = jnp.where(odd == 1, high, low)
    outer[LEAF:] = jnp.where(odd == 1, first, second)
    if far_shares:
        for peer in range(quarter.shape[0]):
            quarter[peer] = level_two
    else:
        quarter[...] = level_two


def join_kernel(theirs, quarter, opening, downward, closing, eighth, wide):
    me = lax.axis_index("seq")
    odd = me & 1
    pair = me >> 1
    first = jnp.where(odd == 1, theirs[...], quarter[...])
    second = jnp.where(odd == 1, quarter[...], theirs[...])
    level_three = average_pairs(jnp.concatenate([first, second], axis=0), wide)
    opening[:HALF] = jnp.where(pair == 0, first, level_three)
    downward[:HALF] = jnp.where(pair == 0, level_three, first)
    closing[:HALF] = jnp.where(pair == 3, level_three, first)
    for sent in (opening, downward, closing):
        sent[HALF:] = second
    eighth[...] = level_three


NEAR_ROWS = 4 * LEAF
PAD = 16


def last_row_count(seq_size, paired):
    if paired:
        return 2 * LEAF
    rows = 0
    for far in range(1, seq_size.bit_length() - 1):
        if seq_size >> far == 2:
            rows += LEAF
        elif far == 1:
            rows += 3 * HALF
        else:
            rows += 2 * LEAF
    return rows


def bias_of(valid):
    return jnp.where(valid, jnp.float32(0.0), jnp.float32(NEG))


def gathered_pieces(seq_size, far_rows, wide):
    me = lax.axis_index("seq")
    pieces = []
    for far in range(1, seq_size.bit_length() - 1):
        span = 1 << far
        group = me >> far
        parity = (me >> (far - 1)) & 1
        blocks = seq_size >> far

        def block(number, span=span, far=far):
            found = far_rows[pl.ds(number * span, span)].reshape(span * HALF, far_rows.shape[2])
            for _ in range(far - 1):
                found = average_pairs(found, wide)
            return found

        if blocks == 2:
            rows = block(1 - group)
            first = bias_of((group == 1) | (parity == 0))
            second = bias_of((group == 0) | (parity == 1))
            pieces += [(rows[:HALF], first), (rows[HALF:], second)]
        elif far == 1:
            third = jnp.where(parity == 0, me + 3, me - 3)
            for peer in (me - 2, me + 2, third):
                ok = (peer >= 0) & (peer < seq_size)
                pieces.append((far_rows[jnp.clip(peer, 0, seq_size - 1)], bias_of(ok)))
        else:
            lower = block(jnp.maximum(group - 1, 0))
            upper = block(jnp.minimum(group + 1, blocks - 1))
            has_lower, has_upper = group >= 1, group + 1 < blocks
            pieces += [
                (lower[:HALF], bias_of(has_lower)),
                (lower[HALF:], bias_of(has_lower & (parity == 1))),
                (upper[:HALF], bias_of(has_upper & (parity == 0))),
                (upper[HALF:], bias_of(has_upper)),
            ]
    return pieces


def early_pieces(opening, eighth):
    pair = lax.axis_index("seq") >> 1
    return [(jnp.where(pair == 2, eighth[...], opening[:HALF]), None)]


def late_pieces(opening, eighth, upper, closing):
    me = lax.axis_index("seq")
    odd = (me & 1) == 1
    pair = me >> 1
    return [
        (jnp.where(pair == 0, eighth[...], closing[:HALF]), None),
        (jnp.where(pair == 1, opening[HALF:], closing[HALF:]), bias_of(odd & (pair >= 1))),
        (upper[:HALF], bias_of(jnp.logical_not(odd) | (pair == 3))),
        (upper[HALF:], bias_of(pair <= 2)),
    ]


def place(pieces, values, keys):
    at = 0
    width = values.shape[1]
    total_rows = values.shape[0]
    position = lax.broadcasted_iota(jnp.int32, (1, total_rows), 1)
    bias = jnp.zeros((1, total_rows), jnp.float32)
    for rows, value in pieces:
        count = rows.shape[0]
        keys[at : at + count] = rows[:, :width]
        values[at : at + count] = rows[:, width:]
        if value is not None:
            bias = jnp.where((position >= at) & (position < at + count), value, bias)
        at += count
    return bias


def split_heads(rows):
    first_head = lax.broadcasted_iota(jnp.int32, (1, rows.shape[1]), 1) < HD
    none = jnp.zeros_like(rows)
    return jnp.concatenate(
        [jnp.where(first_head, rows, none), jnp.where(first_head, none, rows)], axis=0
    )


def scores_of(queries, keys):
    return lax.dot_general(
        queries, keys[...], (((1,), (1,)), ((), ())), preferred_element_type=jnp.float32
    )


def near_kernel(seq_size, queries, own, inner, outer, scores, values, shared, keys, wide):
    me = lax.axis_index("seq")
    odd = me & 1
    from_inner, from_outer = inner[...], outer[...]
    before = jnp.where(odd == 1, from_inner, from_outer)
    after = jnp.where(odd == 1, from_outer, from_inner)
    edge_before, edge_after = before[:LEAF], after[:LEAF]
    far_half_after = after[LEAF:]
    shared[...] = before[LEAF:]
    near_half_before = average_pairs(edge_before, wide)
    near_half_after = average_pairs(edge_after, wide)
    has_before, has_after = bias_of(me >= 1), bias_of(me + 1 < seq_size)
    for leaf in range(2):
        if leaf == 0:
            near = [
                (edge_before, has_before),
                (own[...], None),
                (near_half_after, has_after),
                (far_half_after, has_after),
            ]
        else:
            near = [
                (own[...], None),
                (edge_after, has_after),
                (near_half_before, has_before),
                (far_half_after, has_after),
            ]
        bias = place(near, values.at[leaf], keys)
        rows = split_heads(queries[leaf * LEAF : (leaf + 1) * LEAF])
        scores[leaf] = scores_of(rows, keys) + bias


def mid_kernel(queries, shared, *rest):
    *early, scores, values, keys = rest
    pieces = [(shared, bias_of(lax.axis_index("seq") >= 1))]
    if early:
        pieces += early_pieces(*early)
    bias = place(pieces, values, keys)
    for leaf in range(2):
        rows = split_heads(queries[leaf * LEAF : (leaf + 1) * LEAF])
        scores[leaf] = scores_of(rows, keys) + bias


def attend_leaf(leaf, queries, scored, keys, values, bias, same, other):
    first_head = lax.broadcasted_iota(jnp.int32, (1, values.shape[1]), 1) < HD
    exponent = math.log2(math.e) / math.sqrt(HD)
    rows = split_heads(queries[pl.ds(pl.multiple_of(leaf * LEAF, LEAF), LEAF)])
    near_scores, near_values, mid_scores, mid_values = scored
    parts = [
        (near_scores[leaf], near_values[leaf]),
        (mid_scores[leaf], mid_values[...]),
        (scores_of(rows, keys) + bias, values[...]),
    ]
    peak = functools.reduce(
        jnp.maximum, [jnp.max(scores, axis=1, keepdims=True) for scores, _ in parts]
    )
    total, numer = 0.0, 0.0
    for scores, part_values in parts:
        weights = jnp.exp2((scores - peak) * exponent)
        total = total + jnp.sum(weights, axis=1, keepdims=True)
        numer = numer + jnp.dot(
            weights.astype(jnp.bfloat16), part_values, preferred_element_type=jnp.float32
        )
    mean = numer / total
    attended = jnp.where(first_head, mean[:LEAF], mean[LEAF:]).astype(jnp.bfloat16)
    second = (lax.axis_index("head") & 1) == 1
    same[:HALF] = jnp.where(second, attended[HALF:], attended[:HALF])
    other[:HALF] = jnp.where(second, attended[:HALF], attended[HALF:])


def leaves_kernel(seq_size, paired, queries, near_scores, near_values, mid_scores, mid_values, *rest):
    *late, same, other, keys, values, bias, wide = rest
    pieces = late_pieces(*late) if paired else gathered_pieces(seq_size, late[0], wide)
    bias[...] = jnp.broadcast_to(place(pieces, values, keys), bias.shape)
    leaf = (lax.axis_index("head") >> 1) ^ 1
    scored = (near_scores, near_values, mid_scores, mid_values)
    attend_leaf(leaf, queries, scored, keys, values, bias[:1], same, other)
    for share in (same, other):
        share[HALF:] = jnp.zeros((PAD, share.shape[1]), share.dtype)


def stays_kernel(
    queries, near_scores, near_values, mid_scores, mid_values, keys, values, bias, same, other
):
    leaf = lax.axis_index("head") >> 1
    scored = (near_scores, near_values, mid_scores, mid_values)
    attend_leaf(leaf, queries, scored, keys, values, bias[:1], same, other)


def side_by_side(same, other, rows, columns):
    second = (lax.axis_index("head") & 1) == 1
    width = same.shape[1]
    columns[:, :width] = jnp.where(second, other[:rows], same[:rows])
    columns[:, width:] = jnp.where(second, same[:rows], other[:rows])
    return columns[...]


def chip_rows(weight, chip, count):
    return weight[pl.ds(pl.multiple_of(chip * count, count), count)]


def begin_kernel(same, other, weight, partial, columns):
    chip = lax.axis_index("head") >> 1
    shares = side_by_side(same, other, partial.shape[0], columns)
    partial[...] = jnp.dot(
        shares, chip_rows(weight, chip, columns.shape[1]), preferred_element_type=jnp.float32
    )


def project_kernel(partial, other, same, weight, mixed, columns):
    chip = (lax.axis_index("head") >> 1) ^ 1
    shares = side_by_side(same, other, partial.shape[0], columns)
    total = partial[...] + jnp.dot(
        shares, chip_rows(weight, chip, columns.shape[1]), preferred_element_type=jnp.float32
    )
    mixed[...] = total.astype(mixed.dtype)


VMEM = pl.BlockSpec(memory_space=pltpu.VMEM)
HBM = pl.BlockSpec(memory_space=pltpu.HBM)


def kernel_call(body, name, megabytes, ins, outs, scratch, flops=0):
    shapes = tuple(
        out if isinstance(out, jax.ShapeDtypeStruct) else jax.ShapeDtypeStruct(out, jnp.bfloat16)
        for out in outs
    )
    return pl.pallas_call(
        body,
        out_shape=shapes,
        in_specs=ins,
        out_specs=(VMEM,) * len(outs),
        scratch_shapes=scratch,
        compiler_params=pltpu.CompilerParams(vmem_limit_bytes=megabytes << 20),
        cost_estimate=pl.CostEstimate(flops=flops, bytes_accessed=1 << 20, transcendentals=0),
        name=name,
    )


def shards(queries, keys, values, out_weight):
    tokens, width = queries.shape
    seq_size = lax.axis_size("seq")
    head_size = lax.axis_size("head")
    pair_width = 2 * width
    paired = seq_size == 8
    wide_rows = 2 * LEAF if paired else max(2 * LEAF, seq_size // 2 * HALF)
    wide = pltpu.VMEM((wide_rows, width), jnp.float32)

    def swap(array, bit, axis="seq"):
        return lax.ppermute(array, axis, [(i, i ^ bit) for i in range(lax.axis_size(axis))])

    own_queries, own, inner, outer, quarter = kernel_call(
        functools.partial(pack_kernel, not paired),
        "pack",
        16,
        [HBM] * 3,
        [
            (tokens, width),
            (tokens, pair_width),
            (LEAF + HALF, pair_width),
            (LEAF + HALF, pair_width),
            (HALF, pair_width) if paired else (seq_size, HALF, pair_width),
        ],
        [wide, pltpu.SemaphoreType.DMA((3,))],
    )(*(pltpu.with_memory_space_constraint(array, pltpu.HBM) for array in (queries, keys, values)))
    inner = swap(inner, 1)

    def to_spans(array, targets):
        return lax.ppermute(
            array,
            ("seq", "head"),
            [
                (s * head_size + h, t * head_size + (h if s != t else h ^ 2))
                for s, t in enumerate(targets)
                for h in range(head_size)
            ],
        )

    last = seq_size - 1
    outer = to_spans(outer, [s if s in (0, last) else s + 1 if s & 1 else s - 1 for s in range(seq_size)])
    if paired:
        opening, downward, closing, eighth = kernel_call(
            join_kernel,
            "join",
            8,
            [VMEM] * 2,
            [(LEAF, pair_width)] * 3 + [(HALF, pair_width)],
            [wide],
            flops=3 * 10**8,
        )(swap(quarter, 1), quarter)

        def over_pairs(array, targets):
            return to_spans(array, [2 * t + x for t in targets for x in range(2)])

        early = (over_pairs(opening, (1, 3, 2, 0)), over_pairs(eighth, (2, 1, 0, 3)))
        late = early + (over_pairs(downward, (3, 0, 1, 2)), over_pairs(closing, (0, 2, 3, 1)))
    else:
        early = ()
        late = (lax.all_to_all(quarter, "seq", split_axis=0, concat_axis=0),)
    share = tokens // head_size
    near_scores, near_values, shared = kernel_call(
        functools.partial(near_kernel, seq_size),
        "near",
        16,
        [VMEM] * 4,
        [
            jax.ShapeDtypeStruct((2, 2 * LEAF, NEAR_ROWS), jnp.float32),
            (2, NEAR_ROWS, width),
            (HALF, pair_width),
        ],
        [pltpu.VMEM((NEAR_ROWS, width), jnp.bfloat16), wide],
        flops=8 * LEAF * NEAR_ROWS * width,
    )(own_queries, own, inner, outer)
    mid_rows = LEAF if paired else HALF
    mid_scores, mid_values = kernel_call(
        mid_kernel,
        "mid",
        8,
        [VMEM] * (2 + len(early)),
        [jax.ShapeDtypeStruct((2, 2 * LEAF, mid_rows), jnp.float32), (mid_rows, width)],
        [pltpu.VMEM((mid_rows, width), jnp.bfloat16)],
        flops=10**9,
    )(own_queries, shared, *early)
    scored = (near_scores, near_values, mid_scores, mid_values)
    last_rows = last_row_count(seq_size, paired)
    leaf_flops = 8 * LEAF * (NEAR_ROWS + mid_rows + last_rows) * width
    share_2, share_3, far_keys, far_values, far_bias = kernel_call(
        functools.partial(leaves_kernel, seq_size, paired),
        "leaves",
        24,
        [VMEM] * (5 + len(late)),
        [
            (share + PAD, width),
            (share + PAD, width),
            (last_rows, width),
            (last_rows, width),
            jax.ShapeDtypeStruct((8, last_rows), jnp.float32),
        ],
        [wide],
        flops=leaf_flops,
    )(own_queries, *scored, *late)
    share_0, share_1 = kernel_call(
        stays_kernel, "stays", 16, [VMEM] * 8, [(share, width)] * 2, [], flops=leaf_flops
    )(own_queries, *scored, far_keys, far_values, far_bias)
    columns = pltpu.VMEM((share, pair_width), jnp.bfloat16)
    part_3, part_2 = swap(share_3, 3, "head"), swap(share_2, 2, "head")
    (partial,) = kernel_call(
        begin_kernel,
        "begin",
        8,
        [VMEM] * 3,
        [jax.ShapeDtypeStruct((share, out_weight.shape[1]), jnp.float32)],
        [columns],
    )(share_0, swap(share_1, 1, "head"), out_weight)
    (mixed,) = kernel_call(
        project_kernel, "project", 8, [VMEM] * 4, [(share, out_weight.shape[1])], [columns]
    )(partial, part_3, part_2, out_weight)
    return mixed


def solution(mesh):
    in_specs = (P("seq", "head"), P("seq", "head"), P("seq", "head"), P())
    out_specs = P(("seq", "head"), None)
    return jax.shard_map(shards, mesh=mesh, in_specs=in_specs, out_specs=out_specs, check_vma=False)
```

```python
import functools
import math

import jax
import jax.numpy as jnp
from jax import lax
from jax.experimental import pallas as pl
from jax.experimental.pallas import tpu as pltpu
from jax.sharding import PartitionSpec as P

HD = 64
LEAF = 128
HALF = LEAF // 2
NEG = -math.inf


def average_pairs(rows, wide):
    count = rows.shape[0]
    halves = []
    for low in range(0, rows.shape[1], LEAF):
        wide[:count] = rows[:, low : low + LEAF].astype(jnp.float32)
        even = wide[pl.ds(0, count // 2, stride=2), :]
        odd = wide[pl.ds(1, count // 2, stride=2), :]
        halves.append((0.5 * (even + odd)).astype(jnp.bfloat16))
    return jnp.concatenate(halves, axis=1)


def pack_kernel(far_shares, queries, keys, values, own_queries, own, inner, outer, quarter, wide, arrived):
    width = keys.shape[1]
    copies = [
        pltpu.make_async_copy(keys, own.at[:, :width], arrived.at[0]),
        pltpu.make_async_copy(values, own.at[:, width:], arrived.at[1]),
        pltpu.make_async_copy(queries, own_queries, arrived.at[2]),
    ]
    for copy in copies:
        copy.start()
    me = lax.axis_index("seq")
    odd = me & 1
    for copy in copies:
        copy.wait()
    rows = own[...]
    low, high = rows[:LEAF], rows[LEAF:]
    level_one = average_pairs(rows, wide)
    level_two = average_pairs(level_one, wide)
    first, second = level_one[:HALF], level_one[HALF:]
    inner[:LEAF] = jnp.where(odd == 1, low, high)
    inner[LEAF:] = jnp.where(odd == 1, second, first)
    outer[:LEAF] = jnp.where(odd == 1, high, low)
    outer[LEAF:] = jnp.where(odd == 1, first, second)
    if far_shares:
        for peer in range(quarter.shape[0]):
            quarter[peer] = level_two
    else:
        quarter[...] = level_two


def join_kernel(theirs, quarter, upward, downward, eighth, wide):
    me = lax.axis_index("seq")
    odd = me & 1
    first = jnp.where(odd == 1, theirs[...], quarter[...])
    second = jnp.where(odd == 1, quarter[...], theirs[...])
    level_three = average_pairs(jnp.concatenate([first, second], axis=0), wide)
    upward[:HALF] = jnp.where(me >= 6, level_three, first)
    upward[HALF:] = second
    downward[:HALF] = jnp.where(me < 2, level_three, first)
    downward[HALF:] = second
    eighth[...] = level_three


NEAR_ROWS = 4 * LEAF
PAD = 16


def last_row_count(seq_size, paired):
    if paired:
        return LEAF
    rows = 0
    for far in range(1, seq_size.bit_length() - 1):
        if seq_size >> far == 2:
            rows += LEAF
        elif far == 1:
            rows += 3 * HALF
        else:
            rows += 2 * LEAF
    return rows


def bias_of(valid):
    return jnp.where(valid, jnp.float32(0.0), jnp.float32(NEG))


def gathered_pieces(seq_size, far_rows, wide):
    me = lax.axis_index("seq")
    pieces = []
    for far in range(1, seq_size.bit_length() - 1):
        span = 1 << far
        group = me >> far
        parity = (me >> (far - 1)) & 1
        blocks = seq_size >> far

        def block(number, span=span, far=far):
            found = far_rows[pl.ds(number * span, span)].reshape(span * HALF, far_rows.shape[2])
            for _ in range(far - 1):
                found = average_pairs(found, wide)
            return found

        if blocks == 2:
            rows = block(1 - group)
            first = bias_of((group == 1) | (parity == 0))
            second = bias_of((group == 0) | (parity == 1))
            pieces += [(rows[:HALF], first), (rows[HALF:], second)]
        elif far == 1:
            third = jnp.where(parity == 0, me + 3, me - 3)
            for peer in (me - 2, me + 2, third):
                ok = (peer >= 0) & (peer < seq_size)
                pieces.append((far_rows[jnp.clip(peer, 0, seq_size - 1)], bias_of(ok)))
        else:
            lower = block(jnp.maximum(group - 1, 0))
            upper = block(jnp.minimum(group + 1, blocks - 1))
            has_lower, has_upper = group >= 1, group + 1 < blocks
            pieces += [
                (lower[:HALF], bias_of(has_lower)),
                (lower[HALF:], bias_of(has_lower & (parity == 1))),
                (upper[:HALF], bias_of(has_upper & (parity == 0))),
                (upper[HALF:], bias_of(has_upper)),
            ]
    return pieces


def early_pieces(lower, eighth):
    me = lax.axis_index("seq")
    whole = ((me & 1) == 1) & (me >= 2)
    return [(lower[:HALF], None), (lower[HALF:], bias_of(whole)), (eighth[...], None)]


def late_pieces(upper):
    me = lax.axis_index("seq")
    whole = ((me & 1) == 0) | (me >= 6)
    return [(upper[:HALF], bias_of(whole)), (upper[HALF:], bias_of(me < 6))]


def place(pieces, values, keys):
    at = 0
    width = values.shape[1]
    total_rows = values.shape[0]
    position = lax.broadcasted_iota(jnp.int32, (1, total_rows), 1)
    bias = jnp.zeros((1, total_rows), jnp.float32)
    for rows, value in pieces:
        count = rows.shape[0]
        keys[at : at + count] = rows[:, :width]
        values[at : at + count] = rows[:, width:]
        if value is not None:
            bias = jnp.where((position >= at) & (position < at + count), value, bias)
        at += count
    return bias


def split_heads(rows):
    first_head = lax.broadcasted_iota(jnp.int32, (1, rows.shape[1]), 1) < HD
    none = jnp.zeros_like(rows)
    return jnp.concatenate(
        [jnp.where(first_head, rows, none), jnp.where(first_head, none, rows)], axis=0
    )


def scores_of(queries, keys):
    return lax.dot_general(
        queries, keys[...], (((1,), (1,)), ((), ())), preferred_element_type=jnp.float32
    )


def near_kernel(seq_size, queries, own, inner, outer, scores, values, shared, keys, wide):
    me = lax.axis_index("seq")
    odd = me & 1
    from_inner, from_outer = inner[...], outer[...]
    before = jnp.where(odd == 1, from_inner, from_outer)
    after = jnp.where(odd == 1, from_outer, from_inner)
    edge_before, edge_after = before[:LEAF], after[:LEAF]
    far_half_after = after[LEAF:]
    shared[...] = before[LEAF:]
    near_half_before = average_pairs(edge_before, wide)
    near_half_after = average_pairs(edge_after, wide)
    has_before, has_after = bias_of(me >= 1), bias_of(me + 1 < seq_size)
    for leaf in range(2):
        if leaf == 0:
            near = [
                (edge_before, has_before),
                (own[...], None),
                (near_half_after, has_after),
                (far_half_after, has_after),
            ]
        else:
            near = [
                (own[...], None),
                (edge_after, has_after),
                (near_half_before, has_before),
                (far_half_after, has_after),
            ]
        bias = place(near, values.at[leaf], keys)
        rows = split_heads(queries[leaf * LEAF : (leaf + 1) * LEAF])
        scores[leaf] = scores_of(rows, keys) + bias


def mid_kernel(queries, shared, *rest):
    *early, scores, values, keys = rest
    pieces = [(shared, bias_of(lax.axis_index("seq") >= 1))]
    if early:
        pieces += early_pieces(*early)
    bias = place(pieces, values, keys)
    for leaf in range(2):
        rows = split_heads(queries[leaf * LEAF : (leaf + 1) * LEAF])
        scores[leaf] = scores_of(rows, keys) + bias


def attend_leaf(leaf, queries, scored, keys, values, bias, same, other):
    first_head = lax.broadcasted_iota(jnp.int32, (1, values.shape[1]), 1) < HD
    exponent = math.log2(math.e) / math.sqrt(HD)
    rows = split_heads(queries[pl.ds(pl.multiple_of(leaf * LEAF, LEAF), LEAF)])
    near_scores, near_values, mid_scores, mid_values = scored
    parts = [
        (near_scores[leaf], near_values[leaf]),
        (mid_scores[leaf], mid_values[...]),
        (scores_of(rows, keys) + bias, values[...]),
    ]
    peak = functools.reduce(
        jnp.maximum, [jnp.max(scores, axis=1, keepdims=True) for scores, _ in parts]
    )
    total, numer = 0.0, 0.0
    for scores, part_values in parts:
        weights = jnp.exp2((scores - peak) * exponent)
        total = total + jnp.sum(weights, axis=1, keepdims=True)
        numer = numer + jnp.dot(
            weights.astype(jnp.bfloat16), part_values, preferred_element_type=jnp.float32
        )
    mean = numer / total
    attended = jnp.where(first_head, mean[:LEAF], mean[LEAF:]).astype(jnp.bfloat16)
    second = (lax.axis_index("head") & 1) == 1
    same[:HALF] = jnp.where(second, attended[HALF:], attended[:HALF])
    other[:HALF] = jnp.where(second, attended[:HALF], attended[HALF:])


def leaves_kernel(seq_size, paired, queries, near_scores, near_values, mid_scores, mid_values, *rest):
    late, same, other, keys, values, bias, wide = rest
    pieces = late_pieces(late) if paired else gathered_pieces(seq_size, late, wide)
    bias[...] = jnp.broadcast_to(place(pieces, values, keys), bias.shape)
    leaf = (lax.axis_index("head") >> 1) ^ 1
    scored = (near_scores, near_values, mid_scores, mid_values)
    attend_leaf(leaf, queries, scored, keys, values, bias[:1], same, other)
    for share in (same, other):
        share[HALF:] = jnp.zeros((PAD, share.shape[1]), share.dtype)


def stays_kernel(
    queries, near_scores, near_values, mid_scores, mid_values, keys, values, bias, same, other
):
    leaf = lax.axis_index("head") >> 1
    scored = (near_scores, near_values, mid_scores, mid_values)
    attend_leaf(leaf, queries, scored, keys, values, bias[:1], same, other)


def side_by_side(same, other, rows, columns):
    second = (lax.axis_index("head") & 1) == 1
    width = same.shape[1]
    columns[:, :width] = jnp.where(second, other[:rows], same[:rows])
    columns[:, width:] = jnp.where(second, same[:rows], other[:rows])
    return columns[...]


def chip_rows(weight, chip, count):
    return weight[pl.ds(pl.multiple_of(chip * count, count), count)]


def begin_kernel(same, other, weight, partial, columns):
    chip = lax.axis_index("head") >> 1
    shares = side_by_side(same, other, partial.shape[0], columns)
    partial[...] = jnp.dot(
        shares, chip_rows(weight, chip, columns.shape[1]), preferred_element_type=jnp.float32
    )


def project_kernel(partial, other, same, weight, mixed, columns):
    chip = (lax.axis_index("head") >> 1) ^ 1
    shares = side_by_side(same, other, partial.shape[0], columns)
    total = partial[...] + jnp.dot(
        shares, chip_rows(weight, chip, columns.shape[1]), preferred_element_type=jnp.float32
    )
    mixed[...] = total.astype(mixed.dtype)


VMEM = pl.BlockSpec(memory_space=pltpu.VMEM)
HBM = pl.BlockSpec(memory_space=pltpu.HBM)


def kernel_call(body, name, megabytes, ins, outs, scratch, flops=0):
    shapes = tuple(
        out if isinstance(out, jax.ShapeDtypeStruct) else jax.ShapeDtypeStruct(out, jnp.bfloat16)
        for out in outs
    )
    return pl.pallas_call(
        body,
        out_shape=shapes,
        in_specs=ins,
        out_specs=(VMEM,) * len(outs),
        scratch_shapes=scratch,
        compiler_params=pltpu.CompilerParams(vmem_limit_bytes=megabytes << 20),
        cost_estimate=pl.CostEstimate(flops=flops, bytes_accessed=1 << 20, transcendentals=0),
        name=name,
    )


def shards(queries, keys, values, out_weight):
    tokens, width = queries.shape
    seq_size = lax.axis_size("seq")
    head_size = lax.axis_size("head")
    pair_width = 2 * width
    paired = seq_size == 8
    wide_rows = 2 * LEAF if paired else max(2 * LEAF, seq_size // 2 * HALF)
    wide = pltpu.VMEM((wide_rows, width), jnp.float32)

    def swap(array, bit, axis="seq"):
        return lax.ppermute(array, axis, [(i, i ^ bit) for i in range(lax.axis_size(axis))])

    own_queries, own, inner, outer, quarter = kernel_call(
        functools.partial(pack_kernel, not paired),
        "pack",
        16,
        [HBM] * 3,
        [
            (tokens, width),
            (tokens, pair_width),
            (LEAF + HALF, pair_width),
            (LEAF + HALF, pair_width),
            (HALF, pair_width) if paired else (seq_size, HALF, pair_width),
        ],
        [wide, pltpu.SemaphoreType.DMA((3,))],
    )(*(pltpu.with_memory_space_constraint(array, pltpu.HBM) for array in (queries, keys, values)))
    inner = swap(inner, 1)

    def to_spans(array, targets):
        return lax.ppermute(
            array,
            ("seq", "head"),
            [
                (s * head_size + h, t * head_size + (h if s != t else h ^ 1))
                for s, t in enumerate(targets)
                for h in range(head_size)
            ],
        )

    last = seq_size - 1
    outer = to_spans(outer, [s if s in (0, last) else s + 1 if s & 1 else s - 1 for s in range(seq_size)])
    if paired:
        upward, downward, eighth = kernel_call(
            join_kernel,
            "join",
            8,
            [VMEM] * 2,
            [(LEAF, pair_width), (LEAF, pair_width), (HALF, pair_width)],
            [wide],
            flops=3 * 10**8,
        )(swap(quarter, 1), quarter)
        shift = [(i, (i + 2) % seq_size) for i in range(seq_size)]
        early = (lax.ppermute(upward, "seq", shift), swap(eighth, 4))
        late = lax.ppermute(downward, "seq", [(target, source) for source, target in shift])
    else:
        early = ()
        late = lax.all_to_all(quarter, "seq", split_axis=0, concat_axis=0)
    share = tokens // head_size
    near_scores, near_values, shared = kernel_call(
        functools.partial(near_kernel, seq_size),
        "near",
        16,
        [VMEM] * 4,
        [
            jax.ShapeDtypeStruct((2, 2 * LEAF, NEAR_ROWS), jnp.float32),
            (2, NEAR_ROWS, width),
            (HALF, pair_width),
        ],
        [pltpu.VMEM((NEAR_ROWS, width), jnp.bfloat16), wide],
        flops=8 * LEAF * NEAR_ROWS * width,
    )(own_queries, own, inner, outer)
    mid_rows = 4 * HALF if paired else HALF
    mid_scores, mid_values = kernel_call(
        mid_kernel,
        "mid",
        8,
        [VMEM] * (2 + len(early)),
        [jax.ShapeDtypeStruct((2, 2 * LEAF, mid_rows), jnp.float32), (mid_rows, width)],
        [pltpu.VMEM((mid_rows, width), jnp.bfloat16)],
        flops=10**9,
    )(own_queries, shared, *early)
    scored = (near_scores, near_values, mid_scores, mid_values)
    last_rows = last_row_count(seq_size, paired)
    leaf_flops = 8 * LEAF * (NEAR_ROWS + mid_rows + last_rows) * width
    share_2, share_3, far_keys, far_values, far_bias = kernel_call(
        functools.partial(leaves_kernel, seq_size, paired),
        "leaves",
        24,
        [VMEM] * 6,
        [
            (share + PAD, width),
            (share + PAD, width),
            (last_rows, width),
            (last_rows, width),
            jax.ShapeDtypeStruct((8, last_rows), jnp.float32),
        ],
        [wide],
        flops=leaf_flops,
    )(own_queries, *scored, late)
    share_0, share_1 = kernel_call(
        stays_kernel, "stays", 16, [VMEM] * 8, [(share, width)] * 2, [], flops=leaf_flops
    )(own_queries, *scored, far_keys, far_values, far_bias)
    columns = pltpu.VMEM((share, pair_width), jnp.bfloat16)
    part_3, part_2 = swap(share_3, 3, "head"), swap(share_2, 2, "head")
    (partial,) = kernel_call(
        begin_kernel,
        "begin",
        8,
        [VMEM] * 3,
        [jax.ShapeDtypeStruct((share, out_weight.shape[1]), jnp.float32)],
        [columns],
    )(share_0, swap(share_1, 1, "head"), out_weight)
    (mixed,) = kernel_call(
        project_kernel, "project", 8, [VMEM] * 4, [(share, out_weight.shape[1])], [columns]
    )(partial, part_3, part_2, out_weight)
    return mixed


def solution(mesh):
    in_specs = (P("seq", "head"), P("seq", "head"), P("seq", "head"), P())
    out_specs = P(("seq", "head"), None)
    return jax.shard_map(shards, mesh=mesh, in_specs=in_specs, out_specs=out_specs, check_vma=False)
```

```python
import functools
import math

import jax
import jax.numpy as jnp
from jax import lax
from jax.experimental import pallas as pl
from jax.experimental.pallas import tpu as pltpu
from jax.sharding import PartitionSpec as P

HD = 64
LEAF = 128
HALF = LEAF // 2
NEG = -math.inf


def average_pairs(rows, wide):
    count = rows.shape[0]
    halves = []
    for half, low in enumerate(range(0, rows.shape[1], LEAF)):
        wide[half, :count] = rows[:, low : low + LEAF].astype(jnp.float32)
    for half in range(rows.shape[1] // LEAF):
        even = wide[half, pl.ds(0, count // 2, stride=2), :]
        odd = wide[half, pl.ds(1, count // 2, stride=2), :]
        halves.append((0.5 * (even + odd)).astype(jnp.bfloat16))
    return jnp.concatenate(halves, axis=1)


def pack_kernel(far_shares, queries, keys, values, own_queries, own, inner, outer, quarter, wide, arrived):
    width = keys.shape[1]
    copies = [
        pltpu.make_async_copy(keys, own.at[:, :width], arrived.at[0]),
        pltpu.make_async_copy(values, own.at[:, width:], arrived.at[1]),
        pltpu.make_async_copy(queries, own_queries, arrived.at[2]),
    ]
    for copy in copies:
        copy.start()
    me = lax.axis_index("seq")
    odd = me & 1
    for copy in copies:
        copy.wait()
    rows = own[...]
    low, high = rows[:LEAF], rows[LEAF:]
    level_one = average_pairs(rows, wide)
    level_two = average_pairs(level_one, wide)
    first, second = level_one[:HALF], level_one[HALF:]
    inner[:LEAF] = jnp.where(odd == 1, low, high)
    inner[LEAF:] = jnp.where(odd == 1, second, first)
    outer[:LEAF] = jnp.where(odd == 1, high, low)
    outer[LEAF:] = jnp.where(odd == 1, first, second)
    if far_shares:
        for peer in range(quarter.shape[0]):
            quarter[peer] = level_two
    else:
        quarter[...] = level_two


def join_kernel(theirs, quarter, upward, downward, eighth, wide):
    me = lax.axis_index("seq")
    odd = me & 1
    first = jnp.where(odd == 1, theirs[...], quarter[...])
    second = jnp.where(odd == 1, quarter[...], theirs[...])
    level_three = average_pairs(jnp.concatenate([first, second], axis=0), wide)
    upward[:HALF] = jnp.where(me >= 6, level_three, first)
    upward[HALF:] = second
    downward[:HALF] = jnp.where(me < 2, level_three, first)
    downward[HALF:] = second
    eighth[...] = level_three


NEAR_ROWS = 4 * LEAF
PAD = 16


def last_row_count(seq_size, paired):
    if paired:
        return LEAF
    rows = 0
    for far in range(1, seq_size.bit_length() - 1):
        if seq_size >> far == 2:
            rows += LEAF
        elif far == 1:
            rows += 3 * HALF
        else:
            rows += 2 * LEAF
    return rows


def bias_of(valid):
    return jnp.where(valid, jnp.float32(0.0), jnp.float32(NEG))


def gathered_pieces(seq_size, far_rows, wide):
    me = lax.axis_index("seq")
    pieces = []
    for far in range(1, seq_size.bit_length() - 1):
        span = 1 << far
        group = me >> far
        parity = (me >> (far - 1)) & 1
        blocks = seq_size >> far

        def block(number, span=span, far=far):
            found = far_rows[pl.ds(number * span, span)].reshape(span * HALF, far_rows.shape[2])
            for _ in range(far - 1):
                found = average_pairs(found, wide)
            return found

        if blocks == 2:
            rows = block(1 - group)
            first = bias_of((group == 1) | (parity == 0))
            second = bias_of((group == 0) | (parity == 1))
            pieces += [(rows[:HALF], first), (rows[HALF:], second)]
        elif far == 1:
            third = jnp.where(parity == 0, me + 3, me - 3)
            for peer in (me - 2, me + 2, third):
                ok = (peer >= 0) & (peer < seq_size)
                pieces.append((far_rows[jnp.clip(peer, 0, seq_size - 1)], bias_of(ok)))
        else:
            lower = block(jnp.maximum(group - 1, 0))
            upper = block(jnp.minimum(group + 1, blocks - 1))
            has_lower, has_upper = group >= 1, group + 1 < blocks
            pieces += [
                (lower[:HALF], bias_of(has_lower)),
                (lower[HALF:], bias_of(has_lower & (parity == 1))),
                (upper[:HALF], bias_of(has_upper & (parity == 0))),
                (upper[HALF:], bias_of(has_upper)),
            ]
    return pieces


def early_pieces(lower, eighth):
    me = lax.axis_index("seq")
    whole = ((me & 1) == 1) & (me >= 2)
    return [(lower[:HALF], None), (lower[HALF:], bias_of(whole)), (eighth[...], None)]


def late_pieces(upper):
    me = lax.axis_index("seq")
    whole = ((me & 1) == 0) | (me >= 6)
    return [(upper[:HALF], bias_of(whole)), (upper[HALF:], bias_of(me < 6))]


def place(pieces, values, keys):
    at = 0
    width = values.shape[1]
    total_rows = values.shape[0]
    position = lax.broadcasted_iota(jnp.int32, (1, total_rows), 1)
    bias = jnp.zeros((1, total_rows), jnp.float32)
    for rows, value in pieces:
        count = rows.shape[0]
        keys[at : at + count] = rows[:, :width]
        values[at : at + count] = rows[:, width:]
        if value is not None:
            bias = jnp.where((position >= at) & (position < at + count), value, bias)
        at += count
    return bias


def split_heads(rows):
    first_head = lax.broadcasted_iota(jnp.int32, (1, rows.shape[1]), 1) < HD
    none = jnp.zeros_like(rows)
    return jnp.concatenate(
        [jnp.where(first_head, rows, none), jnp.where(first_head, none, rows)], axis=0
    )


def scores_of(queries, keys):
    return lax.dot_general(
        queries, keys[...], (((1,), (1,)), ((), ())), preferred_element_type=jnp.float32
    )


def near_kernel(seq_size, queries, own, inner, outer, scores, values, shared, keys, wide):
    me = lax.axis_index("seq")
    odd = me & 1
    from_inner, from_outer = inner[...], outer[...]
    before = jnp.where(odd == 1, from_inner, from_outer)
    after = jnp.where(odd == 1, from_outer, from_inner)
    edge_before, edge_after = before[:LEAF], after[:LEAF]
    far_half_after = after[LEAF:]
    shared[...] = before[LEAF:]
    near_half_before = average_pairs(edge_before, wide)
    near_half_after = average_pairs(edge_after, wide)
    has_before, has_after = bias_of(me >= 1), bias_of(me + 1 < seq_size)
    for leaf in range(2):
        if leaf == 0:
            near = [
                (edge_before, has_before),
                (own[...], None),
                (near_half_after, has_after),
                (far_half_after, has_after),
            ]
        else:
            near = [
                (own[...], None),
                (edge_after, has_after),
                (near_half_before, has_before),
                (far_half_after, has_after),
            ]
        bias = place(near, values.at[leaf], keys)
        rows = split_heads(queries[leaf * LEAF : (leaf + 1) * LEAF])
        scores[leaf] = scores_of(rows, keys) + bias


def mid_kernel(queries, near_scores, shared, *rest):
    *early, scores, values, peak, keys = rest
    pieces = [(shared, bias_of(lax.axis_index("seq") >= 1))]
    if early:
        pieces += early_pieces(*early)
    bias = place(pieces, values, keys)
    for leaf in range(2):
        rows = split_heads(queries[leaf * LEAF : (leaf + 1) * LEAF])
        found = scores_of(rows, keys) + bias
        scores[leaf] = found
        peak[leaf] = jnp.maximum(
            jnp.max(near_scores[leaf], axis=1, keepdims=True), jnp.max(found, axis=1, keepdims=True)
        )


def attend_leaf(leaf, queries, scored, keys, values, bias, same, other):
    first_head = lax.broadcasted_iota(jnp.int32, (1, values.shape[1]), 1) < HD
    exponent = math.log2(math.e) / math.sqrt(HD)
    rows = split_heads(queries[pl.ds(pl.multiple_of(leaf * LEAF, LEAF), LEAF)])
    near_scores, near_values, mid_scores, mid_values, peaks = scored
    last_scores = scores_of(rows, keys) + bias
    parts = [
        (near_scores[leaf], near_values[leaf]),
        (mid_scores[leaf], mid_values[...]),
        (last_scores, values[...]),
    ]
    peak = jnp.maximum(peaks[leaf], jnp.max(last_scores, axis=1, keepdims=True))
    total, numer = 0.0, 0.0
    for scores, part_values in parts:
        weights = jnp.exp2((scores - peak) * exponent)
        total = total + jnp.sum(weights, axis=1, keepdims=True)
        numer = numer + jnp.dot(
            weights.astype(jnp.bfloat16), part_values, preferred_element_type=jnp.float32
        )
    mean = numer / total
    attended = jnp.where(first_head, mean[:LEAF], mean[LEAF:]).astype(jnp.bfloat16)
    second = (lax.axis_index("head") & 1) == 1
    same[:HALF] = jnp.where(second, attended[HALF:], attended[:HALF])
    other[:HALF] = jnp.where(second, attended[:HALF], attended[HALF:])


def leaves_kernel(seq_size, paired, queries, *rest):
    scored, (late, same, other, keys, values, bias, wide) = rest[:5], rest[5:]
    pieces = late_pieces(late) if paired else gathered_pieces(seq_size, late, wide)
    bias[...] = jnp.broadcast_to(place(pieces, values, keys), bias.shape)
    leaf = (lax.axis_index("head") >> 1) ^ 1
    attend_leaf(leaf, queries, scored, keys, values, bias[:1], same, other)
    for share in (same, other):
        share[HALF:] = jnp.zeros((PAD, share.shape[1]), share.dtype)


def stays_kernel(queries, *rest):
    scored, (keys, values, bias, same, other) = rest[:5], rest[5:]
    leaf = lax.axis_index("head") >> 1
    attend_leaf(leaf, queries, scored, keys, values, bias[:1], same, other)


def side_by_side(same, other, rows, columns):
    second = (lax.axis_index("head") & 1) == 1
    width = same.shape[1]
    columns[:, :width] = jnp.where(second, other[:rows], same[:rows])
    columns[:, width:] = jnp.where(second, same[:rows], other[:rows])
    return columns[...]


def chip_rows(weight, chip, count):
    return weight[pl.ds(pl.multiple_of(chip * count, count), count)]


def begin_kernel(same, other, weight, partial, columns):
    chip = lax.axis_index("head") >> 1
    shares = side_by_side(same, other, partial.shape[0], columns)
    partial[...] = jnp.dot(
        shares, chip_rows(weight, chip, columns.shape[1]), preferred_element_type=jnp.float32
    )


def project_kernel(partial, other, same, weight, mixed, columns):
    chip = (lax.axis_index("head") >> 1) ^ 1
    shares = side_by_side(same, other, partial.shape[0], columns)
    total = partial[...] + jnp.dot(
        shares, chip_rows(weight, chip, columns.shape[1]), preferred_element_type=jnp.float32
    )
    mixed[...] = total.astype(mixed.dtype)


VMEM = pl.BlockSpec(memory_space=pltpu.VMEM)
HBM = pl.BlockSpec(memory_space=pltpu.HBM)


def kernel_call(body, name, megabytes, ins, outs, scratch, flops=0):
    shapes = tuple(
        out if isinstance(out, jax.ShapeDtypeStruct) else jax.ShapeDtypeStruct(out, jnp.bfloat16)
        for out in outs
    )
    return pl.pallas_call(
        body,
        out_shape=shapes,
        in_specs=ins,
        out_specs=(VMEM,) * len(outs),
        scratch_shapes=scratch,
        compiler_params=pltpu.CompilerParams(vmem_limit_bytes=megabytes << 20),
        cost_estimate=pl.CostEstimate(flops=flops, bytes_accessed=1 << 20, transcendentals=0),
        name=name,
    )


def shards(queries, keys, values, out_weight):
    tokens, width = queries.shape
    seq_size = lax.axis_size("seq")
    head_size = lax.axis_size("head")
    pair_width = 2 * width
    paired = seq_size == 8
    wide_rows = 2 * LEAF if paired else max(2 * LEAF, seq_size // 2 * HALF)
    wide = pltpu.VMEM((2, wide_rows, width), jnp.float32)

    def swap(array, bit, axis="seq"):
        return lax.ppermute(array, axis, [(i, i ^ bit) for i in range(lax.axis_size(axis))])

    own_queries, own, inner, outer, quarter = kernel_call(
        functools.partial(pack_kernel, not paired),
        "pack",
        16,
        [HBM] * 3,
        [
            (tokens, width),
            (tokens, pair_width),
            (LEAF + HALF, pair_width),
            (LEAF + HALF, pair_width),
            (HALF, pair_width) if paired else (seq_size, HALF, pair_width),
        ],
        [wide, pltpu.SemaphoreType.DMA((3,))],
    )(*(pltpu.with_memory_space_constraint(array, pltpu.HBM) for array in (queries, keys, values)))
    inner = swap(inner, 1)

    def to_spans(array, targets):
        return lax.ppermute(
            array,
            ("seq", "head"),
            [
                (s * head_size + h, t * head_size + (h if s != t else h ^ 1))
                for s, t in enumerate(targets)
                for h in range(head_size)
            ],
        )

    last = seq_size - 1
    outer = to_spans(outer, [s if s in (0, last) else s + 1 if s & 1 else s - 1 for s in range(seq_size)])
    if paired:
        upward, downward, eighth = kernel_call(
            join_kernel,
            "join",
            8,
            [VMEM] * 2,
            [(LEAF, pair_width), (LEAF, pair_width), (HALF, pair_width)],
            [wide],
            flops=3 * 10**8,
        )(swap(quarter, 1), quarter)
        shift = [(i, (i + 2) % seq_size) for i in range(seq_size)]
        early = (lax.ppermute(upward, "seq", shift), swap(eighth, 4))
        late = lax.ppermute(downward, "seq", [(target, source) for source, target in shift])
    else:
        early = ()
        late = lax.all_to_all(quarter, "seq", split_axis=0, concat_axis=0)
    share = tokens // head_size
    near_scores, near_values, shared = kernel_call(
        functools.partial(near_kernel, seq_size),
        "near",
        16,
        [VMEM] * 4,
        [
            jax.ShapeDtypeStruct((2, 2 * LEAF, NEAR_ROWS), jnp.float32),
            (2, NEAR_ROWS, width),
            (HALF, pair_width),
        ],
        [pltpu.VMEM((NEAR_ROWS, width), jnp.bfloat16), wide],
        flops=8 * LEAF * NEAR_ROWS * width,
    )(own_queries, own, inner, outer)
    mid_rows = 4 * HALF if paired else HALF
    mid_scores, mid_values, peaks = kernel_call(
        mid_kernel,
        "mid",
        8,
        [VMEM] * (3 + len(early)),
        [
            jax.ShapeDtypeStruct((2, 2 * LEAF, mid_rows), jnp.float32),
            (mid_rows, width),
            jax.ShapeDtypeStruct((2, 2 * LEAF, 1), jnp.float32),
        ],
        [pltpu.VMEM((mid_rows, width), jnp.bfloat16)],
        flops=10**9,
    )(own_queries, near_scores, shared, *early)
    scored = (near_scores, near_values, mid_scores, mid_values, peaks)
    last_rows = last_row_count(seq_size, paired)
    leaf_flops = 8 * LEAF * (NEAR_ROWS + mid_rows + last_rows) * width
    share_2, share_3, far_keys, far_values, far_bias = kernel_call(
        functools.partial(leaves_kernel, seq_size, paired),
        "leaves",
        24,
        [VMEM] * 7,
        [
            (share + PAD, width),
            (share + PAD, width),
            (last_rows, width),
            (last_rows, width),
            jax.ShapeDtypeStruct((8, last_rows), jnp.float32),
        ],
        [wide],
        flops=leaf_flops,
    )(own_queries, *scored, late)
    share_0, share_1 = kernel_call(
        stays_kernel, "stays", 16, [VMEM] * 9, [(share, width)] * 2, [], flops=leaf_flops
    )(own_queries, *scored, far_keys, far_values, far_bias)
    columns = pltpu.VMEM((share, pair_width), jnp.bfloat16)
    part_3, part_2 = swap(share_3, 3, "head"), swap(share_2, 2, "head")
    (partial,) = kernel_call(
        begin_kernel,
        "begin",
        8,
        [VMEM] * 3,
        [jax.ShapeDtypeStruct((share, out_weight.shape[1]), jnp.float32)],
        [columns],
    )(share_0, swap(share_1, 1, "head"), out_weight)
    (mixed,) = kernel_call(
        project_kernel, "project", 8, [VMEM] * 4, [(share, out_weight.shape[1])], [columns]
    )(partial, part_3, part_2, out_weight)
    return mixed


def solution(mesh):
    in_specs = (P("seq", "head"), P("seq", "head"), P("seq", "head"), P())
    out_specs = P(("seq", "head"), None)
    return jax.shard_map(shards, mesh=mesh, in_specs=in_specs, out_specs=out_specs, check_vma=False)
```

```python
import functools
import math

import jax
import jax.numpy as jnp
from jax import lax
from jax.experimental import pallas as pl
from jax.experimental.pallas import tpu as pltpu
from jax.sharding import PartitionSpec as P

HD = 64
LEAF = 128
HALF = LEAF // 2
NEG = -math.inf


def average_pairs(rows, wide):
    count = rows.shape[0]
    halves = []
    for low in range(0, rows.shape[1], LEAF):
        wide[:count] = rows[:, low : low + LEAF].astype(jnp.float32)
        even = wide[pl.ds(0, count // 2, stride=2), :]
        odd = wide[pl.ds(1, count // 2, stride=2), :]
        halves.append((0.5 * (even + odd)).astype(jnp.bfloat16))
    return jnp.concatenate(halves, axis=1)


def pack_kernel(far_shares, queries, keys, values, own_queries, own, inner, outer, quarter, wide, arrived):
    width = keys.shape[1]
    copies = [
        pltpu.make_async_copy(keys, own.at[:, :width], arrived.at[0]),
        pltpu.make_async_copy(values, own.at[:, width:], arrived.at[1]),
        pltpu.make_async_copy(queries, own_queries, arrived.at[2]),
    ]
    for copy in copies:
        copy.start()
    me = lax.axis_index("seq")
    odd = me & 1
    for copy in copies:
        copy.wait()
    rows = own[...]
    low, high = rows[:LEAF], rows[LEAF:]
    level_one = average_pairs(rows, wide)
    level_two = average_pairs(level_one, wide)
    first, second = level_one[:HALF], level_one[HALF:]
    inner[:LEAF] = jnp.where(odd == 1, low, high)
    inner[LEAF:] = jnp.where(odd == 1, second, first)
    outer[:LEAF] = jnp.where(odd == 1, high, low)
    outer[LEAF:] = jnp.where(odd == 1, first, second)
    if far_shares:
        for peer in range(quarter.shape[0]):
            quarter[peer] = level_two
    else:
        quarter[...] = level_two


def join_kernel(theirs, quarter, opening, downward, closing, eighth, wide):
    me = lax.axis_index("seq")
    odd = me & 1
    pair = me >> 1
    first = jnp.where(odd == 1, theirs[...], quarter[...])
    second = jnp.where(odd == 1, quarter[...], theirs[...])
    level_three = average_pairs(jnp.concatenate([first, second], axis=0), wide)
    opening[:HALF] = jnp.where(pair == 0, first, level_three)
    downward[:HALF] = jnp.where(pair == 0, level_three, first)
    closing[:HALF] = jnp.where(pair == 3, level_three, first)
    for sent in (opening, downward, closing):
        sent[HALF:] = second
    eighth[...] = level_three


NEAR_ROWS = 4 * LEAF
PAD = 16


def last_row_count(seq_size, paired):
    if paired:
        return 2 * LEAF
    rows = 0
    for far in range(1, seq_size.bit_length() - 1):
        if seq_size >> far == 2:
            rows += LEAF
        elif far == 1:
            rows += 3 * HALF
        else:
            rows += 2 * LEAF
    return rows


def bias_of(valid):
    return jnp.where(valid, jnp.float32(0.0), jnp.float32(NEG))


def gathered_pieces(seq_size, far_rows, wide):
    me = lax.axis_index("seq")
    pieces = []
    for far in range(1, seq_size.bit_length() - 1):
        span = 1 << far
        group = me >> far
        parity = (me >> (far - 1)) & 1
        blocks = seq_size >> far

        def block(number, span=span, far=far):
            found = far_rows[pl.ds(number * span, span)].reshape(span * HALF, far_rows.shape[2])
            for _ in range(far - 1):
                found = average_pairs(found, wide)
            return found

        if blocks == 2:
            rows = block(1 - group)
            first = bias_of((group == 1) | (parity == 0))
            second = bias_of((group == 0) | (parity == 1))
            pieces += [(rows[:HALF], first), (rows[HALF:], second)]
        elif far == 1:
            third = jnp.where(parity == 0, me + 3, me - 3)
            for peer in (me - 2, me + 2, third):
                ok = (peer >= 0) & (peer < seq_size)
                pieces.append((far_rows[jnp.clip(peer, 0, seq_size - 1)], bias_of(ok)))
        else:
            lower = block(jnp.maximum(group - 1, 0))
            upper = block(jnp.minimum(group + 1, blocks - 1))
            has_lower, has_upper = group >= 1, group + 1 < blocks
            pieces += [
                (lower[:HALF], bias_of(has_lower)),
                (lower[HALF:], bias_of(has_lower & (parity == 1))),
                (upper[:HALF], bias_of(has_upper & (parity == 0))),
                (upper[HALF:], bias_of(has_upper)),
            ]
    return pieces


def early_pieces(opening, eighth):
    pair = lax.axis_index("seq") >> 1
    return [(jnp.where(pair == 2, eighth[...], opening[:HALF]), None)]


def late_pieces(opening, eighth, upper, closing):
    me = lax.axis_index("seq")
    odd = (me & 1) == 1
    pair = me >> 1
    return [
        (jnp.where(pair == 0, eighth[...], closing[:HALF]), None),
        (jnp.where(pair == 1, opening[HALF:], closing[HALF:]), bias_of(odd & (pair >= 1))),
        (upper[:HALF], bias_of(jnp.logical_not(odd) | (pair == 3))),
        (upper[HALF:], bias_of(pair <= 2)),
    ]


def place(pieces, values, keys):
    at = 0
    width = values.shape[1]
    total_rows = values.shape[0]
    position = lax.broadcasted_iota(jnp.int32, (1, total_rows), 1)
    bias = jnp.zeros((1, total_rows), jnp.float32)
    for rows, value in pieces:
        count = rows.shape[0]
        keys[at : at + count] = rows[:, :width]
        values[at : at + count] = rows[:, width:]
        if value is not None:
            bias = jnp.where((position >= at) & (position < at + count), value, bias)
        at += count
    return bias


def split_heads(rows):
    first_head = lax.broadcasted_iota(jnp.int32, (1, rows.shape[1]), 1) < HD
    none = jnp.zeros_like(rows)
    return jnp.concatenate(
        [jnp.where(first_head, rows, none), jnp.where(first_head, none, rows)], axis=0
    )


def scores_of(queries, keys):
    return lax.dot_general(
        queries, keys[...], (((1,), (1,)), ((), ())), preferred_element_type=jnp.float32
    )


def near_kernel(seq_size, queries, own, inner, outer, scores, values, shared, keys, wide):
    me = lax.axis_index("seq")
    odd = me & 1
    from_inner, from_outer = inner[...], outer[...]
    before = jnp.where(odd == 1, from_inner, from_outer)
    after = jnp.where(odd == 1, from_outer, from_inner)
    edge_before, edge_after = before[:LEAF], after[:LEAF]
    far_half_after = after[LEAF:]
    shared[...] = before[LEAF:]
    near_half_before = average_pairs(edge_before, wide)
    near_half_after = average_pairs(edge_after, wide)
    has_before, has_after = bias_of(me >= 1), bias_of(me + 1 < seq_size)
    for leaf in range(2):
        if leaf == 0:
            near = [
                (edge_before, has_before),
                (own[...], None),
                (near_half_after, has_after),
                (far_half_after, has_after),
            ]
        else:
            near = [
                (own[...], None),
                (edge_after, has_after),
                (near_half_before, has_before),
                (far_half_after, has_after),
            ]
        bias = place(near, values.at[leaf], keys)
        rows = split_heads(queries[leaf * LEAF : (leaf + 1) * LEAF])
        scores[leaf] = scores_of(rows, keys) + bias


def mid_kernel(queries, shared, *rest):
    *early, scores, values, keys = rest
    pieces = [(shared, bias_of(lax.axis_index("seq") >= 1))]
    if early:
        pieces += early_pieces(*early)
    bias = place(pieces, values, keys)
    for leaf in range(2):
        rows = split_heads(queries[leaf * LEAF : (leaf + 1) * LEAF])
        scores[leaf] = scores_of(rows, keys) + bias


def attend_leaf(leaf, queries, scored, keys, values, bias, same, other):
    first_head = lax.broadcasted_iota(jnp.int32, (1, values.shape[1]), 1) < HD
    exponent = math.log2(math.e) / math.sqrt(HD)
    rows = split_heads(queries[pl.ds(pl.multiple_of(leaf * LEAF, LEAF), LEAF)])
    near_scores, near_values, mid_scores, mid_values = scored
    parts = [
        (near_scores[leaf], near_values[leaf]),
        (mid_scores[leaf], mid_values[...]),
        (scores_of(rows, keys) + bias, values[...]),
    ]
    peak = functools.reduce(
        jnp.maximum, [jnp.max(scores, axis=1, keepdims=True) for scores, _ in parts]
    )
    total, numer = 0.0, 0.0
    for scores, part_values in parts:
        weights = jnp.exp2((scores - peak) * exponent)
        total = total + jnp.sum(weights, axis=1, keepdims=True)
        numer = numer + jnp.dot(
            weights.astype(jnp.bfloat16), part_values, preferred_element_type=jnp.float32
        )
    mean = numer / total
    attended = jnp.where(first_head, mean[:LEAF], mean[LEAF:]).astype(jnp.bfloat16)
    second = (lax.axis_index("head") & 1) == 1
    same[:HALF] = jnp.where(second, attended[HALF:], attended[:HALF])
    other[:HALF] = jnp.where(second, attended[:HALF], attended[HALF:])


def leaves_kernel(seq_size, paired, queries, near_scores, near_values, mid_scores, mid_values, *rest):
    *late, same, other, keys, values, bias, wide = rest
    pieces = late_pieces(*late) if paired else gathered_pieces(seq_size, late[0], wide)
    bias[...] = jnp.broadcast_to(place(pieces, values, keys), bias.shape)
    leaf = (lax.axis_index("head") >> 1) ^ 1
    scored = (near_scores, near_values, mid_scores, mid_values)
    attend_leaf(leaf, queries, scored, keys, values, bias[:1], same, other)
    for share in (same, other):
        share[HALF:] = jnp.zeros((PAD, share.shape[1]), share.dtype)


def stays_kernel(
    queries, near_scores, near_values, mid_scores, mid_values, keys, values, bias, same, other
):
    leaf = lax.axis_index("head") >> 1
    scored = (near_scores, near_values, mid_scores, mid_values)
    attend_leaf(leaf, queries, scored, keys, values, bias[:1], same, other)


def side_by_side(same, other, rows, columns):
    second = (lax.axis_index("head") & 1) == 1
    width = same.shape[1]
    columns[:, :width] = jnp.where(second, other[:rows], same[:rows])
    columns[:, width:] = jnp.where(second, same[:rows], other[:rows])
    return columns[...]


def chip_rows(weight, chip, count):
    return weight[pl.ds(pl.multiple_of(chip * count, count), count)]


def begin_kernel(same, other, weight, partial, columns):
    chip = lax.axis_index("head") >> 1
    shares = side_by_side(same, other, partial.shape[0], columns)
    partial[...] = jnp.dot(
        shares, chip_rows(weight, chip, columns.shape[1]), preferred_element_type=jnp.float32
    )


def project_kernel(partial, other, same, weight, mixed, columns):
    chip = (lax.axis_index("head") >> 1) ^ 1
    shares = side_by_side(same, other, partial.shape[0], columns)
    total = partial[...] + jnp.dot(
        shares, chip_rows(weight, chip, columns.shape[1]), preferred_element_type=jnp.float32
    )
    mixed[...] = total.astype(mixed.dtype)


VMEM = pl.BlockSpec(memory_space=pltpu.VMEM)
HBM = pl.BlockSpec(memory_space=pltpu.HBM)


def kernel_call(body, name, megabytes, ins, outs, scratch, flops=0):
    shapes = tuple(
        out if isinstance(out, jax.ShapeDtypeStruct) else jax.ShapeDtypeStruct(out, jnp.bfloat16)
        for out in outs
    )
    return pl.pallas_call(
        body,
        out_shape=shapes,
        in_specs=ins,
        out_specs=(VMEM,) * len(outs),
        scratch_shapes=scratch,
        compiler_params=pltpu.CompilerParams(vmem_limit_bytes=megabytes << 20),
        cost_estimate=pl.CostEstimate(flops=flops, bytes_accessed=1 << 20, transcendentals=0),
        name=name,
    )


def shards(queries, keys, values, out_weight):
    tokens, width = queries.shape
    seq_size = lax.axis_size("seq")
    head_size = lax.axis_size("head")
    pair_width = 2 * width
    paired = seq_size == 8
    wide_rows = 2 * LEAF if paired else max(2 * LEAF, seq_size // 2 * HALF)
    wide = pltpu.VMEM((wide_rows, width), jnp.float32)

    def swap(array, bit, axis="seq"):
        return lax.ppermute(array, axis, [(i, i ^ bit) for i in range(lax.axis_size(axis))])

    own_queries, own, inner, outer, quarter = kernel_call(
        functools.partial(pack_kernel, not paired),
        "pack",
        16,
        [HBM] * 3,
        [
            (tokens, width),
            (tokens, pair_width),
            (LEAF + HALF, pair_width),
            (LEAF + HALF, pair_width),
            (HALF, pair_width) if paired else (seq_size, HALF, pair_width),
        ],
        [wide, pltpu.SemaphoreType.DMA((3,))],
    )(*(pltpu.with_memory_space_constraint(array, pltpu.HBM) for array in (queries, keys, values)))
    inner = swap(inner, 1)

    def to_spans(array, targets):
        return lax.ppermute(
            array,
            ("seq", "head"),
            [
                (s * head_size + h, t * head_size + (h if s != t else h ^ 1))
                for s, t in enumerate(targets)
                for h in range(head_size)
            ],
        )

    last = seq_size - 1
    outer = to_spans(outer, [s if s in (0, last) else s + 1 if s & 1 else s - 1 for s in range(seq_size)])
    if paired:
        opening, downward, closing, eighth = kernel_call(
            join_kernel,
            "join",
            8,
            [VMEM] * 2,
            [(LEAF, pair_width)] * 3 + [(HALF, pair_width)],
            [wide],
            flops=3 * 10**8,
        )(swap(quarter, 1), quarter)

        def over_pairs(array, targets):
            return to_spans(array, [2 * t + x for t in targets for x in range(2)])

        early = (over_pairs(opening, (1, 3, 2, 0)), over_pairs(eighth, (2, 3, 0, 1)))
        late = early + (over_pairs(downward, (3, 0, 1, 2)), over_pairs(closing, (0, 2, 3, 1)))
    else:
        early = ()
        late = (lax.all_to_all(quarter, "seq", split_axis=0, concat_axis=0),)
    share = tokens // head_size
    near_scores, near_values, shared = kernel_call(
        functools.partial(near_kernel, seq_size),
        "near",
        16,
        [VMEM] * 4,
        [
            jax.ShapeDtypeStruct((2, 2 * LEAF, NEAR_ROWS), jnp.float32),
            (2, NEAR_ROWS, width),
            (HALF, pair_width),
        ],
        [pltpu.VMEM((NEAR_ROWS, width), jnp.bfloat16), wide],
        flops=8 * LEAF * NEAR_ROWS * width,
    )(own_queries, own, inner, outer)
    mid_rows = LEAF if paired else HALF
    mid_scores, mid_values = kernel_call(
        mid_kernel,
        "mid",
        8,
        [VMEM] * (2 + len(early)),
        [jax.ShapeDtypeStruct((2, 2 * LEAF, mid_rows), jnp.float32), (mid_rows, width)],
        [pltpu.VMEM((mid_rows, width), jnp.bfloat16)],
        flops=10**9,
    )(own_queries, shared, *early)
    scored = (near_scores, near_values, mid_scores, mid_values)
    last_rows = last_row_count(seq_size, paired)
    leaf_flops = 8 * LEAF * (NEAR_ROWS + mid_rows + last_rows) * width
    share_2, share_3, far_keys, far_values, far_bias = kernel_call(
        functools.partial(leaves_kernel, seq_size, paired),
        "leaves",
        24,
        [VMEM] * (5 + len(late)),
        [
            (share + PAD, width),
            (share + PAD, width),
            (last_rows, width),
            (last_rows, width),
            jax.ShapeDtypeStruct((8, last_rows), jnp.float32),
        ],
        [wide],
        flops=leaf_flops,
    )(own_queries, *scored, *late)
    share_0, share_1 = kernel_call(
        stays_kernel, "stays", 16, [VMEM] * 8, [(share, width)] * 2, [], flops=leaf_flops
    )(own_queries, *scored, far_keys, far_values, far_bias)
    columns = pltpu.VMEM((share, pair_width), jnp.bfloat16)
    part_3, part_2 = swap(share_3, 3, "head"), swap(share_2, 2, "head")
    (partial,) = kernel_call(
        begin_kernel,
        "begin",
        8,
        [VMEM] * 3,
        [jax.ShapeDtypeStruct((share, out_weight.shape[1]), jnp.float32)],
        [columns],
    )(share_0, swap(share_1, 1, "head"), out_weight)
    (mixed,) = kernel_call(
        project_kernel, "project", 8, [VMEM] * 4, [(share, out_weight.shape[1])], [columns]
    )(partial, part_3, part_2, out_weight)
    return mixed


def solution(mesh):
    in_specs = (P("seq", "head"), P("seq", "head"), P("seq", "head"), P())
    out_specs = P(("seq", "head"), None)
    return jax.shard_map(shards, mesh=mesh, in_specs=in_specs, out_specs=out_specs, check_vma=False)
```

```python
import functools
import math

import jax
import jax.numpy as jnp
from jax import lax
from jax.experimental import pallas as pl
from jax.experimental.pallas import tpu as pltpu
from jax.sharding import PartitionSpec as P

HD = 64
LEAF = 128
HALF = LEAF // 2
NEG = -math.inf


def average_pairs(rows, wide):
    count = rows.shape[0]
    halves = []
    for low in range(0, rows.shape[1], LEAF):
        wide[:count] = rows[:, low : low + LEAF].astype(jnp.float32)
        even = wide[pl.ds(0, count // 2, stride=2), :]
        odd = wide[pl.ds(1, count // 2, stride=2), :]
        halves.append((0.5 * (even + odd)).astype(jnp.bfloat16))
    return jnp.concatenate(halves, axis=1)


def pack_kernel(far_shares, queries, keys, values, own_queries, own, inner, outer, quarter, wide, arrived):
    width = keys.shape[1]
    copies = [
        pltpu.make_async_copy(keys, own.at[:, :width], arrived.at[0]),
        pltpu.make_async_copy(values, own.at[:, width:], arrived.at[1]),
        pltpu.make_async_copy(queries, own_queries, arrived.at[2]),
    ]
    for copy in copies:
        copy.start()
    me = lax.axis_index("seq")
    odd = me & 1
    for copy in copies:
        copy.wait()
    rows = own[...]
    low, high = rows[:LEAF], rows[LEAF:]
    level_one = average_pairs(rows, wide)
    level_two = average_pairs(level_one, wide)
    first, second = level_one[:HALF], level_one[HALF:]
    inner[:LEAF] = jnp.where(odd == 1, low, high)
    inner[LEAF:] = jnp.where(odd == 1, second, first)
    outer[:LEAF] = jnp.where(odd == 1, high, low)
    outer[LEAF:] = jnp.where(odd == 1, first, second)
    if far_shares:
        for peer in range(quarter.shape[0]):
            quarter[peer] = level_two
    else:
        quarter[...] = level_two


def join_kernel(theirs, quarter, upward, downward, eighth, wide):
    me = lax.axis_index("seq")
    odd = me & 1
    first = jnp.where(odd == 1, theirs[...], quarter[...])
    second = jnp.where(odd == 1, quarter[...], theirs[...])
    level_three = average_pairs(jnp.concatenate([first, second], axis=0), wide)
    upward[:HALF] = jnp.where(me >= 6, level_three, first)
    upward[HALF:] = second
    downward[:HALF] = jnp.where(me < 2, level_three, first)
    downward[HALF:] = second
    eighth[...] = level_three


NEAR_ROWS = 4 * LEAF
PAD = 16


def last_row_count(seq_size, paired):
    if paired:
        return LEAF
    rows = 0
    for far in range(1, seq_size.bit_length() - 1):
        if seq_size >> far == 2:
            rows += LEAF
        elif far == 1:
            rows += 3 * HALF
        else:
            rows += 2 * LEAF
    return rows


def bias_of(valid):
    return jnp.where(valid, jnp.float32(0.0), jnp.float32(NEG))


def gathered_pieces(seq_size, far_rows, wide):
    me = lax.axis_index("seq")
    pieces = []
    for far in range(1, seq_size.bit_length() - 1):
        span = 1 << far
        group = me >> far
        parity = (me >> (far - 1)) & 1
        blocks = seq_size >> far

        def block(number, span=span, far=far):
            found = far_rows[pl.ds(number * span, span)].reshape(span * HALF, far_rows.shape[2])
            for _ in range(far - 1):
                found = average_pairs(found, wide)
            return found

        if blocks == 2:
            rows = block(1 - group)
            first = bias_of((group == 1) | (parity == 0))
            second = bias_of((group == 0) | (parity == 1))
            pieces += [(rows[:HALF], first), (rows[HALF:], second)]
        elif far == 1:
            third = jnp.where(parity == 0, me + 3, me - 3)
            for peer in (me - 2, me + 2, third):
                ok = (peer >= 0) & (peer < seq_size)
                pieces.append((far_rows[jnp.clip(peer, 0, seq_size - 1)], bias_of(ok)))
        else:
            lower = block(jnp.maximum(group - 1, 0))
            upper = block(jnp.minimum(group + 1, blocks - 1))
            has_lower, has_upper = group >= 1, group + 1 < blocks
            pieces += [
                (lower[:HALF], bias_of(has_lower)),
                (lower[HALF:], bias_of(has_lower & (parity == 1))),
                (upper[:HALF], bias_of(has_upper & (parity == 0))),
                (upper[HALF:], bias_of(has_upper)),
            ]
    return pieces


def early_pieces(lower, eighth):
    me = lax.axis_index("seq")
    whole = ((me & 1) == 1) & (me >= 2)
    return [(lower[:HALF], None), (lower[HALF:], bias_of(whole)), (eighth[...], None)]


def late_pieces(upper):
    me = lax.axis_index("seq")
    whole = ((me & 1) == 0) | (me >= 6)
    return [(upper[:HALF], bias_of(whole)), (upper[HALF:], bias_of(me < 6))]


def place(pieces, values, keys):
    at = 0
    width = values.shape[1]
    total_rows = values.shape[0]
    position = lax.broadcasted_iota(jnp.int32, (1, total_rows), 1)
    bias = jnp.zeros((1, total_rows), jnp.float32)
    for rows, value in pieces:
        count = rows.shape[0]
        keys[at : at + count] = rows[:, :width]
        values[at : at + count] = rows[:, width:]
        if value is not None:
            bias = jnp.where((position >= at) & (position < at + count), value, bias)
        at += count
    return bias


def split_heads(rows):
    first_head = lax.broadcasted_iota(jnp.int32, (1, rows.shape[1]), 1) < HD
    none = jnp.zeros_like(rows)
    return jnp.concatenate(
        [jnp.where(first_head, rows, none), jnp.where(first_head, none, rows)], axis=0
    )


def scores_of(queries, keys):
    return lax.dot_general(
        queries, keys[...], (((1,), (1,)), ((), ())), preferred_element_type=jnp.float32
    )


def near_kernel(seq_size, queries, own, outer, inner, scores, values, shared, keys, wide):
    me = lax.axis_index("seq")
    odd = me & 1
    from_inner, from_outer = inner[...], outer[...]
    before = jnp.where(odd == 1, from_inner, from_outer)
    after = jnp.where(odd == 1, from_outer, from_inner)
    edge_before, edge_after = before[:LEAF], after[:LEAF]
    far_half_after = after[LEAF:]
    shared[...] = before[LEAF:]
    near_half_before = average_pairs(edge_before, wide)
    near_half_after = average_pairs(edge_after, wide)
    has_before, has_after = bias_of(me >= 1), bias_of(me + 1 < seq_size)
    for leaf in range(2):
        if leaf == 0:
            near = [
                (edge_before, has_before),
                (own[...], None),
                (near_half_after, has_after),
                (far_half_after, has_after),
            ]
        else:
            near = [
                (own[...], None),
                (edge_after, has_after),
                (near_half_before, has_before),
                (far_half_after, has_after),
            ]
        bias = place(near, values.at[leaf], keys)
        rows = split_heads(queries[leaf * LEAF : (leaf + 1) * LEAF])
        scores[leaf] = scores_of(rows, keys) + bias


def mid_kernel(queries, shared, *rest):
    *early, scores, values, keys = rest
    pieces = [(shared, bias_of(lax.axis_index("seq") >= 1))]
    if early:
        pieces += early_pieces(*early)
    bias = place(pieces, values, keys)
    for leaf in range(2):
        rows = split_heads(queries[leaf * LEAF : (leaf + 1) * LEAF])
        scores[leaf] = scores_of(rows, keys) + bias


def attend_leaf(leaf, queries, scored, keys, values, bias, same, other):
    first_head = lax.broadcasted_iota(jnp.int32, (1, values.shape[1]), 1) < HD
    exponent = math.log2(math.e) / math.sqrt(HD)
    rows = split_heads(queries[pl.ds(pl.multiple_of(leaf * LEAF, LEAF), LEAF)])
    near_scores, near_values, mid_scores, mid_values = scored
    parts = [
        (near_scores[leaf], near_values[leaf]),
        (mid_scores[leaf], mid_values[...]),
        (scores_of(rows, keys) + bias, values[...]),
    ]
    peak = functools.reduce(
        jnp.maximum, [jnp.max(scores, axis=1, keepdims=True) for scores, _ in parts]
    )
    total, numer = 0.0, 0.0
    for scores, part_values in parts:
        weights = jnp.exp2((scores - peak) * exponent)
        total = total + jnp.sum(weights, axis=1, keepdims=True)
        numer = numer + jnp.dot(
            weights.astype(jnp.bfloat16), part_values, preferred_element_type=jnp.float32
        )
    mean = numer / total
    attended = jnp.where(first_head, mean[:LEAF], mean[LEAF:]).astype(jnp.bfloat16)
    second = (lax.axis_index("head") & 1) == 1
    same[:HALF] = jnp.where(second, attended[HALF:], attended[:HALF])
    other[:HALF] = jnp.where(second, attended[:HALF], attended[HALF:])


def leaves_kernel(seq_size, paired, queries, near_scores, near_values, mid_scores, mid_values, *rest):
    late, same, other, keys, values, bias, wide = rest
    pieces = late_pieces(late) if paired else gathered_pieces(seq_size, late, wide)
    bias[...] = jnp.broadcast_to(place(pieces, values, keys), bias.shape)
    leaf = (lax.axis_index("head") >> 1) ^ 1
    scored = (near_scores, near_values, mid_scores, mid_values)
    attend_leaf(leaf, queries, scored, keys, values, bias[:1], same, other)
    for share in (same, other):
        share[HALF:] = jnp.zeros((PAD, share.shape[1]), share.dtype)


def stays_kernel(
    queries, near_scores, near_values, mid_scores, mid_values, keys, values, bias, same, other
):
    leaf = lax.axis_index("head") >> 1
    scored = (near_scores, near_values, mid_scores, mid_values)
    attend_leaf(leaf, queries, scored, keys, values, bias[:1], same, other)


def side_by_side(same, other, rows, columns):
    second = (lax.axis_index("head") & 1) == 1
    width = same.shape[1]
    columns[:, :width] = jnp.where(second, other[:rows], same[:rows])
    columns[:, width:] = jnp.where(second, same[:rows], other[:rows])
    return columns[...]


def chip_rows(weight, chip, count):
    return weight[pl.ds(pl.multiple_of(chip * count, count), count)]


def begin_kernel(same, other, weight, partial, columns):
    chip = lax.axis_index("head") >> 1
    shares = side_by_side(same, other, partial.shape[0], columns)
    partial[...] = jnp.dot(
        shares, chip_rows(weight, chip, columns.shape[1]), preferred_element_type=jnp.float32
    )


def project_kernel(partial, other, same, weight, mixed, columns):
    chip = (lax.axis_index("head") >> 1) ^ 1
    shares = side_by_side(same, other, partial.shape[0], columns)
    total = partial[...] + jnp.dot(
        shares, chip_rows(weight, chip, columns.shape[1]), preferred_element_type=jnp.float32
    )
    mixed[...] = total.astype(mixed.dtype)


VMEM = pl.BlockSpec(memory_space=pltpu.VMEM)
HBM = pl.BlockSpec(memory_space=pltpu.HBM)


def kernel_call(body, name, megabytes, ins, outs, scratch, flops=0):
    shapes = tuple(
        out if isinstance(out, jax.ShapeDtypeStruct) else jax.ShapeDtypeStruct(out, jnp.bfloat16)
        for out in outs
    )
    return pl.pallas_call(
        body,
        out_shape=shapes,
        in_specs=ins,
        out_specs=(VMEM,) * len(outs),
        scratch_shapes=scratch,
        compiler_params=pltpu.CompilerParams(vmem_limit_bytes=megabytes << 20),
        cost_estimate=pl.CostEstimate(flops=flops, bytes_accessed=1 << 20, transcendentals=0),
        name=name,
    )


def shards(queries, keys, values, out_weight):
    tokens, width = queries.shape
    seq_size = lax.axis_size("seq")
    head_size = lax.axis_size("head")
    pair_width = 2 * width
    paired = seq_size == 8
    wide_rows = 2 * LEAF if paired else max(2 * LEAF, seq_size // 2 * HALF)
    wide = pltpu.VMEM((wide_rows, width), jnp.float32)

    def swap(array, bit, axis="seq"):
        return lax.ppermute(array, axis, [(i, i ^ bit) for i in range(lax.axis_size(axis))])

    own_queries, own, inner, outer, quarter = kernel_call(
        functools.partial(pack_kernel, not paired),
        "pack",
        16,
        [HBM] * 3,
        [
            (tokens, width),
            (tokens, pair_width),
            (LEAF + HALF, pair_width),
            (LEAF + HALF, pair_width),
            (HALF, pair_width) if paired else (seq_size, HALF, pair_width),
        ],
        [wide, pltpu.SemaphoreType.DMA((3,))],
    )(*(pltpu.with_memory_space_constraint(array, pltpu.HBM) for array in (queries, keys, values)))
    inner = swap(inner, 1)

    def to_spans(array, targets):
        return lax.ppermute(
            array,
            ("seq", "head"),
            [
                (s * head_size + h, t * head_size + (h if s != t else h ^ 1))
                for s, t in enumerate(targets)
                for h in range(head_size)
            ],
        )

    last = seq_size - 1
    outer = to_spans(outer, [s if s in (0, last) else s + 1 if s & 1 else s - 1 for s in range(seq_size)])
    if paired:
        upward, downward, eighth = kernel_call(
            join_kernel,
            "join",
            8,
            [VMEM] * 2,
            [(LEAF, pair_width), (LEAF, pair_width), (HALF, pair_width)],
            [wide],
            flops=3 * 10**8,
        )(swap(quarter, 1), quarter)
        shift = [(i, (i + 2) % seq_size) for i in range(seq_size)]
        early = (lax.ppermute(upward, "seq", shift), swap(eighth, 4))
        late = lax.ppermute(downward, "seq", [(target, source) for source, target in shift])
    else:
        early = ()
        late = lax.all_to_all(quarter, "seq", split_axis=0, concat_axis=0)
    share = tokens // head_size
    near_scores, near_values, shared = kernel_call(
        functools.partial(near_kernel, seq_size),
        "near",
        16,
        [VMEM] * 4,
        [
            jax.ShapeDtypeStruct((2, 2 * LEAF, NEAR_ROWS), jnp.float32),
            (2, NEAR_ROWS, width),
            (HALF, pair_width),
        ],
        [pltpu.VMEM((NEAR_ROWS, width), jnp.bfloat16), wide],
        flops=8 * LEAF * NEAR_ROWS * width,
    )(own_queries, own, outer, inner)
    mid_rows = 4 * HALF if paired else HALF
    mid_scores, mid_values = kernel_call(
        mid_kernel,
        "mid",
        8,
        [VMEM] * (2 + len(early)),
        [jax.ShapeDtypeStruct((2, 2 * LEAF, mid_rows), jnp.float32), (mid_rows, width)],
        [pltpu.VMEM((mid_rows, width), jnp.bfloat16)],
        flops=10**9,
    )(own_queries, shared, *early)
    scored = (near_scores, near_values, mid_scores, mid_values)
    last_rows = last_row_count(seq_size, paired)
    leaf_flops = 8 * LEAF * (NEAR_ROWS + mid_rows + last_rows) * width
    share_2, share_3, far_keys, far_values, far_bias = kernel_call(
        functools.partial(leaves_kernel, seq_size, paired),
        "leaves",
        24,
        [VMEM] * 6,
        [
            (share + PAD, width),
            (share + PAD, width),
            (last_rows, width),
            (last_rows, width),
            jax.ShapeDtypeStruct((8, last_rows), jnp.float32),
        ],
        [wide],
        flops=leaf_flops,
    )(own_queries, *scored, late)
    share_0, share_1 = kernel_call(
        stays_kernel, "stays", 16, [VMEM] * 8, [(share, width)] * 2, [], flops=leaf_flops
    )(own_queries, *scored, far_keys, far_values, far_bias)
    columns = pltpu.VMEM((share, pair_width), jnp.bfloat16)
    part_3, part_2 = swap(share_3, 3, "head"), swap(share_2, 2, "head")
    (partial,) = kernel_call(
        begin_kernel,
        "begin",
        8,
        [VMEM] * 3,
        [jax.ShapeDtypeStruct((share, out_weight.shape[1]), jnp.float32)],
        [columns],
    )(share_0, swap(share_1, 1, "head"), out_weight)
    (mixed,) = kernel_call(
        project_kernel, "project", 8, [VMEM] * 4, [(share, out_weight.shape[1])], [columns]
    )(partial, part_3, part_2, out_weight)
    return mixed


def solution(mesh):
    in_specs = (P("seq", "head"), P("seq", "head"), P("seq", "head"), P())
    out_specs = P(("seq", "head"), None)
    return jax.shard_map(shards, mesh=mesh, in_specs=in_specs, out_specs=out_specs, check_vma=False)
```

```python
import functools
import math

import jax
import jax.numpy as jnp
from jax import lax
from jax.experimental import pallas as pl
from jax.experimental.pallas import tpu as pltpu
from jax.sharding import PartitionSpec as P

HD = 64
LEAF = 128
HALF = LEAF // 2
NEG = -math.inf


def average_pairs(rows, wide):
    count = rows.shape[0]
    halves = []
    for low in range(0, rows.shape[1], LEAF):
        wide[:count] = rows[:, low : low + LEAF].astype(jnp.float32)
        even = wide[pl.ds(0, count // 2, stride=2), :]
        odd = wide[pl.ds(1, count // 2, stride=2), :]
        halves.append((0.5 * (even + odd)).astype(jnp.bfloat16))
    return jnp.concatenate(halves, axis=1)


def pack_kernel(far_shares, queries, keys, values, own_queries, own, inner, outer, quarter, wide, arrived):
    width = keys.shape[1]
    copies = [
        pltpu.make_async_copy(keys, own.at[:, :width], arrived.at[0]),
        pltpu.make_async_copy(values, own.at[:, width:], arrived.at[1]),
        pltpu.make_async_copy(queries, own_queries, arrived.at[2]),
    ]
    for copy in copies:
        copy.start()
    me = lax.axis_index("seq")
    odd = me & 1
    for copy in copies:
        copy.wait()
    rows = own[...]
    low, high = rows[:LEAF], rows[LEAF:]
    level_one = average_pairs(rows, wide)
    level_two = average_pairs(level_one, wide)
    first, second = level_one[:HALF], level_one[HALF:]
    inner[:LEAF] = jnp.where(odd == 1, low, high)
    inner[LEAF:] = jnp.where(odd == 1, second, first)
    outer[:LEAF] = jnp.where(odd == 1, high, low)
    outer[LEAF:] = jnp.where(odd == 1, first, second)
    if far_shares:
        for peer in range(quarter.shape[0]):
            quarter[peer] = level_two
    else:
        quarter[...] = level_two


def join_kernel(theirs, quarter, upward, downward, eighth, wide):
    me = lax.axis_index("seq")
    odd = me & 1
    first = jnp.where(odd == 1, theirs[...], quarter[...])
    second = jnp.where(odd == 1, quarter[...], theirs[...])
    level_three = average_pairs(jnp.concatenate([first, second], axis=0), wide)
    upward[...] = jnp.where(me >= 6, level_three, first)
    downward[...] = jnp.where(me < 2, level_three, second)
    eighth[...] = level_three


NEAR_ROWS = 4 * LEAF
PAD = 16


def last_row_count(seq_size, paired):
    if paired:
        return HALF
    rows = 0
    for far in range(1, seq_size.bit_length() - 1):
        if seq_size >> far == 2:
            rows += LEAF
        elif far == 1:
            rows += 3 * HALF
        else:
            rows += 2 * LEAF
    return rows


def bias_of(valid):
    return jnp.where(valid, jnp.float32(0.0), jnp.float32(NEG))


def gathered_pieces(seq_size, far_rows, wide):
    me = lax.axis_index("seq")
    pieces = []
    for far in range(1, seq_size.bit_length() - 1):
        span = 1 << far
        group = me >> far
        parity = (me >> (far - 1)) & 1
        blocks = seq_size >> far

        def block(number, span=span, far=far):
            found = far_rows[pl.ds(number * span, span)].reshape(span * HALF, far_rows.shape[2])
            for _ in range(far - 1):
                found = average_pairs(found, wide)
            return found

        if blocks == 2:
            rows = block(1 - group)
            first = bias_of((group == 1) | (parity == 0))
            second = bias_of((group == 0) | (parity == 1))
            pieces += [(rows[:HALF], first), (rows[HALF:], second)]
        elif far == 1:
            third = jnp.where(parity == 0, me + 3, me - 3)
            for peer in (me - 2, me + 2, third):
                ok = (peer >= 0) & (peer < seq_size)
                pieces.append((far_rows[jnp.clip(peer, 0, seq_size - 1)], bias_of(ok)))
        else:
            lower = block(jnp.maximum(group - 1, 0))
            upper = block(jnp.minimum(group + 1, blocks - 1))
            has_lower, has_upper = group >= 1, group + 1 < blocks
            pieces += [
                (lower[:HALF], bias_of(has_lower)),
                (lower[HALF:], bias_of(has_lower & (parity == 1))),
                (upper[:HALF], bias_of(has_upper & (parity == 0))),
                (upper[HALF:], bias_of(has_upper)),
            ]
    return pieces


def early_pieces(beside, lower, eighth):
    me = lax.axis_index("seq")
    has_beside = jnp.where((me & 1) == 1, me >= 2, me < 6)
    return [(beside, bias_of(has_beside)), (lower, None), (eighth, None)]


def place(pieces, values, keys):
    at = 0
    width = values.shape[1]
    total_rows = values.shape[0]
    position = lax.broadcasted_iota(jnp.int32, (1, total_rows), 1)
    bias = jnp.zeros((1, total_rows), jnp.float32)
    for rows, value in pieces:
        count = rows.shape[0]
        keys[at : at + count] = rows[:, :width]
        values[at : at + count] = rows[:, width:]
        if value is not None:
            bias = jnp.where((position >= at) & (position < at + count), value, bias)
        at += count
    return bias


def split_heads(rows):
    first_head = lax.broadcasted_iota(jnp.int32, (1, rows.shape[1]), 1) < HD
    none = jnp.zeros_like(rows)
    return jnp.concatenate(
        [jnp.where(first_head, rows, none), jnp.where(first_head, none, rows)], axis=0
    )


def scores_of(queries, keys):
    return lax.dot_general(
        queries, keys[...], (((1,), (1,)), ((), ())), preferred_element_type=jnp.float32
    )


def near_kernel(seq_size, queries, own, inner, outer, scores, values, shared, keys, wide):
    me = lax.axis_index("seq")
    odd = me & 1
    from_inner, from_outer = inner[...], outer[...]
    before = jnp.where(odd == 1, from_inner, from_outer)
    after = jnp.where(odd == 1, from_outer, from_inner)
    edge_before, edge_after = before[:LEAF], after[:LEAF]
    far_half_after = after[LEAF:]
    shared[...] = before[LEAF:]
    near_half_before = average_pairs(edge_before, wide)
    near_half_after = average_pairs(edge_after, wide)
    has_before, has_after = bias_of(me >= 1), bias_of(me + 1 < seq_size)
    for leaf in range(2):
        if leaf == 0:
            near = [
                (edge_before, has_before),
                (own[...], None),
                (near_half_after, has_after),
                (far_half_after, has_after),
            ]
        else:
            near = [
                (own[...], None),
                (edge_after, has_after),
                (near_half_before, has_before),
                (far_half_after, has_after),
            ]
        bias = place(near, values.at[leaf], keys)
        rows = split_heads(queries[leaf * LEAF : (leaf + 1) * LEAF])
        scores[leaf] = scores_of(rows, keys) + bias


def mid_kernel(queries, shared, *rest):
    *early, scores, values, keys = rest
    pieces = [(shared, bias_of(lax.axis_index("seq") >= 1))]
    if early:
        pieces += early_pieces(*early)
    bias = place(pieces, values, keys)
    for leaf in range(2):
        rows = split_heads(queries[leaf * LEAF : (leaf + 1) * LEAF])
        scores[leaf] = scores_of(rows, keys) + bias


def attend_leaf(leaf, queries, scored, keys, values, bias, same, other):
    first_head = lax.broadcasted_iota(jnp.int32, (1, values.shape[1]), 1) < HD
    exponent = math.log2(math.e) / math.sqrt(HD)
    rows = split_heads(queries[pl.ds(pl.multiple_of(leaf * LEAF, LEAF), LEAF)])
    near_scores, near_values, mid_scores, mid_values = scored
    parts = [
        (near_scores[leaf], near_values[leaf]),
        (mid_scores[leaf], mid_values[...]),
        (scores_of(rows, keys) + bias, values[...]),
    ]
    peak = functools.reduce(
        jnp.maximum, [jnp.max(scores, axis=1, keepdims=True) for scores, _ in parts]
    )
    total, numer = 0.0, 0.0
    for scores, part_values in parts:
        weights = jnp.exp2((scores - peak) * exponent)
        total = total + jnp.sum(weights, axis=1, keepdims=True)
        numer = numer + jnp.dot(
            weights.astype(jnp.bfloat16), part_values, preferred_element_type=jnp.float32
        )
    mean = numer / total
    attended = jnp.where(first_head, mean[:LEAF], mean[LEAF:]).astype(jnp.bfloat16)
    second = (lax.axis_index("head") & 1) == 1
    same[:HALF] = jnp.where(second, attended[HALF:], attended[:HALF])
    other[:HALF] = jnp.where(second, attended[:HALF], attended[HALF:])


def leaves_kernel(seq_size, paired, queries, near_scores, near_values, mid_scores, mid_values, *rest):
    late, same, other, keys, values, bias, wide = rest
    pieces = [(late, None)] if paired else gathered_pieces(seq_size, late, wide)
    bias[...] = jnp.broadcast_to(place(pieces, values, keys), bias.shape)
    leaf = (lax.axis_index("head") >> 1) ^ 1
    scored = (near_scores, near_values, mid_scores, mid_values)
    attend_leaf(leaf, queries, scored, keys, values, bias[:1], same, other)
    for share in (same, other):
        share[HALF:] = jnp.zeros((PAD, share.shape[1]), share.dtype)


def stays_kernel(
    queries, near_scores, near_values, mid_scores, mid_values, keys, values, bias, same, other
):
    leaf = lax.axis_index("head") >> 1
    scored = (near_scores, near_values, mid_scores, mid_values)
    attend_leaf(leaf, queries, scored, keys, values, bias[:1], same, other)


def side_by_side(same, other, rows, columns):
    second = (lax.axis_index("head") & 1) == 1
    width = same.shape[1]
    columns[:, :width] = jnp.where(second, other[:rows], same[:rows])
    columns[:, width:] = jnp.where(second, same[:rows], other[:rows])
    return columns[...]


def chip_rows(weight, chip, count):
    return weight[pl.ds(pl.multiple_of(chip * count, count), count)]


def begin_kernel(same, other, weight, partial, columns):
    chip = lax.axis_index("head") >> 1
    shares = side_by_side(same, other, partial.shape[0], columns)
    partial[...] = jnp.dot(
        shares, chip_rows(weight, chip, columns.shape[1]), preferred_element_type=jnp.float32
    )


def project_kernel(partial, other, same, weight, mixed, columns):
    chip = (lax.axis_index("head") >> 1) ^ 1
    shares = side_by_side(same, other, partial.shape[0], columns)
    total = partial[...] + jnp.dot(
        shares, chip_rows(weight, chip, columns.shape[1]), preferred_element_type=jnp.float32
    )
    mixed[...] = total.astype(mixed.dtype)


VMEM = pl.BlockSpec(memory_space=pltpu.VMEM)
HBM = pl.BlockSpec(memory_space=pltpu.HBM)


def kernel_call(body, name, megabytes, ins, outs, scratch, flops=0):
    shapes = tuple(
        out if isinstance(out, jax.ShapeDtypeStruct) else jax.ShapeDtypeStruct(out, jnp.bfloat16)
        for out in outs
    )
    return pl.pallas_call(
        body,
        out_shape=shapes,
        in_specs=ins,
        out_specs=(VMEM,) * len(outs),
        scratch_shapes=scratch,
        compiler_params=pltpu.CompilerParams(vmem_limit_bytes=megabytes << 20),
        cost_estimate=pl.CostEstimate(flops=flops, bytes_accessed=1 << 20, transcendentals=0),
        name=name,
    )


def shards(queries, keys, values, out_weight):
    tokens, width = queries.shape
    seq_size = lax.axis_size("seq")
    head_size = lax.axis_size("head")
    pair_width = 2 * width
    paired = seq_size == 8
    wide_rows = 2 * LEAF if paired else max(2 * LEAF, seq_size // 2 * HALF)
    wide = pltpu.VMEM((wide_rows, width), jnp.float32)

    def swap(array, bit, axis="seq"):
        return lax.ppermute(array, axis, [(i, i ^ bit) for i in range(lax.axis_size(axis))])

    own_queries, own, inner, outer, quarter = kernel_call(
        functools.partial(pack_kernel, not paired),
        "pack",
        16,
        [HBM] * 3,
        [
            (tokens, width),
            (tokens, pair_width),
            (LEAF + HALF, pair_width),
            (LEAF + HALF, pair_width),
            (HALF, pair_width) if paired else (seq_size, HALF, pair_width),
        ],
        [wide, pltpu.SemaphoreType.DMA((3,))],
    )(*(pltpu.with_memory_space_constraint(array, pltpu.HBM) for array in (queries, keys, values)))
    inner = swap(inner, 1)

    def to_spans(array, targets):
        return lax.ppermute(
            array,
            ("seq", "head"),
            [
                (s * head_size + h, t * head_size + (h if s != t else h ^ 1))
                for s, t in enumerate(targets)
                for h in range(head_size)
            ],
        )

    last = seq_size - 1
    outer = to_spans(outer, [s if s in (0, last) else s + 1 if s & 1 else s - 1 for s in range(seq_size)])
    if paired:
        upward, downward, eighth = kernel_call(
            join_kernel,
            "join",
            8,
            [VMEM] * 2,
            [(HALF, pair_width)] * 3,
            [wide],
            flops=2 * 10**9,
        )(swap(quarter, 1), quarter)
        shift = [(i, (i + 2) % seq_size) for i in range(seq_size)]
        cycle = [(i, i + 2 if i & 1 else i - 2) for i in range(1, seq_size - 1)]
        cycle += [(0, 1), (seq_size - 1, seq_size - 2)]
        beside = lax.ppermute(quarter, "seq", cycle)
        early = (beside, lax.ppermute(upward, "seq", shift), swap(eighth, 4))
        late = lax.ppermute(downward, "seq", [(target, source) for source, target in shift])
    else:
        early = ()
        late = lax.all_to_all(quarter, "seq", split_axis=0, concat_axis=0)
    share = tokens // head_size
    near_scores, near_values, shared = kernel_call(
        functools.partial(near_kernel, seq_size),
        "near",
        16,
        [VMEM] * 4,
        [
            jax.ShapeDtypeStruct((2, 2 * LEAF, NEAR_ROWS), jnp.float32),
            (2, NEAR_ROWS, width),
            (HALF, pair_width),
        ],
        [pltpu.VMEM((NEAR_ROWS, width), jnp.bfloat16), wide],
        flops=8 * LEAF * NEAR_ROWS * width,
    )(own_queries, own, inner, outer)
    mid_rows = 4 * HALF if paired else HALF
    mid_scores, mid_values = kernel_call(
        mid_kernel,
        "mid",
        8,
        [VMEM] * (2 + len(early)),
        [jax.ShapeDtypeStruct((2, 2 * LEAF, mid_rows), jnp.float32), (mid_rows, width)],
        [pltpu.VMEM((mid_rows, width), jnp.bfloat16)],
        flops=10**9,
    )(own_queries, shared, *early)
    scored = (near_scores, near_values, mid_scores, mid_values)
    last_rows = last_row_count(seq_size, paired)
    leaf_flops = 8 * LEAF * (NEAR_ROWS + mid_rows + last_rows) * width
    share_2, share_3, far_keys, far_values, far_bias = kernel_call(
        functools.partial(leaves_kernel, seq_size, paired),
        "leaves",
        24,
        [VMEM] * 6,
        [
            (share + PAD, width),
            (share + PAD, width),
            (last_rows, width),
            (last_rows, width),
            jax.ShapeDtypeStruct((8, last_rows), jnp.float32),
        ],
        [wide],
        flops=leaf_flops,
    )(own_queries, *scored, late)
    share_0, share_1 = kernel_call(
        stays_kernel, "stays", 16, [VMEM] * 8, [(share, width)] * 2, [], flops=leaf_flops
    )(own_queries, *scored, far_keys, far_values, far_bias)
    columns = pltpu.VMEM((share, pair_width), jnp.bfloat16)
    part_3, part_2 = swap(share_3, 3, "head"), swap(share_2, 2, "head")
    (partial,) = kernel_call(
        begin_kernel,
        "begin",
        8,
        [VMEM] * 3,
        [jax.ShapeDtypeStruct((share, out_weight.shape[1]), jnp.float32)],
        [columns],
    )(share_0, swap(share_1, 1, "head"), out_weight)
    (mixed,) = kernel_call(
        project_kernel, "project", 8, [VMEM] * 4, [(share, out_weight.shape[1])], [columns]
    )(partial, part_3, part_2, out_weight)
    return mixed


def solution(mesh):
    in_specs = (P("seq", "head"), P("seq", "head"), P("seq", "head"), P())
    out_specs = P(("seq", "head"), None)
    return jax.shard_map(shards, mesh=mesh, in_specs=in_specs, out_specs=out_specs, check_vma=False)
```

```python
import functools
import math

import jax
import jax.numpy as jnp
from jax import lax
from jax.experimental import pallas as pl
from jax.experimental.pallas import tpu as pltpu
from jax.sharding import PartitionSpec as P

HD = 64
LEAF = 128
HALF = LEAF // 2
NEG = -math.inf


def average_pairs(rows, wide):
    count = rows.shape[0]
    halves = []
    for low in range(0, rows.shape[1], LEAF):
        wide[:count] = rows[:, low : low + LEAF].astype(jnp.float32)
        even = wide[pl.ds(0, count // 2, stride=2), :]
        odd = wide[pl.ds(1, count // 2, stride=2), :]
        halves.append((0.5 * (even + odd)).astype(jnp.bfloat16))
    return jnp.concatenate(halves, axis=1)


def pack_kernel(far_shares, queries, keys, values, own_queries, own, inner, outer, quarter, wide, arrived):
    width = keys.shape[1]
    copies = [
        pltpu.make_async_copy(keys, own.at[:, :width], arrived.at[0]),
        pltpu.make_async_copy(values, own.at[:, width:], arrived.at[1]),
        pltpu.make_async_copy(queries, own_queries, arrived.at[2]),
    ]
    for copy in copies:
        copy.start()
    me = lax.axis_index("seq")
    odd = me & 1
    for copy in copies:
        copy.wait()
    rows = own[...]
    low, high = rows[:LEAF], rows[LEAF:]
    level_one = average_pairs(rows, wide)
    level_two = average_pairs(level_one, wide)
    first, second = level_one[:HALF], level_one[HALF:]
    inner[:LEAF] = jnp.where(odd == 1, low, high)
    inner[LEAF:] = jnp.where(odd == 1, second, first)
    outer[:LEAF] = jnp.where(odd == 1, high, low)
    outer[LEAF:] = jnp.where(odd == 1, first, second)
    if far_shares:
        for peer in range(quarter.shape[0]):
            quarter[peer] = level_two
    else:
        quarter[...] = level_two


def join_kernel(theirs, quarter, upward, downward, eighth, wide):
    me = lax.axis_index("seq")
    odd = me & 1
    first = jnp.where(odd == 1, theirs[...], quarter[...])
    second = jnp.where(odd == 1, quarter[...], theirs[...])
    level_three = average_pairs(jnp.concatenate([first, second], axis=0), wide)
    upward[...] = jnp.where(me >= 6, level_three, first)
    downward[...] = jnp.where(me < 2, level_three, second)
    eighth[...] = level_three


NEAR_ROWS = 4 * LEAF
PAD = 16


def last_row_count(seq_size, paired):
    if paired:
        return HALF
    rows = 0
    for far in range(1, seq_size.bit_length() - 1):
        if seq_size >> far == 2:
            rows += LEAF
        elif far == 1:
            rows += 3 * HALF
        else:
            rows += 2 * LEAF
    return rows


def bias_of(valid):
    return jnp.where(valid, jnp.float32(0.0), jnp.float32(NEG))


def gathered_pieces(seq_size, far_rows, wide):
    me = lax.axis_index("seq")
    pieces = []
    for far in range(1, seq_size.bit_length() - 1):
        span = 1 << far
        group = me >> far
        parity = (me >> (far - 1)) & 1
        blocks = seq_size >> far

        def block(number, span=span, far=far):
            found = far_rows[pl.ds(number * span, span)].reshape(span * HALF, far_rows.shape[2])
            for _ in range(far - 1):
                found = average_pairs(found, wide)
            return found

        if blocks == 2:
            rows = block(1 - group)
            first = bias_of((group == 1) | (parity == 0))
            second = bias_of((group == 0) | (parity == 1))
            pieces += [(rows[:HALF], first), (rows[HALF:], second)]
        elif far == 1:
            third = jnp.where(parity == 0, me + 3, me - 3)
            for peer in (me - 2, me + 2, third):
                ok = (peer >= 0) & (peer < seq_size)
                pieces.append((far_rows[jnp.clip(peer, 0, seq_size - 1)], bias_of(ok)))
        else:
            lower = block(jnp.maximum(group - 1, 0))
            upper = block(jnp.minimum(group + 1, blocks - 1))
            has_lower, has_upper = group >= 1, group + 1 < blocks
            pieces += [
                (lower[:HALF], bias_of(has_lower)),
                (lower[HALF:], bias_of(has_lower & (parity == 1))),
                (upper[:HALF], bias_of(has_upper & (parity == 0))),
                (upper[HALF:], bias_of(has_upper)),
            ]
    return pieces


def early_pieces(beside, lower, eighth):
    me = lax.axis_index("seq")
    has_beside = jnp.where((me & 1) == 1, me >= 2, me < 6)
    return [(beside, bias_of(has_beside)), (lower, None), (eighth, None)]


def place(pieces, values, keys):
    at = 0
    width = values.shape[1]
    total_rows = values.shape[0]
    position = lax.broadcasted_iota(jnp.int32, (1, total_rows), 1)
    bias = jnp.zeros((1, total_rows), jnp.float32)
    for rows, value in pieces:
        count = rows.shape[0]
        keys[at : at + count] = rows[:, :width]
        values[at : at + count] = rows[:, width:]
        if value is not None:
            bias = jnp.where((position >= at) & (position < at + count), value, bias)
        at += count
    return bias


def split_heads(rows):
    first_head = lax.broadcasted_iota(jnp.int32, (1, rows.shape[1]), 1) < HD
    none = jnp.zeros_like(rows)
    return jnp.concatenate(
        [jnp.where(first_head, rows, none), jnp.where(first_head, none, rows)], axis=0
    )


def scores_of(queries, keys):
    return lax.dot_general(
        queries, keys[...], (((1,), (1,)), ((), ())), preferred_element_type=jnp.float32
    )


def near_kernel(seq_size, queries, own, inner, outer, *rest):
    *beside, scores, values, shared, keys, wide = rest
    me = lax.axis_index("seq")
    odd = me & 1
    from_inner, from_outer = inner[...], outer[...]
    before = jnp.where(odd == 1, from_inner, from_outer)
    after = jnp.where(odd == 1, from_outer, from_inner)
    edge_before, edge_after = before[:LEAF], after[:LEAF]
    far_half_after = after[LEAF:]
    shared[:HALF] = before[LEAF:]
    for rows in beside:
        shared[HALF:] = rows[...]
    near_half_before = average_pairs(edge_before, wide)
    near_half_after = average_pairs(edge_after, wide)
    has_before, has_after = bias_of(me >= 1), bias_of(me + 1 < seq_size)
    for leaf in range(2):
        if leaf == 0:
            near = [
                (edge_before, has_before),
                (own[...], None),
                (near_half_after, has_after),
                (far_half_after, has_after),
            ]
        else:
            near = [
                (own[...], None),
                (edge_after, has_after),
                (near_half_before, has_before),
                (far_half_after, has_after),
            ]
        bias = place(near, values.at[leaf], keys)
        rows = split_heads(queries[leaf * LEAF : (leaf + 1) * LEAF])
        scores[leaf] = scores_of(rows, keys) + bias


def mid_kernel(queries, shared, *rest):
    *early, scores, values, keys = rest
    pieces = [(shared[:HALF], bias_of(lax.axis_index("seq") >= 1))]
    if early:
        pieces += early_pieces(shared[HALF:], *early)
    bias = place(pieces, values, keys)
    for leaf in range(2):
        rows = split_heads(queries[leaf * LEAF : (leaf + 1) * LEAF])
        scores[leaf] = scores_of(rows, keys) + bias


def attend_leaf(leaf, queries, scored, keys, values, bias, same, other):
    first_head = lax.broadcasted_iota(jnp.int32, (1, values.shape[1]), 1) < HD
    exponent = math.log2(math.e) / math.sqrt(HD)
    rows = split_heads(queries[pl.ds(pl.multiple_of(leaf * LEAF, LEAF), LEAF)])
    near_scores, near_values, mid_scores, mid_values = scored
    parts = [
        (near_scores[leaf], near_values[leaf]),
        (mid_scores[leaf], mid_values[...]),
        (scores_of(rows, keys) + bias, values[...]),
    ]
    peak = functools.reduce(
        jnp.maximum, [jnp.max(scores, axis=1, keepdims=True) for scores, _ in parts]
    )
    total, numer = 0.0, 0.0
    for scores, part_values in parts:
        weights = jnp.exp2((scores - peak) * exponent)
        total = total + jnp.sum(weights, axis=1, keepdims=True)
        numer = numer + jnp.dot(
            weights.astype(jnp.bfloat16), part_values, preferred_element_type=jnp.float32
        )
    mean = numer / total
    attended = jnp.where(first_head, mean[:LEAF], mean[LEAF:]).astype(jnp.bfloat16)
    second = (lax.axis_index("head") & 1) == 1
    same[:HALF] = jnp.where(second, attended[HALF:], attended[:HALF])
    other[:HALF] = jnp.where(second, attended[:HALF], attended[HALF:])


def leaves_kernel(seq_size, paired, queries, near_scores, near_values, mid_scores, mid_values, *rest):
    late, same, other, keys, values, bias, wide = rest
    pieces = [(late, None)] if paired else gathered_pieces(seq_size, late, wide)
    bias[...] = jnp.broadcast_to(place(pieces, values, keys), bias.shape)
    leaf = (lax.axis_index("head") >> 1) ^ 1
    scored = (near_scores, near_values, mid_scores, mid_values)
    attend_leaf(leaf, queries, scored, keys, values, bias[:1], same, other)
    for share in (same, other):
        share[HALF:] = jnp.zeros((PAD, share.shape[1]), share.dtype)


def stays_kernel(
    queries, near_scores, near_values, mid_scores, mid_values, keys, values, bias, same, other
):
    leaf = lax.axis_index("head") >> 1
    scored = (near_scores, near_values, mid_scores, mid_values)
    attend_leaf(leaf, queries, scored, keys, values, bias[:1], same, other)


def side_by_side(same, other, rows, columns):
    second = (lax.axis_index("head") & 1) == 1
    width = same.shape[1]
    columns[:, :width] = jnp.where(second, other[:rows], same[:rows])
    columns[:, width:] = jnp.where(second, same[:rows], other[:rows])
    return columns[...]


def chip_rows(weight, chip, count):
    return weight[pl.ds(pl.multiple_of(chip * count, count), count)]


def begin_kernel(same, other, weight, partial, columns):
    chip = lax.axis_index("head") >> 1
    shares = side_by_side(same, other, partial.shape[0], columns)
    partial[...] = jnp.dot(
        shares, chip_rows(weight, chip, columns.shape[1]), preferred_element_type=jnp.float32
    )


def project_kernel(partial, other, same, weight, mixed, columns):
    chip = (lax.axis_index("head") >> 1) ^ 1
    shares = side_by_side(same, other, partial.shape[0], columns)
    total = partial[...] + jnp.dot(
        shares, chip_rows(weight, chip, columns.shape[1]), preferred_element_type=jnp.float32
    )
    mixed[...] = total.astype(mixed.dtype)


VMEM = pl.BlockSpec(memory_space=pltpu.VMEM)
HBM = pl.BlockSpec(memory_space=pltpu.HBM)


def kernel_call(body, name, megabytes, ins, outs, scratch, flops=0):
    shapes = tuple(
        out if isinstance(out, jax.ShapeDtypeStruct) else jax.ShapeDtypeStruct(out, jnp.bfloat16)
        for out in outs
    )
    return pl.pallas_call(
        body,
        out_shape=shapes,
        in_specs=ins,
        out_specs=(VMEM,) * len(outs),
        scratch_shapes=scratch,
        compiler_params=pltpu.CompilerParams(vmem_limit_bytes=megabytes << 20),
        cost_estimate=pl.CostEstimate(flops=flops, bytes_accessed=1 << 20, transcendentals=0),
        name=name,
    )


def shards(queries, keys, values, out_weight):
    tokens, width = queries.shape
    seq_size = lax.axis_size("seq")
    head_size = lax.axis_size("head")
    pair_width = 2 * width
    paired = seq_size == 8
    wide_rows = 2 * LEAF if paired else max(2 * LEAF, seq_size // 2 * HALF)
    wide = pltpu.VMEM((wide_rows, width), jnp.float32)

    def swap(array, bit, axis="seq"):
        return lax.ppermute(array, axis, [(i, i ^ bit) for i in range(lax.axis_size(axis))])

    own_queries, own, inner, outer, quarter = kernel_call(
        functools.partial(pack_kernel, not paired),
        "pack",
        16,
        [HBM] * 3,
        [
            (tokens, width),
            (tokens, pair_width),
            (LEAF + HALF, pair_width),
            (LEAF + HALF, pair_width),
            (HALF, pair_width) if paired else (seq_size, HALF, pair_width),
        ],
        [wide, pltpu.SemaphoreType.DMA((3,))],
    )(*(pltpu.with_memory_space_constraint(array, pltpu.HBM) for array in (queries, keys, values)))
    inner = swap(inner, 1)

    def to_spans(array, targets):
        return lax.ppermute(
            array,
            ("seq", "head"),
            [
                (s * head_size + h, t * head_size + (h if s != t else h ^ 1))
                for s, t in enumerate(targets)
                for h in range(head_size)
            ],
        )

    last = seq_size - 1
    outer = to_spans(outer, [s if s in (0, last) else s + 1 if s & 1 else s - 1 for s in range(seq_size)])
    if paired:
        upward, downward, eighth = kernel_call(
            join_kernel,
            "join",
            8,
            [VMEM] * 2,
            [(HALF, pair_width)] * 3,
            [wide],
            flops=2 * 10**9,
        )(swap(quarter, 1), quarter)
        shift = [(i, (i + 2) % seq_size) for i in range(seq_size)]
        cycle = [(i, i + 2 if i & 1 else i - 2) for i in range(1, seq_size - 1)]
        cycle += [(0, 1), (seq_size - 1, seq_size - 2)]
        beside = (lax.ppermute(quarter, "seq", cycle),)
        early = (lax.ppermute(upward, "seq", shift), swap(eighth, 4))
        late = lax.ppermute(downward, "seq", [(target, source) for source, target in shift])
    else:
        beside, early = (), ()
        late = lax.all_to_all(quarter, "seq", split_axis=0, concat_axis=0)
    share = tokens // head_size
    near_scores, near_values, shared = kernel_call(
        functools.partial(near_kernel, seq_size),
        "near",
        16,
        [VMEM] * (4 + len(beside)),
        [
            jax.ShapeDtypeStruct((2, 2 * LEAF, NEAR_ROWS), jnp.float32),
            (2, NEAR_ROWS, width),
            (HALF * (1 + len(beside)), pair_width),
        ],
        [pltpu.VMEM((NEAR_ROWS, width), jnp.bfloat16), wide],
        flops=8 * LEAF * NEAR_ROWS * width,
    )(own_queries, own, inner, outer, *beside)
    mid_rows = 4 * HALF if paired else HALF
    mid_scores, mid_values = kernel_call(
        mid_kernel,
        "mid",
        8,
        [VMEM] * (2 + len(early)),
        [jax.ShapeDtypeStruct((2, 2 * LEAF, mid_rows), jnp.float32), (mid_rows, width)],
        [pltpu.VMEM((mid_rows, width), jnp.bfloat16)],
        flops=10**9,
    )(own_queries, shared, *early)
    scored = (near_scores, near_values, mid_scores, mid_values)
    last_rows = last_row_count(seq_size, paired)
    leaf_flops = 8 * LEAF * (NEAR_ROWS + mid_rows + last_rows) * width
    share_2, share_3, far_keys, far_values, far_bias = kernel_call(
        functools.partial(leaves_kernel, seq_size, paired),
        "leaves",
        24,
        [VMEM] * 6,
        [
            (share + PAD, width),
            (share + PAD, width),
            (last_rows, width),
            (last_rows, width),
            jax.ShapeDtypeStruct((8, last_rows), jnp.float32),
        ],
        [wide],
        flops=leaf_flops,
    )(own_queries, *scored, late)
    share_0, share_1 = kernel_call(
        stays_kernel, "stays", 16, [VMEM] * 8, [(share, width)] * 2, [], flops=leaf_flops
    )(own_queries, *scored, far_keys, far_values, far_bias)
    columns = pltpu.VMEM((share, pair_width), jnp.bfloat16)
    part_3, part_2 = swap(share_3, 3, "head"), swap(share_2, 2, "head")
    (partial,) = kernel_call(
        begin_kernel,
        "begin",
        8,
        [VMEM] * 3,
        [jax.ShapeDtypeStruct((share, out_weight.shape[1]), jnp.float32)],
        [columns],
    )(share_0, swap(share_1, 1, "head"), out_weight)
    (mixed,) = kernel_call(
        project_kernel, "project", 8, [VMEM] * 4, [(share, out_weight.shape[1])], [columns]
    )(partial, part_3, part_2, out_weight)
    return mixed


def solution(mesh):
    in_specs = (P("seq", "head"), P("seq", "head"), P("seq", "head"), P())
    out_specs = P(("seq", "head"), None)
    return jax.shard_map(shards, mesh=mesh, in_specs=in_specs, out_specs=out_specs, check_vma=False)
```

```python
import functools
import math

import jax
import jax.numpy as jnp
from jax import lax
from jax.experimental import pallas as pl
from jax.experimental.pallas import tpu as pltpu
from jax.sharding import PartitionSpec as P

HD = 64
LEAF = 128
HALF = LEAF // 2
NEG = -math.inf


def average_pairs(rows, wide):
    count = rows.shape[0]
    halves = []
    for low in range(0, rows.shape[1], LEAF):
        wide[:count] = rows[:, low : low + LEAF].astype(jnp.float32)
        even = wide[pl.ds(0, count // 2, stride=2), :]
        odd = wide[pl.ds(1, count // 2, stride=2), :]
        halves.append((0.5 * (even + odd)).astype(jnp.bfloat16))
    return jnp.concatenate(halves, axis=1)


def pack_kernel(far_shares, queries, keys, values, own_queries, own, inner, outer, quarter, wide, arrived):
    width = keys.shape[1]
    copies = [
        pltpu.make_async_copy(keys, own.at[:, :width], arrived.at[0]),
        pltpu.make_async_copy(values, own.at[:, width:], arrived.at[1]),
        pltpu.make_async_copy(queries, own_queries, arrived.at[2]),
    ]
    for copy in copies:
        copy.start()
    me = lax.axis_index("seq")
    odd = me & 1
    for copy in copies:
        copy.wait()
    rows = own[...]
    low, high = rows[:LEAF], rows[LEAF:]
    level_one = average_pairs(rows, wide)
    level_two = average_pairs(level_one, wide)
    first, second = level_one[:HALF], level_one[HALF:]
    inner[:LEAF] = jnp.where(odd == 1, low, high)
    inner[LEAF:] = jnp.where(odd == 1, second, first)
    outer[:LEAF] = jnp.where(odd == 1, high, low)
    outer[LEAF:] = jnp.where(odd == 1, first, second)
    if far_shares:
        for peer in range(quarter.shape[0]):
            quarter[peer] = level_two
    else:
        quarter[...] = level_two


def join_kernel(theirs, quarter, upward, downward, eighth, wide):
    me = lax.axis_index("seq")
    odd = me & 1
    first = jnp.where(odd == 1, theirs[...], quarter[...])
    second = jnp.where(odd == 1, quarter[...], theirs[...])
    level_three = average_pairs(jnp.concatenate([first, second], axis=0), wide)
    upward[...] = jnp.where(me >= 6, level_three, first)
    downward[...] = jnp.where(me < 2, level_three, second)
    eighth[...] = level_three


NEAR_ROWS = 4 * LEAF
PAD = 16


def last_row_count(seq_size, paired):
    if paired:
        return HALF
    rows = 0
    for far in range(1, seq_size.bit_length() - 1):
        if seq_size >> far == 2:
            rows += LEAF
        elif far == 1:
            rows += 3 * HALF
        else:
            rows += 2 * LEAF
    return rows


def bias_of(valid):
    return jnp.where(valid, jnp.float32(0.0), jnp.float32(NEG))


def gathered_pieces(seq_size, far_rows, wide):
    me = lax.axis_index("seq")
    pieces = []
    for far in range(1, seq_size.bit_length() - 1):
        span = 1 << far
        group = me >> far
        parity = (me >> (far - 1)) & 1
        blocks = seq_size >> far

        def block(number, span=span, far=far):
            found = far_rows[pl.ds(number * span, span)].reshape(span * HALF, far_rows.shape[2])
            for _ in range(far - 1):
                found = average_pairs(found, wide)
            return found

        if blocks == 2:
            rows = block(1 - group)
            first = bias_of((group == 1) | (parity == 0))
            second = bias_of((group == 0) | (parity == 1))
            pieces += [(rows[:HALF], first), (rows[HALF:], second)]
        elif far == 1:
            third = jnp.where(parity == 0, me + 3, me - 3)
            for peer in (me - 2, me + 2, third):
                ok = (peer >= 0) & (peer < seq_size)
                pieces.append((far_rows[jnp.clip(peer, 0, seq_size - 1)], bias_of(ok)))
        else:
            lower = block(jnp.maximum(group - 1, 0))
            upper = block(jnp.minimum(group + 1, blocks - 1))
            has_lower, has_upper = group >= 1, group + 1 < blocks
            pieces += [
                (lower[:HALF], bias_of(has_lower)),
                (lower[HALF:], bias_of(has_lower & (parity == 1))),
                (upper[:HALF], bias_of(has_upper & (parity == 0))),
                (upper[HALF:], bias_of(has_upper)),
            ]
    return pieces


def early_pieces(beside, lower, eighth):
    me = lax.axis_index("seq")
    has_beside = jnp.where((me & 1) == 1, me >= 2, me < 6)
    return [(beside, bias_of(has_beside)), (lower, None), (eighth, None)]


def place(pieces, values, keys):
    at = 0
    width = values.shape[1]
    total_rows = values.shape[0]
    position = lax.broadcasted_iota(jnp.int32, (1, total_rows), 1)
    bias = jnp.zeros((1, total_rows), jnp.float32)
    for rows, value in pieces:
        count = rows.shape[0]
        keys[at : at + count] = rows[:, :width]
        values[at : at + count] = rows[:, width:]
        if value is not None:
            bias = jnp.where((position >= at) & (position < at + count), value, bias)
        at += count
    return bias


def split_heads(rows):
    first_head = lax.broadcasted_iota(jnp.int32, (1, rows.shape[1]), 1) < HD
    none = jnp.zeros_like(rows)
    return jnp.concatenate(
        [jnp.where(first_head, rows, none), jnp.where(first_head, none, rows)], axis=0
    )


def scores_of(queries, keys):
    return lax.dot_general(
        queries, keys[...], (((1,), (1,)), ((), ())), preferred_element_type=jnp.float32
    )


def near_kernel(seq_size, queries, own, outer, inner, *rest):
    *beside, scores, values, shared, keys, wide = rest
    me = lax.axis_index("seq")
    odd = me & 1
    from_inner, from_outer = inner[...], outer[...]
    before = jnp.where(odd == 1, from_inner, from_outer)
    after = jnp.where(odd == 1, from_outer, from_inner)
    edge_before, edge_after = before[:LEAF], after[:LEAF]
    far_half_after = after[LEAF:]
    shared[:HALF] = before[LEAF:]
    for rows in beside:
        shared[HALF:] = rows[...]
    near_half_before = average_pairs(edge_before, wide)
    near_half_after = average_pairs(edge_after, wide)
    has_before, has_after = bias_of(me >= 1), bias_of(me + 1 < seq_size)
    for leaf in range(2):
        if leaf == 0:
            near = [
                (edge_before, has_before),
                (own[...], None),
                (near_half_after, has_after),
                (far_half_after, has_after),
            ]
        else:
            near = [
                (own[...], None),
                (edge_after, has_after),
                (near_half_before, has_before),
                (far_half_after, has_after),
            ]
        bias = place(near, values.at[leaf], keys)
        rows = split_heads(queries[leaf * LEAF : (leaf + 1) * LEAF])
        scores[leaf] = scores_of(rows, keys) + bias


def mid_kernel(queries, shared, *rest):
    *early, scores, values, keys = rest
    pieces = [(shared[:HALF], bias_of(lax.axis_index("seq") >= 1))]
    if early:
        pieces += early_pieces(shared[HALF:], *early)
    bias = place(pieces, values, keys)
    for leaf in range(2):
        rows = split_heads(queries[leaf * LEAF : (leaf + 1) * LEAF])
        scores[leaf] = scores_of(rows, keys) + bias


def attend_leaf(leaf, queries, scored, keys, values, bias, same, other):
    first_head = lax.broadcasted_iota(jnp.int32, (1, values.shape[1]), 1) < HD
    exponent = math.log2(math.e) / math.sqrt(HD)
    rows = split_heads(queries[pl.ds(pl.multiple_of(leaf * LEAF, LEAF), LEAF)])
    near_scores, near_values, mid_scores, mid_values = scored
    parts = [
        (near_scores[leaf], near_values[leaf]),
        (mid_scores[leaf], mid_values[...]),
        (scores_of(rows, keys) + bias, values[...]),
    ]
    peak = functools.reduce(
        jnp.maximum, [jnp.max(scores, axis=1, keepdims=True) for scores, _ in parts]
    )
    total, numer = 0.0, 0.0
    for scores, part_values in parts:
        weights = jnp.exp2((scores - peak) * exponent)
        total = total + jnp.sum(weights, axis=1, keepdims=True)
        numer = numer + jnp.dot(
            weights.astype(jnp.bfloat16), part_values, preferred_element_type=jnp.float32
        )
    mean = numer / total
    attended = jnp.where(first_head, mean[:LEAF], mean[LEAF:]).astype(jnp.bfloat16)
    second = (lax.axis_index("head") & 1) == 1
    same[:HALF] = jnp.where(second, attended[HALF:], attended[:HALF])
    other[:HALF] = jnp.where(second, attended[:HALF], attended[HALF:])


def leaves_kernel(seq_size, paired, queries, near_scores, near_values, mid_scores, mid_values, *rest):
    late, same, other, keys, values, bias, wide = rest
    pieces = [(late, None)] if paired else gathered_pieces(seq_size, late, wide)
    bias[...] = jnp.broadcast_to(place(pieces, values, keys), bias.shape)
    leaf = (lax.axis_index("head") >> 1) ^ 1
    scored = (near_scores, near_values, mid_scores, mid_values)
    attend_leaf(leaf, queries, scored, keys, values, bias[:1], same, other)
    for share in (same, other):
        share[HALF:] = jnp.zeros((PAD, share.shape[1]), share.dtype)


def stays_kernel(
    queries, near_scores, near_values, mid_scores, mid_values, keys, values, bias, same, other
):
    leaf = lax.axis_index("head") >> 1
    scored = (near_scores, near_values, mid_scores, mid_values)
    attend_leaf(leaf, queries, scored, keys, values, bias[:1], same, other)


def side_by_side(same, other, rows, columns):
    second = (lax.axis_index("head") & 1) == 1
    width = same.shape[1]
    columns[:, :width] = jnp.where(second, other[:rows], same[:rows])
    columns[:, width:] = jnp.where(second, same[:rows], other[:rows])
    return columns[...]


def chip_rows(weight, chip, count):
    return weight[pl.ds(pl.multiple_of(chip * count, count), count)]


def begin_kernel(same, other, weight, partial, columns):
    chip = lax.axis_index("head") >> 1
    shares = side_by_side(same, other, partial.shape[0], columns)
    partial[...] = jnp.dot(
        shares, chip_rows(weight, chip, columns.shape[1]), preferred_element_type=jnp.float32
    )


def project_kernel(partial, other, same, weight, mixed, columns):
    chip = (lax.axis_index("head") >> 1) ^ 1
    shares = side_by_side(same, other, partial.shape[0], columns)
    total = partial[...] + jnp.dot(
        shares, chip_rows(weight, chip, columns.shape[1]), preferred_element_type=jnp.float32
    )
    mixed[...] = total.astype(mixed.dtype)


VMEM = pl.BlockSpec(memory_space=pltpu.VMEM)
HBM = pl.BlockSpec(memory_space=pltpu.HBM)


def kernel_call(body, name, megabytes, ins, outs, scratch, flops=0):
    shapes = tuple(
        out if isinstance(out, jax.ShapeDtypeStruct) else jax.ShapeDtypeStruct(out, jnp.bfloat16)
        for out in outs
    )
    return pl.pallas_call(
        body,
        out_shape=shapes,
        in_specs=ins,
        out_specs=(VMEM,) * len(outs),
        scratch_shapes=scratch,
        compiler_params=pltpu.CompilerParams(vmem_limit_bytes=megabytes << 20),
        cost_estimate=pl.CostEstimate(flops=flops, bytes_accessed=1 << 20, transcendentals=0),
        name=name,
    )


def shards(queries, keys, values, out_weight):
    tokens, width = queries.shape
    seq_size = lax.axis_size("seq")
    head_size = lax.axis_size("head")
    pair_width = 2 * width
    paired = seq_size == 8
    wide_rows = 2 * LEAF if paired else max(2 * LEAF, seq_size // 2 * HALF)
    wide = pltpu.VMEM((wide_rows, width), jnp.float32)

    def swap(array, bit, axis="seq"):
        return lax.ppermute(array, axis, [(i, i ^ bit) for i in range(lax.axis_size(axis))])

    own_queries, own, inner, outer, quarter = kernel_call(
        functools.partial(pack_kernel, not paired),
        "pack",
        16,
        [HBM] * 3,
        [
            (tokens, width),
            (tokens, pair_width),
            (LEAF + HALF, pair_width),
            (LEAF + HALF, pair_width),
            (HALF, pair_width) if paired else (seq_size, HALF, pair_width),
        ],
        [wide, pltpu.SemaphoreType.DMA((3,))],
    )(*(pltpu.with_memory_space_constraint(array, pltpu.HBM) for array in (queries, keys, values)))
    inner = swap(inner, 1)

    def to_spans(array, targets):
        return lax.ppermute(
            array,
            ("seq", "head"),
            [
                (s * head_size + h, t * head_size + (h if s != t else h ^ 1))
                for s, t in enumerate(targets)
                for h in range(head_size)
            ],
        )

    last = seq_size - 1
    outer = to_spans(outer, [s if s in (0, last) else s + 1 if s & 1 else s - 1 for s in range(seq_size)])
    if paired:
        upward, downward, eighth = kernel_call(
            join_kernel,
            "join",
            8,
            [VMEM] * 2,
            [(HALF, pair_width)] * 3,
            [wide],
            flops=2 * 10**9,
        )(swap(quarter, 1), quarter)
        shift = [(i, (i + 2) % seq_size) for i in range(seq_size)]
        cycle = [(i, i + 2 if i & 1 else i - 2) for i in range(1, seq_size - 1)]
        cycle += [(0, 1), (seq_size - 1, seq_size - 2)]
        beside = (lax.ppermute(quarter, "seq", cycle),)
        early = (lax.ppermute(upward, "seq", shift), swap(eighth, 4))
        late = lax.ppermute(downward, "seq", [(target, source) for source, target in shift])
    else:
        beside, early = (), ()
        late = lax.all_to_all(quarter, "seq", split_axis=0, concat_axis=0)
    share = tokens // head_size
    near_scores, near_values, shared = kernel_call(
        functools.partial(near_kernel, seq_size),
        "near",
        16,
        [VMEM] * (4 + len(beside)),
        [
            jax.ShapeDtypeStruct((2, 2 * LEAF, NEAR_ROWS), jnp.float32),
            (2, NEAR_ROWS, width),
            (HALF * (1 + len(beside)), pair_width),
        ],
        [pltpu.VMEM((NEAR_ROWS, width), jnp.bfloat16), wide],
        flops=8 * LEAF * NEAR_ROWS * width,
    )(own_queries, own, outer, inner, *beside)
    mid_rows = 4 * HALF if paired else HALF
    mid_scores, mid_values = kernel_call(
        mid_kernel,
        "mid",
        8,
        [VMEM] * (2 + len(early)),
        [jax.ShapeDtypeStruct((2, 2 * LEAF, mid_rows), jnp.float32), (mid_rows, width)],
        [pltpu.VMEM((mid_rows, width), jnp.bfloat16)],
        flops=10**9,
    )(own_queries, shared, *early)
    scored = (near_scores, near_values, mid_scores, mid_values)
    last_rows = last_row_count(seq_size, paired)
    leaf_flops = 8 * LEAF * (NEAR_ROWS + mid_rows + last_rows) * width
    share_2, share_3, far_keys, far_values, far_bias = kernel_call(
        functools.partial(leaves_kernel, seq_size, paired),
        "leaves",
        24,
        [VMEM] * 6,
        [
            (share + PAD, width),
            (share + PAD, width),
            (last_rows, width),
            (last_rows, width),
            jax.ShapeDtypeStruct((8, last_rows), jnp.float32),
        ],
        [wide],
        flops=leaf_flops,
    )(own_queries, *scored, late)
    share_0, share_1 = kernel_call(
        stays_kernel, "stays", 16, [VMEM] * 8, [(share, width)] * 2, [], flops=leaf_flops
    )(own_queries, *scored, far_keys, far_values, far_bias)
    columns = pltpu.VMEM((share, pair_width), jnp.bfloat16)
    part_3, part_2 = swap(share_3, 3, "head"), swap(share_2, 2, "head")
    (partial,) = kernel_call(
        begin_kernel,
        "begin",
        8,
        [VMEM] * 3,
        [jax.ShapeDtypeStruct((share, out_weight.shape[1]), jnp.float32)],
        [columns],
    )(share_0, swap(share_1, 1, "head"), out_weight)
    (mixed,) = kernel_call(
        project_kernel, "project", 8, [VMEM] * 4, [(share, out_weight.shape[1])], [columns]
    )(partial, part_3, part_2, out_weight)
    return mixed


def solution(mesh):
    in_specs = (P("seq", "head"), P("seq", "head"), P("seq", "head"), P())
    out_specs = P(("seq", "head"), None)
    return jax.shard_map(shards, mesh=mesh, in_specs=in_specs, out_specs=out_specs, check_vma=False)
```

```python
import functools
import math

import jax
import jax.numpy as jnp
from jax import lax
from jax.experimental import pallas as pl
from jax.experimental.pallas import tpu as pltpu
from jax.sharding import PartitionSpec as P

HD = 64
LEAF = 128
HALF = LEAF // 2
NEG = -math.inf


def average_pairs(rows, wide):
    count = rows.shape[0]
    halves = []
    for low in range(0, rows.shape[1], LEAF):
        wide[:count] = rows[:, low : low + LEAF].astype(jnp.float32)
        even = wide[pl.ds(0, count // 2, stride=2), :]
        odd = wide[pl.ds(1, count // 2, stride=2), :]
        halves.append((0.5 * (even + odd)).astype(jnp.bfloat16))
    return jnp.concatenate(halves, axis=1)


def pack_kernel(far_shares, queries, keys, values, own_queries, own, inner, outer, quarter, wide, arrived):
    width = keys.shape[1]
    copies = [
        pltpu.make_async_copy(keys, own.at[:, :width], arrived.at[0]),
        pltpu.make_async_copy(values, own.at[:, width:], arrived.at[1]),
        pltpu.make_async_copy(queries, own_queries, arrived.at[2]),
    ]
    for copy in copies:
        copy.start()
    me = lax.axis_index("seq")
    odd = me & 1
    for copy in copies:
        copy.wait()
    rows = own[...]
    low, high = rows[:LEAF], rows[LEAF:]
    level_one = average_pairs(rows, wide)
    level_two = average_pairs(level_one, wide)
    first, second = level_one[:HALF], level_one[HALF:]
    inner[:LEAF] = jnp.where(odd == 1, low, high)
    inner[LEAF:] = jnp.where(odd == 1, second, first)
    outer[:LEAF] = jnp.where(odd == 1, high, low)
    outer[LEAF:] = jnp.where(odd == 1, first, second)
    if far_shares:
        for peer in range(quarter.shape[0]):
            quarter[peer] = level_two
    else:
        quarter[...] = level_two


def join_kernel(theirs, quarter, upward, third, fourth, eighth, wide):
    me = lax.axis_index("seq")
    odd = me & 1
    pair = me >> 1
    first = jnp.where(odd == 1, theirs[...], quarter[...])
    second = jnp.where(odd == 1, quarter[...], theirs[...])
    level_three = average_pairs(jnp.concatenate([first, second], axis=0), wide)
    upward[...] = jnp.where(pair == 3, level_three, first)
    third[...] = jnp.where(pair == 1, second, level_three)
    fourth[...] = jnp.where(pair == 1, level_three, second)
    eighth[...] = level_three


NEAR_ROWS = 4 * LEAF
PAD = 16


def last_row_count(seq_size, paired):
    if paired:
        return LEAF
    rows = 0
    for far in range(1, seq_size.bit_length() - 1):
        if seq_size >> far == 2:
            rows += LEAF
        elif far == 1:
            rows += 3 * HALF
        else:
            rows += 2 * LEAF
    return rows


def bias_of(valid):
    return jnp.where(valid, jnp.float32(0.0), jnp.float32(NEG))


def gathered_pieces(seq_size, far_rows, wide):
    me = lax.axis_index("seq")
    pieces = []
    for far in range(1, seq_size.bit_length() - 1):
        span = 1 << far
        group = me >> far
        parity = (me >> (far - 1)) & 1
        blocks = seq_size >> far

        def block(number, span=span, far=far):
            found = far_rows[pl.ds(number * span, span)].reshape(span * HALF, far_rows.shape[2])
            for _ in range(far - 1):
                found = average_pairs(found, wide)
            return found

        if blocks == 2:
            rows = block(1 - group)
            first = bias_of((group == 1) | (parity == 0))
            second = bias_of((group == 0) | (parity == 1))
            pieces += [(rows[:HALF], first), (rows[HALF:], second)]
        elif far == 1:
            third = jnp.where(parity == 0, me + 3, me - 3)
            for peer in (me - 2, me + 2, third):
                ok = (peer >= 0) & (peer < seq_size)
                pieces.append((far_rows[jnp.clip(peer, 0, seq_size - 1)], bias_of(ok)))
        else:
            lower = block(jnp.maximum(group - 1, 0))
            upper = block(jnp.minimum(group + 1, blocks - 1))
            has_lower, has_upper = group >= 1, group + 1 < blocks
            pieces += [
                (lower[:HALF], bias_of(has_lower)),
                (lower[HALF:], bias_of(has_lower & (parity == 1))),
                (upper[:HALF], bias_of(has_upper & (parity == 0))),
                (upper[HALF:], bias_of(has_upper)),
            ]
    return pieces


def early_pieces(beside, lower):
    me = lax.axis_index("seq")
    has_beside = jnp.where((me & 1) == 1, me >= 2, me < 6)
    return [(beside, bias_of(has_beside)), (lower, None)]


def late_pieces(second, third, fourth):
    pair = lax.axis_index("seq") >> 1
    return [
        (jnp.where(pair == 2, third[...], second[...]), None),
        (jnp.where(pair == 0, third[...], fourth[...]), None),
    ]


def place(pieces, values, keys):
    at = 0
    width = values.shape[1]
    total_rows = values.shape[0]
    position = lax.broadcasted_iota(jnp.int32, (1, total_rows), 1)
    bias = jnp.zeros((1, total_rows), jnp.float32)
    for rows, value in pieces:
        count = rows.shape[0]
        keys[at : at + count] = rows[:, :width]
        values[at : at + count] = rows[:, width:]
        if value is not None:
            bias = jnp.where((position >= at) & (position < at + count), value, bias)
        at += count
    return bias


def split_heads(rows):
    first_head = lax.broadcasted_iota(jnp.int32, (1, rows.shape[1]), 1) < HD
    none = jnp.zeros_like(rows)
    return jnp.concatenate(
        [jnp.where(first_head, rows, none), jnp.where(first_head, none, rows)], axis=0
    )


def scores_of(queries, keys):
    return lax.dot_general(
        queries, keys[...], (((1,), (1,)), ((), ())), preferred_element_type=jnp.float32
    )


def near_kernel(seq_size, queries, own, inner, outer, *rest):
    *beside, scores, values, shared, keys, wide = rest
    me = lax.axis_index("seq")
    odd = me & 1
    from_inner, from_outer = inner[...], outer[...]
    before = jnp.where(odd == 1, from_inner, from_outer)
    after = jnp.where(odd == 1, from_outer, from_inner)
    edge_before, edge_after = before[:LEAF], after[:LEAF]
    far_half_after = after[LEAF:]
    shared[:HALF] = before[LEAF:]
    for rows in beside:
        shared[HALF:] = rows[...]
    near_half_before = average_pairs(edge_before, wide)
    near_half_after = average_pairs(edge_after, wide)
    has_before, has_after = bias_of(me >= 1), bias_of(me + 1 < seq_size)
    for leaf in range(2):
        if leaf == 0:
            near = [
                (edge_before, has_before),
                (own[...], None),
                (near_half_after, has_after),
                (far_half_after, has_after),
            ]
        else:
            near = [
                (own[...], None),
                (edge_after, has_after),
                (near_half_before, has_before),
                (far_half_after, has_after),
            ]
        bias = place(near, values.at[leaf], keys)
        rows = split_heads(queries[leaf * LEAF : (leaf + 1) * LEAF])
        scores[leaf] = scores_of(rows, keys) + bias


def mid_kernel(queries, shared, *rest):
    *early, scores, values, keys = rest
    pieces = [(shared[:HALF], bias_of(lax.axis_index("seq") >= 1))]
    if early:
        pieces += early_pieces(shared[HALF:], *early)
    bias = place(pieces, values, keys)
    for leaf in range(2):
        rows = split_heads(queries[leaf * LEAF : (leaf + 1) * LEAF])
        scores[leaf] = scores_of(rows, keys) + bias


def attend_leaf(leaf, queries, scored, keys, values, bias, same, other):
    first_head = lax.broadcasted_iota(jnp.int32, (1, values.shape[1]), 1) < HD
    exponent = math.log2(math.e) / math.sqrt(HD)
    rows = split_heads(queries[pl.ds(pl.multiple_of(leaf * LEAF, LEAF), LEAF)])
    near_scores, near_values, mid_scores, mid_values = scored
    parts = [
        (near_scores[leaf], near_values[leaf]),
        (mid_scores[leaf], mid_values[...]),
        (scores_of(rows, keys) + bias, values[...]),
    ]
    peak = functools.reduce(
        jnp.maximum, [jnp.max(scores, axis=1, keepdims=True) for scores, _ in parts]
    )
    total, numer = 0.0, 0.0
    for scores, part_values in parts:
        weights = jnp.exp2((scores - peak) * exponent)
        total = total + jnp.sum(weights, axis=1, keepdims=True)
        numer = numer + jnp.dot(
            weights.astype(jnp.bfloat16), part_values, preferred_element_type=jnp.float32
        )
    mean = numer / total
    attended = jnp.where(first_head, mean[:LEAF], mean[LEAF:]).astype(jnp.bfloat16)
    second = (lax.axis_index("head") & 1) == 1
    same[:HALF] = jnp.where(second, attended[HALF:], attended[:HALF])
    other[:HALF] = jnp.where(second, attended[:HALF], attended[HALF:])


def leaves_kernel(seq_size, paired, queries, near_scores, near_values, mid_scores, mid_values, *rest):
    *late, same, other, keys, values, bias, wide = rest
    pieces = late_pieces(*late) if paired else gathered_pieces(seq_size, late[0], wide)
    bias[...] = jnp.broadcast_to(place(pieces, values, keys), bias.shape)
    leaf = (lax.axis_index("head") >> 1) ^ 1
    scored = (near_scores, near_values, mid_scores, mid_values)
    attend_leaf(leaf, queries, scored, keys, values, bias[:1], same, other)
    for share in (same, other):
        share[HALF:] = jnp.zeros((PAD, share.shape[1]), share.dtype)


def stays_kernel(
    queries, near_scores, near_values, mid_scores, mid_values, keys, values, bias, same, other
):
    leaf = lax.axis_index("head") >> 1
    scored = (near_scores, near_values, mid_scores, mid_values)
    attend_leaf(leaf, queries, scored, keys, values, bias[:1], same, other)


def side_by_side(same, other, rows, columns):
    second = (lax.axis_index("head") & 1) == 1
    width = same.shape[1]
    columns[:, :width] = jnp.where(second, other[:rows], same[:rows])
    columns[:, width:] = jnp.where(second, same[:rows], other[:rows])
    return columns[...]


def chip_rows(weight, chip, count):
    return weight[pl.ds(pl.multiple_of(chip * count, count), count)]


def begin_kernel(same, other, weight, partial, columns):
    chip = lax.axis_index("head") >> 1
    shares = side_by_side(same, other, partial.shape[0], columns)
    partial[...] = jnp.dot(
        shares, chip_rows(weight, chip, columns.shape[1]), preferred_element_type=jnp.float32
    )


def project_kernel(partial, other, same, weight, mixed, columns):
    chip = (lax.axis_index("head") >> 1) ^ 1
    shares = side_by_side(same, other, partial.shape[0], columns)
    total = partial[...] + jnp.dot(
        shares, chip_rows(weight, chip, columns.shape[1]), preferred_element_type=jnp.float32
    )
    mixed[...] = total.astype(mixed.dtype)


VMEM = pl.BlockSpec(memory_space=pltpu.VMEM)
HBM = pl.BlockSpec(memory_space=pltpu.HBM)


def kernel_call(body, name, megabytes, ins, outs, scratch, flops=0):
    shapes = tuple(
        out if isinstance(out, jax.ShapeDtypeStruct) else jax.ShapeDtypeStruct(out, jnp.bfloat16)
        for out in outs
    )
    return pl.pallas_call(
        body,
        out_shape=shapes,
        in_specs=ins,
        out_specs=(VMEM,) * len(outs),
        scratch_shapes=scratch,
        compiler_params=pltpu.CompilerParams(vmem_limit_bytes=megabytes << 20),
        cost_estimate=pl.CostEstimate(flops=flops, bytes_accessed=1 << 20, transcendentals=0),
        name=name,
    )


def shards(queries, keys, values, out_weight):
    tokens, width = queries.shape
    seq_size = lax.axis_size("seq")
    head_size = lax.axis_size("head")
    pair_width = 2 * width
    paired = seq_size == 8
    wide_rows = 2 * LEAF if paired else max(2 * LEAF, seq_size // 2 * HALF)
    wide = pltpu.VMEM((wide_rows, width), jnp.float32)

    def swap(array, bit, axis="seq"):
        return lax.ppermute(array, axis, [(i, i ^ bit) for i in range(lax.axis_size(axis))])

    own_queries, own, inner, outer, quarter = kernel_call(
        functools.partial(pack_kernel, not paired),
        "pack",
        16,
        [HBM] * 3,
        [
            (tokens, width),
            (tokens, pair_width),
            (LEAF + HALF, pair_width),
            (LEAF + HALF, pair_width),
            (HALF, pair_width) if paired else (seq_size, HALF, pair_width),
        ],
        [wide, pltpu.SemaphoreType.DMA((3,))],
    )(*(pltpu.with_memory_space_constraint(array, pltpu.HBM) for array in (queries, keys, values)))
    inner = swap(inner, 1)

    def to_spans(array, targets):
        return lax.ppermute(
            array,
            ("seq", "head"),
            [
                (s * head_size + h, t * head_size + (h if s != t else h ^ 1))
                for s, t in enumerate(targets)
                for h in range(head_size)
            ],
        )

    last = seq_size - 1
    outer = to_spans(outer, [s if s in (0, last) else s + 1 if s & 1 else s - 1 for s in range(seq_size)])
    if paired:
        upward, third, fourth, eighth = kernel_call(
            join_kernel,
            "join",
            8,
            [VMEM] * 2,
            [(HALF, pair_width)] * 4,
            [wide],
            flops=2 * 10**9,
        )(swap(quarter, 1), quarter)

        def over_pairs(array, targets):
            return to_spans(array, [2 * t + x for t in targets for x in range(2)])

        cycle = [(i, i + 2 if i & 1 else i - 2) for i in range(1, seq_size - 1)]
        cycle += [(0, 1), (seq_size - 1, seq_size - 2)]
        beside = (lax.ppermute(quarter, "seq", cycle),)
        early = (over_pairs(upward, (1, 2, 3, 0)),)
        late = (
            over_pairs(eighth, (3, 2, 0, 1)),
            over_pairs(third, (2, 0, 3, 1)),
            over_pairs(fourth, (0, 3, 1, 2)),
        )
    else:
        beside, early = (), ()
        late = (lax.all_to_all(quarter, "seq", split_axis=0, concat_axis=0),)
    share = tokens // head_size
    near_scores, near_values, shared = kernel_call(
        functools.partial(near_kernel, seq_size),
        "near",
        16,
        [VMEM] * (4 + len(beside)),
        [
            jax.ShapeDtypeStruct((2, 2 * LEAF, NEAR_ROWS), jnp.float32),
            (2, NEAR_ROWS, width),
            (HALF * (1 + len(beside)), pair_width),
        ],
        [pltpu.VMEM((NEAR_ROWS, width), jnp.bfloat16), wide],
        flops=8 * LEAF * NEAR_ROWS * width,
    )(own_queries, own, inner, outer, *beside)
    mid_rows = 3 * HALF if paired else HALF
    mid_scores, mid_values = kernel_call(
        mid_kernel,
        "mid",
        8,
        [VMEM] * (2 + len(early)),
        [jax.ShapeDtypeStruct((2, 2 * LEAF, mid_rows), jnp.float32), (mid_rows, width)],
        [pltpu.VMEM((mid_rows, width), jnp.bfloat16)],
        flops=10**9,
    )(own_queries, shared, *early)
    scored = (near_scores, near_values, mid_scores, mid_values)
    last_rows = last_row_count(seq_size, paired)
    leaf_flops = 8 * LEAF * (NEAR_ROWS + mid_rows + last_rows) * width
    share_2, share_3, far_keys, far_values, far_bias = kernel_call(
        functools.partial(leaves_kernel, seq_size, paired),
        "leaves",
        24,
        [VMEM] * (5 + len(late)),
        [
            (share + PAD, width),
            (share + PAD, width),
            (last_rows, width),
            (last_rows, width),
            jax.ShapeDtypeStruct((8, last_rows), jnp.float32),
        ],
        [wide],
        flops=leaf_flops,
    )(own_queries, *scored, *late)
    share_0, share_1 = kernel_call(
        stays_kernel, "stays", 16, [VMEM] * 8, [(share, width)] * 2, [], flops=leaf_flops
    )(own_queries, *scored, far_keys, far_values, far_bias)
    columns = pltpu.VMEM((share, pair_width), jnp.bfloat16)
    part_3, part_2 = swap(share_3, 3, "head"), swap(share_2, 2, "head")
    (partial,) = kernel_call(
        begin_kernel,
        "begin",
        8,
        [VMEM] * 3,
        [jax.ShapeDtypeStruct((share, out_weight.shape[1]), jnp.float32)],
        [columns],
    )(share_0, swap(share_1, 1, "head"), out_weight)
    (mixed,) = kernel_call(
        project_kernel, "project", 8, [VMEM] * 4, [(share, out_weight.shape[1])], [columns]
    )(partial, part_3, part_2, out_weight)
    return mixed


def solution(mesh):
    in_specs = (P("seq", "head"), P("seq", "head"), P("seq", "head"), P())
    out_specs = P(("seq", "head"), None)
    return jax.shard_map(shards, mesh=mesh, in_specs=in_specs, out_specs=out_specs, check_vma=False)
```

```python
import functools
import math

import jax
import jax.numpy as jnp
from jax import lax
from jax.experimental import pallas as pl
from jax.experimental.pallas import tpu as pltpu
from jax.sharding import PartitionSpec as P

HD = 64
LEAF = 128
HALF = LEAF // 2
NEG = -math.inf


def average_pairs(rows, wide):
    count = rows.shape[0]
    halves = []
    for low in range(0, rows.shape[1], LEAF):
        wide[:count] = rows[:, low : low + LEAF].astype(jnp.float32)
        even = wide[pl.ds(0, count // 2, stride=2), :]
        odd = wide[pl.ds(1, count // 2, stride=2), :]
        halves.append((0.5 * (even + odd)).astype(jnp.bfloat16))
    return jnp.concatenate(halves, axis=1)


def pack_kernel(far_shares, queries, keys, values, own_queries, own, inner, outer, quarter, wide, arrived):
    width = keys.shape[1]
    copies = [
        pltpu.make_async_copy(keys, own.at[:, :width], arrived.at[0]),
        pltpu.make_async_copy(values, own.at[:, width:], arrived.at[1]),
        pltpu.make_async_copy(queries, own_queries, arrived.at[2]),
    ]
    for copy in copies:
        copy.start()
    me = lax.axis_index("seq")
    odd = me & 1
    for copy in copies:
        copy.wait()
    rows = own[...]
    low, high = rows[:LEAF], rows[LEAF:]
    level_one = average_pairs(rows, wide)
    level_two = average_pairs(level_one, wide)
    first, second = level_one[:HALF], level_one[HALF:]
    inner[:LEAF] = jnp.where(odd == 1, low, high)
    inner[LEAF:] = jnp.where(odd == 1, second, first)
    outer[:LEAF] = jnp.where(odd == 1, high, low)
    outer[LEAF:] = jnp.where(odd == 1, first, second)
    if far_shares:
        for peer in range(quarter.shape[0]):
            quarter[peer] = level_two
    else:
        quarter[...] = level_two


def join_kernel(theirs, quarter, upward, third, fourth, eighth, wide):
    me = lax.axis_index("seq")
    odd = me & 1
    pair = me >> 1
    first = jnp.where(odd == 1, theirs[...], quarter[...])
    second = jnp.where(odd == 1, quarter[...], theirs[...])
    level_three = average_pairs(jnp.concatenate([first, second], axis=0), wide)
    upward[...] = jnp.where(pair == 3, level_three, first)
    third[...] = jnp.where(pair == 1, second, level_three)
    fourth[...] = jnp.where(pair == 1, level_three, second)
    eighth[...] = level_three


NEAR_ROWS = 4 * LEAF
PAD = 16


def last_row_count(seq_size, paired):
    if paired:
        return LEAF
    rows = 0
    for far in range(1, seq_size.bit_length() - 1):
        if seq_size >> far == 2:
            rows += LEAF
        elif far == 1:
            rows += 3 * HALF
        else:
            rows += 2 * LEAF
    return rows


def bias_of(valid):
    return jnp.where(valid, jnp.float32(0.0), jnp.float32(NEG))


def gathered_pieces(seq_size, far_rows, wide):
    me = lax.axis_index("seq")
    pieces = []
    for far in range(1, seq_size.bit_length() - 1):
        span = 1 << far
        group = me >> far
        parity = (me >> (far - 1)) & 1
        blocks = seq_size >> far

        def block(number, span=span, far=far):
            found = far_rows[pl.ds(number * span, span)].reshape(span * HALF, far_rows.shape[2])
            for _ in range(far - 1):
                found = average_pairs(found, wide)
            return found

        if blocks == 2:
            rows = block(1 - group)
            first = bias_of((group == 1) | (parity == 0))
            second = bias_of((group == 0) | (parity == 1))
            pieces += [(rows[:HALF], first), (rows[HALF:], second)]
        elif far == 1:
            third = jnp.where(parity == 0, me + 3, me - 3)
            for peer in (me - 2, me + 2, third):
                ok = (peer >= 0) & (peer < seq_size)
                pieces.append((far_rows[jnp.clip(peer, 0, seq_size - 1)], bias_of(ok)))
        else:
            lower = block(jnp.maximum(group - 1, 0))
            upper = block(jnp.minimum(group + 1, blocks - 1))
            has_lower, has_upper = group >= 1, group + 1 < blocks
            pieces += [
                (lower[:HALF], bias_of(has_lower)),
                (lower[HALF:], bias_of(has_lower & (parity == 1))),
                (upper[:HALF], bias_of(has_upper & (parity == 0))),
                (upper[HALF:], bias_of(has_upper)),
            ]
    return pieces


def early_pieces(beside, lower):
    me = lax.axis_index("seq")
    has_beside = jnp.where((me & 1) == 1, me >= 2, me < 6)
    return [(beside, bias_of(has_beside)), (lower, None)]


def late_pieces(second, third, fourth):
    pair = lax.axis_index("seq") >> 1
    return [
        (jnp.where(pair == 2, third[...], second[...]), None),
        (jnp.where(pair == 0, third[...], fourth[...]), None),
    ]


def place(pieces, values, keys):
    at = 0
    width = values.shape[1]
    total_rows = values.shape[0]
    position = lax.broadcasted_iota(jnp.int32, (1, total_rows), 1)
    bias = jnp.zeros((1, total_rows), jnp.float32)
    for rows, value in pieces:
        count = rows.shape[0]
        keys[at : at + count] = rows[:, :width]
        values[at : at + count] = rows[:, width:]
        if value is not None:
            bias = jnp.where((position >= at) & (position < at + count), value, bias)
        at += count
    return bias


def split_heads(rows):
    first_head = lax.broadcasted_iota(jnp.int32, (1, rows.shape[1]), 1) < HD
    none = jnp.zeros_like(rows)
    return jnp.concatenate(
        [jnp.where(first_head, rows, none), jnp.where(first_head, none, rows)], axis=0
    )


def scores_of(queries, keys):
    return lax.dot_general(
        queries, keys[...], (((1,), (1,)), ((), ())), preferred_element_type=jnp.float32
    )


def near_kernel(seq_size, queries, own, inner, outer, *rest):
    *beside, scores, values, shared, keys, wide = rest
    me = lax.axis_index("seq")
    odd = me & 1
    from_inner, from_outer = inner[...], outer[...]
    before = jnp.where(odd == 1, from_inner, from_outer)
    after = jnp.where(odd == 1, from_outer, from_inner)
    edge_before, edge_after = before[:LEAF], after[:LEAF]
    far_half_after = after[LEAF:]
    shared[:HALF] = before[LEAF:]
    for rows in beside:
        shared[HALF:] = rows[...]
    near_half_before = average_pairs(edge_before, wide)
    near_half_after = average_pairs(edge_after, wide)
    has_before, has_after = bias_of(me >= 1), bias_of(me + 1 < seq_size)
    for leaf in range(2):
        if leaf == 0:
            near = [
                (edge_before, has_before),
                (own[...], None),
                (near_half_after, has_after),
                (far_half_after, has_after),
            ]
        else:
            near = [
                (own[...], None),
                (edge_after, has_after),
                (near_half_before, has_before),
                (far_half_after, has_after),
            ]
        bias = place(near, values.at[leaf], keys)
        rows = split_heads(queries[leaf * LEAF : (leaf + 1) * LEAF])
        scores[leaf] = scores_of(rows, keys) + bias


def mid_kernel(queries, shared, *rest):
    *early, scores, values, keys = rest
    pieces = [(shared[:HALF], bias_of(lax.axis_index("seq") >= 1))]
    if early:
        pieces += early_pieces(shared[HALF:], *early)
    bias = place(pieces, values, keys)
    for leaf in range(2):
        rows = split_heads(queries[leaf * LEAF : (leaf + 1) * LEAF])
        scores[leaf] = scores_of(rows, keys) + bias


def attend_leaf(leaf, queries, scored, keys, values, bias, same, other):
    first_head = lax.broadcasted_iota(jnp.int32, (1, values.shape[1]), 1) < HD
    exponent = math.log2(math.e) / math.sqrt(HD)
    rows = split_heads(queries[pl.ds(pl.multiple_of(leaf * LEAF, LEAF), LEAF)])
    near_scores, near_values, mid_scores, mid_values = scored
    parts = [
        (near_scores[leaf], near_values[leaf]),
        (mid_scores[leaf], mid_values[...]),
        (scores_of(rows, keys) + bias, values[...]),
    ]
    peak = functools.reduce(
        jnp.maximum, [jnp.max(scores, axis=1, keepdims=True) for scores, _ in parts]
    )
    total, numer = 0.0, 0.0
    for scores, part_values in parts:
        weights = jnp.exp2((scores - peak) * exponent)
        total = total + jnp.sum(weights, axis=1, keepdims=True)
        numer = numer + jnp.dot(
            weights.astype(jnp.bfloat16), part_values, preferred_element_type=jnp.float32
        )
    mean = numer / total
    attended = jnp.where(first_head, mean[:LEAF], mean[LEAF:]).astype(jnp.bfloat16)
    second = (lax.axis_index("head") & 1) == 1
    same[:HALF] = jnp.where(second, attended[HALF:], attended[:HALF])
    other[:HALF] = jnp.where(second, attended[:HALF], attended[HALF:])


def leaves_kernel(seq_size, paired, queries, near_scores, near_values, mid_scores, mid_values, *rest):
    *late, same, other, keys, values, bias, wide = rest
    pieces = late_pieces(*late) if paired else gathered_pieces(seq_size, late[0], wide)
    bias[...] = jnp.broadcast_to(place(pieces, values, keys), bias.shape)
    leaf = (lax.axis_index("head") >> 1) ^ 1
    scored = (near_scores, near_values, mid_scores, mid_values)
    attend_leaf(leaf, queries, scored, keys, values, bias[:1], same, other)
    for share in (same, other):
        share[HALF:] = jnp.zeros((PAD, share.shape[1]), share.dtype)


def stays_kernel(
    queries, near_scores, near_values, mid_scores, mid_values, keys, values, bias, same, other
):
    leaf = lax.axis_index("head") >> 1
    scored = (near_scores, near_values, mid_scores, mid_values)
    attend_leaf(leaf, queries, scored, keys, values, bias[:1], same, other)


def side_by_side(same, other, rows, columns):
    second = (lax.axis_index("head") & 1) == 1
    width = same.shape[1]
    columns[:, :width] = jnp.where(second, other[:rows], same[:rows])
    columns[:, width:] = jnp.where(second, same[:rows], other[:rows])
    return columns[...]


def chip_rows(weight, chip, count):
    return weight[pl.ds(pl.multiple_of(chip * count, count), count)]


def begin_kernel(same, other, weight, partial, columns):
    chip = lax.axis_index("head") >> 1
    shares = side_by_side(same, other, partial.shape[0], columns)
    partial[...] = jnp.dot(
        shares, chip_rows(weight, chip, columns.shape[1]), preferred_element_type=jnp.float32
    )


def project_kernel(partial, other, same, weight, mixed, columns):
    chip = (lax.axis_index("head") >> 1) ^ 1
    shares = side_by_side(same, other, partial.shape[0], columns)
    total = partial[...] + jnp.dot(
        shares, chip_rows(weight, chip, columns.shape[1]), preferred_element_type=jnp.float32
    )
    mixed[...] = total.astype(mixed.dtype)


VMEM = pl.BlockSpec(memory_space=pltpu.VMEM)
HBM = pl.BlockSpec(memory_space=pltpu.HBM)


def kernel_call(body, name, megabytes, ins, outs, scratch, flops=0):
    shapes = tuple(
        out if isinstance(out, jax.ShapeDtypeStruct) else jax.ShapeDtypeStruct(out, jnp.bfloat16)
        for out in outs
    )
    return pl.pallas_call(
        body,
        out_shape=shapes,
        in_specs=ins,
        out_specs=(VMEM,) * len(outs),
        scratch_shapes=scratch,
        compiler_params=pltpu.CompilerParams(vmem_limit_bytes=megabytes << 20),
        cost_estimate=pl.CostEstimate(flops=flops, bytes_accessed=1 << 20, transcendentals=0),
        name=name,
    )


def shards(queries, keys, values, out_weight):
    tokens, width = queries.shape
    seq_size = lax.axis_size("seq")
    head_size = lax.axis_size("head")
    pair_width = 2 * width
    paired = seq_size == 8
    wide_rows = 2 * LEAF if paired else max(2 * LEAF, seq_size // 2 * HALF)
    wide = pltpu.VMEM((wide_rows, width), jnp.float32)

    def swap(array, bit, axis="seq"):
        return lax.ppermute(array, axis, [(i, i ^ bit) for i in range(lax.axis_size(axis))])

    own_queries, own, inner, outer, quarter = kernel_call(
        functools.partial(pack_kernel, not paired),
        "pack",
        16,
        [HBM] * 3,
        [
            (tokens, width),
            (tokens, pair_width),
            (LEAF + HALF, pair_width),
            (LEAF + HALF, pair_width),
            (HALF, pair_width) if paired else (seq_size, HALF, pair_width),
        ],
        [wide, pltpu.SemaphoreType.DMA((3,))],
    )(*(pltpu.with_memory_space_constraint(array, pltpu.HBM) for array in (queries, keys, values)))
    inner = swap(inner, 1)

    def to_spans(array, targets):
        return lax.ppermute(
            array,
            ("seq", "head"),
            [
                (s * head_size + h, t * head_size + (h if s != t else h ^ 1))
                for s, t in enumerate(targets)
                for h in range(head_size)
            ],
        )

    last = seq_size - 1
    outer = to_spans(outer, [s if s in (0, last) else s + 1 if s & 1 else s - 1 for s in range(seq_size)])
    if paired:
        upward, third, fourth, eighth = kernel_call(
            join_kernel,
            "join",
            8,
            [VMEM] * 2,
            [(HALF, pair_width)] * 4,
            [wide],
            flops=55 * 10**7,
        )(swap(quarter, 1), quarter)

        def over_pairs(array, targets):
            return to_spans(array, [2 * t + x for t in targets for x in range(2)])

        cycle = [(i, i + 2 if i & 1 else i - 2) for i in range(1, seq_size - 1)]
        cycle += [(0, 1), (seq_size - 1, seq_size - 2)]
        beside = (lax.ppermute(quarter, "seq", cycle),)
        early = (over_pairs(upward, (1, 2, 3, 0)),)
        late = (
            over_pairs(eighth, (3, 2, 0, 1)),
            over_pairs(third, (2, 0, 3, 1)),
            over_pairs(fourth, (0, 3, 1, 2)),
        )
    else:
        beside, early = (), ()
        late = (lax.all_to_all(quarter, "seq", split_axis=0, concat_axis=0),)
    share = tokens // head_size
    near_scores, near_values, shared = kernel_call(
        functools.partial(near_kernel, seq_size),
        "near",
        16,
        [VMEM] * (4 + len(beside)),
        [
            jax.ShapeDtypeStruct((2, 2 * LEAF, NEAR_ROWS), jnp.float32),
            (2, NEAR_ROWS, width),
            (HALF * (1 + len(beside)), pair_width),
        ],
        [pltpu.VMEM((NEAR_ROWS, width), jnp.bfloat16), wide],
        flops=8 * LEAF * NEAR_ROWS * width,
    )(own_queries, own, inner, outer, *beside)
    mid_rows = 3 * HALF if paired else HALF
    mid_scores, mid_values = kernel_call(
        mid_kernel,
        "mid",
        8,
        [VMEM] * (2 + len(early)),
        [jax.ShapeDtypeStruct((2, 2 * LEAF, mid_rows), jnp.float32), (mid_rows, width)],
        [pltpu.VMEM((mid_rows, width), jnp.bfloat16)],
        flops=10**9,
    )(own_queries, shared, *early)
    scored = (near_scores, near_values, mid_scores, mid_values)
    last_rows = last_row_count(seq_size, paired)
    leaf_flops = 8 * LEAF * (NEAR_ROWS + mid_rows + last_rows) * width
    share_2, share_3, far_keys, far_values, far_bias = kernel_call(
        functools.partial(leaves_kernel, seq_size, paired),
        "leaves",
        24,
        [VMEM] * (5 + len(late)),
        [
            (share + PAD, width),
            (share + PAD, width),
            (last_rows, width),
            (last_rows, width),
            jax.ShapeDtypeStruct((8, last_rows), jnp.float32),
        ],
        [wide],
        flops=leaf_flops,
    )(own_queries, *scored, *late)
    share_0, share_1 = kernel_call(
        stays_kernel, "stays", 16, [VMEM] * 8, [(share, width)] * 2, [], flops=leaf_flops
    )(own_queries, *scored, far_keys, far_values, far_bias)
    columns = pltpu.VMEM((share, pair_width), jnp.bfloat16)
    part_3, part_2 = swap(share_3, 3, "head"), swap(share_2, 2, "head")
    (partial,) = kernel_call(
        begin_kernel,
        "begin",
        8,
        [VMEM] * 3,
        [jax.ShapeDtypeStruct((share, out_weight.shape[1]), jnp.float32)],
        [columns],
    )(share_0, swap(share_1, 1, "head"), out_weight)
    (mixed,) = kernel_call(
        project_kernel, "project", 8, [VMEM] * 4, [(share, out_weight.shape[1])], [columns]
    )(partial, part_3, part_2, out_weight)
    return mixed


def solution(mesh):
    in_specs = (P("seq", "head"), P("seq", "head"), P("seq", "head"), P())
    out_specs = P(("seq", "head"), None)
    return jax.shard_map(shards, mesh=mesh, in_specs=in_specs, out_specs=out_specs, check_vma=False)
```

```python
import functools
import math

import jax
import jax.numpy as jnp
from jax import lax
from jax.experimental import pallas as pl
from jax.experimental.pallas import tpu as pltpu
from jax.sharding import PartitionSpec as P

HD = 64
LEAF = 128
HALF = LEAF // 2
NEG = -math.inf


def average_pairs(rows, wide):
    count = rows.shape[0]
    halves = []
    for low in range(0, rows.shape[1], LEAF):
        wide[:count] = rows[:, low : low + LEAF].astype(jnp.float32)
        even = wide[pl.ds(0, count // 2, stride=2), :]
        odd = wide[pl.ds(1, count // 2, stride=2), :]
        halves.append((0.5 * (even + odd)).astype(jnp.bfloat16))
    return jnp.concatenate(halves, axis=1)


def pack_kernel(far_shares, queries, keys, values, own_queries, own, inner, outer, quarter, wide, arrived):
    width = keys.shape[1]
    copies = [
        pltpu.make_async_copy(keys, own.at[:, :width], arrived.at[0]),
        pltpu.make_async_copy(values, own.at[:, width:], arrived.at[1]),
        pltpu.make_async_copy(queries, own_queries, arrived.at[2]),
    ]
    for copy in copies:
        copy.start()
    me = lax.axis_index("seq")
    odd = me & 1
    for copy in copies:
        copy.wait()
    rows = own[...]
    low, high = rows[:LEAF], rows[LEAF:]
    level_one = average_pairs(rows, wide)
    level_two = average_pairs(level_one, wide)
    first, second = level_one[:HALF], level_one[HALF:]
    inner[:LEAF] = jnp.where(odd == 1, low, high)
    inner[LEAF:] = jnp.where(odd == 1, second, first)
    outer[:LEAF] = jnp.where(odd == 1, high, low)
    outer[LEAF:] = jnp.where(odd == 1, first, second)
    if far_shares:
        for peer in range(quarter.shape[0]):
            quarter[peer] = level_two
    else:
        quarter[...] = level_two


def join_kernel(theirs, quarter, upward, third, fourth, eighth, wide):
    me = lax.axis_index("seq")
    odd = me & 1
    pair = me >> 1
    first = jnp.where(odd == 1, theirs[...], quarter[...])
    second = jnp.where(odd == 1, quarter[...], theirs[...])
    level_three = average_pairs(jnp.concatenate([first, second], axis=0), wide)
    upward[...] = jnp.where(pair == 3, level_three, first)
    third[...] = jnp.where(pair == 1, second, level_three)
    fourth[...] = jnp.where(pair == 1, level_three, second)
    eighth[...] = level_three


NEAR_ROWS = 4 * LEAF
PAD = 16


def last_row_count(seq_size, paired):
    if paired:
        return LEAF
    rows = 0
    for far in range(1, seq_size.bit_length() - 1):
        if seq_size >> far == 2:
            rows += LEAF
        elif far == 1:
            rows += 3 * HALF
        else:
            rows += 2 * LEAF
    return rows


def bias_of(valid):
    return jnp.where(valid, jnp.float32(0.0), jnp.float32(NEG))


def gathered_pieces(seq_size, far_rows, wide):
    me = lax.axis_index("seq")
    pieces = []
    for far in range(1, seq_size.bit_length() - 1):
        span = 1 << far
        group = me >> far
        parity = (me >> (far - 1)) & 1
        blocks = seq_size >> far

        def block(number, span=span, far=far):
            found = far_rows[pl.ds(number * span, span)].reshape(span * HALF, far_rows.shape[2])
            for _ in range(far - 1):
                found = average_pairs(found, wide)
            return found

        if blocks == 2:
            rows = block(1 - group)
            first = bias_of((group == 1) | (parity == 0))
            second = bias_of((group == 0) | (parity == 1))
            pieces += [(rows[:HALF], first), (rows[HALF:], second)]
        elif far == 1:
            third = jnp.where(parity == 0, me + 3, me - 3)
            for peer in (me - 2, me + 2, third):
                ok = (peer >= 0) & (peer < seq_size)
                pieces.append((far_rows[jnp.clip(peer, 0, seq_size - 1)], bias_of(ok)))
        else:
            lower = block(jnp.maximum(group - 1, 0))
            upper = block(jnp.minimum(group + 1, blocks - 1))
            has_lower, has_upper = group >= 1, group + 1 < blocks
            pieces += [
                (lower[:HALF], bias_of(has_lower)),
                (lower[HALF:], bias_of(has_lower & (parity == 1))),
                (upper[:HALF], bias_of(has_upper & (parity == 0))),
                (upper[HALF:], bias_of(has_upper)),
            ]
    return pieces


def early_pieces(beside, lower):
    me = lax.axis_index("seq")
    has_beside = jnp.where((me & 1) == 1, me >= 2, me < 6)
    return [(beside, bias_of(has_beside)), (lower, None)]


def late_pieces(second, third, fourth):
    pair = lax.axis_index("seq") >> 1
    return [
        (jnp.where(pair == 2, third[...], second[...]), None),
        (jnp.where(pair == 0, third[...], fourth[...]), None),
    ]


def place(pieces, values, keys):
    at = 0
    width = values.shape[1]
    total_rows = values.shape[0]
    position = lax.broadcasted_iota(jnp.int32, (1, total_rows), 1)
    bias = jnp.zeros((1, total_rows), jnp.float32)
    for rows, value in pieces:
        count = rows.shape[0]
        keys[at : at + count] = rows[:, :width]
        values[at : at + count] = rows[:, width:]
        if value is not None:
            bias = jnp.where((position >= at) & (position < at + count), value, bias)
        at += count
    return bias


def split_heads(rows):
    first_head = lax.broadcasted_iota(jnp.int32, (1, rows.shape[1]), 1) < HD
    none = jnp.zeros_like(rows)
    return jnp.concatenate(
        [jnp.where(first_head, rows, none), jnp.where(first_head, none, rows)], axis=0
    )


def scores_of(queries, keys):
    return lax.dot_general(
        queries, keys[...], (((1,), (1,)), ((), ())), preferred_element_type=jnp.float32
    )


def near_kernel(seq_size, queries, own, outer, inner, *rest):
    *beside, scores, values, shared, keys, wide = rest
    me = lax.axis_index("seq")
    odd = me & 1
    from_inner, from_outer = inner[...], outer[...]
    before = jnp.where(odd == 1, from_inner, from_outer)
    after = jnp.where(odd == 1, from_outer, from_inner)
    edge_before, edge_after = before[:LEAF], after[:LEAF]
    far_half_after = after[LEAF:]
    shared[:HALF] = before[LEAF:]
    for rows in beside:
        shared[HALF:] = rows[...]
    near_half_before = average_pairs(edge_before, wide)
    near_half_after = average_pairs(edge_after, wide)
    has_before, has_after = bias_of(me >= 1), bias_of(me + 1 < seq_size)
    for leaf in range(2):
        if leaf == 0:
            near = [
                (edge_before, has_before),
                (own[...], None),
                (near_half_after, has_after),
                (far_half_after, has_after),
            ]
        else:
            near = [
                (own[...], None),
                (edge_after, has_after),
                (near_half_before, has_before),
                (far_half_after, has_after),
            ]
        bias = place(near, values.at[leaf], keys)
        rows = split_heads(queries[leaf * LEAF : (leaf + 1) * LEAF])
        scores[leaf] = scores_of(rows, keys) + bias


def mid_kernel(queries, shared, *rest):
    *early, scores, values, keys = rest
    pieces = [(shared[:HALF], bias_of(lax.axis_index("seq") >= 1))]
    if early:
        pieces += early_pieces(shared[HALF:], *early)
    bias = place(pieces, values, keys)
    for leaf in range(2):
        rows = split_heads(queries[leaf * LEAF : (leaf + 1) * LEAF])
        scores[leaf] = scores_of(rows, keys) + bias


def attend_leaf(leaf, queries, scored, keys, values, bias, same, other):
    first_head = lax.broadcasted_iota(jnp.int32, (1, values.shape[1]), 1) < HD
    exponent = math.log2(math.e) / math.sqrt(HD)
    rows = split_heads(queries[pl.ds(pl.multiple_of(leaf * LEAF, LEAF), LEAF)])
    near_scores, near_values, mid_scores, mid_values = scored
    parts = [
        (near_scores[leaf], near_values[leaf]),
        (mid_scores[leaf], mid_values[...]),
        (scores_of(rows, keys) + bias, values[...]),
    ]
    peak = functools.reduce(
        jnp.maximum, [jnp.max(scores, axis=1, keepdims=True) for scores, _ in parts]
    )
    total, numer = 0.0, 0.0
    for scores, part_values in parts:
        weights = jnp.exp2((scores - peak) * exponent)
        total = total + jnp.sum(weights, axis=1, keepdims=True)
        numer = numer + jnp.dot(
            weights.astype(jnp.bfloat16), part_values, preferred_element_type=jnp.float32
        )
    mean = numer / total
    attended = jnp.where(first_head, mean[:LEAF], mean[LEAF:]).astype(jnp.bfloat16)
    second = (lax.axis_index("head") & 1) == 1
    same[:HALF] = jnp.where(second, attended[HALF:], attended[:HALF])
    other[:HALF] = jnp.where(second, attended[:HALF], attended[HALF:])


def leaves_kernel(seq_size, paired, queries, near_scores, near_values, mid_scores, mid_values, *rest):
    *late, same, other, keys, values, bias, wide = rest
    pieces = late_pieces(*late) if paired else gathered_pieces(seq_size, late[0], wide)
    bias[...] = jnp.broadcast_to(place(pieces, values, keys), bias.shape)
    leaf = (lax.axis_index("head") >> 1) ^ 1
    scored = (near_scores, near_values, mid_scores, mid_values)
    attend_leaf(leaf, queries, scored, keys, values, bias[:1], same, other)
    for share in (same, other):
        share[HALF:] = jnp.zeros((PAD, share.shape[1]), share.dtype)


def stays_kernel(
    queries, near_scores, near_values, mid_scores, mid_values, keys, values, bias, same, other
):
    leaf = lax.axis_index("head") >> 1
    scored = (near_scores, near_values, mid_scores, mid_values)
    attend_leaf(leaf, queries, scored, keys, values, bias[:1], same, other)


def side_by_side(same, other, rows, columns):
    second = (lax.axis_index("head") & 1) == 1
    width = same.shape[1]
    columns[:, :width] = jnp.where(second, other[:rows], same[:rows])
    columns[:, width:] = jnp.where(second, same[:rows], other[:rows])
    return columns[...]


def chip_rows(weight, chip, count):
    return weight[pl.ds(pl.multiple_of(chip * count, count), count)]


def begin_kernel(same, other, weight, partial, columns):
    chip = lax.axis_index("head") >> 1
    shares = side_by_side(same, other, partial.shape[0], columns)
    partial[...] = jnp.dot(
        shares, chip_rows(weight, chip, columns.shape[1]), preferred_element_type=jnp.float32
    )


def project_kernel(partial, other, same, weight, mixed, columns):
    chip = (lax.axis_index("head") >> 1) ^ 1
    shares = side_by_side(same, other, partial.shape[0], columns)
    total = partial[...] + jnp.dot(
        shares, chip_rows(weight, chip, columns.shape[1]), preferred_element_type=jnp.float32
    )
    mixed[...] = total.astype(mixed.dtype)


VMEM = pl.BlockSpec(memory_space=pltpu.VMEM)
HBM = pl.BlockSpec(memory_space=pltpu.HBM)


def kernel_call(body, name, megabytes, ins, outs, scratch, flops=0):
    shapes = tuple(
        out if isinstance(out, jax.ShapeDtypeStruct) else jax.ShapeDtypeStruct(out, jnp.bfloat16)
        for out in outs
    )
    return pl.pallas_call(
        body,
        out_shape=shapes,
        in_specs=ins,
        out_specs=(VMEM,) * len(outs),
        scratch_shapes=scratch,
        compiler_params=pltpu.CompilerParams(vmem_limit_bytes=megabytes << 20),
        cost_estimate=pl.CostEstimate(flops=flops, bytes_accessed=1 << 20, transcendentals=0),
        name=name,
    )


def shards(queries, keys, values, out_weight):
    tokens, width = queries.shape
    seq_size = lax.axis_size("seq")
    head_size = lax.axis_size("head")
    pair_width = 2 * width
    paired = seq_size == 8
    wide_rows = 2 * LEAF if paired else max(2 * LEAF, seq_size // 2 * HALF)
    wide = pltpu.VMEM((wide_rows, width), jnp.float32)

    def swap(array, bit, axis="seq"):
        return lax.ppermute(array, axis, [(i, i ^ bit) for i in range(lax.axis_size(axis))])

    own_queries, own, inner, outer, quarter = kernel_call(
        functools.partial(pack_kernel, not paired),
        "pack",
        16,
        [HBM] * 3,
        [
            (tokens, width),
            (tokens, pair_width),
            (LEAF + HALF, pair_width),
            (LEAF + HALF, pair_width),
            (HALF, pair_width) if paired else (seq_size, HALF, pair_width),
        ],
        [wide, pltpu.SemaphoreType.DMA((3,))],
    )(*(pltpu.with_memory_space_constraint(array, pltpu.HBM) for array in (queries, keys, values)))
    inner = swap(inner, 1)

    def to_spans(array, targets):
        return lax.ppermute(
            array,
            ("seq", "head"),
            [
                (s * head_size + h, t * head_size + (h if s != t else h ^ 1))
                for s, t in enumerate(targets)
                for h in range(head_size)
            ],
        )

    last = seq_size - 1
    outer = to_spans(outer, [s if s in (0, last) else s + 1 if s & 1 else s - 1 for s in range(seq_size)])
    if paired:
        upward, third, fourth, eighth = kernel_call(
            join_kernel,
            "join",
            8,
            [VMEM] * 2,
            [(HALF, pair_width)] * 4,
            [wide],
            flops=2 * 10**9,
        )(swap(quarter, 1), quarter)

        def over_pairs(array, targets):
            return to_spans(array, [2 * t + x for t in targets for x in range(2)])

        cycle = [(i, i + 2 if i & 1 else i - 2) for i in range(1, seq_size - 1)]
        cycle += [(0, 1), (seq_size - 1, seq_size - 2)]
        beside = (lax.ppermute(quarter, "seq", cycle),)
        early = (over_pairs(upward, (1, 2, 3, 0)),)
        late = (
            over_pairs(eighth, (3, 2, 0, 1)),
            over_pairs(third, (2, 0, 3, 1)),
            over_pairs(fourth, (0, 3, 1, 2)),
        )
    else:
        beside, early = (), ()
        late = (lax.all_to_all(quarter, "seq", split_axis=0, concat_axis=0),)
    share = tokens // head_size
    near_scores, near_values, shared = kernel_call(
        functools.partial(near_kernel, seq_size),
        "near",
        16,
        [VMEM] * (4 + len(beside)),
        [
            jax.ShapeDtypeStruct((2, 2 * LEAF, NEAR_ROWS), jnp.float32),
            (2, NEAR_ROWS, width),
            (HALF * (1 + len(beside)), pair_width),
        ],
        [pltpu.VMEM((NEAR_ROWS, width), jnp.bfloat16), wide],
        flops=8 * LEAF * NEAR_ROWS * width,
    )(own_queries, own, outer, inner, *beside)
    mid_rows = 3 * HALF if paired else HALF
    mid_scores, mid_values = kernel_call(
        mid_kernel,
        "mid",
        8,
        [VMEM] * (2 + len(early)),
        [jax.ShapeDtypeStruct((2, 2 * LEAF, mid_rows), jnp.float32), (mid_rows, width)],
        [pltpu.VMEM((mid_rows, width), jnp.bfloat16)],
        flops=10**9,
    )(own_queries, shared, *early)
    scored = (near_scores, near_values, mid_scores, mid_values)
    last_rows = last_row_count(seq_size, paired)
    leaf_flops = 8 * LEAF * (NEAR_ROWS + mid_rows + last_rows) * width
    share_2, share_3, far_keys, far_values, far_bias = kernel_call(
        functools.partial(leaves_kernel, seq_size, paired),
        "leaves",
        24,
        [VMEM] * (5 + len(late)),
        [
            (share + PAD, width),
            (share + PAD, width),
            (last_rows, width),
            (last_rows, width),
            jax.ShapeDtypeStruct((8, last_rows), jnp.float32),
        ],
        [wide],
        flops=leaf_flops,
    )(own_queries, *scored, *late)
    share_0, share_1 = kernel_call(
        stays_kernel, "stays", 16, [VMEM] * 8, [(share, width)] * 2, [], flops=leaf_flops
    )(own_queries, *scored, far_keys, far_values, far_bias)
    columns = pltpu.VMEM((share, pair_width), jnp.bfloat16)
    part_3, part_2 = swap(share_3, 3, "head"), swap(share_2, 2, "head")
    (partial,) = kernel_call(
        begin_kernel,
        "begin",
        8,
        [VMEM] * 3,
        [jax.ShapeDtypeStruct((share, out_weight.shape[1]), jnp.float32)],
        [columns],
    )(share_0, swap(share_1, 1, "head"), out_weight)
    (mixed,) = kernel_call(
        project_kernel, "project", 8, [VMEM] * 4, [(share, out_weight.shape[1])], [columns]
    )(partial, part_3, part_2, out_weight)
    return mixed


def solution(mesh):
    in_specs = (P("seq", "head"), P("seq", "head"), P("seq", "head"), P())
    out_specs = P(("seq", "head"), None)
    return jax.shard_map(shards, mesh=mesh, in_specs=in_specs, out_specs=out_specs, check_vma=False)
```

```python
import functools
import math

import jax
import jax.numpy as jnp
from jax import lax
from jax.experimental import pallas as pl
from jax.experimental.pallas import tpu as pltpu
from jax.sharding import PartitionSpec as P

HD = 64
LEAF = 128
HALF = LEAF // 2
NEG = -math.inf


def average_pairs(rows, wide):
    count = rows.shape[0]
    halves = []
    for low in range(0, rows.shape[1], LEAF):
        wide[:count] = rows[:, low : low + LEAF].astype(jnp.float32)
        even = wide[pl.ds(0, count // 2, stride=2), :]
        odd = wide[pl.ds(1, count // 2, stride=2), :]
        halves.append((0.5 * (even + odd)).astype(jnp.bfloat16))
    return jnp.concatenate(halves, axis=1)


def pack_kernel(far_shares, queries, keys, values, own_queries, own, level_one, quarter, wide, arrived):
    width = keys.shape[1]
    copies = [
        pltpu.make_async_copy(keys, own.at[:, :width], arrived.at[0]),
        pltpu.make_async_copy(values, own.at[:, width:], arrived.at[1]),
        pltpu.make_async_copy(queries, own_queries, arrived.at[2]),
    ]
    for copy in copies:
        copy.start()
    for copy in copies:
        copy.wait()
    level_one[...] = average_pairs(own[...], wide)
    level_two = average_pairs(level_one[...], wide)
    if far_shares:
        for peer in range(quarter.shape[0]):
            quarter[peer] = level_two
    else:
        quarter[...] = level_two


def edges_kernel(own, level_one, inner, outer):
    odd = lax.axis_index("seq") & 1
    low, high = own[:LEAF], own[LEAF:]
    first, second = level_one[:HALF], level_one[HALF:]
    inner[:LEAF] = jnp.where(odd == 1, low, high)
    inner[LEAF:] = jnp.where(odd == 1, second, first)
    outer[:LEAF] = jnp.where(odd == 1, high, low)
    outer[LEAF:] = jnp.where(odd == 1, first, second)


def join_kernel(theirs, quarter, upward, downward, eighth, wide):
    me = lax.axis_index("seq")
    odd = me & 1
    first = jnp.where(odd == 1, theirs[...], quarter[...])
    second = jnp.where(odd == 1, quarter[...], theirs[...])
    level_three = average_pairs(jnp.concatenate([first, second], axis=0), wide)
    upward[...] = jnp.where(me >= 6, level_three, first)
    downward[...] = jnp.where(me < 2, level_three, second)
    eighth[...] = level_three


NEAR_ROWS = 4 * LEAF
PAD = 16


def last_row_count(seq_size, paired):
    if paired:
        return HALF
    rows = 0
    for far in range(1, seq_size.bit_length() - 1):
        if seq_size >> far == 2:
            rows += LEAF
        elif far == 1:
            rows += 3 * HALF
        else:
            rows += 2 * LEAF
    return rows


def bias_of(valid):
    return jnp.where(valid, jnp.float32(0.0), jnp.float32(NEG))


def gathered_pieces(seq_size, far_rows, wide):
    me = lax.axis_index("seq")
    pieces = []
    for far in range(1, seq_size.bit_length() - 1):
        span = 1 << far
        group = me >> far
        parity = (me >> (far - 1)) & 1
        blocks = seq_size >> far

        def block(number, span=span, far=far):
            found = far_rows[pl.ds(number * span, span)].reshape(span * HALF, far_rows.shape[2])
            for _ in range(far - 1):
                found = average_pairs(found, wide)
            return found

        if blocks == 2:
            rows = block(1 - group)
            first = bias_of((group == 1) | (parity == 0))
            second = bias_of((group == 0) | (parity == 1))
            pieces += [(rows[:HALF], first), (rows[HALF:], second)]
        elif far == 1:
            third = jnp.where(parity == 0, me + 3, me - 3)
            for peer in (me - 2, me + 2, third):
                ok = (peer >= 0) & (peer < seq_size)
                pieces.append((far_rows[jnp.clip(peer, 0, seq_size - 1)], bias_of(ok)))
        else:
            lower = block(jnp.maximum(group - 1, 0))
            upper = block(jnp.minimum(group + 1, blocks - 1))
            has_lower, has_upper = group >= 1, group + 1 < blocks
            pieces += [
                (lower[:HALF], bias_of(has_lower)),
                (lower[HALF:], bias_of(has_lower & (parity == 1))),
                (upper[:HALF], bias_of(has_upper & (parity == 0))),
                (upper[HALF:], bias_of(has_upper)),
            ]
    return pieces


def early_pieces(beside, lower, eighth):
    me = lax.axis_index("seq")
    has_beside = jnp.where((me & 1) == 1, me >= 2, me < 6)
    return [(beside, bias_of(has_beside)), (lower, None), (eighth, None)]


def place(pieces, values, keys):
    at = 0
    width = values.shape[1]
    total_rows = values.shape[0]
    position = lax.broadcasted_iota(jnp.int32, (1, total_rows), 1)
    bias = jnp.zeros((1, total_rows), jnp.float32)
    for rows, value in pieces:
        count = rows.shape[0]
        keys[at : at + count] = rows[:, :width]
        values[at : at + count] = rows[:, width:]
        if value is not None:
            bias = jnp.where((position >= at) & (position < at + count), value, bias)
        at += count
    return bias


def split_heads(rows):
    first_head = lax.broadcasted_iota(jnp.int32, (1, rows.shape[1]), 1) < HD
    none = jnp.zeros_like(rows)
    return jnp.concatenate(
        [jnp.where(first_head, rows, none), jnp.where(first_head, none, rows)], axis=0
    )


def scores_of(queries, keys):
    return lax.dot_general(
        queries, keys[...], (((1,), (1,)), ((), ())), preferred_element_type=jnp.float32
    )


def near_kernel(seq_size, queries, own, inner, outer, *rest):
    *beside, scores, values, shared, keys, wide = rest
    me = lax.axis_index("seq")
    odd = me & 1
    from_inner, from_outer = inner[...], outer[...]
    before = jnp.where(odd == 1, from_inner, from_outer)
    after = jnp.where(odd == 1, from_outer, from_inner)
    edge_before, edge_after = before[:LEAF], after[:LEAF]
    far_half_after = after[LEAF:]
    shared[:HALF] = before[LEAF:]
    for rows in beside:
        shared[HALF:] = rows[...]
    near_half_before = average_pairs(edge_before, wide)
    near_half_after = average_pairs(edge_after, wide)
    has_before, has_after = bias_of(me >= 1), bias_of(me + 1 < seq_size)
    for leaf in range(2):
        if leaf == 0:
            near = [
                (edge_before, has_before),
                (own[...], None),
                (near_half_after, has_after),
                (far_half_after, has_after),
            ]
        else:
            near = [
                (own[...], None),
                (edge_after, has_after),
                (near_half_before, has_before),
                (far_half_after, has_after),
            ]
        bias = place(near, values.at[leaf], keys)
        rows = split_heads(queries[leaf * LEAF : (leaf + 1) * LEAF])
        scores[leaf] = scores_of(rows, keys) + bias


def mid_kernel(queries, shared, *rest):
    *early, scores, values, keys = rest
    pieces = [(shared[:HALF], bias_of(lax.axis_index("seq") >= 1))]
    if early:
        pieces += early_pieces(shared[HALF:], *early)
    bias = place(pieces, values, keys)
    for leaf in range(2):
        rows = split_heads(queries[leaf * LEAF : (leaf + 1) * LEAF])
        scores[leaf] = scores_of(rows, keys) + bias


def attend_leaf(leaf, queries, scored, keys, values, bias, same, other):
    first_head = lax.broadcasted_iota(jnp.int32, (1, values.shape[1]), 1) < HD
    exponent = math.log2(math.e) / math.sqrt(HD)
    rows = split_heads(queries[pl.ds(pl.multiple_of(leaf * LEAF, LEAF), LEAF)])
    near_scores, near_values, mid_scores, mid_values = scored
    parts = [
        (near_scores[leaf], near_values[leaf]),
        (mid_scores[leaf], mid_values[...]),
        (scores_of(rows, keys) + bias, values[...]),
    ]
    peak = functools.reduce(
        jnp.maximum, [jnp.max(scores, axis=1, keepdims=True) for scores, _ in parts]
    )
    total, numer = 0.0, 0.0
    for scores, part_values in parts:
        weights = jnp.exp2((scores - peak) * exponent)
        total = total + jnp.sum(weights, axis=1, keepdims=True)
        numer = numer + jnp.dot(
            weights.astype(jnp.bfloat16), part_values, preferred_element_type=jnp.float32
        )
    mean = numer / total
    attended = jnp.where(first_head, mean[:LEAF], mean[LEAF:]).astype(jnp.bfloat16)
    second = (lax.axis_index("head") & 1) == 1
    same[:HALF] = jnp.where(second, attended[HALF:], attended[:HALF])
    other[:HALF] = jnp.where(second, attended[:HALF], attended[HALF:])


def leaves_kernel(seq_size, paired, queries, near_scores, near_values, mid_scores, mid_values, *rest):
    late, same, other, keys, values, bias, wide = rest
    pieces = [(late, None)] if paired else gathered_pieces(seq_size, late, wide)
    bias[...] = jnp.broadcast_to(place(pieces, values, keys), bias.shape)
    leaf = (lax.axis_index("head") >> 1) ^ 1
    scored = (near_scores, near_values, mid_scores, mid_values)
    attend_leaf(leaf, queries, scored, keys, values, bias[:1], same, other)
    for share in (same, other):
        share[HALF:] = jnp.zeros((PAD, share.shape[1]), share.dtype)


def stays_kernel(
    queries, near_scores, near_values, mid_scores, mid_values, keys, values, bias, same, other
):
    leaf = lax.axis_index("head") >> 1
    scored = (near_scores, near_values, mid_scores, mid_values)
    attend_leaf(leaf, queries, scored, keys, values, bias[:1], same, other)


def side_by_side(same, other, rows, columns):
    second = (lax.axis_index("head") & 1) == 1
    width = same.shape[1]
    columns[:, :width] = jnp.where(second, other[:rows], same[:rows])
    columns[:, width:] = jnp.where(second, same[:rows], other[:rows])
    return columns[...]


def chip_rows(weight, chip, count):
    return weight[pl.ds(pl.multiple_of(chip * count, count), count)]


def begin_kernel(same, other, weight, partial, columns):
    chip = lax.axis_index("head") >> 1
    shares = side_by_side(same, other, partial.shape[0], columns)
    partial[...] = jnp.dot(
        shares, chip_rows(weight, chip, columns.shape[1]), preferred_element_type=jnp.float32
    )


def project_kernel(partial, other, same, weight, mixed, columns):
    chip = (lax.axis_index("head") >> 1) ^ 1
    shares = side_by_side(same, other, partial.shape[0], columns)
    total = partial[...] + jnp.dot(
        shares, chip_rows(weight, chip, columns.shape[1]), preferred_element_type=jnp.float32
    )
    mixed[...] = total.astype(mixed.dtype)


VMEM = pl.BlockSpec(memory_space=pltpu.VMEM)
HBM = pl.BlockSpec(memory_space=pltpu.HBM)


def kernel_call(body, name, megabytes, ins, outs, scratch, flops=0):
    shapes = tuple(
        out if isinstance(out, jax.ShapeDtypeStruct) else jax.ShapeDtypeStruct(out, jnp.bfloat16)
        for out in outs
    )
    return pl.pallas_call(
        body,
        out_shape=shapes,
        in_specs=ins,
        out_specs=(VMEM,) * len(outs),
        scratch_shapes=scratch,
        compiler_params=pltpu.CompilerParams(vmem_limit_bytes=megabytes << 20),
        cost_estimate=pl.CostEstimate(flops=flops, bytes_accessed=1 << 20, transcendentals=0),
        name=name,
    )


def shards(queries, keys, values, out_weight):
    tokens, width = queries.shape
    seq_size = lax.axis_size("seq")
    head_size = lax.axis_size("head")
    pair_width = 2 * width
    paired = seq_size == 8
    wide_rows = 2 * LEAF if paired else max(2 * LEAF, seq_size // 2 * HALF)
    wide = pltpu.VMEM((wide_rows, width), jnp.float32)

    def swap(array, bit, axis="seq"):
        return lax.ppermute(array, axis, [(i, i ^ bit) for i in range(lax.axis_size(axis))])

    own_queries, own, level_one, quarter = kernel_call(
        functools.partial(pack_kernel, not paired),
        "pack",
        16,
        [HBM] * 3,
        [
            (tokens, width),
            (tokens, pair_width),
            (LEAF, pair_width),
            (HALF, pair_width) if paired else (seq_size, HALF, pair_width),
        ],
        [wide, pltpu.SemaphoreType.DMA((3,))],
    )(*(pltpu.with_memory_space_constraint(array, pltpu.HBM) for array in (queries, keys, values)))
    inner, outer = kernel_call(
        edges_kernel, "edges", 8, [VMEM] * 2, [(LEAF + HALF, pair_width)] * 2, []
    )(own, level_one)
    inner = swap(inner, 1)

    def to_spans(array, targets):
        return lax.ppermute(
            array,
            ("seq", "head"),
            [
                (s * head_size + h, t * head_size + (h if s != t else h ^ 1))
                for s, t in enumerate(targets)
                for h in range(head_size)
            ],
        )

    last = seq_size - 1
    outer = to_spans(outer, [s if s in (0, last) else s + 1 if s & 1 else s - 1 for s in range(seq_size)])
    if paired:
        upward, downward, eighth = kernel_call(
            join_kernel,
            "join",
            8,
            [VMEM] * 2,
            [(HALF, pair_width)] * 3,
            [wide],
            flops=2 * 10**9,
        )(swap(quarter, 1), quarter)
        shift = [(i, (i + 2) % seq_size) for i in range(seq_size)]
        cycle = [(i, i + 2 if i & 1 else i - 2) for i in range(1, seq_size - 1)]
        cycle += [(0, 1), (seq_size - 1, seq_size - 2)]
        beside = (lax.ppermute(quarter, "seq", cycle),)
        early = (lax.ppermute(upward, "seq", shift), swap(eighth, 4))
        late = lax.ppermute(downward, "seq", [(target, source) for source, target in shift])
    else:
        beside, early = (), ()
        late = lax.all_to_all(quarter, "seq", split_axis=0, concat_axis=0)
    share = tokens // head_size
    near_scores, near_values, shared = kernel_call(
        functools.partial(near_kernel, seq_size),
        "near",
        16,
        [VMEM] * (4 + len(beside)),
        [
            jax.ShapeDtypeStruct((2, 2 * LEAF, NEAR_ROWS), jnp.float32),
            (2, NEAR_ROWS, width),
            (HALF * (1 + len(beside)), pair_width),
        ],
        [pltpu.VMEM((NEAR_ROWS, width), jnp.bfloat16), wide],
        flops=8 * LEAF * NEAR_ROWS * width,
    )(own_queries, own, inner, outer, *beside)
    mid_rows = 4 * HALF if paired else HALF
    mid_scores, mid_values = kernel_call(
        mid_kernel,
        "mid",
        8,
        [VMEM] * (2 + len(early)),
        [jax.ShapeDtypeStruct((2, 2 * LEAF, mid_rows), jnp.float32), (mid_rows, width)],
        [pltpu.VMEM((mid_rows, width), jnp.bfloat16)],
        flops=10**9,
    )(own_queries, shared, *early)
    scored = (near_scores, near_values, mid_scores, mid_values)
    last_rows = last_row_count(seq_size, paired)
    leaf_flops = 8 * LEAF * (NEAR_ROWS + mid_rows + last_rows) * width
    share_2, share_3, far_keys, far_values, far_bias = kernel_call(
        functools.partial(leaves_kernel, seq_size, paired),
        "leaves",
        24,
        [VMEM] * 6,
        [
            (share + PAD, width),
            (share + PAD, width),
            (last_rows, width),
            (last_rows, width),
            jax.ShapeDtypeStruct((8, last_rows), jnp.float32),
        ],
        [wide],
        flops=leaf_flops,
    )(own_queries, *scored, late)
    share_0, share_1 = kernel_call(
        stays_kernel, "stays", 16, [VMEM] * 8, [(share, width)] * 2, [], flops=leaf_flops
    )(own_queries, *scored, far_keys, far_values, far_bias)
    columns = pltpu.VMEM((share, pair_width), jnp.bfloat16)
    part_3, part_2 = swap(share_3, 3, "head"), swap(share_2, 2, "head")
    (partial,) = kernel_call(
        begin_kernel,
        "begin",
        8,
        [VMEM] * 3,
        [jax.ShapeDtypeStruct((share, out_weight.shape[1]), jnp.float32)],
        [columns],
    )(share_0, swap(share_1, 1, "head"), out_weight)
    (mixed,) = kernel_call(
        project_kernel, "project", 8, [VMEM] * 4, [(share, out_weight.shape[1])], [columns]
    )(partial, part_3, part_2, out_weight)
    return mixed


def solution(mesh):
    in_specs = (P("seq", "head"), P("seq", "head"), P("seq", "head"), P())
    out_specs = P(("seq", "head"), None)
    return jax.shard_map(shards, mesh=mesh, in_specs=in_specs, out_specs=out_specs, check_vma=False)
```

```python
import functools
import math

import jax
import jax.numpy as jnp
from jax import lax
from jax.experimental import pallas as pl
from jax.experimental.pallas import tpu as pltpu
from jax.sharding import PartitionSpec as P

HD = 64
LEAF = 128
HALF = LEAF // 2
NEG = -math.inf


def average_pairs(rows, wide):
    count = rows.shape[0]
    halves = []
    for low in range(0, rows.shape[1], LEAF):
        wide[:count] = rows[:, low : low + LEAF].astype(jnp.float32)
        even = wide[pl.ds(0, count // 2, stride=2), :]
        odd = wide[pl.ds(1, count // 2, stride=2), :]
        halves.append((0.5 * (even + odd)).astype(jnp.bfloat16))
    return jnp.concatenate(halves, axis=1)


def pack_kernel(far_shares, queries, keys, values, own_queries, own, inner, outer, quarter, wide, arrived):
    width = keys.shape[1]
    copies = [
        pltpu.make_async_copy(keys, own.at[:, :width], arrived.at[0]),
        pltpu.make_async_copy(values, own.at[:, width:], arrived.at[1]),
        pltpu.make_async_copy(queries, own_queries, arrived.at[2]),
    ]
    for copy in copies:
        copy.start()
    me = lax.axis_index("seq")
    odd = me & 1
    for copy in copies:
        copy.wait()
    rows = own[...]
    low, high = rows[:LEAF], rows[LEAF:]
    level_one = average_pairs(rows, wide)
    level_two = average_pairs(level_one, wide)
    first, second = level_one[:HALF], level_one[HALF:]
    inner[:LEAF] = jnp.where(odd == 1, low, high)
    inner[LEAF:] = jnp.where(odd == 1, second, first)
    outer[:LEAF] = jnp.where(odd == 1, high, low)
    outer[LEAF:] = jnp.where(odd == 1, first, second)
    if far_shares:
        for peer in range(quarter.shape[0]):
            quarter[peer] = level_two
    else:
        quarter[...] = level_two


def join_kernel(theirs, quarter, upward, downward, eighth, wide):
    me = lax.axis_index("seq")
    odd = me & 1
    first = jnp.where(odd == 1, theirs[...], quarter[...])
    second = jnp.where(odd == 1, quarter[...], theirs[...])
    level_three = average_pairs(jnp.concatenate([first, second], axis=0), wide)
    upward[...] = jnp.where(me >= 6, level_three, first)
    downward[...] = jnp.where(me < 2, level_three, second)
    eighth[...] = level_three


NEAR_ROWS = 4 * LEAF
PAD = 16


def last_row_count(seq_size, paired):
    if paired:
        return HALF
    rows = 0
    for far in range(1, seq_size.bit_length() - 1):
        if seq_size >> far == 2:
            rows += LEAF
        elif far == 1:
            rows += 3 * HALF
        else:
            rows += 2 * LEAF
    return rows


def bias_of(valid):
    return jnp.where(valid, jnp.float32(0.0), jnp.float32(NEG))


def gathered_pieces(seq_size, far_rows, wide):
    me = lax.axis_index("seq")
    pieces = []
    for far in range(1, seq_size.bit_length() - 1):
        span = 1 << far
        group = me >> far
        parity = (me >> (far - 1)) & 1
        blocks = seq_size >> far

        def block(number, span=span, far=far):
            found = far_rows[pl.ds(number * span, span)].reshape(span * HALF, far_rows.shape[2])
            for _ in range(far - 1):
                found = average_pairs(found, wide)
            return found

        if blocks == 2:
            rows = block(1 - group)
            first = bias_of((group == 1) | (parity == 0))
            second = bias_of((group == 0) | (parity == 1))
            pieces += [(rows[:HALF], first), (rows[HALF:], second)]
        elif far == 1:
            third = jnp.where(parity == 0, me + 3, me - 3)
            for peer in (me - 2, me + 2, third):
                ok = (peer >= 0) & (peer < seq_size)
                pieces.append((far_rows[jnp.clip(peer, 0, seq_size - 1)], bias_of(ok)))
        else:
            lower = block(jnp.maximum(group - 1, 0))
            upper = block(jnp.minimum(group + 1, blocks - 1))
            has_lower, has_upper = group >= 1, group + 1 < blocks
            pieces += [
                (lower[:HALF], bias_of(has_lower)),
                (lower[HALF:], bias_of(has_lower & (parity == 1))),
                (upper[:HALF], bias_of(has_upper & (parity == 0))),
                (upper[HALF:], bias_of(has_upper)),
            ]
    return pieces


def early_pieces(beside, lower, eighth):
    me = lax.axis_index("seq")
    has_beside = jnp.where((me & 1) == 1, me >= 2, me < 6)
    return [(beside, bias_of(has_beside)), (lower, None), (eighth, None)]


def place(pieces, values, keys):
    at = 0
    width = values.shape[1]
    total_rows = values.shape[0]
    position = lax.broadcasted_iota(jnp.int32, (1, total_rows), 1)
    bias = jnp.zeros((1, total_rows), jnp.float32)
    for rows, value in pieces:
        count = rows.shape[0]
        keys[at : at + count] = rows[:, :width]
        values[at : at + count] = rows[:, width:]
        if value is not None:
            bias = jnp.where((position >= at) & (position < at + count), value, bias)
        at += count
    return bias


def split_heads(rows):
    first_head = lax.broadcasted_iota(jnp.int32, (1, rows.shape[1]), 1) < HD
    none = jnp.zeros_like(rows)
    return jnp.concatenate(
        [jnp.where(first_head, rows, none), jnp.where(first_head, none, rows)], axis=0
    )


def scores_of(queries, keys):
    return lax.dot_general(
        queries, keys[...], (((1,), (1,)), ((), ())), preferred_element_type=jnp.float32
    )


def near_kernel(seq_size, queries, own, inner, outer, *rest):
    *beside, scores, values, shared, keys, wide = rest
    me = lax.axis_index("seq")
    odd = me & 1
    from_inner, from_outer = inner[...], outer[...]
    before = jnp.where(odd == 1, from_inner, from_outer)
    after = jnp.where(odd == 1, from_outer, from_inner)
    edge_before, edge_after = before[:LEAF], after[:LEAF]
    far_half_after = after[LEAF:]
    shared[:HALF] = before[LEAF:]
    for rows in beside:
        shared[HALF:] = rows[...]
    near_half_before = average_pairs(edge_before, wide)
    near_half_after = average_pairs(edge_after, wide)
    has_before, has_after = bias_of(me >= 1), bias_of(me + 1 < seq_size)
    for leaf in range(2):
        if leaf == 0:
            near = [
                (edge_before, has_before),
                (own[...], None),
                (near_half_after, has_after),
                (far_half_after, has_after),
            ]
        else:
            near = [
                (own[...], None),
                (edge_after, has_after),
                (near_half_before, has_before),
                (far_half_after, has_after),
            ]
        bias = place(near, values.at[leaf], keys)
        rows = split_heads(queries[leaf * LEAF : (leaf + 1) * LEAF])
        scores[leaf] = scores_of(rows, keys) + bias


def mid_kernel(queries, shared, *rest):
    *early, scores, values, keys = rest
    pieces = [(shared[:HALF], bias_of(lax.axis_index("seq") >= 1))]
    if early:
        pieces += early_pieces(shared[HALF:], *early)
    bias = place(pieces, values, keys)
    for leaf in range(2):
        rows = split_heads(queries[leaf * LEAF : (leaf + 1) * LEAF])
        scores[leaf] = scores_of(rows, keys) + bias


def attend_leaf(leaf, queries, scored, keys, values, bias, same, other):
    first_head = lax.broadcasted_iota(jnp.int32, (1, values.shape[1]), 1) < HD
    exponent = math.log2(math.e) / math.sqrt(HD)
    rows = split_heads(queries[pl.ds(pl.multiple_of(leaf * LEAF, LEAF), LEAF)])
    near_scores, near_values, mid_scores, mid_values = scored
    parts = [
        (near_scores[leaf], near_values[leaf]),
        (mid_scores[leaf], mid_values[...]),
        (scores_of(rows, keys) + bias, values[...]),
    ]
    peak = functools.reduce(
        jnp.maximum, [jnp.max(scores, axis=1, keepdims=True) for scores, _ in parts]
    )
    total, numer = 0.0, 0.0
    for scores, part_values in parts:
        weights = jnp.exp2((scores - peak) * exponent)
        total = total + jnp.sum(weights, axis=1, keepdims=True)
        numer = numer + jnp.dot(
            weights.astype(jnp.bfloat16), part_values, preferred_element_type=jnp.float32
        )
    mean = numer / total
    attended = jnp.where(first_head, mean[:LEAF], mean[LEAF:]).astype(jnp.bfloat16)
    second = (lax.axis_index("head") & 1) == 1
    same[:HALF] = jnp.where(second, attended[HALF:], attended[:HALF])
    other[:HALF] = jnp.where(second, attended[:HALF], attended[HALF:])


def leaves_kernel(seq_size, paired, queries, near_scores, near_values, mid_scores, mid_values, *rest):
    late, same, other, keys, values, bias, wide = rest
    pieces = [(late, None)] if paired else gathered_pieces(seq_size, late, wide)
    bias[...] = jnp.broadcast_to(place(pieces, values, keys), bias.shape)
    leaf = (lax.axis_index("head") >> 1) ^ 1
    scored = (near_scores, near_values, mid_scores, mid_values)
    attend_leaf(leaf, queries, scored, keys, values, bias[:1], same, other)
    for share in (same, other):
        share[HALF:] = jnp.zeros((PAD, share.shape[1]), share.dtype)


def stays_kernel(
    queries, near_scores, near_values, mid_scores, mid_values, keys, values, bias, same, other
):
    leaf = lax.axis_index("head") >> 1
    scored = (near_scores, near_values, mid_scores, mid_values)
    attend_leaf(leaf, queries, scored, keys, values, bias[:1], same, other)


def side_by_side(same, other, rows, columns):
    second = (lax.axis_index("head") & 1) == 1
    width = same.shape[1]
    columns[:, :width] = jnp.where(second, other[:rows], same[:rows])
    columns[:, width:] = jnp.where(second, same[:rows], other[:rows])
    return columns[...]


def chip_rows(weight, chip, count):
    return weight[pl.ds(pl.multiple_of(chip * count, count), count)]


def begin_kernel(same, other, weight, partial, columns):
    chip = lax.axis_index("head") >> 1
    shares = side_by_side(same, other, partial.shape[0], columns)
    partial[...] = jnp.dot(
        shares, chip_rows(weight, chip, columns.shape[1]), preferred_element_type=jnp.float32
    )


def project_kernel(partial, other, same, weight, mixed, columns, held, sent):
    chip = (lax.axis_index("head") >> 1) ^ 1
    count, width = partial.shape
    shares = side_by_side(same, other, count, columns)
    rows = pl.ds(pl.multiple_of(chip * columns.shape[1], columns.shape[1]), columns.shape[1])
    copies = []
    for half in range(2):
        span = slice(half * width // 2, (half + 1) * width // 2)
        total = partial[:, span] + jnp.dot(
            shares, weight[rows, span], preferred_element_type=jnp.float32
        )
        held[:, span] = total.astype(mixed.dtype)
        copies.append(pltpu.make_async_copy(held.at[:, span], mixed.at[:, span], sent.at[half]))
        copies[-1].start()
    for copy in copies:
        copy.wait()


VMEM = pl.BlockSpec(memory_space=pltpu.VMEM)
HBM = pl.BlockSpec(memory_space=pltpu.HBM)


def kernel_call(body, name, megabytes, ins, outs, scratch, flops=0):
    shapes = tuple(
        out if isinstance(out, jax.ShapeDtypeStruct) else jax.ShapeDtypeStruct(out, jnp.bfloat16)
        for out in outs
    )
    return pl.pallas_call(
        body,
        out_shape=shapes,
        in_specs=ins,
        out_specs=(VMEM,) * len(outs),
        scratch_shapes=scratch,
        compiler_params=pltpu.CompilerParams(vmem_limit_bytes=megabytes << 20),
        cost_estimate=pl.CostEstimate(flops=flops, bytes_accessed=1 << 20, transcendentals=0),
        name=name,
    )


def shards(queries, keys, values, out_weight):
    tokens, width = queries.shape
    seq_size = lax.axis_size("seq")
    head_size = lax.axis_size("head")
    pair_width = 2 * width
    paired = seq_size == 8
    wide_rows = 2 * LEAF if paired else max(2 * LEAF, seq_size // 2 * HALF)
    wide = pltpu.VMEM((wide_rows, width), jnp.float32)

    def swap(array, bit, axis="seq"):
        return lax.ppermute(array, axis, [(i, i ^ bit) for i in range(lax.axis_size(axis))])

    own_queries, own, inner, outer, quarter = kernel_call(
        functools.partial(pack_kernel, not paired),
        "pack",
        16,
        [HBM] * 3,
        [
            (tokens, width),
            (tokens, pair_width),
            (LEAF + HALF, pair_width),
            (LEAF + HALF, pair_width),
            (HALF, pair_width) if paired else (seq_size, HALF, pair_width),
        ],
        [wide, pltpu.SemaphoreType.DMA((3,))],
    )(*(pltpu.with_memory_space_constraint(array, pltpu.HBM) for array in (queries, keys, values)))
    inner = swap(inner, 1)

    def to_spans(array, targets):
        return lax.ppermute(
            array,
            ("seq", "head"),
            [
                (s * head_size + h, t * head_size + (h if s != t else h ^ 1))
                for s, t in enumerate(targets)
                for h in range(head_size)
            ],
        )

    last = seq_size - 1
    outer = to_spans(outer, [s if s in (0, last) else s + 1 if s & 1 else s - 1 for s in range(seq_size)])
    if paired:
        upward, downward, eighth = kernel_call(
            join_kernel,
            "join",
            8,
            [VMEM] * 2,
            [(HALF, pair_width)] * 3,
            [wide],
            flops=2 * 10**9,
        )(swap(quarter, 1), quarter)
        shift = [(i, (i + 2) % seq_size) for i in range(seq_size)]
        cycle = [(i, i + 2 if i & 1 else i - 2) for i in range(1, seq_size - 1)]
        cycle += [(0, 1), (seq_size - 1, seq_size - 2)]
        beside = (lax.ppermute(quarter, "seq", cycle),)
        early = (lax.ppermute(upward, "seq", shift), swap(eighth, 4))
        late = lax.ppermute(downward, "seq", [(target, source) for source, target in shift])
    else:
        beside, early = (), ()
        late = lax.all_to_all(quarter, "seq", split_axis=0, concat_axis=0)
    share = tokens // head_size
    near_scores, near_values, shared = kernel_call(
        functools.partial(near_kernel, seq_size),
        "near",
        16,
        [VMEM] * (4 + len(beside)),
        [
            jax.ShapeDtypeStruct((2, 2 * LEAF, NEAR_ROWS), jnp.float32),
            (2, NEAR_ROWS, width),
            (HALF * (1 + len(beside)), pair_width),
        ],
        [pltpu.VMEM((NEAR_ROWS, width), jnp.bfloat16), wide],
        flops=8 * LEAF * NEAR_ROWS * width,
    )(own_queries, own, inner, outer, *beside)
    mid_rows = 4 * HALF if paired else HALF
    mid_scores, mid_values = kernel_call(
        mid_kernel,
        "mid",
        8,
        [VMEM] * (2 + len(early)),
        [jax.ShapeDtypeStruct((2, 2 * LEAF, mid_rows), jnp.float32), (mid_rows, width)],
        [pltpu.VMEM((mid_rows, width), jnp.bfloat16)],
        flops=10**9,
    )(own_queries, shared, *early)
    scored = (near_scores, near_values, mid_scores, mid_values)
    last_rows = last_row_count(seq_size, paired)
    leaf_flops = 8 * LEAF * (NEAR_ROWS + mid_rows + last_rows) * width
    share_2, share_3, far_keys, far_values, far_bias = kernel_call(
        functools.partial(leaves_kernel, seq_size, paired),
        "leaves",
        24,
        [VMEM] * 6,
        [
            (share + PAD, width),
            (share + PAD, width),
            (last_rows, width),
            (last_rows, width),
            jax.ShapeDtypeStruct((8, last_rows), jnp.float32),
        ],
        [wide],
        flops=leaf_flops,
    )(own_queries, *scored, late)
    share_0, share_1 = kernel_call(
        stays_kernel, "stays", 16, [VMEM] * 8, [(share, width)] * 2, [], flops=leaf_flops
    )(own_queries, *scored, far_keys, far_values, far_bias)
    columns = pltpu.VMEM((share, pair_width), jnp.bfloat16)
    part_3, part_2 = swap(share_3, 3, "head"), swap(share_2, 2, "head")
    (partial,) = kernel_call(
        begin_kernel,
        "begin",
        8,
        [VMEM] * 3,
        [jax.ShapeDtypeStruct((share, out_weight.shape[1]), jnp.float32)],
        [columns],
    )(share_0, swap(share_1, 1, "head"), out_weight)
    out_shape = (share, out_weight.shape[1])
    return pl.pallas_call(
        project_kernel,
        out_shape=jax.ShapeDtypeStruct(out_shape, jnp.bfloat16),
        in_specs=[VMEM] * 4,
        out_specs=HBM,
        scratch_shapes=[
            columns,
            pltpu.VMEM(out_shape, jnp.bfloat16),
            pltpu.SemaphoreType.DMA((2,)),
        ],
        compiler_params=pltpu.CompilerParams(vmem_limit_bytes=8 << 20),
        name="project",
    )(partial, part_3, part_2, out_weight)


def solution(mesh):
    in_specs = (P("seq", "head"), P("seq", "head"), P("seq", "head"), P())
    out_specs = P(("seq", "head"), None)
    return jax.shard_map(shards, mesh=mesh, in_specs=in_specs, out_specs=out_specs, check_vma=False)
```

```python
import functools
import math

import jax
import jax.numpy as jnp
from jax import lax
from jax.experimental import pallas as pl
from jax.experimental.pallas import tpu as pltpu
from jax.sharding import PartitionSpec as P

HD = 64
LEAF = 128
HALF = LEAF // 2
NEG = -math.inf


def average_pairs(rows, wide):
    count = rows.shape[0]
    halves = []
    for low in range(0, rows.shape[1], LEAF):
        wide[:count] = rows[:, low : low + LEAF].astype(jnp.float32)
        even = wide[pl.ds(0, count // 2, stride=2), :]
        odd = wide[pl.ds(1, count // 2, stride=2), :]
        halves.append((0.5 * (even + odd)).astype(jnp.bfloat16))
    return jnp.concatenate(halves, axis=1)


def pack_kernel(far_shares, queries, keys, values, own_queries, own, inner, outer, quarter, wide, arrived):
    width = keys.shape[1]
    copies = [
        pltpu.make_async_copy(keys, own.at[:, :width], arrived.at[0]),
        pltpu.make_async_copy(values, own.at[:, width:], arrived.at[1]),
        pltpu.make_async_copy(queries, own_queries, arrived.at[2]),
    ]
    for copy in copies:
        copy.start()
    me = lax.axis_index("seq")
    odd = me & 1
    for copy in copies:
        copy.wait()
    rows = own[...]
    low, high = rows[:LEAF], rows[LEAF:]
    level_one = average_pairs(rows, wide)
    level_two = average_pairs(level_one, wide)
    first, second = level_one[:HALF], level_one[HALF:]
    inner[:LEAF] = jnp.where(odd == 1, low, high)
    inner[LEAF:] = jnp.where(odd == 1, second, first)
    outer[:LEAF] = jnp.where(odd == 1, high, low)
    outer[LEAF:] = jnp.where(odd == 1, first, second)
    if far_shares:
        for peer in range(quarter.shape[0]):
            quarter[peer] = level_two
    else:
        quarter[...] = level_two


def join_kernel(theirs, quarter, upward, downward, eighth, wide):
    me = lax.axis_index("seq")
    odd = me & 1
    first = jnp.where(odd == 1, theirs[...], quarter[...])
    second = jnp.where(odd == 1, quarter[...], theirs[...])
    level_three = average_pairs(jnp.concatenate([first, second], axis=0), wide)
    upward[...] = jnp.where(me >= 6, level_three, first)
    downward[...] = jnp.where(me < 2, level_three, second)
    eighth[...] = level_three


NEAR_ROWS = 4 * LEAF
PAD = 16


def last_row_count(seq_size, paired):
    if paired:
        return HALF
    rows = 0
    for far in range(1, seq_size.bit_length() - 1):
        if seq_size >> far == 2:
            rows += LEAF
        elif far == 1:
            rows += 3 * HALF
        else:
            rows += 2 * LEAF
    return rows


def bias_of(valid):
    return jnp.where(valid, jnp.float32(0.0), jnp.float32(NEG))


def gathered_pieces(seq_size, far_rows, wide):
    me = lax.axis_index("seq")
    pieces = []
    for far in range(1, seq_size.bit_length() - 1):
        span = 1 << far
        group = me >> far
        parity = (me >> (far - 1)) & 1
        blocks = seq_size >> far

        def block(number, span=span, far=far):
            found = far_rows[pl.ds(number * span, span)].reshape(span * HALF, far_rows.shape[2])
            for _ in range(far - 1):
                found = average_pairs(found, wide)
            return found

        if blocks == 2:
            rows = block(1 - group)
            first = bias_of((group == 1) | (parity == 0))
            second = bias_of((group == 0) | (parity == 1))
            pieces += [(rows[:HALF], first), (rows[HALF:], second)]
        elif far == 1:
            third = jnp.where(parity == 0, me + 3, me - 3)
            for peer in (me - 2, me + 2, third):
                ok = (peer >= 0) & (peer < seq_size)
                pieces.append((far_rows[jnp.clip(peer, 0, seq_size - 1)], bias_of(ok)))
        else:
            lower = block(jnp.maximum(group - 1, 0))
            upper = block(jnp.minimum(group + 1, blocks - 1))
            has_lower, has_upper = group >= 1, group + 1 < blocks
            pieces += [
                (lower[:HALF], bias_of(has_lower)),
                (lower[HALF:], bias_of(has_lower & (parity == 1))),
                (upper[:HALF], bias_of(has_upper & (parity == 0))),
                (upper[HALF:], bias_of(has_upper)),
            ]
    return pieces


def early_pieces(beside, lower, eighth):
    me = lax.axis_index("seq")
    has_beside = jnp.where((me & 1) == 1, me >= 2, me < 6)
    return [(beside, bias_of(has_beside)), (lower, None), (eighth, None)]


def place(pieces, values, keys):
    at = 0
    width = values.shape[1]
    total_rows = values.shape[0]
    position = lax.broadcasted_iota(jnp.int32, (1, total_rows), 1)
    bias = jnp.zeros((1, total_rows), jnp.float32)
    for rows, value in pieces:
        count = rows.shape[0]
        keys[at : at + count] = rows[:, :width]
        values[at : at + count] = rows[:, width:]
        if value is not None:
            bias = jnp.where((position >= at) & (position < at + count), value, bias)
        at += count
    return bias


def split_heads(rows):
    first_head = lax.broadcasted_iota(jnp.int32, (1, rows.shape[1]), 1) < HD
    none = jnp.zeros_like(rows)
    return jnp.concatenate(
        [jnp.where(first_head, rows, none), jnp.where(first_head, none, rows)], axis=0
    )


def scores_of(queries, keys):
    return lax.dot_general(
        queries, keys[...], (((1,), (1,)), ((), ())), preferred_element_type=jnp.float32
    )


def near_kernel(seq_size, queries, own, inner, outer, *rest):
    *beside, scores, values, shared, keys, wide = rest
    me = lax.axis_index("seq")
    odd = me & 1
    from_inner, from_outer = inner[...], outer[...]
    before = jnp.where(odd == 1, from_inner, from_outer)
    after = jnp.where(odd == 1, from_outer, from_inner)
    edge_before, edge_after = before[:LEAF], after[:LEAF]
    far_half_after = after[LEAF:]
    shared[:HALF] = before[LEAF:]
    for rows in beside:
        shared[HALF:] = rows[...]
    near_half_before = average_pairs(edge_before, wide)
    near_half_after = average_pairs(edge_after, wide)
    has_before, has_after = bias_of(me >= 1), bias_of(me + 1 < seq_size)
    for leaf in range(2):
        if leaf == 0:
            near = [
                (edge_before, has_before),
                (own[...], None),
                (near_half_after, has_after),
                (far_half_after, has_after),
            ]
        else:
            near = [
                (own[...], None),
                (edge_after, has_after),
                (near_half_before, has_before),
                (far_half_after, has_after),
            ]
        bias = place(near, values.at[leaf], keys)
        rows = split_heads(queries[leaf * LEAF : (leaf + 1) * LEAF])
        scores[leaf] = scores_of(rows, keys) + bias


def mid_kernel(queries, shared, *rest):
    *early, scores, values, keys = rest
    pieces = [(shared[:HALF], bias_of(lax.axis_index("seq") >= 1))]
    if early:
        pieces += early_pieces(shared[HALF:], *early)
    bias = place(pieces, values, keys)
    for leaf in range(2):
        rows = split_heads(queries[leaf * LEAF : (leaf + 1) * LEAF])
        scores[leaf] = scores_of(rows, keys) + bias


def attend_leaf(leaf, queries, scored, keys, values, bias, same, other):
    first_head = lax.broadcasted_iota(jnp.int32, (1, values.shape[1]), 1) < HD
    exponent = math.log2(math.e) / math.sqrt(HD)
    rows = split_heads(queries[pl.ds(pl.multiple_of(leaf * LEAF, LEAF), LEAF)])
    near_scores, near_values, mid_scores, mid_values = scored
    parts = [
        (near_scores[leaf], near_values[leaf]),
        (mid_scores[leaf], mid_values[...]),
        (scores_of(rows, keys) + bias, values[...]),
    ]
    peak = functools.reduce(
        jnp.maximum, [jnp.max(scores, axis=1, keepdims=True) for scores, _ in parts]
    )
    total, numer = 0.0, 0.0
    for scores, part_values in parts:
        weights = jnp.exp2((scores - peak) * exponent)
        total = total + jnp.sum(weights, axis=1, keepdims=True)
        numer = numer + jnp.dot(
            weights.astype(jnp.bfloat16), part_values, preferred_element_type=jnp.float32
        )
    own_numer = jnp.where(first_head, numer[:LEAF], numer[LEAF:])
    own_total = jnp.where(first_head, total[:LEAF], total[LEAF:])
    attended = (own_numer / own_total).astype(jnp.bfloat16)
    second = (lax.axis_index("head") & 1) == 1
    same[:HALF] = jnp.where(second, attended[HALF:], attended[:HALF])
    other[:HALF] = jnp.where(second, attended[:HALF], attended[HALF:])


def leaves_kernel(seq_size, paired, queries, near_scores, near_values, mid_scores, mid_values, *rest):
    late, same, other, keys, values, bias, wide = rest
    pieces = [(late, None)] if paired else gathered_pieces(seq_size, late, wide)
    bias[...] = jnp.broadcast_to(place(pieces, values, keys), bias.shape)
    leaf = (lax.axis_index("head") >> 1) ^ 1
    scored = (near_scores, near_values, mid_scores, mid_values)
    attend_leaf(leaf, queries, scored, keys, values, bias[:1], same, other)
    for share in (same, other):
        share[HALF:] = jnp.zeros((PAD, share.shape[1]), share.dtype)


def stays_kernel(
    queries, near_scores, near_values, mid_scores, mid_values, keys, values, bias, same, other
):
    leaf = lax.axis_index("head") >> 1
    scored = (near_scores, near_values, mid_scores, mid_values)
    attend_leaf(leaf, queries, scored, keys, values, bias[:1], same, other)


def side_by_side(same, other, rows, columns):
    second = (lax.axis_index("head") & 1) == 1
    width = same.shape[1]
    columns[:, :width] = jnp.where(second, other[:rows], same[:rows])
    columns[:, width:] = jnp.where(second, same[:rows], other[:rows])
    return columns[...]


def chip_rows(weight, chip, count):
    return weight[pl.ds(pl.multiple_of(chip * count, count), count)]


def begin_kernel(same, other, weight, partial, columns):
    chip = lax.axis_index("head") >> 1
    shares = side_by_side(same, other, partial.shape[0], columns)
    partial[...] = jnp.dot(
        shares, chip_rows(weight, chip, columns.shape[1]), preferred_element_type=jnp.float32
    )


def project_kernel(partial, other, same, weight, mixed, columns):
    chip = (lax.axis_index("head") >> 1) ^ 1
    shares = side_by_side(same, other, partial.shape[0], columns)
    total = partial[...] + jnp.dot(
        shares, chip_rows(weight, chip, columns.shape[1]), preferred_element_type=jnp.float32
    )
    mixed[...] = total.astype(mixed.dtype)


VMEM = pl.BlockSpec(memory_space=pltpu.VMEM)
HBM = pl.BlockSpec(memory_space=pltpu.HBM)


def kernel_call(body, name, megabytes, ins, outs, scratch, flops=0):
    shapes = tuple(
        out if isinstance(out, jax.ShapeDtypeStruct) else jax.ShapeDtypeStruct(out, jnp.bfloat16)
        for out in outs
    )
    return pl.pallas_call(
        body,
        out_shape=shapes,
        in_specs=ins,
        out_specs=(VMEM,) * len(outs),
        scratch_shapes=scratch,
        compiler_params=pltpu.CompilerParams(vmem_limit_bytes=megabytes << 20),
        cost_estimate=pl.CostEstimate(flops=flops, bytes_accessed=1 << 20, transcendentals=0),
        name=name,
    )


def shards(queries, keys, values, out_weight):
    tokens, width = queries.shape
    seq_size = lax.axis_size("seq")
    head_size = lax.axis_size("head")
    pair_width = 2 * width
    paired = seq_size == 8
    wide_rows = 2 * LEAF if paired else max(2 * LEAF, seq_size // 2 * HALF)
    wide = pltpu.VMEM((wide_rows, width), jnp.float32)

    def swap(array, bit, axis="seq"):
        return lax.ppermute(array, axis, [(i, i ^ bit) for i in range(lax.axis_size(axis))])

    own_queries, own, inner, outer, quarter = kernel_call(
        functools.partial(pack_kernel, not paired),
        "pack",
        16,
        [HBM] * 3,
        [
            (tokens, width),
            (tokens, pair_width),
            (LEAF + HALF, pair_width),
            (LEAF + HALF, pair_width),
            (HALF, pair_width) if paired else (seq_size, HALF, pair_width),
        ],
        [wide, pltpu.SemaphoreType.DMA((3,))],
    )(*(pltpu.with_memory_space_constraint(array, pltpu.HBM) for array in (queries, keys, values)))
    inner = swap(inner, 1)

    def to_spans(array, targets):
        return lax.ppermute(
            array,
            ("seq", "head"),
            [
                (s * head_size + h, t * head_size + (h if s != t else h ^ 1))
                for s, t in enumerate(targets)
                for h in range(head_size)
            ],
        )

    last = seq_size - 1
    outer = to_spans(outer, [s if s in (0, last) else s + 1 if s & 1 else s - 1 for s in range(seq_size)])
    if paired:
        upward, downward, eighth = kernel_call(
            join_kernel,
            "join",
            8,
            [VMEM] * 2,
            [(HALF, pair_width)] * 3,
            [wide],
            flops=2 * 10**9,
        )(swap(quarter, 1), quarter)
        shift = [(i, (i + 2) % seq_size) for i in range(seq_size)]
        cycle = [(i, i + 2 if i & 1 else i - 2) for i in range(1, seq_size - 1)]
        cycle += [(0, 1), (seq_size - 1, seq_size - 2)]
        beside = (lax.ppermute(quarter, "seq", cycle),)
        early = (lax.ppermute(upward, "seq", shift), swap(eighth, 4))
        late = lax.ppermute(downward, "seq", [(target, source) for source, target in shift])
    else:
        beside, early = (), ()
        late = lax.all_to_all(quarter, "seq", split_axis=0, concat_axis=0)
    share = tokens // head_size
    near_scores, near_values, shared = kernel_call(
        functools.partial(near_kernel, seq_size),
        "near",
        16,
        [VMEM] * (4 + len(beside)),
        [
            jax.ShapeDtypeStruct((2, 2 * LEAF, NEAR_ROWS), jnp.float32),
            (2, NEAR_ROWS, width),
            (HALF * (1 + len(beside)), pair_width),
        ],
        [pltpu.VMEM((NEAR_ROWS, width), jnp.bfloat16), wide],
        flops=8 * LEAF * NEAR_ROWS * width,
    )(own_queries, own, inner, outer, *beside)
    mid_rows = 4 * HALF if paired else HALF
    mid_scores, mid_values = kernel_call(
        mid_kernel,
        "mid",
        8,
        [VMEM] * (2 + len(early)),
        [jax.ShapeDtypeStruct((2, 2 * LEAF, mid_rows), jnp.float32), (mid_rows, width)],
        [pltpu.VMEM((mid_rows, width), jnp.bfloat16)],
        flops=10**9,
    )(own_queries, shared, *early)
    scored = (near_scores, near_values, mid_scores, mid_values)
    last_rows = last_row_count(seq_size, paired)
    leaf_flops = 8 * LEAF * (NEAR_ROWS + mid_rows + last_rows) * width
    share_2, share_3, far_keys, far_values, far_bias = kernel_call(
        functools.partial(leaves_kernel, seq_size, paired),
        "leaves",
        24,
        [VMEM] * 6,
        [
            (share + PAD, width),
            (share + PAD, width),
            (last_rows, width),
            (last_rows, width),
            jax.ShapeDtypeStruct((8, last_rows), jnp.float32),
        ],
        [wide],
        flops=leaf_flops,
    )(own_queries, *scored, late)
    share_0, share_1 = kernel_call(
        stays_kernel, "stays", 16, [VMEM] * 8, [(share, width)] * 2, [], flops=leaf_flops
    )(own_queries, *scored, far_keys, far_values, far_bias)
    columns = pltpu.VMEM((share, pair_width), jnp.bfloat16)
    part_3, part_2 = swap(share_3, 3, "head"), swap(share_2, 2, "head")
    (partial,) = kernel_call(
        begin_kernel,
        "begin",
        8,
        [VMEM] * 3,
        [jax.ShapeDtypeStruct((share, out_weight.shape[1]), jnp.float32)],
        [columns],
    )(share_0, swap(share_1, 1, "head"), out_weight)
    (mixed,) = kernel_call(
        project_kernel, "project", 8, [VMEM] * 4, [(share, out_weight.shape[1])], [columns]
    )(partial, part_3, part_2, out_weight)
    return mixed


def solution(mesh):
    in_specs = (P("seq", "head"), P("seq", "head"), P("seq", "head"), P())
    out_specs = P(("seq", "head"), None)
    return jax.shard_map(shards, mesh=mesh, in_specs=in_specs, out_specs=out_specs, check_vma=False)
```

```python
import functools
import math

import jax
import jax.numpy as jnp
from jax import lax
from jax.experimental import pallas as pl
from jax.experimental.pallas import tpu as pltpu
from jax.sharding import PartitionSpec as P

HD = 64
LEAF = 128
HALF = LEAF // 2
NEG = -math.inf


def average_pairs(rows, wide):
    count = rows.shape[0]
    halves = []
    for low in range(0, rows.shape[1], LEAF):
        wide[:count] = rows[:, low : low + LEAF].astype(jnp.float32)
        even = wide[pl.ds(0, count // 2, stride=2), :]
        odd = wide[pl.ds(1, count // 2, stride=2), :]
        halves.append((0.5 * (even + odd)).astype(jnp.bfloat16))
    return jnp.concatenate(halves, axis=1)


def pack_kernel(far_shares, queries, keys, values, own_queries, own, level_one, quarter, wide, arrived):
    width = keys.shape[1]
    copies = [
        pltpu.make_async_copy(keys, own.at[:, :width], arrived.at[0]),
        pltpu.make_async_copy(values, own.at[:, width:], arrived.at[1]),
        pltpu.make_async_copy(queries, own_queries, arrived.at[2]),
    ]
    for copy in copies:
        copy.start()
    for copy in copies:
        copy.wait()
    level_one[...] = average_pairs(own[...], wide)
    level_two = average_pairs(level_one[...], wide)
    if far_shares:
        for peer in range(quarter.shape[0]):
            quarter[peer] = level_two
    else:
        quarter[...] = level_two


def edges_kernel(own, level_one, inner, outer):
    odd = lax.axis_index("seq") & 1
    low, high = own[:LEAF], own[LEAF:]
    first, second = level_one[:HALF], level_one[HALF:]
    inner[:LEAF] = jnp.where(odd == 1, low, high)
    inner[LEAF:] = jnp.where(odd == 1, second, first)
    outer[:LEAF] = jnp.where(odd == 1, high, low)
    outer[LEAF:] = jnp.where(odd == 1, first, second)


def join_kernel(theirs, quarter, upward, downward, eighth, wide):
    me = lax.axis_index("seq")
    odd = me & 1
    first = jnp.where(odd == 1, theirs[...], quarter[...])
    second = jnp.where(odd == 1, quarter[...], theirs[...])
    level_three = average_pairs(jnp.concatenate([first, second], axis=0), wide)
    upward[...] = jnp.where(me >= 6, level_three, first)
    downward[...] = jnp.where(me < 2, level_three, second)
    eighth[...] = level_three


NEAR_ROWS = 4 * LEAF
PAD = 16


def last_row_count(seq_size, paired):
    if paired:
        return HALF
    rows = 0
    for far in range(1, seq_size.bit_length() - 1):
        if seq_size >> far == 2:
            rows += LEAF
        elif far == 1:
            rows += 3 * HALF
        else:
            rows += 2 * LEAF
    return rows


def bias_of(valid):
    return jnp.where(valid, jnp.float32(0.0), jnp.float32(NEG))


def gathered_pieces(seq_size, far_rows, wide):
    me = lax.axis_index("seq")
    pieces = []
    for far in range(1, seq_size.bit_length() - 1):
        span = 1 << far
        group = me >> far
        parity = (me >> (far - 1)) & 1
        blocks = seq_size >> far

        def block(number, span=span, far=far):
            found = far_rows[pl.ds(number * span, span)].reshape(span * HALF, far_rows.shape[2])
            for _ in range(far - 1):
                found = average_pairs(found, wide)
            return found

        if blocks == 2:
            rows = block(1 - group)
            first = bias_of((group == 1) | (parity == 0))
            second = bias_of((group == 0) | (parity == 1))
            pieces += [(rows[:HALF], first), (rows[HALF:], second)]
        elif far == 1:
            third = jnp.where(parity == 0, me + 3, me - 3)
            for peer in (me - 2, me + 2, third):
                ok = (peer >= 0) & (peer < seq_size)
                pieces.append((far_rows[jnp.clip(peer, 0, seq_size - 1)], bias_of(ok)))
        else:
            lower = block(jnp.maximum(group - 1, 0))
            upper = block(jnp.minimum(group + 1, blocks - 1))
            has_lower, has_upper = group >= 1, group + 1 < blocks
            pieces += [
                (lower[:HALF], bias_of(has_lower)),
                (lower[HALF:], bias_of(has_lower & (parity == 1))),
                (upper[:HALF], bias_of(has_upper & (parity == 0))),
                (upper[HALF:], bias_of(has_upper)),
            ]
    return pieces


def early_pieces(beside, lower, eighth):
    me = lax.axis_index("seq")
    has_beside = jnp.where((me & 1) == 1, me >= 2, me < 6)
    return [(beside, bias_of(has_beside)), (lower, None), (eighth, None)]


def place(pieces, values, keys):
    at = 0
    width = values.shape[1]
    total_rows = values.shape[0]
    position = lax.broadcasted_iota(jnp.int32, (1, total_rows), 1)
    bias = jnp.zeros((1, total_rows), jnp.float32)
    for rows, value in pieces:
        count = rows.shape[0]
        keys[at : at + count] = rows[:, :width]
        values[at : at + count] = rows[:, width:]
        if value is not None:
            bias = jnp.where((position >= at) & (position < at + count), value, bias)
        at += count
    return bias


def split_heads(rows):
    first_head = lax.broadcasted_iota(jnp.int32, (1, rows.shape[1]), 1) < HD
    none = jnp.zeros_like(rows)
    return jnp.concatenate(
        [jnp.where(first_head, rows, none), jnp.where(first_head, none, rows)], axis=0
    )


def scores_of(queries, keys):
    return lax.dot_general(
        queries, keys[...], (((1,), (1,)), ((), ())), preferred_element_type=jnp.float32
    )


def near_kernel(seq_size, queries, own, inner, outer, *rest):
    *beside, scores, values, shared, keys, wide = rest
    me = lax.axis_index("seq")
    odd = me & 1
    from_inner, from_outer = inner[...], outer[...]
    before = jnp.where(odd == 1, from_inner, from_outer)
    after = jnp.where(odd == 1, from_outer, from_inner)
    edge_before, edge_after = before[:LEAF], after[:LEAF]
    far_half_after = after[LEAF:]
    shared[:HALF] = before[LEAF:]
    for rows in beside:
        shared[HALF:] = rows[...]
    near_half_before = average_pairs(edge_before, wide)
    near_half_after = average_pairs(edge_after, wide)
    has_before, has_after = bias_of(me >= 1), bias_of(me + 1 < seq_size)
    for leaf in range(2):
        if leaf == 0:
            near = [
                (edge_before, has_before),
                (own[...], None),
                (near_half_after, has_after),
                (far_half_after, has_after),
            ]
        else:
            near = [
                (own[...], None),
                (edge_after, has_after),
                (near_half_before, has_before),
                (far_half_after, has_after),
            ]
        bias = place(near, values.at[leaf], keys)
        rows = split_heads(queries[leaf * LEAF : (leaf + 1) * LEAF])
        scores[leaf] = scores_of(rows, keys) + bias


def mid_kernel(queries, shared, *rest):
    *early, scores, values, keys = rest
    pieces = [(shared[:HALF], bias_of(lax.axis_index("seq") >= 1))]
    if early:
        pieces += early_pieces(shared[HALF:], *early)
    bias = place(pieces, values, keys)
    for leaf in range(2):
        rows = split_heads(queries[leaf * LEAF : (leaf + 1) * LEAF])
        scores[leaf] = scores_of(rows, keys) + bias


def attend_leaf(leaf, queries, scored, keys, values, bias, same, other):
    first_head = lax.broadcasted_iota(jnp.int32, (1, values.shape[1]), 1) < HD
    exponent = math.log2(math.e) / math.sqrt(HD)
    rows = split_heads(queries[pl.ds(pl.multiple_of(leaf * LEAF, LEAF), LEAF)])
    near_scores, near_values, mid_scores, mid_values = scored
    parts = [
        (near_scores[leaf], near_values[leaf]),
        (mid_scores[leaf], mid_values[...]),
        (scores_of(rows, keys) + bias, values[...]),
    ]
    peak = functools.reduce(
        jnp.maximum, [jnp.max(scores, axis=1, keepdims=True) for scores, _ in parts]
    )
    total, numer = 0.0, 0.0
    for scores, part_values in parts:
        weights = jnp.exp2((scores - peak) * exponent)
        total = total + jnp.sum(weights, axis=1, keepdims=True)
        numer = numer + jnp.dot(
            weights.astype(jnp.bfloat16), part_values, preferred_element_type=jnp.float32
        )
    own_numer = jnp.where(first_head, numer[:LEAF], numer[LEAF:])
    own_total = jnp.where(first_head, total[:LEAF], total[LEAF:])
    attended = (own_numer / own_total).astype(jnp.bfloat16)
    second = (lax.axis_index("head") & 1) == 1
    same[:HALF] = jnp.where(second, attended[HALF:], attended[:HALF])
    other[:HALF] = jnp.where(second, attended[:HALF], attended[HALF:])


def leaves_kernel(seq_size, paired, queries, near_scores, near_values, mid_scores, mid_values, *rest):
    late, same, other, keys, values, bias, wide = rest
    pieces = [(late, None)] if paired else gathered_pieces(seq_size, late, wide)
    bias[...] = jnp.broadcast_to(place(pieces, values, keys), bias.shape)
    leaf = (lax.axis_index("head") >> 1) ^ 1
    scored = (near_scores, near_values, mid_scores, mid_values)
    attend_leaf(leaf, queries, scored, keys, values, bias[:1], same, other)
    for share in (same, other):
        share[HALF:] = jnp.zeros((PAD, share.shape[1]), share.dtype)


def stays_kernel(
    queries, near_scores, near_values, mid_scores, mid_values, keys, values, bias, same, other
):
    leaf = lax.axis_index("head") >> 1
    scored = (near_scores, near_values, mid_scores, mid_values)
    attend_leaf(leaf, queries, scored, keys, values, bias[:1], same, other)


def side_by_side(same, other, rows, columns):
    second = (lax.axis_index("head") & 1) == 1
    width = same.shape[1]
    columns[:, :width] = jnp.where(second, other[:rows], same[:rows])
    columns[:, width:] = jnp.where(second, same[:rows], other[:rows])
    return columns[...]


def chip_rows(weight, chip, count):
    return weight[pl.ds(pl.multiple_of(chip * count, count), count)]


def begin_kernel(same, other, weight, partial, columns):
    chip = lax.axis_index("head") >> 1
    shares = side_by_side(same, other, partial.shape[0], columns)
    partial[...] = jnp.dot(
        shares, chip_rows(weight, chip, columns.shape[1]), preferred_element_type=jnp.float32
    )


def project_kernel(partial, other, same, weight, mixed, columns):
    chip = (lax.axis_index("head") >> 1) ^ 1
    shares = side_by_side(same, other, partial.shape[0], columns)
    total = partial[...] + jnp.dot(
        shares, chip_rows(weight, chip, columns.shape[1]), preferred_element_type=jnp.float32
    )
    mixed[...] = total.astype(mixed.dtype)


VMEM = pl.BlockSpec(memory_space=pltpu.VMEM)
HBM = pl.BlockSpec(memory_space=pltpu.HBM)


def kernel_call(body, name, megabytes, ins, outs, scratch, flops=0):
    shapes = tuple(
        out if isinstance(out, jax.ShapeDtypeStruct) else jax.ShapeDtypeStruct(out, jnp.bfloat16)
        for out in outs
    )
    return pl.pallas_call(
        body,
        out_shape=shapes,
        in_specs=ins,
        out_specs=(VMEM,) * len(outs),
        scratch_shapes=scratch,
        compiler_params=pltpu.CompilerParams(vmem_limit_bytes=megabytes << 20),
        cost_estimate=pl.CostEstimate(flops=flops, bytes_accessed=1 << 20, transcendentals=0),
        name=name,
    )


def shards(queries, keys, values, out_weight):
    tokens, width = queries.shape
    seq_size = lax.axis_size("seq")
    head_size = lax.axis_size("head")
    pair_width = 2 * width
    paired = seq_size == 8
    wide_rows = 2 * LEAF if paired else max(2 * LEAF, seq_size // 2 * HALF)
    wide = pltpu.VMEM((wide_rows, width), jnp.float32)

    def swap(array, bit, axis="seq"):
        return lax.ppermute(array, axis, [(i, i ^ bit) for i in range(lax.axis_size(axis))])

    own_queries, own, level_one, quarter = kernel_call(
        functools.partial(pack_kernel, not paired),
        "pack",
        16,
        [HBM] * 3,
        [
            (tokens, width),
            (tokens, pair_width),
            (LEAF, pair_width),
            (HALF, pair_width) if paired else (seq_size, HALF, pair_width),
        ],
        [wide, pltpu.SemaphoreType.DMA((3,))],
    )(*(pltpu.with_memory_space_constraint(array, pltpu.HBM) for array in (queries, keys, values)))
    inner, outer = kernel_call(
        edges_kernel, "edges", 8, [VMEM] * 2, [(LEAF + HALF, pair_width)] * 2, []
    )(own, level_one)
    inner = swap(inner, 1)

    def to_spans(array, targets):
        return lax.ppermute(
            array,
            ("seq", "head"),
            [
                (s * head_size + h, t * head_size + (h if s != t else h ^ 1))
                for s, t in enumerate(targets)
                for h in range(head_size)
            ],
        )

    last = seq_size - 1
    outer = to_spans(outer, [s if s in (0, last) else s + 1 if s & 1 else s - 1 for s in range(seq_size)])
    if paired:
        upward, downward, eighth = kernel_call(
            join_kernel,
            "join",
            8,
            [VMEM] * 2,
            [(HALF, pair_width)] * 3,
            [wide],
            flops=2 * 10**9,
        )(swap(quarter, 1), quarter)
        shift = [(i, (i + 2) % seq_size) for i in range(seq_size)]
        cycle = [(i, i + 2 if i & 1 else i - 2) for i in range(1, seq_size - 1)]
        cycle += [(0, 1), (seq_size - 1, seq_size - 2)]
        beside = (lax.ppermute(quarter, "seq", cycle),)
        early = (lax.ppermute(upward, "seq", shift), swap(eighth, 4))
        late = lax.ppermute(downward, "seq", [(target, source) for source, target in shift])
    else:
        beside, early = (), ()
        late = lax.all_to_all(quarter, "seq", split_axis=0, concat_axis=0)
    share = tokens // head_size
    near_scores, near_values, shared = kernel_call(
        functools.partial(near_kernel, seq_size),
        "near",
        16,
        [VMEM] * (4 + len(beside)),
        [
            jax.ShapeDtypeStruct((2, 2 * LEAF, NEAR_ROWS), jnp.float32),
            (2, NEAR_ROWS, width),
            (HALF * (1 + len(beside)), pair_width),
        ],
        [pltpu.VMEM((NEAR_ROWS, width), jnp.bfloat16), wide],
        flops=8 * LEAF * NEAR_ROWS * width,
    )(own_queries, own, inner, outer, *beside)
    mid_rows = 4 * HALF if paired else HALF
    mid_scores, mid_values = kernel_call(
        mid_kernel,
        "mid",
        8,
        [VMEM] * (2 + len(early)),
        [jax.ShapeDtypeStruct((2, 2 * LEAF, mid_rows), jnp.float32), (mid_rows, width)],
        [pltpu.VMEM((mid_rows, width), jnp.bfloat16)],
        flops=10**9,
    )(own_queries, shared, *early)
    scored = (near_scores, near_values, mid_scores, mid_values)
    last_rows = last_row_count(seq_size, paired)
    leaf_flops = 8 * LEAF * (NEAR_ROWS + mid_rows + last_rows) * width
    share_2, share_3, far_keys, far_values, far_bias = kernel_call(
        functools.partial(leaves_kernel, seq_size, paired),
        "leaves",
        24,
        [VMEM] * 6,
        [
            (share + PAD, width),
            (share + PAD, width),
            (last_rows, width),
            (last_rows, width),
            jax.ShapeDtypeStruct((8, last_rows), jnp.float32),
        ],
        [wide],
        flops=leaf_flops,
    )(own_queries, *scored, late)
    share_0, share_1 = kernel_call(
        stays_kernel, "stays", 16, [VMEM] * 8, [(share, width)] * 2, [], flops=leaf_flops
    )(own_queries, *scored, far_keys, far_values, far_bias)
    columns = pltpu.VMEM((share, pair_width), jnp.bfloat16)
    part_3, part_2 = swap(share_3, 3, "head"), swap(share_2, 2, "head")
    (partial,) = kernel_call(
        begin_kernel,
        "begin",
        8,
        [VMEM] * 3,
        [jax.ShapeDtypeStruct((share, out_weight.shape[1]), jnp.float32)],
        [columns],
    )(share_0, swap(share_1, 1, "head"), out_weight)
    (mixed,) = kernel_call(
        project_kernel, "project", 8, [VMEM] * 4, [(share, out_weight.shape[1])], [columns]
    )(partial, part_3, part_2, out_weight)
    return mixed


def solution(mesh):
    in_specs = (P("seq", "head"), P("seq", "head"), P("seq", "head"), P())
    out_specs = P(("seq", "head"), None)
    return jax.shard_map(shards, mesh=mesh, in_specs=in_specs, out_specs=out_specs, check_vma=False)
```
